32 devices in a mesh: tm: 4 (over x, core), tile: 8 (over z, y).
Axes of the slice: x: 2, y: 2, z: 4, core: 2. Of those that a mesh axis runs over, the one named last changes fastest.
Arguments:
- advect_east: float32 [4, 2, 96, 1440], P('tm', None, 'tile'), may hold values from -0.15 to 0.15
- advect_north: float32 [4, 2, 96, 1440], P('tm', None, 'tile'), may hold values from -0.15 to 0.15
- diffusion: float32 [4, 2, 96, 1440], P('tm', None, 'tile'), may hold values from 0.06 to 0.22
- background_var: float32 [4, 4, 2, 96, 1440], P('tm', None, None, 'tile'), may hold values from 0.3 to 3
- obs_cell: int32 [4, 8, 256], P('tm', 'tile'), may hold values from 0 to 138239
- obs_value: float32 [4, 8, 256], P('tm', 'tile'), may hold values from -6 to 6
- obs_weight: float32 [4, 8, 256], P('tm', 'tile'), may hold values from 0.5 to 2
- obs_count: int32 [4, 8, 8], P('tm', 'tile'), may hold values from 10 to 32, as said below
Outputs:
- increment: float32 [4, 4, 2, 96, 1440], P('tm', None, None, 'tile')
The draws below stay inside these ranges and needn't reach their ends.
Inputs may be any that keep to these rules, and one draw needn't show every extreme that they name: In every sub-window one tile, drawn from the seed, gets 32 filled slots from every source device; only the first obs_count slots of a block hold observations.
All inputs are finite; a program needn't handle non-finite values.
Results may differ from the reference program's by a relative error of at most 0.00002.
Values sent between devices are 32-bit elements; how exact they have to be, the bound alone decides.
No kernel may reach another device: no remote copies, remote signals or barrier semaphores. Data moves between devices by JAX's collectives and lax.ppermute only.
A program may use at most 128 MiB of HBM per device.

```python
import math
import jax
import jax.numpy as jnp
from jax import lax

VARS = 4
LEV = 2
LON = 1440
LAT_DEV = 12
CAP = 32
STEPS = 2
ITERS = 2
SUBS = 4
TILES = 8
NLAT = 96
ROWS = 96


def draw_obs_count(key, part):
    drawn = jax.random.randint(key, (SUBS, TILES, TILES), CAP // 3, CAP + 1, dtype=jnp.int32)
    crowded = jax.random.randint(jax.random.fold_in(key, 7), (SUBS, 1, 1), 0, TILES, dtype=jnp.int32)
    column = lax.broadcasted_iota(jnp.int32, (SUBS, TILES, TILES), 2)
    return jnp.where(column == crowded, CAP, drawn)


def touch_ends(entries, stream_key, least, largest):
    dims = entries.shape
    index_at = [jax.random.randint(jax.random.fold_in(stream_key, axis), (), 0, dims[axis]) for axis in range(len(dims))]
    entries = entries.at[tuple(index_at)].set(least)
    longest = dims.index(max(dims))
    index_at[longest] = (index_at[longest] + 1) % dims[longest]
    return entries.at[tuple(index_at)].set(largest)


def block_scale(key, extent, shards, low, high):
    def one(position, parts):
        steps = jax.random.uniform(jax.random.fold_in(jax.random.fold_in(key, 6), position), (parts,), jnp.float32, low / len(shards), high / len(shards))
        return jnp.repeat(jnp.exp(steps), extent[position] // parts).reshape((-1,) + (1,) * (len(extent) - position - 1))

    level = one(*shards[0])
    for cut in shards[1:]:
        level = level * one(*cut)
    return level


def gaussian(rng, extent, deviation, bound, pieces=(), kind=jnp.bfloat16):
    entries = jax.random.normal(rng, extent, jnp.float32) * deviation
    if len(pieces) > 0:
        entries = block_scale(rng, extent, pieces, -0.22, 0.18) * entries
    return jnp.clip(entries, min=-bound, max=bound).astype(kind)


def setup_inputs(seed: int = 0) -> dict:
    streams_of = jax.random.split(jax.random.key(seed), 9)
    advect_east = jnp.clip(jax.random.uniform(streams_of[0], (SUBS, LEV, NLAT, LON), jnp.float32, -0.15, 0.15) * block_scale(streams_of[0], (SUBS, LEV, NLAT, LON), ((0, 4), (2, 8)), -0.4, 0.0), -0.15, 0.15)
    advect_north = jnp.clip(jax.random.uniform(streams_of[1], (SUBS, LEV, NLAT, LON), jnp.float32, -0.15, 0.15) * block_scale(streams_of[1], (SUBS, LEV, NLAT, LON), ((0, 4), (2, 8)), -0.4, 0.0), -0.15, 0.15)
    diffusion = jnp.clip(0.06 + 0.16 * jax.random.uniform(streams_of[2], (SUBS, LEV, NLAT, LON), jnp.float32) ** block_scale(streams_of[2], (SUBS, LEV, NLAT, LON), ((0, 4), (2, 8)), -0.2, 0.2), 0.06, 0.22)
    background_var = jnp.clip(jnp.exp(math.log(3.0) - 2.3025851 * jax.random.uniform(streams_of[3], (SUBS, VARS, LEV, NLAT, LON), jnp.float32) ** block_scale(streams_of[3], (SUBS, VARS, LEV, NLAT, LON), ((0, 4), (3, 8)), -0.2, 0.2)), 0.3, 3.0)
    obs_cell = touch_ends(jax.random.randint(streams_of[4], (SUBS, TILES, TILES * CAP), 0, ROWS * LON), jax.random.fold_in(streams_of[4], 1), 0, (ROWS * LON) - 1).astype(jnp.int32)
    obs_value = gaussian(streams_of[5], (SUBS, TILES, TILES * CAP), 1.0, 6.0, ((0, 4), (1, 8)), jnp.float32)
    obs_weight = jnp.clip(jnp.exp(math.log(2.0) - 1.3862944 * jax.random.uniform(streams_of[6], (SUBS, TILES, TILES * CAP), jnp.float32) ** block_scale(streams_of[6], (SUBS, TILES, TILES * CAP), ((0, 4), (1, 8)), -0.2, 0.2)), 0.5, 2.0)
    obs_count = draw_obs_count(jax.random.fold_in(streams_of[8], 71), 0)
    return dict(advect_east=advect_east, advect_north=advect_north, diffusion=diffusion, background_var=background_var, obs_cell=obs_cell, obs_value=obs_value, obs_weight=obs_weight, obs_count=obs_count)


def model_step(field, east_c, north_c, diff_c):
    padded = jnp.pad(field, ((0, 0), (0, 0), (1, 1), (0, 0)))
    to_north = padded[:, :, 2:]
    to_south = padded[:, :, :-2]
    to_east = jnp.roll(field, -1, axis=-1)
    to_west = jnp.roll(field, 1, axis=-1)
    return (1.0 - 4.0 * diff_c) * field + (diff_c - 0.5 * east_c) * to_east + (diff_c + 0.5 * east_c) * to_west + (diff_c - 0.5 * north_c) * to_north + (diff_c + 0.5 * north_c) * to_south

def forward_map(forcing, advect_east, advect_north, diffusion):
    carried = jnp.zeros(forcing.shape[1:], jnp.float32)
    states = []
    for window in range(SUBS):
        carried = carried + forcing[window]
        for repeat in range(STEPS):
            carried = model_step(carried, advect_east[window], advect_north[window], diffusion[window])
        states.append(carried)
    return jnp.stack(states)

def reference(advect_east, advect_north, diffusion, background_var, obs_cell, obs_value, obs_weight, obs_count):
    shaped = (SUBS, TILES, TILES, CAP)
    cells = obs_cell.reshape(shaped)
    values = obs_value.reshape(shaped)
    weights = obs_weight.reshape(shaped)
    obs_row = cells // LON
    obs_lon = cells % LON
    variable = obs_row // (LEV * LAT_DEV)
    level = obs_row // LAT_DEV % LEV
    owner = jnp.arange(TILES, dtype=jnp.int32)[None, None, :, None]
    latitude = owner * LAT_DEV + obs_row % LAT_DEV
    window_of = jnp.broadcast_to(jnp.arange(SUBS, dtype=jnp.int32)[:, None, None, None], shaped)
    slots = jnp.arange(CAP, dtype=jnp.int32)[None, None, None, :]
    masked_weight = weights * (slots < obs_count[:, :, :, None]).astype(jnp.float32)

    def apply_forward(forcing):
        return forward_map(forcing, advect_east, advect_north, diffusion)
    shape_state = (SUBS, VARS, LEV, NLAT, LON)
    increment = jnp.zeros(shape_state, jnp.float32)
    for iteration in range(ITERS):
        states, pullback = jax.vjp(apply_forward, increment)
        picked = states[window_of, variable, level, latitude, obs_lon]
        innov = masked_weight * (picked - values)
        grad_obs = jnp.zeros(shape_state, jnp.float32).at[window_of, variable, level, latitude, obs_lon].add(innov)
        adjoint = pullback(grad_obs)[0]
        increment = increment - 0.5 * (increment + background_var * adjoint)
    return increment
```

```python
import functools

import jax
import jax.numpy as jnp
from jax import lax
from jax.experimental import pallas as pl
from jax.experimental.pallas import tpu as pltpu
from jax.sharding import PartitionSpec as P

STEPS = 2
ITERS = 2
CHAINS = 3
LANES = 128
VMEM_LIMIT = 48 * 1024 * 1024


def padded(block, sides, width):
    for axis, dim in sides:
        count = lax.axis_size(axis)
        forward = [(i, i + 1) for i in range(count - 1)]
        backward = [(target, source) for source, target in forward]
        low = lax.ppermute(
            lax.slice_in_dim(block, block.shape[dim] - width, None, axis=dim), axis, forward
        )
        high = lax.ppermute(lax.slice_in_dim(block, 0, width, axis=dim), axis, backward)
        block = jnp.concatenate([low, block, high], axis=dim)
    return block


def shifted(value, axis, steps):
    count = lax.axis_size(axis)
    first, last = (max(0, -steps), min(count, count - steps))
    return lax.ppermute(value, axis, [(source, source + steps) for source in range(first, last)])


def apply_step(field, coef, adjoint):
    east_c = coef[0]
    north_c = coef[1]
    diff_c = coef[2]
    if adjoint:
        to_east = (diff_c - 0.5 * east_c) * field
        to_west = (diff_c + 0.5 * east_c) * field
        to_north = (diff_c - 0.5 * north_c) * field
        to_south = (diff_c + 0.5 * north_c) * field
        middle = (1.0 - 4.0 * diff_c[:, 1:-1]) * field[:, :, 1:-1]
        return (
            middle
            + jnp.roll(to_east[:, :, 1:-1], 1, axis=-1)
            + jnp.roll(to_west[:, :, 1:-1], -1, axis=-1)
            + to_north[:, :, :-2]
            + to_south[:, :, 2:]
        )
    inner = field[:, :, 1:-1]
    diff_in = diff_c[:, 1:-1]
    east_in = east_c[:, 1:-1]
    north_in = north_c[:, 1:-1]
    return (
        (1.0 - 4.0 * diff_in) * inner
        + (diff_in - 0.5 * east_in) * jnp.roll(inner, -1, axis=-1)
        + (diff_in + 0.5 * east_in) * jnp.roll(inner, 1, axis=-1)
        + (diff_in - 0.5 * north_in) * field[:, :, 2:]
        + (diff_in + 0.5 * north_in) * field[:, :, :-2]
    )


def advance(field, coef, adjoint):
    for repeat in range(STEPS):
        extended = padded(field, (("tile", 2),), 1)
        field = apply_step(extended, coef, adjoint)
    return field


def per_device(
    advect_east, advect_north, diffusion, background_var, obs_cell, obs_value, obs_weight, obs_count
):
    windows_count = lax.axis_size("tm")
    tiles = lax.axis_size("tile")
    coefs = jnp.stack([advect_east[0], advect_north[0], diffusion[0]])
    coef_ext = padded(coefs, (("tile", 2),), 1)
    cells = obs_cell.reshape(tiles, -1)
    slot_count = cells.shape[1]
    live = jnp.arange(slot_count, dtype=jnp.int32)[None, :] < obs_count.reshape(tiles)[:, None]
    masked = obs_weight.reshape(tiles, -1) * live.astype(jnp.float32)
    received = lax.all_to_all(
        jnp.stack([obs_value.reshape(tiles, -1), masked]),
        "tile",
        split_axis=1,
        concat_axis=1,
        tiled=True,
    )
    received_cells = lax.all_to_all(cells, "tile", split_axis=0, concat_axis=0, tiled=True)
    departures = received[0].reshape(-1)
    obs_weights = received[1].reshape(-1)
    flat_cells = received_cells.reshape(-1)
    local_var = background_var[0]
    state_shape = local_var.shape
    cell_total = state_shape[0] * state_shape[1] * state_shape[2] * state_shape[3]
    increment = jnp.zeros(state_shape, jnp.float32)
    for iteration in range(ITERS):
        if iteration == 0:
            innov = obs_weights * (0.0 - departures)
        else:
            forward_carried = advance(increment, coef_ext, False)
            for forward_window in range(windows_count - 1):
                forward_incoming = shifted(forward_carried, "tm", 1)
                forward_carried = advance(forward_incoming + increment, coef_ext, False)
            innov = obs_weights * (
                jnp.take(forward_carried.reshape(cell_total), flat_cells, axis=0) - departures
            )
        gridded = jnp.zeros((cell_total,), jnp.float32).at[flat_cells].add(innov)
        source = gridded.reshape(state_shape)
        carried = advance(source, coef_ext, True)
        for window in range(windows_count - 1):
            incoming = shifted(carried, "tm", -1)
            carried = advance(incoming + source, coef_ext, True)
        increment = increment - 0.5 * (increment + local_var * carried)
    return increment[None]


class Plan:
    def __init__(self, mesh_shape, var_shape, slot_shape):
        self.subs, self.tiles = mesh_shape["tm"], mesh_shape["tile"]
        self.count = self.subs * self.tiles
        _, self.vars, self.lev, self.nlat, self.lon = var_shape
        self.lat = self.nlat // self.tiles
        self.slots = slot_shape[2] // self.tiles
        self.cols = self.count // self.lev
        self.width = self.lon // self.cols
        self.half = self.width // 2
        self.halo = CHAINS * STEPS * self.subs
        self.margin = (LANES - self.width) // 2
        self.extra = self.halo - self.margin
        self.span = self.width + 2 * self.halo
        self.rows = 96
        self.coef_row = self.lat * self.vars
        self.tail_row = self.coef_row + 3 * self.lat
        self.obs_row = self.tail_row + self.lat // 2

    def fits(self):
        return (
            self.count % self.lev == 0
            and self.lon % self.cols == 0
            and self.width % 2 == 0
            and self.half + 2 * self.halo <= LANES
            and 0 <= self.extra <= 5
            and self.vars == 4
            and self.lat == 12
            and self.tiles == 8
            and self.slots * self.tiles == 2 * LANES
            and (self.width + 2 * self.margin) == LANES
        )


def pack_kernel(
    plan, count_ref, cell_ref, value_ref, weight_ref, east_ref, north_ref, diff_ref, var_ref, out_ref, wide
):
    p = plan
    pad = LANES
    right = wide.shape[-1] - pad - p.lon
    n_var = p.vars * p.lev
    for v in range(p.vars):
        for z in range(p.lev):
            wide[v * p.lev + z, :, pad : pad + p.lon] = var_ref[v, z]
    for c, ref in enumerate((east_ref, north_ref, diff_ref)):
        for z in range(p.lev):
            wide[n_var + c * p.lev + z, :, pad : pad + p.lon] = ref[z]
    for a in range(n_var + 3 * p.lev):
        wide[a, :, :pad] = wide[a, :, p.lon : p.lon + pad]
        wide[a, :, pad + p.lon :] = wide[a, :, pad : pad + right]

    lane = lax.broadcasted_iota(jnp.int32, (1, p.tiles * p.slots), 1)
    filled = jnp.zeros_like(lane)
    for t in range(p.tiles):
        filled = jnp.where(lane // p.slots == t, count_ref[0, t], filled)
    weight = jnp.where(lane % p.slots < filled, weight_ref[...], 0.0)
    obs = []
    for x in (weight, weight * value_ref[...], cell_ref[...].astype(jnp.float32)):
        obs += [x[:, :LANES], x[:, LANES:]]
    obs = jnp.concatenate(obs, axis=0)

    def take(a, rows, start):
        return wide[a, rows, pad + start : pad + start + LANES]

    lanes = lax.broadcasted_iota(jnp.int32, (p.lat // 2, LANES), 1)
    for z in range(p.lev):
        for j in range(p.cols):
            d = z * p.cols + j
            base = d * p.rows
            start = j * p.width - p.margin
            for v in range(p.vars):
                out_ref[pl.ds(base + v, p.lat, stride=p.vars), :] = take(v * p.lev + z, slice(None), start)
            for c in range(3):
                r = base + p.coef_row + c * p.lat
                out_ref[r : r + p.lat, :] = take(n_var + c * p.lev + z, slice(None), start)
            tail = jnp.zeros((p.lat // 2, LANES), jnp.float32)
            for h in range(2):
                rows = slice(h * (p.lat // 2), (h + 1) * (p.lat // 2))
                for c in range(3):
                    at = (h * 3 + c) * 2 * p.extra
                    a = n_var + c * p.lev + z
                    low = take(a, rows, j * p.width - p.halo - at)
                    high = take(a, rows, (j + 1) * p.width + p.margin - p.extra - at)
                    tail = jnp.where(lanes >= at, low, tail)
                    tail = jnp.where(lanes >= at + p.extra, high, tail)
            r = base + p.tail_row
            out_ref[r : r + 2 * (p.lat // 2), :] = jnp.concatenate([tail, obs], axis=0)


def swap_blocks(x, slots):
    size, width = x.shape
    sub = lax.broadcasted_iota(jnp.int32, x.shape, 0)
    block = lax.broadcasted_iota(jnp.int32, x.shape, 1) // slots
    out = x
    for d in range(1, size):
        moved = pltpu.roll(pltpu.roll(x, size - d, 0), d * slots, 1)
        out = jnp.where(block == (sub + d) % size, moved, out)
    return out


def chain_kernel(
    plan,
    recv_ref,
    out_ref,
    mid_c,
    east_c,
    west_c,
    north_c,
    south_c,
    weight_g,
    value_g,
    first,
    other,
    state,
    obs_tab,
    extras,
):
    p = plan
    f32 = jnp.float32
    me = lax.axis_index("tm") * p.tiles + lax.axis_index("tile")
    level = (me // p.cols).astype(f32)
    origin = ((me % p.cols) * p.width - p.halo).astype(f32)
    shape = (2 * p.vars, LANES)
    sub = lax.broadcasted_iota(jnp.int32, shape, 0)
    lane = lax.broadcasted_iota(jnp.int32, shape, 1)
    lower = sub < p.vars

    def spread(a, b):
        return (
            jnp.where(lower, a, pltpu.roll(b, p.vars, 0)),
            jnp.where(lower, pltpu.roll(a, p.vars, 0), b),
        )

    stride = p.rows
    for k in range(p.subs):
        raw = []
        for i in range(6):
            raw.append(recv_ref[pl.ds(k * p.tiles * p.rows + p.obs_row + i, p.tiles, stride=stride), :])
        w, wy, cell = (jnp.concatenate(raw[2 * i : 2 * i + 2], axis=1) for i in range(3))
        w, wy, cell = (swap_blocks(x, p.slots) for x in (w, wy, cell))
        row = jnp.floor((cell + 0.5) * (1.0 / p.lon))
        lon = cell - row * p.lon
        group = jnp.floor((row + 0.5) * (1.0 / p.lat))
        lat = row - group * p.lat
        var = jnp.floor((group + 0.5) * (1.0 / p.lev))
        lev = group - var * p.lev
        at = lon - origin
        at = jnp.where(at < 0, at + p.lon, at)
        at = jnp.where(at >= p.lon, at - p.lon, at)
        place = at - p.extra
        place = jnp.where(place < 0, place + LANES, place)
        place = jnp.where(place >= LANES, place - LANES, place)
        here = lev == level
        in_a = here & (at < p.half + 2 * p.halo)
        in_b = here & (at >= p.half) & (at < p.span)
        rows = slice(k * p.tiles, (k + 1) * p.tiles)
        obs_tab[0, rows, :] = lat * p.vars + var
        obs_tab[1, rows, :] = jnp.where(in_a, place, -1.0)
        obs_tab[2, rows, :] = jnp.where(in_b, place, -1.0)
        for i, x in ((3, w), (6, wy)):
            one = x.astype(jnp.bfloat16).astype(f32)
            two = (x - one).astype(jnp.bfloat16).astype(f32)
            obs_tab[i, rows, :] = one
            obs_tab[i + 1, rows, :] = two
            obs_tab[i + 2, rows, :] = x - one - two

    n_rows = p.lat * p.vars
    slots = p.tiles * p.slots
    row_id = lax.broadcasted_iota(jnp.int32, (n_rows, slots), 0).astype(f32)
    lane_id = lax.broadcasted_iota(jnp.int32, (LANES, slots), 0).astype(f32)

    def grid(kt, carry):
        def entry(i):
            return obs_tab[i, pl.ds(kt, 1), :]

        match = row_id == entry(0)
        left = jnp.concatenate(
            [jnp.where(match, entry(i), 0.0).astype(jnp.bfloat16) for i in range(3, 9)], axis=0
        )
        right = jnp.concatenate(
            [jnp.where(lane_id == entry(i), 1.0, 0.0).astype(jnp.bfloat16) for i in (1, 2)], axis=0
        )
        full = lax.dot_general(left, right, (((1,), (1,)), ((), ())), preferred_element_type=f32)
        for i, ref in ((0, weight_g), (3, value_g)):
            parts = [full[(i + q) * n_rows : (i + q + 1) * n_rows] for q in range(3)]
            total = parts[0] + (parts[1] + parts[2])
            for pair in range(p.lat // 2):
                rows = slice(2 * p.vars * pair, 2 * p.vars * (pair + 1))
                one, two = spread(total[rows, :LANES], total[rows, LANES:])
                ref[kt * p.lat + 2 * pair] = one
                ref[kt * p.lat + 2 * pair + 1] = two
        return carry

    lax.fori_loop(0, p.count, grid, 0)

    mask = (lower & (lane >= LANES - p.extra)) | (~lower & (lane < p.extra))
    part = p.lat // 2

    def widen(kt, carry):
        base = kt * p.rows
        tail = recv_ref[pl.ds(base + p.tail_row, part), :]
        for h in range(2):
            for c in range(3):
                at = (h * 3 + c) * 2 * p.extra
                extras[c, h * part : (h + 1) * part, :] = pltpu.roll(
                    tail, (LANES - p.extra - at) % LANES, 1
                )
        for l in range(p.lat):
            got = []
            for c in range(3):
                main = recv_ref[pl.ds(base + p.coef_row + c * p.lat + l, 1), :]
                edge = extras[c, l : l + 1, :]
                got.append(
                    jnp.where(mask, jnp.broadcast_to(edge, shape), jnp.broadcast_to(main, shape))
                )
            east, north, diff = got
            east = 0.5 * east
            north = 0.5 * north
            at = kt * p.lat + l
            mid_c[at] = 1.0 - 4.0 * diff
            east_c[at] = diff - east
            west_c[at] = diff + east
            north_c[at] = diff - north
            south_c[at] = diff + north
        return carry

    lax.fori_loop(0, p.count, widen, 0)

    n = p.nlat
    zero = jnp.zeros(shape, f32)
    unroll = 8

    def rows_loop(body, carry):
        def many(i, carry):
            for u in range(unroll):
                carry = body(i * unroll + u, carry)
            return carry

        return lax.fori_loop(0, n // unroll, many, carry)

    def step_adjoint(k, load, emit):
        base = k * n

        def terms(l):
            x = load(l)
            at = base + l
            here = (
                mid_c[at] * x
                + pltpu.roll(east_c[at] * x, 1, 1)
                + pltpu.roll(west_c[at] * x, LANES - 1, 1)
            )
            return here, north_c[at] * x, south_c[at] * x

        def body(l, carry):
            here, below, north = carry
            nxt, nxt_north, nxt_south = terms(l + 1)
            emit(l, here + below + nxt_south)
            return nxt, north, nxt_north

        here, north, _ = terms(0)
        carry = (here, zero, north)

        def many(i, carry):
            for u in range(unroll):
                carry = body(i * unroll + u, carry)
            return carry

        carry = lax.fori_loop(0, n // unroll - 1, many, carry)
        for l in range(n - unroll, n - 1):
            carry = body(l, carry)
        here, below, _ = carry
        emit(n - 1, here + below)

    def step_forward(k, load, emit):
        base = k * n

        def value(l, x, above, below):
            at = base + l
            return (
                mid_c[at] * x
                + east_c[at] * pltpu.roll(x, LANES - 1, 1)
                + west_c[at] * pltpu.roll(x, 1, 1)
                + north_c[at] * above
                + south_c[at] * below
            )

        def body(l, carry):
            below, x = carry
            above = load(l + 1)
            emit(l, value(l, x, above, below))
            return x, above

        carry = (zero, load(0))

        def many(i, carry):
            for u in range(unroll):
                carry = body(i * unroll + u, carry)
            return carry

        carry = lax.fori_loop(0, n // unroll - 1, many, carry)
        for l in range(n - unroll, n - 1):
            carry = body(l, carry)
        below, x = carry
        emit(n - 1, value(n - 1, x, zero, below))

    def store(ref):
        def emit(l, y):
            ref[l] = y

        return emit

    for k in reversed(range(p.subs)):
        base = k * n

        def load(l, k=k, base=base):
            g = -value_g[base + l]
            return g if k == p.subs - 1 else g + first[base + n + l]

        step_adjoint(k, load, store(state))

        def emit(l, y, base=base):
            first[base + l] = y

        step_adjoint(k, lambda l: state[l], emit)

    def scale(i, carry):
        var = recv_ref[pl.ds((i // (p.lat // 2)) * p.rows + (i % (p.lat // 2)) * 8, 8), :]
        one, two = spread(var, var)
        other[2 * i] = -0.5 * (one * first[2 * i])
        other[2 * i + 1] = -0.5 * (two * first[2 * i + 1])
        return carry

    lax.fori_loop(0, p.subs * n // 2, scale, 0)

    for k in range(p.subs):
        base = k * n

        def load(l, k=k, base=base):
            f = other[base + l]
            return f if k == 0 else f + other[base - n + l]

        step_forward(k, load, store(state))

        def emit(l, y, base=base):
            other[base + l] = y
            value_g[base + l] = weight_g[base + l] * y - value_g[base + l]

        step_forward(k, lambda l: state[l], emit)

    for k in reversed(range(p.subs)):
        base = k * n

        def load(l, k=k, base=base):
            g = value_g[base + l]
            return g if k == p.subs - 1 else g + other[base + n + l]

        step_adjoint(k, load, store(state))

        def emit(l, y, base=base):
            other[base + l] = y

        step_adjoint(k, lambda l: state[l], emit)

    in_half = lane < p.margin + p.half

    def gather(i, carry):
        one = 0.5 * first[2 * i] + other[2 * i]
        two = 0.5 * first[2 * i + 1] + other[2 * i + 1]
        one = jnp.where(in_half, one, pltpu.roll(one, p.vars, 0))
        two = jnp.where(in_half, pltpu.roll(two, p.vars, 0), two)
        out_ref[pl.ds(i * 8, 8), :] = jnp.where(lower, one, two)
        return carry

    lax.fori_loop(0, p.subs * n // 2, gather, 0)


def finish_kernel(plan, recv_ref, var_ref, out_ref):
    p = plan
    n_rows = p.lat * p.vars
    for z in range(p.lev):
        for j in range(p.cols):
            for v in range(p.vars):
                start = (z * p.cols + j) * n_rows + v
                piece = recv_ref[pl.ds(start, p.lat, stride=p.vars), :]
                cols = slice(j * p.width, (j + 1) * p.width)
                out_ref[v, z, :, cols] = -0.5 * (
                    var_ref[v, z, :, cols] * piece[:, p.margin : p.margin + p.width]
                )


def transposed(
    plan, advect_east, advect_north, diffusion, background_var, obs_cell, obs_value, obs_weight, obs_count
):
    p = plan
    vmem = pl.BlockSpec(memory_space=pltpu.VMEM)
    params = pltpu.CompilerParams(vmem_limit_bytes=VMEM_LIMIT)
    f32 = jnp.float32
    wide = (p.vars + 3) * p.lev
    packed = pl.pallas_call(
        functools.partial(pack_kernel, p),
        out_shape=jax.ShapeDtypeStruct((p.count * p.rows, LANES), f32),
        in_specs=[pl.BlockSpec(memory_space=pltpu.SMEM)] + [vmem] * 7,
        out_specs=vmem,
        scratch_shapes=[pltpu.VMEM((wide, p.lat, 14 * LANES), f32)],
        compiler_params=params,
        name="pack",
    )(
        obs_count.reshape(1, -1),
        obs_cell.reshape(1, -1),
        obs_value.reshape(1, -1),
        obs_weight.reshape(1, -1),
        advect_east[0],
        advect_north[0],
        diffusion[0],
        background_var[0],
    )
    received = lax.all_to_all(packed, ("tm", "tile"), 0, 0, tiled=True)
    field = pltpu.VMEM((p.subs * p.nlat, 2 * p.vars, LANES), f32)
    back = pl.pallas_call(
        functools.partial(chain_kernel, p),
        out_shape=jax.ShapeDtypeStruct((p.count * p.lat * p.vars, LANES), f32),
        in_specs=[vmem],
        out_specs=vmem,
        scratch_shapes=[field] * 9
        + [
            pltpu.VMEM((p.nlat, 2 * p.vars, LANES), f32),
            pltpu.VMEM((9, p.count, p.tiles * p.slots), f32),
            pltpu.VMEM((3, p.lat, LANES), f32),
        ],
        compiler_params=params,
        name="chains",
    )(received)
    returned = lax.all_to_all(back, ("tm", "tile"), 0, 0, tiled=True)
    increment = pl.pallas_call(
        functools.partial(finish_kernel, p),
        out_shape=jax.ShapeDtypeStruct(background_var.shape[1:], f32),
        in_specs=[vmem] * 2,
        out_specs=vmem,
        compiler_params=params,
        name="finish",
    )(returned, background_var[0])
    return increment[None]


def solution(mesh):
    def run(*args):
        plan = Plan(mesh.shape, args[3].shape, args[4].shape)
        work = functools.partial(transposed, plan) if plan.fits() else per_device
        return jax.shard_map(
            work,
            mesh=mesh,
            in_specs=(
                P("tm", None, "tile", None),
                P("tm", None, "tile", None),
                P("tm", None, "tile", None),
                P("tm", None, None, "tile", None),
                P("tm", "tile", None),
                P("tm", "tile", None),
                P("tm", "tile", None),
                P("tm", "tile", None),
            ),
            out_specs=P("tm", None, None, "tile", None),
            check_vma=False,
        )(*args)

    return run
```

```python
import functools

import jax
import jax.numpy as jnp
from jax import lax
from jax.experimental import pallas as pl
from jax.experimental.pallas import tpu as pltpu
from jax.sharding import PartitionSpec as P

STEPS = 2
ITERS = 2
CHAINS = 3
LANES = 128
VMEM_LIMIT = 48 * 1024 * 1024


def padded(block, sides, width):
    for axis, dim in sides:
        count = lax.axis_size(axis)
        forward = [(i, i + 1) for i in range(count - 1)]
        backward = [(target, source) for source, target in forward]
        low = lax.ppermute(
            lax.slice_in_dim(block, block.shape[dim] - width, None, axis=dim), axis, forward
        )
        high = lax.ppermute(lax.slice_in_dim(block, 0, width, axis=dim), axis, backward)
        block = jnp.concatenate([low, block, high], axis=dim)
    return block


def shifted(value, axis, steps):
    count = lax.axis_size(axis)
    first, last = (max(0, -steps), min(count, count - steps))
    return lax.ppermute(value, axis, [(source, source + steps) for source in range(first, last)])


def apply_step(field, coef, adjoint):
    east_c = coef[0]
    north_c = coef[1]
    diff_c = coef[2]
    if adjoint:
        to_east = (diff_c - 0.5 * east_c) * field
        to_west = (diff_c + 0.5 * east_c) * field
        to_north = (diff_c - 0.5 * north_c) * field
        to_south = (diff_c + 0.5 * north_c) * field
        middle = (1.0 - 4.0 * diff_c[:, 1:-1]) * field[:, :, 1:-1]
        return (
            middle
            + jnp.roll(to_east[:, :, 1:-1], 1, axis=-1)
            + jnp.roll(to_west[:, :, 1:-1], -1, axis=-1)
            + to_north[:, :, :-2]
            + to_south[:, :, 2:]
        )
    inner = field[:, :, 1:-1]
    diff_in = diff_c[:, 1:-1]
    east_in = east_c[:, 1:-1]
    north_in = north_c[:, 1:-1]
    return (
        (1.0 - 4.0 * diff_in) * inner
        + (diff_in - 0.5 * east_in) * jnp.roll(inner, -1, axis=-1)
        + (diff_in + 0.5 * east_in) * jnp.roll(inner, 1, axis=-1)
        + (diff_in - 0.5 * north_in) * field[:, :, 2:]
        + (diff_in + 0.5 * north_in) * field[:, :, :-2]
    )


def advance(field, coef, adjoint):
    for repeat in range(STEPS):
        extended = padded(field, (("tile", 2),), 1)
        field = apply_step(extended, coef, adjoint)
    return field


def per_device(
    advect_east, advect_north, diffusion, background_var, obs_cell, obs_value, obs_weight, obs_count
):
    windows_count = lax.axis_size("tm")
    tiles = lax.axis_size("tile")
    coefs = jnp.stack([advect_east[0], advect_north[0], diffusion[0]])
    coef_ext = padded(coefs, (("tile", 2),), 1)
    cells = obs_cell.reshape(tiles, -1)
    slot_count = cells.shape[1]
    live = jnp.arange(slot_count, dtype=jnp.int32)[None, :] < obs_count.reshape(tiles)[:, None]
    masked = obs_weight.reshape(tiles, -1) * live.astype(jnp.float32)
    received = lax.all_to_all(
        jnp.stack([obs_value.reshape(tiles, -1), masked]),
        "tile",
        split_axis=1,
        concat_axis=1,
        tiled=True,
    )
    received_cells = lax.all_to_all(cells, "tile", split_axis=0, concat_axis=0, tiled=True)
    departures = received[0].reshape(-1)
    obs_weights = received[1].reshape(-1)
    flat_cells = received_cells.reshape(-1)
    local_var = background_var[0]
    state_shape = local_var.shape
    cell_total = state_shape[0] * state_shape[1] * state_shape[2] * state_shape[3]
    increment = jnp.zeros(state_shape, jnp.float32)
    for iteration in range(ITERS):
        if iteration == 0:
            innov = obs_weights * (0.0 - departures)
        else:
            forward_carried = advance(increment, coef_ext, False)
            for forward_window in range(windows_count - 1):
                forward_incoming = shifted(forward_carried, "tm", 1)
                forward_carried = advance(forward_incoming + increment, coef_ext, False)
            innov = obs_weights * (
                jnp.take(forward_carried.reshape(cell_total), flat_cells, axis=0) - departures
            )
        gridded = jnp.zeros((cell_total,), jnp.float32).at[flat_cells].add(innov)
        source = gridded.reshape(state_shape)
        carried = advance(source, coef_ext, True)
        for window in range(windows_count - 1):
            incoming = shifted(carried, "tm", -1)
            carried = advance(incoming + source, coef_ext, True)
        increment = increment - 0.5 * (increment + local_var * carried)
    return increment[None]


class Plan:
    def __init__(self, mesh_shape, var_shape, slot_shape):
        self.subs, self.tiles = mesh_shape["tm"], mesh_shape["tile"]
        self.count = self.subs * self.tiles
        _, self.vars, self.lev, self.nlat, self.lon = var_shape
        self.lat = self.nlat // self.tiles
        self.slots = slot_shape[2] // self.tiles
        self.cols = self.count // self.lev
        self.width = self.lon // self.cols
        self.half = self.width // 2
        self.halo = CHAINS * STEPS * self.subs
        self.margin = (LANES - self.width) // 2
        self.extra = self.halo - self.margin
        self.span = self.width + 2 * self.halo
        self.rows = 96
        self.step = 16
        self.back = self.lat - 3
        self.coef_row = self.lat * self.vars
        self.tail_row = self.coef_row + 3 * self.lat
        self.obs_row = self.tail_row + self.lat // 2

    def fits(self):
        return (
            self.count % self.lev == 0
            and self.lon % self.cols == 0
            and self.width % 2 == 0
            and self.half + 2 * self.halo <= LANES
            and 0 <= self.extra <= 5
            and self.vars == 4
            and self.lat == 12
            and self.tiles == 8
            and self.slots * self.tiles == 2 * LANES
            and (self.width + 2 * self.margin) == LANES
            and self.width % 3 == 0
            and self.width * 4 <= 3 * LANES
        )


def pack_kernel(
    plan, count_ref, cell_ref, value_ref, weight_ref, east_ref, north_ref, diff_ref, var_ref, out_ref, wide
):
    p = plan
    pad = LANES
    right = wide.shape[-1] - pad - p.lon
    n_var = p.vars * p.lev
    inner = slice(pad, pad + p.lon)
    for z in range(p.lev):
        for v in range(p.vars):
            first = (v * p.lev + z) * p.step
            wide[first : first + p.lat, inner] = var_ref[v, z]
        for c, ref in enumerate((east_ref, north_ref, diff_ref)):
            first = (n_var + c * p.lev + z) * p.step
            wide[first : first + p.lat, inner] = ref[z]
    for a in range(n_var + 3 * p.lev):
        rows = slice(a * p.step, a * p.step + p.lat)
        wide[rows, :pad] = wide[rows, p.lon : p.lon + pad]
        wide[rows, pad + p.lon :] = wide[rows, pad : pad + right]

    lane = lax.broadcasted_iota(jnp.int32, (1, p.tiles * p.slots), 1)
    filled = jnp.zeros_like(lane)
    for t in range(p.tiles):
        filled = jnp.where(lane // p.slots == t, count_ref[0, t], filled)
    weight = jnp.where(lane % p.slots < filled, weight_ref[...], 0.0)
    obs = []
    for x in (weight, weight * value_ref[...], cell_ref[...].astype(jnp.float32)):
        obs += [x[:, :LANES], x[:, LANES:]]
    obs = jnp.concatenate(obs, axis=0)

    def take(a, rows, start):
        first = a * p.step + rows.start
        return wide[first : first + rows.stop - rows.start, pad + start : pad + start + LANES]

    lanes = lax.broadcasted_iota(jnp.int32, (p.lat // 2, LANES), 1)
    for z in range(p.lev):
        for j in range(p.cols):
            d = z * p.cols + j
            base = d * p.rows
            start = j * p.width - p.margin
            for v in range(p.vars):
                out_ref[pl.ds(base + v, p.lat, stride=p.vars), :] = take(v * p.lev + z, slice(0, p.lat), start)
            for c in range(3):
                r = base + p.coef_row + c * p.lat
                out_ref[r : r + p.lat, :] = take(n_var + c * p.lev + z, slice(0, p.lat), start)
            tail = jnp.zeros((p.lat // 2, LANES), jnp.float32)
            for h in range(2):
                rows = slice(h * (p.lat // 2), (h + 1) * (p.lat // 2))
                for c in range(3):
                    at = (h * 3 + c) * 2 * p.extra
                    a = n_var + c * p.lev + z
                    low = take(a, rows, j * p.width - p.halo - at)
                    high = take(a, rows, (j + 1) * p.width + p.margin - p.extra - at)
                    tail = jnp.where(lanes >= at, low, tail)
                    tail = jnp.where(lanes >= at + p.extra, high, tail)
            r = base + p.tail_row
            out_ref[r : r + 2 * (p.lat // 2), :] = jnp.concatenate([tail, obs], axis=0)


def looped(count, unroll, body):
    def many(i, carry):
        for u in range(unroll):
            body(i * unroll + u)
        return carry

    lax.fori_loop(0, count // unroll, many, 0)


def swap_blocks(x, slots):
    size, width = x.shape
    sub = lax.broadcasted_iota(jnp.int32, x.shape, 0)
    block = lax.broadcasted_iota(jnp.int32, x.shape, 1) // slots
    out = x
    for d in range(1, size):
        moved = pltpu.roll(pltpu.roll(x, size - d, 0), d * slots, 1)
        out = jnp.where(block == (sub + d) % size, moved, out)
    return out


def chain_kernel(
    plan,
    recv_ref,
    out_ref,
    mid_c,
    east_c,
    west_c,
    north_c,
    south_c,
    weight_g,
    value_g,
    first,
    forcing,
    innov,
    total,
    carried,
    obs_tab,
    extras,
):
    p = plan
    f32 = jnp.float32
    me = lax.axis_index("tm") * p.tiles + lax.axis_index("tile")
    level = (me // p.cols).astype(f32)
    origin = ((me % p.cols) * p.width - p.halo).astype(f32)
    shape = (2 * p.vars, LANES)
    sub = lax.broadcasted_iota(jnp.int32, shape, 0)
    lane = lax.broadcasted_iota(jnp.int32, shape, 1)
    lower = sub < p.vars

    def spread(a, b):
        return (
            jnp.where(lower, a, pltpu.roll(b, p.vars, 0)),
            jnp.where(lower, pltpu.roll(a, p.vars, 0), b),
        )

    stride = p.rows
    for k in range(p.subs):
        raw = []
        for i in range(6):
            raw.append(recv_ref[pl.ds(k * p.tiles * p.rows + p.obs_row + i, p.tiles, stride=stride), :])
        w, wy, cell = (jnp.concatenate(raw[2 * i : 2 * i + 2], axis=1) for i in range(3))
        w, wy, cell = (swap_blocks(x, p.slots) for x in (w, wy, cell))
        row = jnp.floor((cell + 0.5) * (1.0 / p.lon))
        lon = cell - row * p.lon
        group = jnp.floor((row + 0.5) * (1.0 / p.lat))
        lat = row - group * p.lat
        var = jnp.floor((group + 0.5) * (1.0 / p.lev))
        lev = group - var * p.lev
        at = lon - origin
        at = jnp.where(at < 0, at + p.lon, at)
        at = jnp.where(at >= p.lon, at - p.lon, at)
        place = at - p.extra
        place = jnp.where(place < 0, place + LANES, place)
        place = jnp.where(place >= LANES, place - LANES, place)
        here = lev == level
        in_a = here & (at < p.half + 2 * p.halo)
        in_b = here & (at >= p.half) & (at < p.span)
        rows = slice(k * p.tiles, (k + 1) * p.tiles)
        obs_tab[0, rows, :] = lat * p.vars + var
        obs_tab[1, rows, :] = jnp.where(in_a, place, -1.0)
        obs_tab[2, rows, :] = jnp.where(in_b, place, -1.0)
        for i, x in ((3, w), (6, wy)):
            one = x.astype(jnp.bfloat16).astype(f32)
            two = (x - one).astype(jnp.bfloat16).astype(f32)
            obs_tab[i, rows, :] = one
            obs_tab[i + 1, rows, :] = two
            obs_tab[i + 2, rows, :] = x - one - two

    n_rows = p.lat * p.vars
    slots = p.tiles * p.slots
    row_id = lax.broadcasted_iota(jnp.int32, (n_rows, slots), 0).astype(f32)
    lane_id = lax.broadcasted_iota(jnp.int32, (LANES, slots), 0).astype(f32)

    def grid(kt):
        def entry(i):
            return obs_tab[i, pl.ds(kt, 1), :]

        match = row_id == entry(0)
        left = jnp.concatenate(
            [jnp.where(match, entry(i), 0.0).astype(jnp.bfloat16) for i in range(3, 9)], axis=0
        )
        right = jnp.concatenate(
            [jnp.where(lane_id == entry(i), 1.0, 0.0).astype(jnp.bfloat16) for i in (1, 2)], axis=0
        )
        full = lax.dot_general(left, right, (((1,), (1,)), ((), ())), preferred_element_type=f32)
        for i, ref in ((0, weight_g), (3, value_g)):
            parts = [full[(i + q) * n_rows : (i + q + 1) * n_rows] for q in range(3)]
            summed = parts[0] + (parts[1] + parts[2])
            for pair in range(p.lat // 2):
                rows = slice(2 * p.vars * pair, 2 * p.vars * (pair + 1))
                one, two = spread(summed[rows, :LANES], summed[rows, LANES:])
                ref[kt * p.lat + 2 * pair] = one
                ref[kt * p.lat + 2 * pair + 1] = two

    looped(p.count, 4, grid)

    mask = (lower & (lane >= LANES - p.extra)) | (~lower & (lane < p.extra))
    part = p.lat // 2

    def edges(kt):
        tail = recv_ref[pl.ds(kt * p.rows + p.tail_row, part), :]
        for h in range(2):
            for c in range(3):
                at = (h * 3 + c) * 2 * p.extra
                extras[c, kt, h * part : (h + 1) * part, :] = pltpu.roll(
                    tail, (LANES - p.extra - at) % LANES, 1
                )

    looped(p.count, 8, edges)

    def widen(kt):
        base = kt * p.rows
        for l in range(p.lat):
            got = []
            for c in range(3):
                main = recv_ref[pl.ds(base + p.coef_row + c * p.lat + l, 1), :]
                edge = extras[c, kt, l : l + 1, :]
                got.append(
                    jnp.where(mask, jnp.broadcast_to(edge, shape), jnp.broadcast_to(main, shape))
                )
            east, north, diff = got
            east = 0.5 * east
            north = 0.5 * north
            at = kt * p.lat + l
            mid_c[at] = 1.0 - 4.0 * diff
            east_c[at] = diff - east
            west_c[at] = diff + east
            north_c[at] = diff - north
            south_c[at] = diff + north

    looped(p.count, 4, widen)

    n = p.nlat
    zero = jnp.zeros(shape, f32)

    def adjoint(base, load, emit):
        def terms(l, x):
            at = base + l
            here = (
                mid_c[at] * x
                + pltpu.roll(east_c[at] * x, 1, 1)
                + pltpu.roll(west_c[at] * x, LANES - 1, 1)
            )
            return here, north_c[at] * x, south_c[at] * x

        nothing = (zero, zero, zero)
        rows = [nothing] * (STEPS * 3)
        for l in range(n + STEPS):
            x = load(l) if l < n else None
            for s in range(STEPS):
                at = l - s
                now = terms(at, x) if 0 <= at < n else nothing
                before, last = rows[3 * s + 1], rows[3 * s + 2]
                rows[3 * s : 3 * s + 3] = [before, last, now]
                x = last[0] + before[1] + now[2] if 1 <= at <= n else None
            if x is not None:
                emit(l - STEPS, x)

    def forward(base, load, emit):
        def value(l, below, x, above):
            at = base + l
            return (
                mid_c[at] * x
                + east_c[at] * pltpu.roll(x, LANES - 1, 1)
                + west_c[at] * pltpu.roll(x, 1, 1)
                + north_c[at] * above
                + south_c[at] * below
            )

        rows = [zero] * (STEPS * 3)
        for l in range(n + STEPS):
            x = load(l) if l < n else None
            for s in range(STEPS):
                at = l - s
                now = x if 0 <= at < n else zero
                below, last = rows[3 * s + 1], rows[3 * s + 2]
                rows[3 * s : 3 * s + 3] = [below, last, now]
                x = value(at - 1, below, last, now) if 1 <= at <= n else None
            if x is not None:
                emit(l - STEPS, x)

    def clear(ref):
        for l in range(n):
            ref[l] = zero

    clear(carried)

    def first_adjoint(i, _):
        k = p.subs - 1 - i
        base = k * n
        held = {}

        def load(l):
            return carried[l] - value_g[base + l]

        def emit(l, y):
            carried[l] = y
            first[base + l] = y
            held[l] = y
            if l % 2:
                row = k * p.tiles * p.rows + (l // p.lat) * p.rows + (l % p.lat) // 2 * 2 * p.vars
                var = recv_ref[pl.ds(pl.multiple_of(row, 8), 2 * p.vars), :]
                one, two = spread(var, var)
                forcing[base + l - 1] = -0.5 * (one * held.pop(l - 1))
                forcing[base + l] = -0.5 * (two * held.pop(l))

        adjoint(base, load, emit)
        return 0

    lax.fori_loop(0, p.subs, first_adjoint, 0)

    clear(carried)

    def run_forward(k, _):
        base = k * n

        def load(l):
            return carried[l] + forcing[base + l]

        def emit(l, y):
            carried[l] = y
            innov[base + l] = weight_g[base + l] * y - value_g[base + l]

        forward(base, load, emit)
        return 0

    lax.fori_loop(0, p.subs, run_forward, 0)

    clear(carried)

    def second_adjoint(i, _):
        base = (p.subs - 1 - i) * n

        def load(l):
            return carried[l] + innov[base + l]

        def emit(l, y):
            carried[l] = y
            total[base + l] = y + 0.5 * first[base + l]

        adjoint(base, load, emit)
        return 0

    lax.fori_loop(0, p.subs, second_adjoint, 0)

    in_half = lane < p.margin + p.half
    own = (lane >= p.margin) & (lane < p.margin + p.width)
    third = p.width // 3

    def fold(kt):
        rows = []
        for l in range(p.lat):
            y = total[kt * p.lat + l]
            rows.append(jnp.where(in_half, y, pltpu.roll(y, p.vars, 0)))
        for l in range(p.back):
            guest = pltpu.roll(rows[p.back + l // 3], p.width - third * (l % 3), 1)
            out_ref[kt * p.back + l] = jnp.where(own, rows[l], guest)[: p.vars]

    looped(p.count, 8, fold)


def finish_kernel(plan, recv_ref, var_ref, out_ref, wide):
    p = plan
    third = p.width // 3
    lane = lax.broadcasted_iota(jnp.int32, (3, LANES), 1)
    own = slice(p.margin, p.margin + p.width)
    for z in range(p.lev):
        for j in range(p.cols):
            cols = slice(j * p.width, (j + 1) * p.width)
            for v in range(p.vars):
                start = (z * p.cols + j) * p.back * p.vars + v
                row = (v * p.lev + z) * p.step
                wide[row : row + p.back, cols] = recv_ref[pl.ds(start, p.back, stride=p.vars), :][:, own]
                late = None
                for i in range(3):
                    got = recv_ref[pl.ds(start + i * p.vars, 3, stride=3 * p.vars), :]
                    got = pltpu.roll(got, LANES - p.width + third * i, 1)
                    late = got if i == 0 else jnp.where(lane >= p.margin + third * i, got, late)
                wide[row + p.back : row + p.lat, cols] = late[:, own]
    for v in range(p.vars):
        for z in range(p.lev):
            row = (v * p.lev + z) * p.step
            out_ref[v, z] = -0.5 * (var_ref[v, z] * wide[row : row + p.lat, :])


def transposed(
    plan, advect_east, advect_north, diffusion, background_var, obs_cell, obs_value, obs_weight, obs_count
):
    p = plan
    vmem = pl.BlockSpec(memory_space=pltpu.VMEM)
    params = pltpu.CompilerParams(vmem_limit_bytes=VMEM_LIMIT)
    f32 = jnp.float32
    wide = (p.vars + 3) * p.lev

    var = background_var[0]
    packed = pl.pallas_call(
        functools.partial(pack_kernel, p),
        out_shape=jax.ShapeDtypeStruct((p.count * p.rows, LANES), f32),
        in_specs=[pl.BlockSpec(memory_space=pltpu.SMEM)] + [vmem] * 7,
        out_specs=vmem,
        scratch_shapes=[pltpu.VMEM((wide * p.step, 14 * LANES), f32)],
        compiler_params=params,
        name="pack",
    )(
        obs_count.reshape(1, -1),
        obs_cell.reshape(1, -1),
        obs_value.reshape(1, -1),
        obs_weight.reshape(1, -1),
        advect_east[0],
        advect_north[0],
        diffusion[0],
        var,
    )
    received = lax.all_to_all(packed, ("tm", "tile"), 0, 0, tiled=True)
    field = pltpu.VMEM((p.subs * p.nlat, 2 * p.vars, LANES), f32)
    back = pl.pallas_call(
        functools.partial(chain_kernel, p),
        out_shape=jax.ShapeDtypeStruct((p.count * p.back, p.vars, LANES), f32),
        in_specs=[vmem],
        out_specs=vmem,
        scratch_shapes=[field] * 11
        + [
            pltpu.VMEM((p.nlat, 2 * p.vars, LANES), f32),
            pltpu.VMEM((9, p.count, p.tiles * p.slots), f32),
            pltpu.VMEM((3, p.count, p.lat, LANES), f32),
        ],
        compiler_params=params,
        name="chains",
    )(received)
    returned = lax.all_to_all(back, ("tm", "tile"), 0, 0, tiled=True)
    returned = returned.reshape(-1, LANES)
    increment = pl.pallas_call(
        functools.partial(finish_kernel, p),
        out_shape=jax.ShapeDtypeStruct(var.shape, f32),
        in_specs=[vmem] * 2,
        out_specs=vmem,
        scratch_shapes=[pltpu.VMEM((p.vars * p.lev * p.step, p.lon), f32)],
        compiler_params=params,
        name="finish",
    )(returned, var)
    return increment[None]


def solution(mesh):
    def run(*args):
        plan = Plan(mesh.shape, args[3].shape, args[4].shape)
        work = functools.partial(transposed, plan) if plan.fits() else per_device
        return jax.shard_map(
            work,
            mesh=mesh,
            in_specs=(
                P("tm", None, "tile", None),
                P("tm", None, "tile", None),
                P("tm", None, "tile", None),
                P("tm", None, None, "tile", None),
                P("tm", "tile", None),
                P("tm", "tile", None),
                P("tm", "tile", None),
                P("tm", "tile", None),
            ),
            out_specs=P("tm", None, None, "tile", None),
            check_vma=False,
        )(*args)

    return run
```

```python
import functools

import jax
import jax.numpy as jnp
from jax import lax
from jax.experimental import pallas as pl
from jax.experimental.pallas import tpu as pltpu
from jax.sharding import PartitionSpec as P

STEPS = 2
ITERS = 2
CHAINS = 3
LANES = 128
VMEM_LIMIT = 48 * 1024 * 1024


def padded(block, sides, width):
    for axis, dim in sides:
        count = lax.axis_size(axis)
        forward = [(i, i + 1) for i in range(count - 1)]
        backward = [(target, source) for source, target in forward]
        low = lax.ppermute(
            lax.slice_in_dim(block, block.shape[dim] - width, None, axis=dim), axis, forward
        )
        high = lax.ppermute(lax.slice_in_dim(block, 0, width, axis=dim), axis, backward)
        block = jnp.concatenate([low, block, high], axis=dim)
    return block


def shifted(value, axis, steps):
    count = lax.axis_size(axis)
    first, last = (max(0, -steps), min(count, count - steps))
    return lax.ppermute(value, axis, [(source, source + steps) for source in range(first, last)])


def apply_step(field, coef, adjoint):
    east_c = coef[0]
    north_c = coef[1]
    diff_c = coef[2]
    if adjoint:
        to_east = (diff_c - 0.5 * east_c) * field
        to_west = (diff_c + 0.5 * east_c) * field
        to_north = (diff_c - 0.5 * north_c) * field
        to_south = (diff_c + 0.5 * north_c) * field
        middle = (1.0 - 4.0 * diff_c[:, 1:-1]) * field[:, :, 1:-1]
        return (
            middle
            + jnp.roll(to_east[:, :, 1:-1], 1, axis=-1)
            + jnp.roll(to_west[:, :, 1:-1], -1, axis=-1)
            + to_north[:, :, :-2]
            + to_south[:, :, 2:]
        )
    inner = field[:, :, 1:-1]
    diff_in = diff_c[:, 1:-1]
    east_in = east_c[:, 1:-1]
    north_in = north_c[:, 1:-1]
    return (
        (1.0 - 4.0 * diff_in) * inner
        + (diff_in - 0.5 * east_in) * jnp.roll(inner, -1, axis=-1)
        + (diff_in + 0.5 * east_in) * jnp.roll(inner, 1, axis=-1)
        + (diff_in - 0.5 * north_in) * field[:, :, 2:]
        + (diff_in + 0.5 * north_in) * field[:, :, :-2]
    )


def advance(field, coef, adjoint):
    for repeat in range(STEPS):
        extended = padded(field, (("tile", 2),), 1)
        field = apply_step(extended, coef, adjoint)
    return field


def per_device(
    advect_east, advect_north, diffusion, background_var, obs_cell, obs_value, obs_weight, obs_count
):
    windows_count = lax.axis_size("tm")
    tiles = lax.axis_size("tile")
    coefs = jnp.stack([advect_east[0], advect_north[0], diffusion[0]])
    coef_ext = padded(coefs, (("tile", 2),), 1)
    cells = obs_cell.reshape(tiles, -1)
    slot_count = cells.shape[1]
    live = jnp.arange(slot_count, dtype=jnp.int32)[None, :] < obs_count.reshape(tiles)[:, None]
    masked = obs_weight.reshape(tiles, -1) * live.astype(jnp.float32)
    received = lax.all_to_all(
        jnp.stack([obs_value.reshape(tiles, -1), masked]),
        "tile",
        split_axis=1,
        concat_axis=1,
        tiled=True,
    )
    received_cells = lax.all_to_all(cells, "tile", split_axis=0, concat_axis=0, tiled=True)
    departures = received[0].reshape(-1)
    obs_weights = received[1].reshape(-1)
    flat_cells = received_cells.reshape(-1)
    local_var = background_var[0]
    state_shape = local_var.shape
    cell_total = state_shape[0] * state_shape[1] * state_shape[2] * state_shape[3]
    increment = jnp.zeros(state_shape, jnp.float32)
    for iteration in range(ITERS):
        if iteration == 0:
            innov = obs_weights * (0.0 - departures)
        else:
            forward_carried = advance(increment, coef_ext, False)
            for forward_window in range(windows_count - 1):
                forward_incoming = shifted(forward_carried, "tm", 1)
                forward_carried = advance(forward_incoming + increment, coef_ext, False)
            innov = obs_weights * (
                jnp.take(forward_carried.reshape(cell_total), flat_cells, axis=0) - departures
            )
        gridded = jnp.zeros((cell_total,), jnp.float32).at[flat_cells].add(innov)
        source = gridded.reshape(state_shape)
        carried = advance(source, coef_ext, True)
        for window in range(windows_count - 1):
            incoming = shifted(carried, "tm", -1)
            carried = advance(incoming + source, coef_ext, True)
        increment = increment - 0.5 * (increment + local_var * carried)
    return increment[None]


class Plan:
    def __init__(self, mesh_shape, var_shape, slot_shape):
        self.subs, self.tiles = mesh_shape["tm"], mesh_shape["tile"]
        self.count = self.subs * self.tiles
        _, self.vars, self.lev, self.nlat, self.lon = var_shape
        self.lat = self.nlat // self.tiles
        self.slots = slot_shape[2] // self.tiles
        self.cols = self.count // self.lev
        self.width = self.lon // self.cols
        self.half = self.width // 2
        self.halo = CHAINS * STEPS * self.subs
        self.margin = (LANES - self.width) // 2
        self.extra = self.halo - self.margin
        self.span = self.width + 2 * self.halo
        self.rows = 96
        self.step = 16
        self.back = self.lat - 3
        self.coef_row = self.lat * self.vars
        self.tail_row = self.coef_row + 3 * self.lat
        self.obs_row = self.tail_row + self.lat // 2

    def fits(self):
        return (
            self.count % self.lev == 0
            and self.lon % self.cols == 0
            and self.width % 2 == 0
            and self.half + 2 * self.halo <= LANES
            and 0 <= self.extra <= 5
            and self.vars == 4
            and self.lat == 12
            and self.tiles == 8
            and self.slots * self.tiles == 2 * LANES
            and (self.width + 2 * self.margin) == LANES
            and self.width % 3 == 0
            and self.width * 4 <= 3 * LANES
        )


def pack_kernel(
    plan, count_ref, cell_ref, value_ref, weight_ref, east_ref, north_ref, diff_ref, var_ref, out_ref, wide
):
    p = plan
    pad = LANES
    right = wide.shape[-1] - pad - p.lon
    n_var = p.vars * p.lev
    inner = slice(pad, pad + p.lon)
    for z in range(p.lev):
        for v in range(p.vars):
            first = (v * p.lev + z) * p.step
            wide[first : first + p.lat, inner] = var_ref[v, z]
        for c, ref in enumerate((east_ref, north_ref, diff_ref)):
            first = (n_var + c * p.lev + z) * p.step
            wide[first : first + p.lat, inner] = ref[z]
    for a in range(n_var + 3 * p.lev):
        rows = slice(a * p.step, a * p.step + p.lat)
        wide[rows, :pad] = wide[rows, p.lon : p.lon + pad]
        wide[rows, pad + p.lon :] = wide[rows, pad : pad + right]

    lane = lax.broadcasted_iota(jnp.int32, (1, p.tiles * p.slots), 1)
    filled = jnp.zeros_like(lane)
    for t in range(p.tiles):
        filled = jnp.where(lane // p.slots == t, count_ref[0, t], filled)
    weight = jnp.where(lane % p.slots < filled, weight_ref[...], 0.0)
    obs = []
    for x in (weight, weight * value_ref[...], cell_ref[...].astype(jnp.float32)):
        obs += [x[:, :LANES], x[:, LANES:]]
    obs = jnp.concatenate(obs, axis=0)

    def take(a, rows, start):
        first = a * p.step + rows.start
        return wide[first : first + rows.stop - rows.start, pad + start : pad + start + LANES]

    lanes = lax.broadcasted_iota(jnp.int32, (p.lat // 2, LANES), 1)
    for z in range(p.lev):
        for j in range(p.cols):
            d = z * p.cols + j
            base = d * p.rows
            start = j * p.width - p.margin
            for v in range(p.vars):
                out_ref[pl.ds(base + v, p.lat, stride=p.vars), :] = take(v * p.lev + z, slice(0, p.lat), start)
            for c in range(3):
                r = base + p.coef_row + c * p.lat
                out_ref[r : r + p.lat, :] = take(n_var + c * p.lev + z, slice(0, p.lat), start)
            tail = jnp.zeros((p.lat // 2, LANES), jnp.float32)
            for h in range(2):
                rows = slice(h * (p.lat // 2), (h + 1) * (p.lat // 2))
                for c in range(3):
                    at = (h * 3 + c) * 2 * p.extra
                    a = n_var + c * p.lev + z
                    low = take(a, rows, j * p.width - p.halo - at)
                    high = take(a, rows, (j + 1) * p.width + p.margin - p.extra - at)
                    tail = jnp.where(lanes >= at, low, tail)
                    tail = jnp.where(lanes >= at + p.extra, high, tail)
            r = base + p.tail_row
            out_ref[r : r + 2 * (p.lat // 2), :] = jnp.concatenate([tail, obs], axis=0)


class Stores:
    def __init__(self):
        self.held = []

    def put(self, ref, at, value):
        self.held.append((ref, at, value))

    def flush(self):
        for ref, at, value in self.held:
            ref[at] = value
        self.held = []


def looped(count, unroll, body):
    def many(i, carry):
        stores = Stores()
        for u in range(unroll):
            body(i * unroll + u, stores)
        stores.flush()
        return carry

    lax.fori_loop(0, count // unroll, many, 0)


def swap_blocks(x, slots):
    size, width = x.shape
    sub = lax.broadcasted_iota(jnp.int32, x.shape, 0)
    block = lax.broadcasted_iota(jnp.int32, x.shape, 1) // slots
    out = x
    for d in range(1, size):
        moved = pltpu.roll(pltpu.roll(x, size - d, 0), d * slots, 1)
        out = jnp.where(block == (sub + d) % size, moved, out)
    return out


def chain_kernel(
    plan,
    recv_ref,
    out_ref,
    mid_c,
    east_c,
    west_c,
    north_c,
    south_c,
    weight_g,
    value_g,
    first,
    forcing,
    innov,
    total,
    carried,
    obs_tab,
    extras,
):
    p = plan
    f32 = jnp.float32
    me = lax.axis_index("tm") * p.tiles + lax.axis_index("tile")
    level = (me // p.cols).astype(f32)
    origin = ((me % p.cols) * p.width - p.halo).astype(f32)
    shape = (2 * p.vars, LANES)
    sub = lax.broadcasted_iota(jnp.int32, shape, 0)
    lane = lax.broadcasted_iota(jnp.int32, shape, 1)
    lower = sub < p.vars

    def spread(a, b):
        return (
            jnp.where(lower, a, pltpu.roll(b, p.vars, 0)),
            jnp.where(lower, pltpu.roll(a, p.vars, 0), b),
        )

    stride = p.rows
    stores = Stores()
    for k in range(p.subs):
        raw = []
        for i in range(6):
            raw.append(recv_ref[pl.ds(k * p.tiles * p.rows + p.obs_row + i, p.tiles, stride=stride), :])
        w, wy, cell = (jnp.concatenate(raw[2 * i : 2 * i + 2], axis=1) for i in range(3))
        w, wy, cell = (swap_blocks(x, p.slots) for x in (w, wy, cell))
        row = jnp.floor((cell + 0.5) * (1.0 / p.lon))
        lon = cell - row * p.lon
        group = jnp.floor((row + 0.5) * (1.0 / p.lat))
        lat = row - group * p.lat
        var = jnp.floor((group + 0.5) * (1.0 / p.lev))
        lev = group - var * p.lev
        at = lon - origin
        at = jnp.where(at < 0, at + p.lon, at)
        at = jnp.where(at >= p.lon, at - p.lon, at)
        place = at - p.extra
        place = jnp.where(place < 0, place + LANES, place)
        place = jnp.where(place >= LANES, place - LANES, place)
        here = lev == level
        in_a = here & (at < p.half + 2 * p.halo)
        in_b = here & (at >= p.half) & (at < p.span)
        rows = slice(k * p.tiles, (k + 1) * p.tiles)
        stores.put(obs_tab, (0, rows), lat * p.vars + var)
        stores.put(obs_tab, (1, rows), jnp.where(in_a, place, -1.0))
        stores.put(obs_tab, (2, rows), jnp.where(in_b, place, -1.0))
        for i, x in ((3, w), (6, wy)):
            one = x.astype(jnp.bfloat16).astype(f32)
            two = (x - one).astype(jnp.bfloat16).astype(f32)
            stores.put(obs_tab, (i, rows), one)
            stores.put(obs_tab, (i + 1, rows), two)
            stores.put(obs_tab, (i + 2, rows), x - one - two)
    stores.flush()

    n_rows = p.lat * p.vars
    slots = p.tiles * p.slots
    row_id = lax.broadcasted_iota(jnp.int32, (n_rows, slots), 0).astype(f32)
    lane_id = lax.broadcasted_iota(jnp.int32, (LANES, slots), 0).astype(f32)

    def grid(kt, stores):
        def entry(i):
            return obs_tab[i, pl.ds(kt, 1), :]

        match = row_id == entry(0)
        left = jnp.concatenate(
            [jnp.where(match, entry(i), 0.0).astype(jnp.bfloat16) for i in range(3, 9)], axis=0
        )
        right = jnp.concatenate(
            [jnp.where(lane_id == entry(i), 1.0, 0.0).astype(jnp.bfloat16) for i in (1, 2)], axis=0
        )
        full = lax.dot_general(left, right, (((1,), (1,)), ((), ())), preferred_element_type=f32)
        for i, ref in ((0, weight_g), (3, value_g)):
            parts = [full[(i + q) * n_rows : (i + q + 1) * n_rows] for q in range(3)]
            summed = parts[0] + (parts[1] + parts[2])
            for pair in range(p.lat // 2):
                rows = slice(2 * p.vars * pair, 2 * p.vars * (pair + 1))
                one, two = spread(summed[rows, :LANES], summed[rows, LANES:])
                stores.put(ref, kt * p.lat + 2 * pair, one)
                stores.put(ref, kt * p.lat + 2 * pair + 1, two)

    looped(p.count, 4, grid)

    mask = (lower & (lane >= LANES - p.extra)) | (~lower & (lane < p.extra))
    part = p.lat // 2

    def edges(kt, stores):
        tail = recv_ref[pl.ds(kt * p.rows + p.tail_row, part), :]
        for h in range(2):
            for c in range(3):
                at = (h * 3 + c) * 2 * p.extra
                moved = pltpu.roll(tail, (LANES - p.extra - at) % LANES, 1)
                stores.put(extras, (c, kt, slice(h * part, (h + 1) * part)), moved)

    looped(p.count, 8, edges)

    def widen(kt, stores):
        base = kt * p.rows
        for l in range(p.lat):
            got = []
            for c in range(3):
                main = recv_ref[pl.ds(base + p.coef_row + c * p.lat + l, 1), :]
                edge = extras[c, kt, l : l + 1, :]
                got.append(
                    jnp.where(mask, jnp.broadcast_to(edge, shape), jnp.broadcast_to(main, shape))
                )
            east, north, diff = got
            east = 0.5 * east
            north = 0.5 * north
            at = kt * p.lat + l
            stores.put(mid_c, at, 1.0 - 4.0 * diff)
            stores.put(east_c, at, diff - east)
            stores.put(west_c, at, diff + east)
            stores.put(north_c, at, diff - north)
            stores.put(south_c, at, diff + north)

    looped(p.count, 2, widen)

    n = p.nlat
    zero = jnp.zeros(shape, f32)

    def adjoint(base, load, emit):
        def terms(l, x):
            at = base + l
            here = (
                mid_c[at] * x
                + pltpu.roll(east_c[at] * x, 1, 1)
                + pltpu.roll(west_c[at] * x, LANES - 1, 1)
            )
            return here, north_c[at] * x, south_c[at] * x

        nothing = (zero, zero, zero)
        rows = [nothing] * (STEPS * 3)
        for l in range(n + STEPS):
            x = load(l) if l < n else None
            for s in range(STEPS):
                at = l - s
                now = terms(at, x) if 0 <= at < n else nothing
                before, last = rows[3 * s + 1], rows[3 * s + 2]
                rows[3 * s : 3 * s + 3] = [before, last, now]
                x = last[0] + before[1] + now[2] if 1 <= at <= n else None
            if x is not None:
                emit(l - STEPS, x)

    def forward(base, load, emit):
        def value(l, below, x, above):
            at = base + l
            return (
                mid_c[at] * x
                + east_c[at] * pltpu.roll(x, LANES - 1, 1)
                + west_c[at] * pltpu.roll(x, 1, 1)
                + north_c[at] * above
                + south_c[at] * below
            )

        rows = [zero] * (STEPS * 3)
        for l in range(n + STEPS):
            x = load(l) if l < n else None
            for s in range(STEPS):
                at = l - s
                now = x if 0 <= at < n else zero
                below, last = rows[3 * s + 1], rows[3 * s + 2]
                rows[3 * s : 3 * s + 3] = [below, last, now]
                x = value(at - 1, below, last, now) if 1 <= at <= n else None
            if x is not None:
                emit(l - STEPS, x)

    def clear(ref):
        for l in range(n):
            ref[l] = zero

    clear(carried)

    def first_adjoint(i, _):
        k = p.subs - 1 - i
        base = k * n
        held = {}
        stores = Stores()

        def load(l):
            return carried[l] - value_g[base + l]

        def emit(l, y):
            stores.put(carried, l, y)
            stores.put(first, base + l, y)
            held[l] = y
            if l % 2:
                row = k * p.tiles * p.rows + (l // p.lat) * p.rows + (l % p.lat) // 2 * 2 * p.vars
                var = recv_ref[pl.ds(pl.multiple_of(row, 8), 2 * p.vars), :]
                one, two = spread(var, var)
                stores.put(forcing, base + l - 1, -0.5 * (one * held.pop(l - 1)))
                stores.put(forcing, base + l, -0.5 * (two * held.pop(l)))

        adjoint(base, load, emit)
        stores.flush()
        return 0

    lax.fori_loop(0, p.subs, first_adjoint, 0)

    clear(carried)

    def run_forward(k, _):
        base = k * n
        stores = Stores()

        def load(l):
            return carried[l] + forcing[base + l]

        def emit(l, y):
            stores.put(carried, l, y)
            stores.put(innov, base + l, weight_g[base + l] * y - value_g[base + l])

        forward(base, load, emit)
        stores.flush()
        return 0

    lax.fori_loop(0, p.subs, run_forward, 0)

    clear(carried)

    def second_adjoint(i, _):
        base = (p.subs - 1 - i) * n
        stores = Stores()

        def load(l):
            return carried[l] + innov[base + l]

        def emit(l, y):
            stores.put(carried, l, y)
            stores.put(total, base + l, y + 0.5 * first[base + l])

        adjoint(base, load, emit)
        stores.flush()
        return 0

    lax.fori_loop(0, p.subs, second_adjoint, 0)

    in_half = lane < p.margin + p.half
    own = (lane >= p.margin) & (lane < p.margin + p.width)
    third = p.width // 3

    def fold(kt, stores):
        rows = []
        for l in range(p.lat):
            y = total[kt * p.lat + l]
            rows.append(jnp.where(in_half, y, pltpu.roll(y, p.vars, 0)))
        for l in range(p.back):
            guest = pltpu.roll(rows[p.back + l % 3], p.width - third * (l // 3), 1)
            stores.put(out_ref, kt * p.back + l, jnp.where(own, rows[l], guest)[: p.vars])

    looped(p.count, 4, fold)


def finish_kernel(plan, recv_ref, var_ref, out_ref, wide):
    p = plan
    third = p.width // 3
    lane = lax.broadcasted_iota(jnp.int32, (p.lat, LANES), 1)
    row = lax.broadcasted_iota(jnp.int32, (p.lat, LANES), 0)
    own = slice(p.margin, p.margin + p.width)
    ahead = p.back * p.vars
    count = recv_ref.shape[0]
    wide[:ahead] = jnp.zeros((ahead, LANES), jnp.float32)
    wide[ahead : ahead + count] = recv_ref[...]
    wide[ahead + count :] = jnp.zeros((wide.shape[0] - ahead - count, LANES), jnp.float32)
    for z in range(p.lev):
        for j in range(p.cols):
            cols = slice(j * p.width, (j + 1) * p.width)
            for v in range(p.vars):
                start = ahead + (z * p.cols + j) * p.back * p.vars + v
                piece = wide[pl.ds(start, p.lat, stride=p.vars), :]
                for i in range(3):
                    guest = wide[pl.ds(start + (3 * i - p.back) * p.vars, p.lat, stride=p.vars), :]
                    guest = pltpu.roll(guest, LANES - p.width + third * i, 1)
                    late = guest if i == 0 else jnp.where(lane >= p.margin + third * i, guest, late)
                piece = jnp.where(row < p.back, piece, late)
                out_ref[v, z, :, cols] = -0.5 * (var_ref[v, z, :, cols] * piece[:, own])


def transposed(
    plan, advect_east, advect_north, diffusion, background_var, obs_cell, obs_value, obs_weight, obs_count
):
    p = plan
    vmem = pl.BlockSpec(memory_space=pltpu.VMEM)
    params = pltpu.CompilerParams(vmem_limit_bytes=VMEM_LIMIT)
    f32 = jnp.float32
    wide = (p.vars + 3) * p.lev

    var = background_var[0]
    packed = pl.pallas_call(
        functools.partial(pack_kernel, p),
        out_shape=jax.ShapeDtypeStruct((p.count * p.rows, LANES), f32),
        in_specs=[pl.BlockSpec(memory_space=pltpu.SMEM)] + [vmem] * 7,
        out_specs=vmem,
        scratch_shapes=[pltpu.VMEM((wide * p.step, 14 * LANES), f32)],
        compiler_params=params,
        name="pack",
    )(
        obs_count.reshape(1, -1),
        obs_cell.reshape(1, -1),
        obs_value.reshape(1, -1),
        obs_weight.reshape(1, -1),
        advect_east[0],
        advect_north[0],
        diffusion[0],
        var,
    )
    received = lax.all_to_all(packed, ("tm", "tile"), 0, 0, tiled=True)
    field = pltpu.VMEM((p.subs * p.nlat, 2 * p.vars, LANES), f32)
    back = pl.pallas_call(
        functools.partial(chain_kernel, p),
        out_shape=jax.ShapeDtypeStruct((p.count * p.back, p.vars, LANES), f32),
        in_specs=[vmem],
        out_specs=vmem,
        scratch_shapes=[field] * 11
        + [
            pltpu.VMEM((p.nlat, 2 * p.vars, LANES), f32),
            pltpu.VMEM((9, p.count, p.tiles * p.slots), f32),
            pltpu.VMEM((3, p.count, p.lat, LANES), f32),
        ],
        compiler_params=params,
        name="chains",
    )(received)
    returned = lax.all_to_all(back, ("tm", "tile"), 0, 0, tiled=True)
    returned = returned.reshape(-1, LANES)
    increment = pl.pallas_call(
        functools.partial(finish_kernel, p),
        out_shape=jax.ShapeDtypeStruct(var.shape, f32),
        in_specs=[vmem] * 2,
        out_specs=vmem,
        scratch_shapes=[pltpu.VMEM((p.count * p.back * p.vars + 2 * p.back * p.vars, LANES), f32)],
        compiler_params=params,
        name="finish",
    )(returned, var)
    return increment[None]


def solution(mesh):
    def run(*args):
        plan = Plan(mesh.shape, args[3].shape, args[4].shape)
        work = functools.partial(transposed, plan) if plan.fits() else per_device
        return jax.shard_map(
            work,
            mesh=mesh,
            in_specs=(
                P("tm", None, "tile", None),
                P("tm", None, "tile", None),
                P("tm", None, "tile", None),
                P("tm", None, None, "tile", None),
                P("tm", "tile", None),
                P("tm", "tile", None),
                P("tm", "tile", None),
                P("tm", "tile", None),
            ),
            out_specs=P("tm", None, None, "tile", None),
            check_vma=False,
        )(*args)

    return run
```

```python
import functools

import jax
import jax.numpy as jnp
from jax import lax
from jax.experimental import pallas as pl
from jax.experimental.pallas import tpu as pltpu
from jax.sharding import PartitionSpec as P

STEPS = 2
ITERS = 2
CHAINS = 3
LANES = 128
BLOCK = 24
VMEM_LIMIT = 48 * 1024 * 1024


def padded(block, sides, width):
    for axis, dim in sides:
        count = lax.axis_size(axis)
        forward = [(i, i + 1) for i in range(count - 1)]
        backward = [(target, source) for source, target in forward]
        low = lax.ppermute(
            lax.slice_in_dim(block, block.shape[dim] - width, None, axis=dim), axis, forward
        )
        high = lax.ppermute(lax.slice_in_dim(block, 0, width, axis=dim), axis, backward)
        block = jnp.concatenate([low, block, high], axis=dim)
    return block


def shifted(value, axis, steps):
    count = lax.axis_size(axis)
    first, last = (max(0, -steps), min(count, count - steps))
    return lax.ppermute(value, axis, [(source, source + steps) for source in range(first, last)])


def apply_step(field, coef, adjoint):
    east_c = coef[0]
    north_c = coef[1]
    diff_c = coef[2]
    if adjoint:
        to_east = (diff_c - 0.5 * east_c) * field
        to_west = (diff_c + 0.5 * east_c) * field
        to_north = (diff_c - 0.5 * north_c) * field
        to_south = (diff_c + 0.5 * north_c) * field
        middle = (1.0 - 4.0 * diff_c[:, 1:-1]) * field[:, :, 1:-1]
        return (
            middle
            + jnp.roll(to_east[:, :, 1:-1], 1, axis=-1)
            + jnp.roll(to_west[:, :, 1:-1], -1, axis=-1)
            + to_north[:, :, :-2]
            + to_south[:, :, 2:]
        )
    inner = field[:, :, 1:-1]
    diff_in = diff_c[:, 1:-1]
    east_in = east_c[:, 1:-1]
    north_in = north_c[:, 1:-1]
    return (
        (1.0 - 4.0 * diff_in) * inner
        + (diff_in - 0.5 * east_in) * jnp.roll(inner, -1, axis=-1)
        + (diff_in + 0.5 * east_in) * jnp.roll(inner, 1, axis=-1)
        + (diff_in - 0.5 * north_in) * field[:, :, 2:]
        + (diff_in + 0.5 * north_in) * field[:, :, :-2]
    )


def advance(field, coef, adjoint):
    for repeat in range(STEPS):
        extended = padded(field, (("tile", 2),), 1)
        field = apply_step(extended, coef, adjoint)
    return field


def per_device(
    advect_east, advect_north, diffusion, background_var, obs_cell, obs_value, obs_weight, obs_count
):
    windows_count = lax.axis_size("tm")
    tiles = lax.axis_size("tile")
    coefs = jnp.stack([advect_east[0], advect_north[0], diffusion[0]])
    coef_ext = padded(coefs, (("tile", 2),), 1)
    cells = obs_cell.reshape(tiles, -1)
    slot_count = cells.shape[1]
    live = jnp.arange(slot_count, dtype=jnp.int32)[None, :] < obs_count.reshape(tiles)[:, None]
    masked = obs_weight.reshape(tiles, -1) * live.astype(jnp.float32)
    received = lax.all_to_all(
        jnp.stack([obs_value.reshape(tiles, -1), masked]),
        "tile",
        split_axis=1,
        concat_axis=1,
        tiled=True,
    )
    received_cells = lax.all_to_all(cells, "tile", split_axis=0, concat_axis=0, tiled=True)
    departures = received[0].reshape(-1)
    obs_weights = received[1].reshape(-1)
    flat_cells = received_cells.reshape(-1)
    local_var = background_var[0]
    state_shape = local_var.shape
    cell_total = state_shape[0] * state_shape[1] * state_shape[2] * state_shape[3]
    increment = jnp.zeros(state_shape, jnp.float32)
    for iteration in range(ITERS):
        if iteration == 0:
            innov = obs_weights * (0.0 - departures)
        else:
            forward_carried = advance(increment, coef_ext, False)
            for forward_window in range(windows_count - 1):
                forward_incoming = shifted(forward_carried, "tm", 1)
                forward_carried = advance(forward_incoming + increment, coef_ext, False)
            innov = obs_weights * (
                jnp.take(forward_carried.reshape(cell_total), flat_cells, axis=0) - departures
            )
        gridded = jnp.zeros((cell_total,), jnp.float32).at[flat_cells].add(innov)
        source = gridded.reshape(state_shape)
        carried = advance(source, coef_ext, True)
        for window in range(windows_count - 1):
            incoming = shifted(carried, "tm", -1)
            carried = advance(incoming + source, coef_ext, True)
        increment = increment - 0.5 * (increment + local_var * carried)
    return increment[None]


class Plan:
    def __init__(self, mesh_shape, var_shape, slot_shape):
        self.subs, self.tiles = mesh_shape["tm"], mesh_shape["tile"]
        self.count = self.subs * self.tiles
        _, self.vars, self.lev, self.nlat, self.lon = var_shape
        self.lat = self.nlat // self.tiles
        self.slots = slot_shape[2] // self.tiles
        self.cols = self.count // self.lev
        self.width = self.lon // self.cols
        self.half = self.width // 2
        self.halo = CHAINS * STEPS * self.subs
        self.margin = (LANES - self.width) // 2
        self.extra = self.halo - self.margin
        self.span = self.width + 2 * self.halo
        self.rows = 96
        self.coef_row = self.lat * self.vars
        self.tail_row = self.coef_row + 3 * self.lat
        self.obs_row = self.tail_row + self.lat // 2

    def fits(self):
        return (
            self.count % self.lev == 0
            and self.lon % self.cols == 0
            and self.width % 2 == 0
            and self.half + 2 * self.halo <= LANES
            and 0 <= self.extra <= 5
            and -(-self.extra // STEPS) <= self.subs
            and self.vars == 4
            and self.lat == 12
            and self.tiles == 8
            and self.slots * self.tiles == 2 * LANES
            and (self.width + 2 * self.margin) == LANES
            and self.nlat % BLOCK == 0
            and BLOCK % self.lat == 0
            and self.width * 4 <= 3 * LANES
        )


def pack_kernel(
    plan, count_ref, cell_ref, value_ref, weight_ref, east_ref, north_ref, diff_ref, var_ref, out_ref, wide
):
    p = plan
    pad = LANES
    right = wide.shape[-1] - pad - p.lon
    inner = slice(pad, pad + p.lon)
    per_level = p.vars + 3

    def widen(z, carry):
        for v in range(p.vars):
            wide[z * per_level + v, :, inner] = var_ref[v, z]
        for c, ref in enumerate((east_ref, north_ref, diff_ref)):
            wide[z * per_level + p.vars + c, :, inner] = ref[z]
        for a in range(per_level):
            at = z * per_level + a
            wide[at, :, :pad] = wide[at, :, p.lon : p.lon + pad]
            wide[at, :, pad + p.lon :] = wide[at, :, pad : pad + right]
        return carry

    lax.fori_loop(0, p.lev, widen, 0)

    lane = lax.broadcasted_iota(jnp.int32, (1, p.tiles * p.slots), 1)
    filled = jnp.zeros_like(lane)
    for t in range(p.tiles):
        filled = jnp.where(lane // p.slots == t, count_ref[0, t], filled)
    weight = jnp.where(lane % p.slots < filled, weight_ref[...], 0.0)
    obs = []
    for x in (weight, weight * value_ref[...], cell_ref[...].astype(jnp.float32)):
        obs += [x[:, :LANES], x[:, LANES:]]
    obs = jnp.concatenate(obs, axis=0)

    lanes = lax.broadcasted_iota(jnp.int32, (p.lat // 2, LANES), 1)

    def blocks(z, carry):
        def take(a, low, high, start):
            return wide[z * per_level + a, low:high, pad + start : pad + start + LANES]

        for j in range(p.cols):
            base = (z * p.cols + j) * p.rows
            start = j * p.width - p.margin
            for v in range(p.vars):
                out_ref[pl.ds(base + v, p.lat, stride=p.vars), :] = take(v, 0, p.lat, start)
            for c in range(3):
                out_ref[pl.ds(base + p.coef_row + c * p.lat, p.lat), :] = take(p.vars + c, 0, p.lat, start)
            tail = jnp.zeros((p.lat // 2, LANES), jnp.float32)
            for h in range(2):
                low, high = h * (p.lat // 2), (h + 1) * (p.lat // 2)
                for c in range(3):
                    at = (h * 3 + c) * 2 * p.extra
                    west = take(p.vars + c, low, high, j * p.width - p.halo - at)
                    east = take(p.vars + c, low, high, (j + 1) * p.width + p.margin - p.extra - at)
                    tail = jnp.where(lanes >= at, west, tail)
                    tail = jnp.where(lanes >= at + p.extra, east, tail)
            out_ref[pl.ds(base + p.tail_row, 2 * (p.lat // 2)), :] = jnp.concatenate([tail, obs], axis=0)
        return carry

    lax.fori_loop(0, p.lev, blocks, 0)


def turn(x, shift, axis):
    size = x.shape[axis]
    shift %= size
    if shift == 0:
        return x
    high = lax.slice_in_dim(x, size - shift, size, axis=axis)
    low = lax.slice_in_dim(x, 0, size - shift, axis=axis)
    return jnp.concatenate([high, low], axis=axis)


def to_east(x, wrap):
    edge = x[:, -1:] if wrap else jnp.zeros_like(x[:, -1:])
    return jnp.concatenate([edge, x[:, :-1]], axis=1)


def to_west(x, wrap):
    edge = x[:, :1] if wrap else jnp.zeros_like(x[:, :1])
    return jnp.concatenate([x[:, 1:], edge], axis=1)


class Stores:
    def __init__(self):
        self.held = []

    def put(self, ref, at, value):
        self.held.append((ref, at, value))

    def flush(self):
        for ref, at, value in self.held:
            ref[at] = value
        self.held = []


def looped(count, unroll, body):
    def many(i, carry):
        stores = Stores()
        for u in range(unroll):
            body(i * unroll + u, stores)
        stores.flush()
        return carry

    lax.fori_loop(0, count // unroll, many, 0)


def swap_blocks(x, slots):
    size, width = x.shape
    sub = lax.broadcasted_iota(jnp.int32, x.shape, 0)
    block = lax.broadcasted_iota(jnp.int32, x.shape, 1) // slots
    out = x
    for d in range(1, size):
        moved = turn(turn(x, size - d, 0), d * slots, 1)
        out = jnp.where(block == (sub + d) % size, moved, out)
    return out


def chain_kernel(
    plan,
    recv_ref,
    out_ref,
    mid_c,
    east_c,
    west_c,
    north_c,
    south_c,
    weight_g,
    value_g,
    first,
    forcing,
    innov,
    total,
    carried,
    by_var,
    obs_tab,
    extras,
):
    p = plan
    f32 = jnp.float32
    me = lax.axis_index("tm") * p.tiles + lax.axis_index("tile")
    level = (me // p.cols).astype(f32)
    origin = ((me % p.cols) * p.width - p.halo).astype(f32)
    shape = (2 * p.vars, LANES)
    sub = lax.broadcasted_iota(jnp.int32, shape, 0)
    lane = lax.broadcasted_iota(jnp.int32, shape, 1)
    lower = sub < p.vars

    def spread(a, b):
        return (
            jnp.concatenate([a[: p.vars], b[: p.vars]], axis=0),
            jnp.concatenate([a[p.vars :], b[p.vars :]], axis=0),
        )

    stride = p.rows

    def observe(k, stores):
        raw = []
        for i in range(6):
            raw.append(recv_ref[pl.ds(k * p.tiles * p.rows + p.obs_row + i, p.tiles, stride=stride), :])
        w, wy, cell = (jnp.concatenate(raw[2 * i : 2 * i + 2], axis=1) for i in range(3))
        w, wy, cell = (swap_blocks(x, p.slots) for x in (w, wy, cell))
        row = jnp.floor((cell + 0.5) * (1.0 / p.lon))
        lon = cell - row * p.lon
        group = jnp.floor((row + 0.5) * (1.0 / p.lat))
        lat = row - group * p.lat
        var = jnp.floor((group + 0.5) * (1.0 / p.lev))
        lev = group - var * p.lev
        at = lon - origin
        at = jnp.where(at < 0, at + p.lon, at)
        at = jnp.where(at >= p.lon, at - p.lon, at)
        place = at - p.extra
        place = jnp.where(place < 0, place + LANES, place)
        place = jnp.where(place >= LANES, place - LANES, place)
        here = lev == level
        in_a = here & (at < p.half + 2 * p.halo)
        in_b = here & (at >= p.half) & (at < p.span)
        rows = pl.ds(k * p.tiles, p.tiles)
        stores.put(obs_tab, (0, rows), lat * p.vars + var)
        stores.put(obs_tab, (1, rows), jnp.where(in_a, place, -1.0))
        stores.put(obs_tab, (2, rows), jnp.where(in_b, place, -1.0))
        for i, x in ((3, w), (6, wy)):
            one = x.astype(jnp.bfloat16).astype(f32)
            two = (x - one).astype(jnp.bfloat16).astype(f32)
            stores.put(obs_tab, (i, rows), one)
            stores.put(obs_tab, (i + 1, rows), two)
            stores.put(obs_tab, (i + 2, rows), x - one - two)

    looped(p.subs, 1, observe)

    n_rows = p.lat * p.vars
    slots = p.tiles * p.slots
    row_id = lax.broadcasted_iota(jnp.int32, (n_rows, slots), 0).astype(f32)
    lane_id = lax.broadcasted_iota(jnp.int32, (LANES, slots), 0).astype(f32)

    def grid(kt, stores):
        def entry(i):
            return obs_tab[i, pl.ds(kt, 1), :]

        match = row_id == entry(0)
        left = jnp.concatenate(
            [jnp.where(match, entry(i), 0.0).astype(jnp.bfloat16) for i in range(3, 9)], axis=0
        )
        right = jnp.concatenate(
            [jnp.where(lane_id == entry(i), 1.0, 0.0).astype(jnp.bfloat16) for i in (1, 2)], axis=0
        )
        full = lax.dot_general(left, right, (((1,), (1,)), ((), ())), preferred_element_type=f32)
        for i, ref in ((0, weight_g), (3, value_g)):
            parts = [full[(i + q) * n_rows : (i + q + 1) * n_rows] for q in range(3)]
            summed = parts[0] + (parts[1] + parts[2])
            for pair in range(p.lat // 2):
                rows = slice(2 * p.vars * pair, 2 * p.vars * (pair + 1))
                one, two = spread(summed[rows, :LANES], summed[rows, LANES:])
                at = kt * p.lat + kt // p.tiles * STEPS + 2 * pair
                stores.put(ref, at, one)
                stores.put(ref, at + 1, two)

    looped(p.count, 2, grid)

    mask = (lower & (lane >= LANES - p.extra)) | (~lower & (lane < p.extra))
    part = p.lat // 2

    def edges(kt, stores):
        tail = recv_ref[pl.ds(kt * p.rows + p.tail_row, part), :]
        for h in range(2):
            for c in range(3):
                at = (h * 3 + c) * 2 * p.extra
                moved = turn(tail, LANES - p.extra - at, 1)
                stores.put(extras, (c, kt, slice(h * part, (h + 1) * part)), moved)

    looped(p.count, 4, edges)

    def widen(kt, stores):
        base = kt * p.rows
        for l in range(p.lat):
            got = []
            for c in range(3):
                main = recv_ref[pl.ds(base + p.coef_row + c * p.lat + l, 1), :]
                edge = extras[c, kt, l : l + 1, :]
                got.append(
                    jnp.where(mask, jnp.broadcast_to(edge, shape), jnp.broadcast_to(main, shape))
                )
            east, north, diff = got
            east = 0.5 * east
            north = 0.5 * north
            at = kt * p.lat + kt // p.tiles * STEPS + l
            stores.put(mid_c, at, 1.0 - 4.0 * diff)
            stores.put(east_c, at, diff - east)
            stores.put(west_c, at, diff + east)
            stores.put(north_c, at, diff - north)
            stores.put(south_c, at, diff + north)

    looped(p.count, 1, widen)

    n = p.nlat
    pitch = n + STEPS
    zero = jnp.zeros(shape, f32)

    for k in range(p.subs):
        for l in range(n, pitch):
            for ref in (mid_c, east_c, west_c, north_c, south_c, value_g, forcing, innov):
                ref[k * pitch + l] = zero

    def sweep(base, load, emit, stage, width):
        states = []
        for l in range(STEPS):
            x = load(l)
            for s in range(l + 1):
                if s == len(states):
                    states.append((zero,) * width)
                states[s], x = stage(base + l - s, states[s], x, s == l)
        states = tuple(states)

        def many(g, states):
            states = list(states)
            stores = Stores()
            for u in range(BLOCK):
                r = g * BLOCK + u
                x = load(r + STEPS)
                for s in range(STEPS):
                    states[s], x = stage(base + r + STEPS - s, states[s], x)
                emit(r, u, x, stores)
            stores.flush()
            return tuple(states)

        lax.fori_loop(0, n // BLOCK, many, states)

    def adjoint_stage(wrap):
        def stage(at, state, x, fresh=False):
            here, below = state[0], state[1]
            now = (
                mid_c[at] * x
                + to_east(east_c[at] * x, wrap)
                + to_west(west_c[at] * x, wrap)
            )
            done = here + below + south_c[at] * x
            return (now, state[2], north_c[at] * x), done

        return stage

    def forward_stage(at, state, x, fresh=False):
        if fresh:
            return (zero, x), None
        below, last = state
        row = at - 1
        done = (
            mid_c[row] * last
            + east_c[row] * to_west(last, False)
            + west_c[row] * to_east(last, False)
            + north_c[row] * x
            + south_c[row] * below
        )
        return (last, x), done

    def clear(ref):
        def body(l, carry):
            ref[l] = zero
            return carry

        lax.fori_loop(0, pitch, body, 0, unroll=2)

    clear(carried)

    def first_adjoint(i, wrap):
        k = p.subs - 1 - i
        base = k * pitch
        held = []

        def load(l):
            return carried[l] - value_g[base + l]

        def emit(r, u, y, stores):
            stores.put(carried, r, y)
            stores.put(first, base + r, y)
            held.append(y)
            if u % 2:
                tile = (r - u) // p.lat + u // p.lat
                row = (k * p.tiles + tile) * p.rows + u % p.lat // 2 * 2 * p.vars
                var = recv_ref[pl.ds(pl.multiple_of(row, 8), 2 * p.vars), :]
                one, two = spread(var, var)
                stores.put(forcing, base + r - 1, -0.5 * (one * held.pop(0)))
                stores.put(forcing, base + r, -0.5 * (two * held.pop(0)))

        sweep(base, load, emit, adjoint_stage(wrap), 3)

    wrapped = -(-p.extra // STEPS)
    lax.fori_loop(0, wrapped, lambda i, _: (first_adjoint(i, True), 0)[1], 0)
    lax.fori_loop(wrapped, p.subs, lambda i, _: (first_adjoint(i, False), 0)[1], 0)

    clear(carried)

    def run_forward(k, carry):
        base = k * pitch

        def load(l):
            return carried[l] + forcing[base + l]

        def emit(r, u, y, stores):
            stores.put(carried, r, y)
            stores.put(innov, base + r, weight_g[base + r] * y - value_g[base + r])

        sweep(base, load, emit, forward_stage, 2)
        return carry

    lax.fori_loop(0, p.subs, run_forward, 0)

    clear(carried)

    def second_adjoint(i, carry):
        base = (p.subs - 1 - i) * pitch

        def load(l):
            return carried[l] + innov[base + l]

        def emit(r, u, y, stores):
            stores.put(carried, r, y)
            stores.put(total, base + r, y + 0.5 * first[base + r])

        sweep(base, load, emit, adjoint_stage(False), 3)
        return carry

    lax.fori_loop(0, p.subs, second_adjoint, 0)

    in_half = lane < p.margin + p.half

    def fold(kt, stores):
        base = kt * p.lat + kt // p.tiles * STEPS
        for l in range(p.lat):
            y = total[base + l]
            y = jnp.where(in_half[: p.vars], y[: p.vars], y[p.vars :])
            stores.put(by_var, (pl.ds(kt * p.lat + l, p.vars, stride=p.count * p.lat),), y)

    looped(p.count, 2, fold)

    def join(kt, stores):
        own = slice(p.margin, p.margin + p.width)
        cols = [by_var[pl.ds(v * p.count * p.lat + kt * p.lat, p.lat), :][:, own] for v in range(p.vars)]
        spare = 3 * LANES - p.vars * p.width
        line = jnp.concatenate(cols + [jnp.zeros((p.lat, spare), f32)], axis=1)
        for i in range(3):
            at = (pl.ds(kt * p.lat * 3 + i, p.lat, stride=3),)
            stores.put(out_ref, at, line[:, i * LANES : (i + 1) * LANES])

    looped(p.count, 2, join)


def finish_kernel(plan, recv_ref, var_ref, out_ref):
    p = plan

    def level(z, carry):
        for j in range(p.cols):
            start = (z * p.cols + j) * p.lat * 3
            rows = [recv_ref[pl.ds(start + i, p.lat, stride=3), :] for i in range(3)]
            for v in range(p.vars):
                at, end = v * p.width, (v + 1) * p.width
                col = j * p.width
                while at < end:
                    i, low = divmod(at, LANES)
                    size = min(end - at, LANES - low)
                    cols = slice(col, col + size)
                    out_ref[v, z, :, cols] = -0.5 * (var_ref[v, z, :, cols] * rows[i][:, low : low + size])
                    at, col = at + size, col + size
        return carry

    lax.fori_loop(0, p.lev, level, 0)


def transposed(
    plan, advect_east, advect_north, diffusion, background_var, obs_cell, obs_value, obs_weight, obs_count
):
    p = plan
    vmem = pl.BlockSpec(memory_space=pltpu.VMEM)
    params = pltpu.CompilerParams(vmem_limit_bytes=VMEM_LIMIT)
    f32 = jnp.float32
    wide = (p.vars + 3) * p.lev

    var = background_var[0]
    packed = pl.pallas_call(
        functools.partial(pack_kernel, p),
        out_shape=jax.ShapeDtypeStruct((p.count * p.rows, LANES), f32),
        in_specs=[pl.BlockSpec(memory_space=pltpu.SMEM)] + [vmem] * 7,
        out_specs=vmem,
        scratch_shapes=[pltpu.VMEM((wide, p.lat, 14 * LANES), f32)],
        compiler_params=params,
        name="pack",
    )(
        obs_count.reshape(1, -1),
        obs_cell.reshape(1, -1),
        obs_value.reshape(1, -1),
        obs_weight.reshape(1, -1),
        advect_east[0],
        advect_north[0],
        diffusion[0],
        var,
    )
    received = lax.all_to_all(packed, ("tm", "tile"), 0, 0, tiled=True)
    field = pltpu.VMEM((p.subs * (p.nlat + STEPS), 2 * p.vars, LANES), f32)
    back = pl.pallas_call(
        functools.partial(chain_kernel, p),
        out_shape=jax.ShapeDtypeStruct((p.count * p.lat * 3, LANES), f32),
        in_specs=[vmem],
        out_specs=vmem,
        scratch_shapes=[field] * 11
        + [
            pltpu.VMEM((p.nlat + STEPS, 2 * p.vars, LANES), f32),
            pltpu.VMEM((p.vars * p.count * p.lat, LANES), f32),
            pltpu.VMEM((9, p.count, p.tiles * p.slots), f32),
            pltpu.VMEM((3, p.count, p.lat, LANES), f32),
        ],
        compiler_params=params,
        name="chains",
    )(received)
    back = back.reshape(-1, 4, LANES)
    returned = lax.all_to_all(back, ("tm", "tile"), 0, 0, tiled=True)
    returned = returned.reshape(-1, LANES)
    increment = pl.pallas_call(
        functools.partial(finish_kernel, p),
        out_shape=jax.ShapeDtypeStruct(var.shape, f32),
        in_specs=[vmem] * 2,
        out_specs=vmem,
        compiler_params=params,
        name="finish",
    )(returned, var)
    return increment[None]


def solution(mesh):
    def run(*args):
        plan = Plan(mesh.shape, args[3].shape, args[4].shape)
        work = functools.partial(transposed, plan) if plan.fits() else per_device
        return jax.shard_map(
            work,
            mesh=mesh,
            in_specs=(
                P("tm", None, "tile", None),
                P("tm", None, "tile", None),
                P("tm", None, "tile", None),
                P("tm", None, None, "tile", None),
                P("tm", "tile", None),
                P("tm", "tile", None),
                P("tm", "tile", None),
                P("tm", "tile", None),
            ),
            out_specs=P("tm", None, None, "tile", None),
            check_vma=False,
        )(*args)

    return run
```

```python
import functools

import jax
import jax.numpy as jnp
from jax import lax
from jax.experimental import pallas as pl
from jax.experimental.pallas import tpu as pltpu
from jax.sharding import PartitionSpec as P

STEPS = 2
ITERS = 2
CHAINS = 3
LANES = 128
BLOCK = 24
VMEM_LIMIT = 48 * 1024 * 1024


def padded(block, sides, width):
    for axis, dim in sides:
        count = lax.axis_size(axis)
        forward = [(i, i + 1) for i in range(count - 1)]
        backward = [(target, source) for source, target in forward]
        low = lax.ppermute(
            lax.slice_in_dim(block, block.shape[dim] - width, None, axis=dim), axis, forward
        )
        high = lax.ppermute(lax.slice_in_dim(block, 0, width, axis=dim), axis, backward)
        block = jnp.concatenate([low, block, high], axis=dim)
    return block


def shifted(value, axis, steps):
    count = lax.axis_size(axis)
    first, last = (max(0, -steps), min(count, count - steps))
    return lax.ppermute(value, axis, [(source, source + steps) for source in range(first, last)])


def apply_step(field, coef, adjoint):
    east_c = coef[0]
    north_c = coef[1]
    diff_c = coef[2]
    if adjoint:
        to_east = (diff_c - 0.5 * east_c) * field
        to_west = (diff_c + 0.5 * east_c) * field
        to_north = (diff_c - 0.5 * north_c) * field
        to_south = (diff_c + 0.5 * north_c) * field
        middle = (1.0 - 4.0 * diff_c[:, 1:-1]) * field[:, :, 1:-1]
        return (
            middle
            + jnp.roll(to_east[:, :, 1:-1], 1, axis=-1)
            + jnp.roll(to_west[:, :, 1:-1], -1, axis=-1)
            + to_north[:, :, :-2]
            + to_south[:, :, 2:]
        )
    inner = field[:, :, 1:-1]
    diff_in = diff_c[:, 1:-1]
    east_in = east_c[:, 1:-1]
    north_in = north_c[:, 1:-1]
    return (
        (1.0 - 4.0 * diff_in) * inner
        + (diff_in - 0.5 * east_in) * jnp.roll(inner, -1, axis=-1)
        + (diff_in + 0.5 * east_in) * jnp.roll(inner, 1, axis=-1)
        + (diff_in - 0.5 * north_in) * field[:, :, 2:]
        + (diff_in + 0.5 * north_in) * field[:, :, :-2]
    )


def advance(field, coef, adjoint):
    for repeat in range(STEPS):
        extended = padded(field, (("tile", 2),), 1)
        field = apply_step(extended, coef, adjoint)
    return field


def per_device(
    advect_east, advect_north, diffusion, background_var, obs_cell, obs_value, obs_weight, obs_count
):
    windows_count = lax.axis_size("tm")
    tiles = lax.axis_size("tile")
    coefs = jnp.stack([advect_east[0], advect_north[0], diffusion[0]])
    coef_ext = padded(coefs, (("tile", 2),), 1)
    cells = obs_cell.reshape(tiles, -1)
    slot_count = cells.shape[1]
    live = jnp.arange(slot_count, dtype=jnp.int32)[None, :] < obs_count.reshape(tiles)[:, None]
    masked = obs_weight.reshape(tiles, -1) * live.astype(jnp.float32)
    received = lax.all_to_all(
        jnp.stack([obs_value.reshape(tiles, -1), masked]),
        "tile",
        split_axis=1,
        concat_axis=1,
        tiled=True,
    )
    received_cells = lax.all_to_all(cells, "tile", split_axis=0, concat_axis=0, tiled=True)
    departures = received[0].reshape(-1)
    obs_weights = received[1].reshape(-1)
    flat_cells = received_cells.reshape(-1)
    local_var = background_var[0]
    state_shape = local_var.shape
    cell_total = state_shape[0] * state_shape[1] * state_shape[2] * state_shape[3]
    increment = jnp.zeros(state_shape, jnp.float32)
    for iteration in range(ITERS):
        if iteration == 0:
            innov = obs_weights * (0.0 - departures)
        else:
            forward_carried = advance(increment, coef_ext, False)
            for forward_window in range(windows_count - 1):
                forward_incoming = shifted(forward_carried, "tm", 1)
                forward_carried = advance(forward_incoming + increment, coef_ext, False)
            innov = obs_weights * (
                jnp.take(forward_carried.reshape(cell_total), flat_cells, axis=0) - departures
            )
        gridded = jnp.zeros((cell_total,), jnp.float32).at[flat_cells].add(innov)
        source = gridded.reshape(state_shape)
        carried = advance(source, coef_ext, True)
        for window in range(windows_count - 1):
            incoming = shifted(carried, "tm", -1)
            carried = advance(incoming + source, coef_ext, True)
        increment = increment - 0.5 * (increment + local_var * carried)
    return increment[None]


class Plan:
    def __init__(self, mesh_shape, var_shape, slot_shape):
        self.subs, self.tiles = mesh_shape["tm"], mesh_shape["tile"]
        self.count = self.subs * self.tiles
        _, self.vars, self.lev, self.nlat, self.lon = var_shape
        self.lat = self.nlat // self.tiles
        self.slots = slot_shape[2] // self.tiles
        self.cols = self.count // self.lev
        self.width = self.lon // self.cols
        self.half = self.width // 2
        self.halo = CHAINS * STEPS * self.subs
        self.margin = (LANES - self.width) // 2
        self.extra = self.halo - self.margin
        self.span = self.width + 2 * self.halo
        self.parts = 4
        self.coef_row = self.lat * self.vars
        self.tail_row = self.coef_row + 3 * self.lat
        self.rows = -(-(self.tail_row + self.lat // self.parts) // 8) * 8

    def fits(self):
        return (
            self.count % self.lev == 0
            and self.lon % self.cols == 0
            and self.width % 2 == 0
            and self.half + 2 * self.halo <= LANES
            and 0 <= self.extra <= 5
            and -(-self.extra // STEPS) <= self.subs
            and self.vars == 4
            and self.lat == 12
            and self.parts * 6 * self.extra <= LANES
            and self.tiles == 8
            and self.slots * self.tiles == 2 * LANES
            and (self.width + 2 * self.margin) == LANES
            and self.nlat % BLOCK == 0
            and BLOCK % self.lat == 0
            and self.width * 4 <= 3 * LANES
        )


def observation_kernel(plan, count_ref, cell_ref, value_ref, weight_ref, out_ref):
    p = plan
    lane = lax.broadcasted_iota(jnp.int32, (1, p.tiles * p.slots), 1)
    filled = jnp.zeros_like(lane)
    for t in range(p.tiles):
        filled = jnp.where(lane // p.slots == t, count_ref[0, t], filled)
    weight = jnp.where(lane % p.slots < filled, weight_ref[...], 0.0)
    obs = []
    for x in (weight, weight * value_ref[...], cell_ref[...].astype(jnp.float32)):
        obs += [x[:, :LANES], x[:, LANES:]]
    out_ref[...] = jnp.concatenate(obs + [jnp.zeros((2, LANES), jnp.float32)], axis=0)


def pack_kernel(plan, east_ref, north_ref, diff_ref, var_ref, out_ref, wide):
    p = plan
    pad = 2 * LANES
    right = wide.shape[-1] - pad - p.lon
    inner = slice(pad, pad + p.lon)
    per_level = p.vars + 3

    def widen(z, carry):
        for v in range(p.vars):
            wide[z * per_level + v, :, inner] = var_ref[v, z]
        for c, ref in enumerate((east_ref, north_ref, diff_ref)):
            wide[z * per_level + p.vars + c, :, inner] = ref[z]
        for a in range(per_level):
            at = z * per_level + a
            wide[at, :, :pad] = wide[at, :, p.lon : p.lon + pad]
            wide[at, :, pad + p.lon :] = wide[at, :, pad : pad + right]
        return carry

    lax.fori_loop(0, p.lev, widen, 0)

    part = p.lat // p.parts
    lanes = lax.broadcasted_iota(jnp.int32, (part, LANES), 1)

    def blocks(z, carry):
        def take(a, low, high, start):
            return wide[z * per_level + a, low:high, pad + start : pad + start + LANES]

        for j in range(p.cols):
            base = (z * p.cols + j) * p.rows
            start = j * p.width - p.margin
            for v in range(p.vars):
                out_ref[pl.ds(base + v, p.lat, stride=p.vars), :] = take(v, 0, p.lat, start)
            for c in range(3):
                out_ref[pl.ds(base + p.coef_row + c * p.lat, p.lat), :] = take(p.vars + c, 0, p.lat, start)
            tail = jnp.zeros((part, LANES), jnp.float32)
            for h in range(p.parts):
                low, high = h * part, (h + 1) * part
                for c in range(3):
                    at = (h * 3 + c) * 2 * p.extra
                    west = take(p.vars + c, low, high, j * p.width - p.halo - at)
                    east = take(p.vars + c, low, high, (j + 1) * p.width + p.margin - p.extra - at)
                    tail = jnp.where(lanes >= at, west, tail)
                    tail = jnp.where(lanes >= at + p.extra, east, tail)
            rest = jnp.zeros((p.rows - p.tail_row - part, LANES), jnp.float32)
            out_ref[pl.ds(base + p.tail_row, p.rows - p.tail_row), :] = jnp.concatenate([tail, rest], axis=0)
        return carry

    lax.fori_loop(0, p.lev, blocks, 0)


def turn(x, shift, axis):
    size = x.shape[axis]
    shift %= size
    if shift == 0:
        return x
    high = lax.slice_in_dim(x, size - shift, size, axis=axis)
    low = lax.slice_in_dim(x, 0, size - shift, axis=axis)
    return jnp.concatenate([high, low], axis=axis)


def to_east(x, wrap):
    edge = x[:, -1:] if wrap else jnp.zeros_like(x[:, -1:])
    return jnp.concatenate([edge, x[:, :-1]], axis=1)


def to_west(x, wrap):
    edge = x[:, :1] if wrap else jnp.zeros_like(x[:, :1])
    return jnp.concatenate([x[:, 1:], edge], axis=1)


class Stores:
    def __init__(self):
        self.held = []

    def put(self, ref, at, value):
        self.held.append((ref, at, value))

    def flush(self):
        for ref, at, value in self.held:
            ref[at] = value
        self.held = []


def looped(count, unroll, body):
    def many(i, carry):
        stores = Stores()
        for u in range(unroll):
            body(i * unroll + u, stores)
        stores.flush()
        return carry

    lax.fori_loop(0, count // unroll, many, 0)


def swap_blocks(x, slots):
    size, width = x.shape
    sub = lax.broadcasted_iota(jnp.int32, x.shape, 0)
    block = lax.broadcasted_iota(jnp.int32, x.shape, 1) // slots
    out = x
    for d in range(1, size):
        moved = turn(turn(x, size - d, 0), d * slots, 1)
        out = jnp.where(block == (sub + d) % size, moved, out)
    return out


def spread(a, b, count):
    return (
        jnp.concatenate([a[:count], b[:count]], axis=0),
        jnp.concatenate([a[count:], b[count:]], axis=0),
    )


def grid_kernel(plan, recv_ref, weight_g, value_g, obs_tab):
    p = plan
    f32 = jnp.float32
    me = lax.axis_index("tm") * p.tiles + lax.axis_index("tile")
    level = (me // p.cols).astype(f32)
    origin = ((me % p.cols) * p.width - p.halo).astype(f32)

    def observe(k, stores):
        raw = []
        for i in range(6):
            raw.append(recv_ref[pl.ds(k * p.tiles * 8 + i, p.tiles, stride=8), :])
        w, wy, cell = (jnp.concatenate(raw[2 * i : 2 * i + 2], axis=1) for i in range(3))
        w, wy, cell = (swap_blocks(x, p.slots) for x in (w, wy, cell))
        row = jnp.floor((cell + 0.5) * (1.0 / p.lon))
        lon = cell - row * p.lon
        group = jnp.floor((row + 0.5) * (1.0 / p.lat))
        lat = row - group * p.lat
        var = jnp.floor((group + 0.5) * (1.0 / p.lev))
        lev = group - var * p.lev
        at = lon - origin
        at = jnp.where(at < 0, at + p.lon, at)
        at = jnp.where(at >= p.lon, at - p.lon, at)
        place = at - p.extra
        place = jnp.where(place < 0, place + LANES, place)
        place = jnp.where(place >= LANES, place - LANES, place)
        here = lev == level
        in_a = here & (at < p.half + 2 * p.halo)
        in_b = here & (at >= p.half) & (at < p.span)
        rows = pl.ds(k * p.tiles, p.tiles)
        stores.put(obs_tab, (0, rows), lat * p.vars + var)
        stores.put(obs_tab, (1, rows), jnp.where(in_a, place, -1.0))
        stores.put(obs_tab, (2, rows), jnp.where(in_b, place, -1.0))
        for i, x in ((3, w), (6, wy)):
            one = x.astype(jnp.bfloat16).astype(f32)
            two = (x - one).astype(jnp.bfloat16).astype(f32)
            stores.put(obs_tab, (i, rows), one)
            stores.put(obs_tab, (i + 1, rows), two)
            stores.put(obs_tab, (i + 2, rows), x - one - two)

    looped(p.subs, 1, observe)

    n_rows = p.lat * p.vars
    slots = p.tiles * p.slots
    row_id = lax.broadcasted_iota(jnp.int32, (n_rows, slots), 0).astype(f32)
    lane_id = lax.broadcasted_iota(jnp.int32, (LANES, slots), 0).astype(f32)

    def grid(kt, stores):
        def entry(i):
            return obs_tab[i, pl.ds(kt, 1), :]

        match = row_id == entry(0)
        left = jnp.concatenate(
            [jnp.where(match, entry(i), 0.0).astype(jnp.bfloat16) for i in range(3, 9)], axis=0
        )
        right = jnp.concatenate(
            [jnp.where(lane_id == entry(i), 1.0, 0.0).astype(jnp.bfloat16) for i in (1, 2)], axis=0
        )
        full = lax.dot_general(left, right, (((1,), (1,)), ((), ())), preferred_element_type=f32)
        for i, ref in ((0, weight_g), (3, value_g)):
            parts = [full[(i + q) * n_rows : (i + q + 1) * n_rows] for q in range(3)]
            summed = parts[0] + (parts[1] + parts[2])
            for pair in range(p.lat // 2):
                rows = slice(2 * p.vars * pair, 2 * p.vars * (pair + 1))
                one, two = spread(summed[rows, :LANES], summed[rows, LANES:], p.vars)
                at = kt * p.lat + kt // p.tiles * STEPS + 2 * pair
                stores.put(ref, at, one)
                stores.put(ref, at + 1, two)

    looped(p.count, 2, grid)


    for k in range(p.subs):
        for l in range(p.nlat, p.nlat + STEPS):
            value_g[k * (p.nlat + STEPS) + l] = jnp.zeros(value_g.shape[1:], f32)


def chain_kernel(
    plan,
    recv_ref,
    weight_g,
    value_g,
    out_ref,
    mid_c,
    east_c,
    west_c,
    north_c,
    south_c,
    first,
    forcing,
    innov,
    total,
    carried,
    by_var,
    extras,
):
    p = plan
    f32 = jnp.float32
    shape = (2 * p.vars, LANES)
    sub = lax.broadcasted_iota(jnp.int32, shape, 0)
    lane = lax.broadcasted_iota(jnp.int32, shape, 1)
    lower = sub < p.vars

    mask = (lower & (lane >= LANES - p.extra)) | (~lower & (lane < p.extra))
    part = p.lat // p.parts

    def edges(kt, stores):
        tail = recv_ref[pl.ds(kt * p.rows + p.tail_row, part), :]
        for h in range(p.parts):
            for c in range(3):
                at = (h * 3 + c) * 2 * p.extra
                moved = turn(tail, LANES - p.extra - at, 1)
                stores.put(extras, (c, kt, slice(h * part, (h + 1) * part)), moved)

    looped(p.count, 4, edges)

    def widen(kt, stores):
        base = kt * p.rows
        for l in range(p.lat):
            got = []
            for c in range(3):
                main = recv_ref[pl.ds(base + p.coef_row + c * p.lat + l, 1), :]
                edge = extras[c, kt, l : l + 1, :]
                got.append(
                    jnp.where(mask, jnp.broadcast_to(edge, shape), jnp.broadcast_to(main, shape))
                )
            east, north, diff = got
            east = 0.5 * east
            north = 0.5 * north
            at = kt * p.lat + kt // p.tiles * STEPS + l
            stores.put(mid_c, at, 1.0 - 4.0 * diff)
            stores.put(east_c, at, diff - east)
            stores.put(west_c, at, diff + east)
            stores.put(north_c, at, diff - north)
            stores.put(south_c, at, diff + north)

    looped(p.count, 1, widen)

    n = p.nlat
    pitch = n + STEPS
    zero = jnp.zeros(shape, f32)

    for k in range(p.subs):
        for l in range(n, pitch):
            for ref in (mid_c, east_c, west_c, north_c, south_c, forcing, innov):
                ref[k * pitch + l] = zero

    def sweep(base, load, emit, stage, width):
        states = []
        for l in range(STEPS):
            x = load(l)
            for s in range(l + 1):
                if s == len(states):
                    states.append((zero,) * width)
                states[s], x = stage(base + l - s, states[s], x, s == l)
        states = tuple(states)

        def many(g, states):
            states = list(states)
            stores = Stores()
            for u in range(BLOCK):
                r = g * BLOCK + u
                x = load(r + STEPS)
                for s in range(STEPS):
                    states[s], x = stage(base + r + STEPS - s, states[s], x)
                emit(r, u, x, stores)
            stores.flush()
            return tuple(states)

        lax.fori_loop(0, n // BLOCK, many, states)

    def adjoint_stage(wrap):
        def stage(at, state, x, fresh=False):
            here, below = state[0], state[1]
            now = (
                mid_c[at] * x
                + to_east(east_c[at] * x, wrap)
                + to_west(west_c[at] * x, wrap)
            )
            done = here + below + south_c[at] * x
            return (now, state[2], north_c[at] * x), done

        return stage

    def forward_stage(at, state, x, fresh=False):
        if fresh:
            return (zero, x), None
        below, last = state
        row = at - 1
        done = (
            mid_c[row] * last
            + east_c[row] * to_west(last, False)
            + west_c[row] * to_east(last, False)
            + north_c[row] * x
            + south_c[row] * below
        )
        return (last, x), done

    def clear(ref):
        def body(l, carry):
            ref[l] = zero
            return carry

        lax.fori_loop(0, pitch, body, 0, unroll=2)

    clear(carried)

    def first_adjoint(i, wrap):
        k = p.subs - 1 - i
        base = k * pitch
        held = []

        def load(l):
            return carried[l] - value_g[base + l]

        def emit(r, u, y, stores):
            stores.put(carried, r, y)
            stores.put(first, base + r, y)
            held.append(y)
            if u % 2:
                tile = (r - u) // p.lat + u // p.lat
                row = (k * p.tiles + tile) * p.rows + u % p.lat // 2 * 2 * p.vars
                var = recv_ref[pl.ds(pl.multiple_of(row, 8), 2 * p.vars), :]
                one, two = spread(var, var, p.vars)
                stores.put(forcing, base + r - 1, -0.5 * (one * held.pop(0)))
                stores.put(forcing, base + r, -0.5 * (two * held.pop(0)))

        sweep(base, load, emit, adjoint_stage(wrap), 3)

    wrapped = -(-p.extra // STEPS)
    lax.fori_loop(0, wrapped, lambda i, _: (first_adjoint(i, True), 0)[1], 0)
    lax.fori_loop(wrapped, p.subs, lambda i, _: (first_adjoint(i, False), 0)[1], 0)

    clear(carried)

    def run_forward(k, carry):
        base = k * pitch

        def load(l):
            return carried[l] + forcing[base + l]

        def emit(r, u, y, stores):
            stores.put(carried, r, y)
            stores.put(innov, base + r, weight_g[base + r] * y - value_g[base + r])

        sweep(base, load, emit, forward_stage, 2)
        return carry

    lax.fori_loop(0, p.subs, run_forward, 0)

    clear(carried)

    def second_adjoint(i, carry):
        base = (p.subs - 1 - i) * pitch

        def load(l):
            return carried[l] + innov[base + l]

        def emit(r, u, y, stores):
            stores.put(carried, r, y)
            stores.put(total, base + r, y + 0.5 * first[base + r])

        sweep(base, load, emit, adjoint_stage(False), 3)
        return carry

    lax.fori_loop(0, p.subs, second_adjoint, 0)

    in_half = lane < p.margin + p.half

    def fold(kt, stores):
        base = kt * p.lat + kt // p.tiles * STEPS
        for l in range(p.lat):
            y = total[base + l]
            y = jnp.where(in_half[: p.vars], y[: p.vars], y[p.vars :])
            stores.put(by_var, (pl.ds(kt * p.lat + l, p.vars, stride=p.count * p.lat),), y)

    looped(p.count, 2, fold)

    def join(kt, stores):
        own = slice(p.margin, p.margin + p.width)
        cols = [by_var[pl.ds(v * p.count * p.lat + kt * p.lat, p.lat), :][:, own] for v in range(p.vars)]
        spare = 3 * LANES - p.vars * p.width
        line = jnp.concatenate(cols + [jnp.zeros((p.lat, spare), f32)], axis=1)
        for i in range(3):
            at = (pl.ds(kt * p.lat * 3 + i, p.lat, stride=3),)
            stores.put(out_ref, at, line[:, i * LANES : (i + 1) * LANES])

    looped(p.count, 2, join)


def finish_kernel(plan, recv_ref, var_ref, out_ref):
    p = plan

    def level(z, carry):
        for j in range(p.cols):
            start = (z * p.cols + j) * p.lat * 3
            rows = [recv_ref[pl.ds(start + i, p.lat, stride=3), :] for i in range(3)]
            for v in range(p.vars):
                at, end = v * p.width, (v + 1) * p.width
                col = j * p.width
                while at < end:
                    i, low = divmod(at, LANES)
                    size = min(end - at, LANES - low)
                    cols = slice(col, col + size)
                    out_ref[v, z, :, cols] = -0.5 * (var_ref[v, z, :, cols] * rows[i][:, low : low + size])
                    at, col = at + size, col + size
        return carry

    lax.fori_loop(0, p.lev, level, 0)


def transposed(
    plan, advect_east, advect_north, diffusion, background_var, obs_cell, obs_value, obs_weight, obs_count
):
    p = plan
    vmem = pl.BlockSpec(memory_space=pltpu.VMEM)
    params = pltpu.CompilerParams(vmem_limit_bytes=VMEM_LIMIT)
    f32 = jnp.float32
    wide = (p.vars + 3) * p.lev
    var = background_var[0]
    obs = pl.pallas_call(
        functools.partial(observation_kernel, p),
        out_shape=jax.ShapeDtypeStruct((8, LANES), f32),
        in_specs=[pl.BlockSpec(memory_space=pltpu.SMEM)] + [vmem] * 3,
        out_specs=vmem,
        name="observations",
    )(obs_count.reshape(1, -1), obs_cell.reshape(1, -1), obs_value.reshape(1, -1), obs_weight.reshape(1, -1))
    all_obs = lax.all_gather(obs, ("tm", "tile"), axis=0, tiled=True)
    packed = pl.pallas_call(
        functools.partial(pack_kernel, p),
        out_shape=jax.ShapeDtypeStruct((p.count * p.rows, LANES), f32),
        in_specs=[vmem] * 4,
        out_specs=vmem,
        scratch_shapes=[pltpu.VMEM((wide, p.lat, 15 * LANES), f32)],
        compiler_params=params,
        name="pack",
    )(advect_east[0], advect_north[0], diffusion[0], var)
    received = lax.all_to_all(packed, ("tm", "tile"), 0, 0, tiled=True)
    rows = p.subs * (p.nlat + STEPS)
    field = pltpu.VMEM((rows, 2 * p.vars, LANES), f32)
    weights, values = pl.pallas_call(
        functools.partial(grid_kernel, p),
        out_shape=[jax.ShapeDtypeStruct((rows, 2 * p.vars, LANES), f32)] * 2,
        in_specs=[vmem],
        out_specs=[vmem] * 2,
        scratch_shapes=[pltpu.VMEM((9, p.count, p.tiles * p.slots), f32)],
        compiler_params=params,
        cost_estimate=pl.CostEstimate(
            flops=p.count * 12 * p.lat * p.vars * (2 * LANES) ** 2, bytes_accessed=8 << 20, transcendentals=0
        ),
        name="grid",
    )(all_obs)
    back = pl.pallas_call(
        functools.partial(chain_kernel, p),
        out_shape=jax.ShapeDtypeStruct((p.count * p.lat * 3, LANES), f32),
        in_specs=[vmem] * 3,
        out_specs=vmem,
        scratch_shapes=[field] * 9
        + [
            pltpu.VMEM((p.nlat + STEPS, 2 * p.vars, LANES), f32),
            pltpu.VMEM((p.vars * p.count * p.lat, LANES), f32),
            pltpu.VMEM((3, p.count, p.lat, LANES), f32),
        ],
        compiler_params=params,
        name="chains",
    )(received, weights, values)
    back = back.reshape(-1, 4, LANES)
    returned = lax.all_to_all(back, ("tm", "tile"), 0, 0, tiled=True)
    returned = returned.reshape(-1, LANES)
    increment = pl.pallas_call(
        functools.partial(finish_kernel, p),
        out_shape=jax.ShapeDtypeStruct(var.shape, f32),
        in_specs=[vmem] * 2,
        out_specs=vmem,
        compiler_params=params,
        name="finish",
    )(returned, var)
    return increment[None]


def solution(mesh):
    def run(*args):
        plan = Plan(mesh.shape, args[3].shape, args[4].shape)
        work = functools.partial(transposed, plan) if plan.fits() else per_device
        return jax.shard_map(
            work,
            mesh=mesh,
            in_specs=(
                P("tm", None, "tile", None),
                P("tm", None, "tile", None),
                P("tm", None, "tile", None),
                P("tm", None, None, "tile", None),
                P("tm", "tile", None),
                P("tm", "tile", None),
                P("tm", "tile", None),
                P("tm", "tile", None),
            ),
            out_specs=P("tm", None, None, "tile", None),
            check_vma=False,
        )(*args)

    return run
```

```python
import functools

import jax
import jax.numpy as jnp
from jax import lax
from jax.experimental import pallas as pl
from jax.experimental.pallas import tpu as pltpu
from jax.sharding import PartitionSpec as P

STEPS = 2
ITERS = 2
CHAINS = 3
LANES = 128
BLOCK = 48
VMEM_LIMIT = 48 * 1024 * 1024


def padded(block, sides, width):
    for axis, dim in sides:
        count = lax.axis_size(axis)
        forward = [(i, i + 1) for i in range(count - 1)]
        backward = [(target, source) for source, target in forward]
        low = lax.ppermute(
            lax.slice_in_dim(block, block.shape[dim] - width, None, axis=dim), axis, forward
        )
        high = lax.ppermute(lax.slice_in_dim(block, 0, width, axis=dim), axis, backward)
        block = jnp.concatenate([low, block, high], axis=dim)
    return block


def shifted(value, axis, steps):
    count = lax.axis_size(axis)
    first, last = (max(0, -steps), min(count, count - steps))
    return lax.ppermute(value, axis, [(source, source + steps) for source in range(first, last)])


def apply_step(field, coef, adjoint):
    east_c = coef[0]
    north_c = coef[1]
    diff_c = coef[2]
    if adjoint:
        to_east = (diff_c - 0.5 * east_c) * field
        to_west = (diff_c + 0.5 * east_c) * field
        to_north = (diff_c - 0.5 * north_c) * field
        to_south = (diff_c + 0.5 * north_c) * field
        middle = (1.0 - 4.0 * diff_c[:, 1:-1]) * field[:, :, 1:-1]
        return (
            middle
            + jnp.roll(to_east[:, :, 1:-1], 1, axis=-1)
            + jnp.roll(to_west[:, :, 1:-1], -1, axis=-1)
            + to_north[:, :, :-2]
            + to_south[:, :, 2:]
        )
    inner = field[:, :, 1:-1]
    diff_in = diff_c[:, 1:-1]
    east_in = east_c[:, 1:-1]
    north_in = north_c[:, 1:-1]
    return (
        (1.0 - 4.0 * diff_in) * inner
        + (diff_in - 0.5 * east_in) * jnp.roll(inner, -1, axis=-1)
        + (diff_in + 0.5 * east_in) * jnp.roll(inner, 1, axis=-1)
        + (diff_in - 0.5 * north_in) * field[:, :, 2:]
        + (diff_in + 0.5 * north_in) * field[:, :, :-2]
    )


def advance(field, coef, adjoint):
    for repeat in range(STEPS):
        extended = padded(field, (("tile", 2),), 1)
        field = apply_step(extended, coef, adjoint)
    return field


def per_device(
    advect_east, advect_north, diffusion, background_var, obs_cell, obs_value, obs_weight, obs_count
):
    windows_count = lax.axis_size("tm")
    tiles = lax.axis_size("tile")
    coefs = jnp.stack([advect_east[0], advect_north[0], diffusion[0]])
    coef_ext = padded(coefs, (("tile", 2),), 1)
    cells = obs_cell.reshape(tiles, -1)
    slot_count = cells.shape[1]
    live = jnp.arange(slot_count, dtype=jnp.int32)[None, :] < obs_count.reshape(tiles)[:, None]
    masked = obs_weight.reshape(tiles, -1) * live.astype(jnp.float32)
    received = lax.all_to_all(
        jnp.stack([obs_value.reshape(tiles, -1), masked]),
        "tile",
        split_axis=1,
        concat_axis=1,
        tiled=True,
    )
    received_cells = lax.all_to_all(cells, "tile", split_axis=0, concat_axis=0, tiled=True)
    departures = received[0].reshape(-1)
    obs_weights = received[1].reshape(-1)
    flat_cells = received_cells.reshape(-1)
    local_var = background_var[0]
    state_shape = local_var.shape
    cell_total = state_shape[0] * state_shape[1] * state_shape[2] * state_shape[3]
    increment = jnp.zeros(state_shape, jnp.float32)
    for iteration in range(ITERS):
        if iteration == 0:
            innov = obs_weights * (0.0 - departures)
        else:
            forward_carried = advance(increment, coef_ext, False)
            for forward_window in range(windows_count - 1):
                forward_incoming = shifted(forward_carried, "tm", 1)
                forward_carried = advance(forward_incoming + increment, coef_ext, False)
            innov = obs_weights * (
                jnp.take(forward_carried.reshape(cell_total), flat_cells, axis=0) - departures
            )
        gridded = jnp.zeros((cell_total,), jnp.float32).at[flat_cells].add(innov)
        source = gridded.reshape(state_shape)
        carried = advance(source, coef_ext, True)
        for window in range(windows_count - 1):
            incoming = shifted(carried, "tm", -1)
            carried = advance(incoming + source, coef_ext, True)
        increment = increment - 0.5 * (increment + local_var * carried)
    return increment[None]


class Plan:
    def __init__(self, mesh_shape, var_shape, slot_shape):
        self.subs, self.tiles = mesh_shape["tm"], mesh_shape["tile"]
        self.count = self.subs * self.tiles
        _, self.vars, self.lev, self.nlat, self.lon = var_shape
        self.lat = self.nlat // self.tiles
        self.slots = slot_shape[2] // self.tiles
        self.cols = self.count // self.lev
        self.width = self.lon // self.cols
        self.half = self.width // 2
        self.halo = CHAINS * STEPS * self.subs
        self.margin = (LANES - self.width) // 2
        self.extra = self.halo - self.margin
        self.span = self.width + 2 * self.halo
        self.coef_row = self.lat * self.vars
        self.obs_row = self.coef_row + 3 * self.lat
        self.rows = self.obs_row + 6
        self.pitch = self.nlat + STEPS

    def borrows(self, k):
        return (CHAINS - 1) * STEPS * self.subs + STEPS * (k + 1) > self.margin

    def fits(self):
        if self.count % self.lev or self.lon % self.cols or self.width % 2:
            return False
        for k in range(self.subs):
            spare = self.margin - STEPS * (2 * self.subs - k)
            if spare < 0 or (self.borrows(k) and spare < self.extra):
                return False
        return (
            self.half + 2 * self.halo <= LANES
            and 0 <= self.extra
            and self.vars == 4
            and self.lat % 2 == 0
            and self.tiles == 8
            and self.slots * self.tiles == 2 * LANES
            and self.width + 2 * self.margin == LANES
            and self.width * self.vars <= 3 * LANES
            and self.nlat % BLOCK == 0
            and BLOCK % self.lat == 0
            and self.count * self.rows % 8 == 0
            and self.rows % 2 == 0
        )


def pack_kernel(
    plan, count_ref, cell_ref, value_ref, weight_ref, east_ref, north_ref, diff_ref, var_ref, out_ref, wide
):
    p = plan
    pad = 2 * LANES
    right = wide.shape[-1] - pad - p.lon
    per_level = p.vars + 3

    def fill(z, carry):
        for v in range(per_level):
            field = var_ref[v, z] if v < p.vars else (east_ref, north_ref, diff_ref)[v - p.vars][z]
            at = z * per_level + v
            wide[at, :, pad : pad + p.lon] = field
            wide[at, :, :pad] = field[:, p.lon - pad :]
            wide[at, :, pad + p.lon :] = field[:, :right]
        return carry

    lax.fori_loop(0, p.lev, fill, 0)

    lane = lax.broadcasted_iota(jnp.int32, (1, p.tiles * p.slots), 1)
    filled = jnp.zeros_like(lane)
    for t in range(p.tiles):
        filled = jnp.where(lane // p.slots == t, count_ref[0, t], filled)
    weight = jnp.where(lane % p.slots < filled, weight_ref[...], 0.0)
    obs = []
    for x in (weight, weight * value_ref[...], cell_ref[...].astype(jnp.float32)):
        obs += [x[:, :LANES], x[:, LANES:]]
    obs = jnp.concatenate(obs, axis=0)
    lanes = lax.broadcasted_iota(jnp.int32, (p.lat, LANES), 1)
    borrows = jnp.where(p.borrows(lax.axis_index("tm")), p.extra, 0)

    def blocks(z, carry):
        for j in range(p.cols):

            def take(a, start):
                return wide[z * per_level + a, :, pad + start : pad + start + LANES]

            base = (z * p.cols + j) * p.rows
            start = j * p.width
            for v in range(p.vars):
                piece = take(v, start - p.margin)
                if v < 3:
                    beyond = take(p.vars + v, start + p.width + p.margin)
                    before = take(p.vars + v, start - p.margin - LANES)
                    piece = jnp.where(lanes < borrows, beyond, piece)
                    piece = jnp.where(lanes >= LANES - borrows, before, piece)
                out_ref[pl.ds(base + v, p.lat, stride=p.vars), :] = piece
            for c in range(3):
                rows = pl.ds(base + p.coef_row + c * p.lat, p.lat)
                out_ref[rows, :] = take(p.vars + c, start - p.margin)
            out_ref[pl.ds(base + p.obs_row, 6), :] = obs
        return carry

    lax.fori_loop(0, p.lev, blocks, 0)


class Stores:
    def __init__(self):
        self.held = []

    def put(self, ref, at, value):
        self.held.append((ref, at, value))

    def flush(self):
        for ref, at, value in self.held:
            ref[at] = value
        self.held = []


def looped(count, unroll, body):
    def many(i, carry):
        stores = Stores()
        for u in range(unroll):
            body(i * unroll + u, stores)
        stores.flush()
        return carry

    lax.fori_loop(0, count // unroll, many, 0)


def swap_blocks(x, slots):
    size = x.shape[0]
    sub = lax.broadcasted_iota(jnp.int32, x.shape, 0)
    block = lax.broadcasted_iota(jnp.int32, x.shape, 1) // slots
    out = x
    for d in range(1, size):
        moved = pltpu.roll(pltpu.roll(x, size - d, 0), d * slots, 1)
        out = jnp.where(block == (sub + d) % size, moved, out)
    return out


def spread(a, b, count):
    return (
        jnp.concatenate([a[:count], b[:count]], axis=0),
        jnp.concatenate([a[count:], b[count:]], axis=0),
    )


def chain_kernel(
    plan,
    recv_ref,
    out_ref,
    mid_c,
    east_c,
    west_c,
    north_c,
    south_c,
    weight_g,
    innov,
    results,
    carried,
    by_var,
    obs_tab,
):
    p = plan
    f32 = jnp.float32
    me = lax.axis_index("tm") * p.tiles + lax.axis_index("tile")
    level = (me // p.cols).astype(f32)
    origin = ((me % p.cols) * p.width - p.halo).astype(f32)
    shape = (2 * p.vars, LANES)
    sub = lax.broadcasted_iota(jnp.int32, shape, 0)
    lane = lax.broadcasted_iota(jnp.int32, shape, 1)
    lower = sub < p.vars
    n = p.nlat
    pitch = p.pitch
    whole = p.subs * pitch
    zero = jnp.zeros(shape, f32)

    def row_of(kt):
        return kt * p.lat + kt // p.tiles * STEPS

    for k in range(p.subs):
        for l in range(n, pitch):
            for ref in (mid_c, east_c, west_c, north_c, south_c, innov, results):
                ref[k * pitch + l] = zero

    def observe(k, stores):
        raw = []
        for i in range(6):
            raw.append(recv_ref[pl.ds(k * p.tiles * p.rows + p.obs_row + i, p.tiles, stride=p.rows), :])
        w, wy, cell = (jnp.concatenate(raw[2 * i : 2 * i + 2], axis=1) for i in range(3))
        w, wy, cell = (swap_blocks(x, p.slots) for x in (w, wy, cell))
        row = jnp.floor((cell + 0.5) * (1.0 / p.lon))
        lon = cell - row * p.lon
        group = jnp.floor((row + 0.5) * (1.0 / p.lat))
        lat = row - group * p.lat
        var = jnp.floor((group + 0.5) * (1.0 / p.lev))
        lev = group - var * p.lev
        at = lon - origin
        at = jnp.where(at < 0, at + p.lon, at)
        at = jnp.where(at >= p.lon, at - p.lon, at)
        place = at - p.extra
        place = jnp.where(place < 0, place + LANES, place)
        place = jnp.where(place >= LANES, place - LANES, place)
        here = lev == level
        in_a = here & (at < p.half + 2 * p.halo)
        in_b = here & (at >= p.half) & (at < p.span)
        rows = pl.ds(k * p.tiles, p.tiles)
        stores.put(obs_tab, (0, rows), lat * p.vars + var)
        stores.put(obs_tab, (1, rows), jnp.where(in_a, place, -1.0))
        stores.put(obs_tab, (2, rows), jnp.where(in_b, place, -1.0))
        for i, x in ((3, w), (6, -wy)):
            one = x.astype(jnp.bfloat16).astype(f32)
            two = (x - one).astype(jnp.bfloat16).astype(f32)
            stores.put(obs_tab, (i, rows), one)
            stores.put(obs_tab, (i + 1, rows), two)
            stores.put(obs_tab, (i + 2, rows), x - one - two)

    looped(p.subs, 1, observe)

    n_rows = p.lat * p.vars
    slots = p.tiles * p.slots
    row_id = lax.broadcasted_iota(jnp.int32, (n_rows, slots), 0).astype(f32)
    lane_id = lax.broadcasted_iota(jnp.int32, (LANES, slots), 0).astype(f32)

    def grid(kt, stores):
        def entry(i):
            return obs_tab[i, pl.ds(kt, 1), :]

        match = row_id == entry(0)
        left = jnp.concatenate(
            [jnp.where(match, entry(i), 0.0).astype(jnp.bfloat16) for i in range(3, 9)], axis=0
        )
        right = jnp.concatenate(
            [jnp.where(lane_id == entry(i), 1.0, 0.0).astype(jnp.bfloat16) for i in (1, 2)], axis=0
        )
        full = lax.dot_general(left, right, (((1,), (1,)), ((), ())), preferred_element_type=f32)
        for i, ref in ((0, weight_g), (3, innov)):
            parts = [full[(i + q) * n_rows : (i + q + 1) * n_rows] for q in range(3)]
            summed = parts[0] + (parts[1] + parts[2])
            for pair in range(p.lat // 2):
                rows = slice(2 * p.vars * pair, 2 * p.vars * (pair + 1))
                one, two = spread(summed[rows, :LANES], summed[rows, LANES:], p.vars)
                at = row_of(kt) + 2 * pair
                stores.put(ref, at, one)
                stores.put(ref, at + 1, two)

    looped(p.count, 4, grid)

    def widen(kt, stores):
        base = kt * p.rows
        count = jnp.where(p.borrows(kt // p.tiles), p.extra, 0)
        mask = (lower & (lane >= LANES - count)) | (~lower & (lane < count))
        for l in range(p.lat):
            got = []
            for c in range(3):
                main = recv_ref[pl.ds(base + p.coef_row + c * p.lat + l, 1), :]
                edge = recv_ref[pl.ds(base + l * p.vars + c, 1), :]
                got.append(
                    jnp.where(mask, jnp.broadcast_to(edge, shape), jnp.broadcast_to(main, shape))
                )
            east, north, diff = got
            east = 0.5 * east
            north = 0.5 * north
            at = row_of(kt) + l
            stores.put(mid_c, at, 1.0 - 4.0 * diff)
            stores.put(east_c, at, diff - east)
            stores.put(west_c, at, diff + east)
            stores.put(north_c, at, diff - north)
            stores.put(south_c, at, diff + north)

    looped(p.count, 2, widen)

    def sweep(base, load, emit, stage, width):
        states = []
        for l in range(STEPS):
            x = load(l, l)
            for s in range(l + 1):
                if s == len(states):
                    states.append((zero,) * width)
                states[s], x = stage(base + l - s, states[s], x, s == l)

        def many(g, states):
            states = list(states)
            stores = Stores()
            for u in range(BLOCK):
                r = g * BLOCK + u
                x = load(r + STEPS, u + STEPS)
                for s in range(STEPS):
                    states[s], x = stage(base + r + STEPS - s, states[s], x, False)
                emit(r, x, stores)
            stores.flush()
            return tuple(states)

        lax.fori_loop(0, n // BLOCK, many, tuple(states))

    def adjoint_stage(at, state, x, fresh):
        here, below, north = state
        now = (
            mid_c[at] * x
            + pltpu.roll(east_c[at] * x, 1, 1)
            + pltpu.roll(west_c[at] * x, LANES - 1, 1)
        )
        done = None if fresh else here + below + south_c[at] * x
        return (now, north, north_c[at] * x), done

    def forward_stage(at, state, x, fresh):
        if fresh:
            return (zero, x), None
        below, last = state
        row = at - 1
        done = (
            mid_c[row] * last
            + east_c[row] * pltpu.roll(last, LANES - 1, 1)
            + west_c[row] * pltpu.roll(last, 1, 1)
            + north_c[row] * x
            + south_c[row] * below
        )
        return (last, x), done

    def clear():
        def body(i, carry):
            for u in range(7):
                carried[i * 7 + u] = zero
            return carry

        lax.fori_loop(0, pitch // 7, body, 0)
        for l in range(pitch // 7 * 7, pitch):
            carried[l] = zero

    def adjoint(phase):
        clear()

        def one(i, carry):
            base = (p.subs - 1 - i) * pitch
            into = phase * whole + base

            def load(l, u):
                return carried[l] + innov[base + l]

            def emit(r, y, stores):
                stores.put(carried, r, y)
                stores.put(results, into + r, y)

            sweep(base, load, emit, adjoint_stage, 3)
            return carry

        lax.fori_loop(0, p.subs, one, 0)

    def forward():
        clear()

        def one(k, carry):
            base = k * pitch
            held = []

            def load(l, u):
                if u % 2 == 0:
                    tile = jnp.minimum((l - u) // p.lat + u // p.lat, p.tiles - 1)
                    row = (k * p.tiles + tile) * p.rows + u % p.lat * p.vars
                    var = recv_ref[pl.ds(row, 2 * p.vars), :]
                    held[:] = spread(var, var, p.vars)
                return carried[l] - 0.5 * (held[u % 2] * results[base + l])

            def emit(r, y, stores):
                stores.put(carried, r, y)
                stores.put(innov, base + r, weight_g[base + r] * y + innov[base + r])

            sweep(base, load, emit, forward_stage, 2)
            return carry

        lax.fori_loop(0, p.subs, one, 0)

    def iteration(phase, carry):
        adjoint(phase)

        @pl.when(phase < ITERS - 1)
        def _():
            forward()

        return carry

    lax.fori_loop(0, ITERS, iteration, 0)

    in_half = (lane < p.margin + p.half)[: p.vars]

    def fold(kt, stores):
        for l in range(p.lat):
            at = row_of(kt) + l
            y = 0.5 * results[at] + results[whole + at]
            y = jnp.where(in_half, y[: p.vars], y[p.vars :])
            stores.put(by_var, (pl.ds(kt * p.lat + l, p.vars, stride=p.count * p.lat),), y)

    looped(p.count, 4, fold)

    def join(kt, stores):
        own = slice(p.margin, p.margin + p.width)
        cols = [by_var[pl.ds(v * p.count * p.lat + kt * p.lat, p.lat), :][:, own] for v in range(p.vars)]
        spare = 3 * LANES - p.vars * p.width
        line = jnp.concatenate(cols + [jnp.zeros((p.lat, spare), f32)], axis=1)
        for i in range(3):
            at = (pl.ds(kt * p.lat * 3 + i, p.lat, stride=3),)
            stores.put(out_ref, at, line[:, i * LANES : (i + 1) * LANES])

    looped(p.count, 4, join)


def finish_kernel(plan, recv_ref, var_ref, out_ref):
    p = plan

    def level(z, carry):
        for j in range(p.cols):
            start = (z * p.cols + j) * p.lat * 3
            rows = [recv_ref[pl.ds(start + i, p.lat, stride=3), :] for i in range(3)]
            for v in range(p.vars):
                at, end = v * p.width, (v + 1) * p.width
                col = j * p.width
                while at < end:
                    i, low = divmod(at, LANES)
                    size = min(end - at, LANES - low)
                    cols = slice(col, col + size)
                    scale = -0.5 * var_ref[v, z, :, cols]
                    out_ref[v, z, :, cols] = scale * rows[i][:, low : low + size]
                    at, col = at + size, col + size
        return carry

    lax.fori_loop(0, p.lev, level, 0)


def transposed(
    plan, advect_east, advect_north, diffusion, background_var, obs_cell, obs_value, obs_weight, obs_count
):
    p = plan
    f32 = jnp.float32
    vmem = pl.BlockSpec(memory_space=pltpu.VMEM)
    params = pltpu.CompilerParams(vmem_limit_bytes=VMEM_LIMIT)
    var = background_var[0]
    packed = pl.pallas_call(
        functools.partial(pack_kernel, p),
        out_shape=jax.ShapeDtypeStruct((p.count * p.rows, LANES), f32),
        in_specs=[pl.BlockSpec(memory_space=pltpu.SMEM)] + [vmem] * 7,
        out_specs=vmem,
        scratch_shapes=[pltpu.VMEM(((p.vars + 3) * p.lev, p.lat, 15 * LANES), f32)],
        compiler_params=params,
        name="pack",
    )(
        obs_count.reshape(1, -1),
        obs_cell.reshape(1, -1),
        obs_value.reshape(1, -1),
        obs_weight.reshape(1, -1),
        advect_east[0],
        advect_north[0],
        diffusion[0],
        var,
    )
    received = lax.all_to_all(packed.reshape(-1, 2, LANES), ("tm", "tile"), 0, 0, tiled=True)
    received = received.reshape(-1, LANES)
    rows = p.subs * p.pitch
    field = pltpu.VMEM((rows, 2 * p.vars, LANES), f32)
    back = pl.pallas_call(
        functools.partial(chain_kernel, p),
        out_shape=jax.ShapeDtypeStruct((p.count * p.lat * 3, LANES), f32),
        in_specs=[vmem],
        out_specs=vmem,
        scratch_shapes=[field] * 7
        + [
            pltpu.VMEM((ITERS * rows, 2 * p.vars, LANES), f32),
            pltpu.VMEM((p.pitch, 2 * p.vars, LANES), f32),
            pltpu.VMEM((p.vars * p.count * p.lat, LANES), f32),
            pltpu.VMEM((9, p.count, p.tiles * p.slots), f32),
        ],
        compiler_params=params,
        name="chains",
    )(received)
    back = back.reshape(-1, 4, LANES)
    returned = lax.all_to_all(back, ("tm", "tile"), 0, 0, tiled=True)
    returned = returned.reshape(-1, LANES)
    increment = pl.pallas_call(
        functools.partial(finish_kernel, p),
        out_shape=jax.ShapeDtypeStruct(var.shape, f32),
        in_specs=[vmem] * 2,
        out_specs=vmem,
        compiler_params=params,
        name="finish",
    )(returned, var)
    return increment[None]


def solution(mesh):
    def run(*args):
        plan = Plan(mesh.shape, args[3].shape, args[4].shape)
        work = functools.partial(transposed, plan) if plan.fits() else per_device
        return jax.shard_map(
            work,
            mesh=mesh,
            in_specs=(
                P("tm", None, "tile", None),
                P("tm", None, "tile", None),
                P("tm", None, "tile", None),
                P("tm", None, None, "tile", None),
                P("tm", "tile", None),
                P("tm", "tile", None),
                P("tm", "tile", None),
                P("tm", "tile", None),
            ),
            out_specs=P("tm", None, None, "tile", None),
            check_vma=False,
        )(*args)

    return run
```

```python
import functools

import jax
import jax.numpy as jnp
from jax import lax
from jax.experimental import pallas as pl
from jax.experimental.pallas import tpu as pltpu
from jax.sharding import PartitionSpec as P

STEPS = 2
ITERS = 2
CHAINS = 3
LANES = 128
BLOCK = 48
VMEM_LIMIT = 48 * 1024 * 1024


def padded(block, sides, width):
    for axis, dim in sides:
        count = lax.axis_size(axis)
        forward = [(i, i + 1) for i in range(count - 1)]
        backward = [(target, source) for source, target in forward]
        low = lax.ppermute(
            lax.slice_in_dim(block, block.shape[dim] - width, None, axis=dim), axis, forward
        )
        high = lax.ppermute(lax.slice_in_dim(block, 0, width, axis=dim), axis, backward)
        block = jnp.concatenate([low, block, high], axis=dim)
    return block


def shifted(value, axis, steps):
    count = lax.axis_size(axis)
    first, last = (max(0, -steps), min(count, count - steps))
    return lax.ppermute(value, axis, [(source, source + steps) for source in range(first, last)])


def apply_step(field, coef, adjoint):
    east_c = coef[0]
    north_c = coef[1]
    diff_c = coef[2]
    if adjoint:
        to_east = (diff_c - 0.5 * east_c) * field
        to_west = (diff_c + 0.5 * east_c) * field
        to_north = (diff_c - 0.5 * north_c) * field
        to_south = (diff_c + 0.5 * north_c) * field
        middle = (1.0 - 4.0 * diff_c[:, 1:-1]) * field[:, :, 1:-1]
        return (
            middle
            + jnp.roll(to_east[:, :, 1:-1], 1, axis=-1)
            + jnp.roll(to_west[:, :, 1:-1], -1, axis=-1)
            + to_north[:, :, :-2]
            + to_south[:, :, 2:]
        )
    inner = field[:, :, 1:-1]
    diff_in = diff_c[:, 1:-1]
    east_in = east_c[:, 1:-1]
    north_in = north_c[:, 1:-1]
    return (
        (1.0 - 4.0 * diff_in) * inner
        + (diff_in - 0.5 * east_in) * jnp.roll(inner, -1, axis=-1)
        + (diff_in + 0.5 * east_in) * jnp.roll(inner, 1, axis=-1)
        + (diff_in - 0.5 * north_in) * field[:, :, 2:]
        + (diff_in + 0.5 * north_in) * field[:, :, :-2]
    )


def advance(field, coef, adjoint):
    for repeat in range(STEPS):
        extended = padded(field, (("tile", 2),), 1)
        field = apply_step(extended, coef, adjoint)
    return field


def per_device(
    advect_east, advect_north, diffusion, background_var, obs_cell, obs_value, obs_weight, obs_count
):
    windows_count = lax.axis_size("tm")
    tiles = lax.axis_size("tile")
    coefs = jnp.stack([advect_east[0], advect_north[0], diffusion[0]])
    coef_ext = padded(coefs, (("tile", 2),), 1)
    cells = obs_cell.reshape(tiles, -1)
    slot_count = cells.shape[1]
    live = jnp.arange(slot_count, dtype=jnp.int32)[None, :] < obs_count.reshape(tiles)[:, None]
    masked = obs_weight.reshape(tiles, -1) * live.astype(jnp.float32)
    received = lax.all_to_all(
        jnp.stack([obs_value.reshape(tiles, -1), masked]),
        "tile",
        split_axis=1,
        concat_axis=1,
        tiled=True,
    )
    received_cells = lax.all_to_all(cells, "tile", split_axis=0, concat_axis=0, tiled=True)
    departures = received[0].reshape(-1)
    obs_weights = received[1].reshape(-1)
    flat_cells = received_cells.reshape(-1)
    local_var = background_var[0]
    state_shape = local_var.shape
    cell_total = state_shape[0] * state_shape[1] * state_shape[2] * state_shape[3]
    increment = jnp.zeros(state_shape, jnp.float32)
    for iteration in range(ITERS):
        if iteration == 0:
            innov = obs_weights * (0.0 - departures)
        else:
            forward_carried = advance(increment, coef_ext, False)
            for forward_window in range(windows_count - 1):
                forward_incoming = shifted(forward_carried, "tm", 1)
                forward_carried = advance(forward_incoming + increment, coef_ext, False)
            innov = obs_weights * (
                jnp.take(forward_carried.reshape(cell_total), flat_cells, axis=0) - departures
            )
        gridded = jnp.zeros((cell_total,), jnp.float32).at[flat_cells].add(innov)
        source = gridded.reshape(state_shape)
        carried = advance(source, coef_ext, True)
        for window in range(windows_count - 1):
            incoming = shifted(carried, "tm", -1)
            carried = advance(incoming + source, coef_ext, True)
        increment = increment - 0.5 * (increment + local_var * carried)
    return increment[None]


class Plan:
    def __init__(self, mesh_shape, var_shape, slot_shape):
        self.subs, self.tiles = mesh_shape["tm"], mesh_shape["tile"]
        self.count = self.subs * self.tiles
        _, self.vars, self.lev, self.nlat, self.lon = var_shape
        self.lat = self.nlat // self.tiles
        self.slots = slot_shape[2] // self.tiles
        self.cols = self.count // self.lev
        self.width = self.lon // self.cols
        self.half = self.width // 2
        self.halo = CHAINS * STEPS * self.subs
        self.margin = (LANES - self.width) // 2
        self.extra = self.halo - self.margin
        self.span = self.width + 2 * self.halo
        self.coef_row = self.lat * self.vars
        self.obs_row = self.coef_row + 3 * self.lat
        self.rows = self.obs_row + 6
        self.pitch = self.nlat + STEPS

    def borrows(self, k):
        return (CHAINS - 1) * STEPS * self.subs + STEPS * (k + 1) > self.margin

    def fits(self):
        if self.count % self.lev or self.lon % self.cols or self.width % 2:
            return False
        for k in range(self.subs):
            spare = self.margin - STEPS * (2 * self.subs - k)
            if spare < 0 or (self.borrows(k) and spare < self.extra):
                return False
        return (
            self.half + 2 * self.halo <= LANES
            and 0 <= self.extra
            and self.vars == 4
            and self.lat % 2 == 0
            and self.tiles == 8
            and self.slots * self.tiles == 2 * LANES
            and self.width + 2 * self.margin == LANES
            and self.width * self.vars <= 3 * LANES
            and self.nlat % BLOCK == 0
            and BLOCK % self.lat == 0
            and self.count * self.rows % 8 == 0
            and self.rows % 2 == 0
        )


def pack_kernel(
    plan, count_ref, cell_ref, value_ref, weight_ref, east_ref, north_ref, diff_ref, var_ref, out_ref, wide
):
    p = plan
    pad = 2 * LANES
    right = wide.shape[-1] - pad - p.lon
    per_level = p.vars + 3

    def fill(z, carry):
        for v in range(per_level):
            field = var_ref[v, z] if v < p.vars else (east_ref, north_ref, diff_ref)[v - p.vars][z]
            at = z * per_level + v
            wide[at, :, pad : pad + p.lon] = field
            wide[at, :, :pad] = field[:, p.lon - pad :]
            wide[at, :, pad + p.lon :] = field[:, :right]
        return carry

    lax.fori_loop(0, p.lev, fill, 0)

    lane = lax.broadcasted_iota(jnp.int32, (1, p.tiles * p.slots), 1)
    filled = jnp.zeros_like(lane)
    for t in range(p.tiles):
        filled = jnp.where(lane // p.slots == t, count_ref[0, t], filled)
    weight = jnp.where(lane % p.slots < filled, weight_ref[...], 0.0)
    obs = []
    for x in (weight, weight * value_ref[...], cell_ref[...].astype(jnp.float32)):
        obs += [x[:, :LANES], x[:, LANES:]]
    obs = jnp.concatenate(obs, axis=0)
    lanes = lax.broadcasted_iota(jnp.int32, (p.lat, LANES), 1)
    borrows = jnp.where(p.borrows(lax.axis_index("tm")), p.extra, 0)

    def blocks(z, carry):
        for j in range(p.cols):

            def take(a, start):
                return wide[z * per_level + a, :, pad + start : pad + start + LANES]

            base = (z * p.cols + j) * p.rows
            start = j * p.width
            for v in range(p.vars):
                piece = take(v, start - p.margin)
                if v < 3:
                    beyond = take(p.vars + v, start + p.width + p.margin)
                    before = take(p.vars + v, start - p.margin - LANES)
                    piece = jnp.where(lanes < borrows, beyond, piece)
                    piece = jnp.where(lanes >= LANES - borrows, before, piece)
                out_ref[pl.ds(base + v, p.lat, stride=p.vars), :] = piece
            for c in range(3):
                rows = pl.ds(base + p.coef_row + c * p.lat, p.lat)
                out_ref[rows, :] = take(p.vars + c, start - p.margin)
            out_ref[pl.ds(base + p.obs_row, 6), :] = obs
        return carry

    lax.fori_loop(0, p.lev, blocks, 0)


class Stores:
    def __init__(self):
        self.held = []

    def put(self, ref, at, value):
        self.held.append((ref, at, value))

    def flush(self):
        for ref, at, value in self.held:
            ref[at] = value
        self.held = []


def looped(count, unroll, body):
    def many(i, carry):
        stores = Stores()
        for u in range(unroll):
            body(i * unroll + u, stores)
        stores.flush()
        return carry

    lax.fori_loop(0, count // unroll, many, 0)


def swap_blocks(x, slots):
    size = x.shape[0]
    sub = lax.broadcasted_iota(jnp.int32, x.shape, 0)
    block = lax.broadcasted_iota(jnp.int32, x.shape, 1) // slots
    out = x
    for d in range(1, size):
        moved = pltpu.roll(pltpu.roll(x, size - d, 0), d * slots, 1)
        out = jnp.where(block == (sub + d) % size, moved, out)
    return out


def spread(a, b, count):
    return (
        jnp.concatenate([a[:count], b[:count]], axis=0),
        jnp.concatenate([a[count:], b[count:]], axis=0),
    )


def chain_kernel(
    plan,
    recv_ref,
    out_ref,
    mid_c,
    east_c,
    west_c,
    north_c,
    south_c,
    weight_g,
    innov,
    states,
    results,
    carried,
    by_var,
    obs_tab,
):
    p = plan
    f32 = jnp.float32
    me = lax.axis_index("tm") * p.tiles + lax.axis_index("tile")
    level = (me // p.cols).astype(f32)
    origin = ((me % p.cols) * p.width - p.halo).astype(f32)
    shape = (2 * p.vars, LANES)
    sub = lax.broadcasted_iota(jnp.int32, shape, 0)
    lane = lax.broadcasted_iota(jnp.int32, shape, 1)
    lower = sub < p.vars
    n = p.nlat
    pitch = p.pitch
    whole = p.subs * pitch
    zero = jnp.zeros(shape, f32)

    def row_of(kt):
        return kt * p.lat + kt // p.tiles * STEPS

    for k in range(p.subs):
        for l in range(n, pitch):
            for ref in (mid_c, east_c, west_c, north_c, south_c, innov, weight_g, states, results):
                ref[k * pitch + l] = zero

    def observe(k, stores):
        raw = []
        for i in range(6):
            raw.append(recv_ref[pl.ds(k * p.tiles * p.rows + p.obs_row + i, p.tiles, stride=p.rows), :])
        w, wy, cell = (jnp.concatenate(raw[2 * i : 2 * i + 2], axis=1) for i in range(3))
        w, wy, cell = (swap_blocks(x, p.slots) for x in (w, wy, cell))
        row = jnp.floor((cell + 0.5) * (1.0 / p.lon))
        lon = cell - row * p.lon
        group = jnp.floor((row + 0.5) * (1.0 / p.lat))
        lat = row - group * p.lat
        var = jnp.floor((group + 0.5) * (1.0 / p.lev))
        lev = group - var * p.lev
        at = lon - origin
        at = jnp.where(at < 0, at + p.lon, at)
        at = jnp.where(at >= p.lon, at - p.lon, at)
        place = at - p.extra
        place = jnp.where(place < 0, place + LANES, place)
        place = jnp.where(place >= LANES, place - LANES, place)
        here = lev == level
        in_a = here & (at < p.half + 2 * p.halo)
        in_b = here & (at >= p.half) & (at < p.span)
        rows = pl.ds(k * p.tiles, p.tiles)
        stores.put(obs_tab, (0, rows), lat * p.vars + var)
        stores.put(obs_tab, (1, rows), jnp.where(in_a, place, -1.0))
        stores.put(obs_tab, (2, rows), jnp.where(in_b, place, -1.0))
        for i, x in ((3, w), (6, -wy)):
            one = x.astype(jnp.bfloat16).astype(f32)
            two = (x - one).astype(jnp.bfloat16).astype(f32)
            stores.put(obs_tab, (i, rows), one)
            stores.put(obs_tab, (i + 1, rows), two)
            stores.put(obs_tab, (i + 2, rows), x - one - two)

    looped(p.subs, 1, observe)

    n_rows = p.lat * p.vars
    slots = p.tiles * p.slots
    row_id = lax.broadcasted_iota(jnp.int32, (n_rows, slots), 0).astype(f32)
    lane_id = lax.broadcasted_iota(jnp.int32, (LANES, slots), 0).astype(f32)

    def grid(kt, stores):
        def entry(i):
            return obs_tab[i, pl.ds(kt, 1), :]

        match = row_id == entry(0)
        left = jnp.concatenate(
            [jnp.where(match, entry(i), 0.0).astype(jnp.bfloat16) for i in range(3, 9)], axis=0
        )
        right = jnp.concatenate(
            [jnp.where(lane_id == entry(i), 1.0, 0.0).astype(jnp.bfloat16) for i in (1, 2)], axis=0
        )
        full = lax.dot_general(left, right, (((1,), (1,)), ((), ())), preferred_element_type=f32)
        for i, ref in ((0, weight_g), (3, innov)):
            parts = [full[(i + q) * n_rows : (i + q + 1) * n_rows] for q in range(3)]
            summed = parts[0] + (parts[1] + parts[2])
            for pair in range(p.lat // 2):
                rows = slice(2 * p.vars * pair, 2 * p.vars * (pair + 1))
                one, two = spread(summed[rows, :LANES], summed[rows, LANES:], p.vars)
                at = row_of(kt) + 2 * pair
                stores.put(ref, at, one)
                stores.put(ref, at + 1, two)

    looped(p.count, 2, grid)

    def widen(kt, stores):
        base = kt * p.rows
        count = jnp.where(p.borrows(kt // p.tiles), p.extra, 0)
        mask = (lower & (lane >= LANES - count)) | (~lower & (lane < count))
        for l in range(p.lat):
            got = []
            for c in range(3):
                main = recv_ref[pl.ds(base + p.coef_row + c * p.lat + l, 1), :]
                edge = recv_ref[pl.ds(base + l * p.vars + c, 1), :]
                got.append(
                    jnp.where(mask, jnp.broadcast_to(edge, shape), jnp.broadcast_to(main, shape))
                )
            east, north, diff = got
            east = 0.5 * east
            north = 0.5 * north
            at = row_of(kt) + l
            stores.put(mid_c, at, 1.0 - 4.0 * diff)
            stores.put(east_c, at, diff - east)
            stores.put(west_c, at, diff + east)
            stores.put(north_c, at, diff - north)
            stores.put(south_c, at, diff + north)

    looped(p.count, 1, widen)

    nothing = p.subs * pitch
    nothing_yet = ITERS * whole

    def sweep(base, load, emit, stage, width):
        state, _ = stage(base, (zero,) * width, load(0, 0), True)

        def many(g, state):
            stores = Stores()
            for u in range(BLOCK):
                r = g * BLOCK + u
                x = load(r + 1, u + 1)
                state, y = stage(base + r + 1, state, x, False)
                emit(r, y, stores)
            stores.flush()
            return state

        lax.fori_loop(0, n // BLOCK, many, state)

    def adjoint_stage(at, state, x, fresh):
        here, below, north = state
        now = (
            mid_c[at] * x
            + pltpu.roll(east_c[at] * x, 1, 1)
            + pltpu.roll(west_c[at] * x, LANES - 1, 1)
        )
        done = None if fresh else here + below + south_c[at] * x
        return (now, north, north_c[at] * x), done

    def forward_stage(at, state, x, fresh):
        if fresh:
            return (zero, x), None
        below, last = state
        row = at - 1
        done = (
            mid_c[row] * last
            + east_c[row] * pltpu.roll(last, LANES - 1, 1)
            + west_c[row] * pltpu.roll(last, 1, 1)
            + north_c[row] * x
            + south_c[row] * below
        )
        return (last, x), done

    def clear(ref, start):
        def body(i, carry):
            for u in range(7):
                ref[start + i * 7 + u] = zero
            return carry

        lax.fori_loop(0, pitch // 7, body, 0)
        for l in range(pitch // 7 * 7, pitch):
            ref[start + l] = zero

    for ref, start in ((weight_g, nothing), (innov, nothing), (states, nothing), (results, nothing_yet)):
        clear(ref, start)

    def adjoint(phase):
        clear(carried, 0)

        def one(i, carry):
            base = (p.subs - 1 - i // STEPS) * pitch
            into = phase * whole + base
            starts = i % STEPS == 0
            source = jnp.where(starts, base, nothing)
            seen = jnp.where(starts & (phase > 0), base, nothing)

            def load(l, u):
                return carried[l] + (innov[source + l] + weight_g[source + l] * states[seen + l])

            def emit(r, y, stores):
                stores.put(carried, r, y)
                stores.put(results, into + r, y)

            sweep(base, load, emit, adjoint_stage, 3)
            return carry

        lax.fori_loop(0, p.subs * STEPS, one, 0)

    def forward():
        clear(carried, 0)

        def one(i, carry):
            k = i // STEPS
            base = k * pitch
            source = jnp.where(i % STEPS == 0, base, nothing_yet)
            held = {}

            def load(l, u):
                even = u - u % 2
                if held.get("pair") != even or u == 1:
                    tile = jnp.minimum((l - u) // p.lat + even // p.lat, p.tiles - 1)
                    row = (k * p.tiles + tile) * p.rows + even % p.lat * p.vars
                    var = recv_ref[pl.ds(row, 2 * p.vars), :]
                    held.update(pair=even, var=spread(var, var, p.vars))
                return carried[l] - 0.5 * (held["var"][u % 2] * results[source + l])

            def emit(r, y, stores):
                stores.put(carried, r, y)
                stores.put(states, base + r, y)

            sweep(base, load, emit, forward_stage, 2)
            return carry

        lax.fori_loop(0, p.subs * STEPS, one, 0)

    def iteration(phase, carry):
        adjoint(phase)

        @pl.when(phase < ITERS - 1)
        def _():
            forward()

        return carry

    lax.fori_loop(0, ITERS, iteration, 0)

    in_half = (lane < p.margin + p.half)[: p.vars]

    def fold(kt, stores):
        for l in range(p.lat):
            at = row_of(kt) + l
            y = 0.5 * results[at] + results[whole + at]
            y = jnp.where(in_half, y[: p.vars], y[p.vars :])
            stores.put(by_var, (pl.ds(kt * p.lat + l, p.vars, stride=p.count * p.lat),), y)

    looped(p.count, 2, fold)

    def join(kt, stores):
        own = slice(p.margin, p.margin + p.width)
        cols = [by_var[pl.ds(v * p.count * p.lat + kt * p.lat, p.lat), :][:, own] for v in range(p.vars)]
        spare = 3 * LANES - p.vars * p.width
        line = jnp.concatenate(cols + [jnp.zeros((p.lat, spare), f32)], axis=1)
        for i in range(3):
            at = (pl.ds(kt * p.lat * 3 + i, p.lat, stride=3),)
            stores.put(out_ref, at, line[:, i * LANES : (i + 1) * LANES])

    looped(p.count, 2, join)


def finish_kernel(plan, recv_ref, var_ref, out_ref):
    p = plan

    def level(z, carry):
        for j in range(p.cols):
            start = (z * p.cols + j) * p.lat * 3
            rows = [recv_ref[pl.ds(start + i, p.lat, stride=3), :] for i in range(3)]
            for v in range(p.vars):
                at, end = v * p.width, (v + 1) * p.width
                col = j * p.width
                while at < end:
                    i, low = divmod(at, LANES)
                    size = min(end - at, LANES - low)
                    cols = slice(col, col + size)
                    scale = -0.5 * var_ref[v, z, :, cols]
                    out_ref[v, z, :, cols] = scale * rows[i][:, low : low + size]
                    at, col = at + size, col + size
        return carry

    lax.fori_loop(0, p.lev, level, 0)


def transposed(
    plan, advect_east, advect_north, diffusion, background_var, obs_cell, obs_value, obs_weight, obs_count
):
    p = plan
    f32 = jnp.float32
    vmem = pl.BlockSpec(memory_space=pltpu.VMEM)
    params = pltpu.CompilerParams(vmem_limit_bytes=VMEM_LIMIT)
    var = background_var[0]
    packed = pl.pallas_call(
        functools.partial(pack_kernel, p),
        out_shape=jax.ShapeDtypeStruct((p.count * p.rows, LANES), f32),
        in_specs=[pl.BlockSpec(memory_space=pltpu.SMEM)] + [vmem] * 7,
        out_specs=vmem,
        scratch_shapes=[pltpu.VMEM(((p.vars + 3) * p.lev, p.lat, 15 * LANES), f32)],
        compiler_params=params,
        name="pack",
    )(
        obs_count.reshape(1, -1),
        obs_cell.reshape(1, -1),
        obs_value.reshape(1, -1),
        obs_weight.reshape(1, -1),
        advect_east[0],
        advect_north[0],
        diffusion[0],
        var,
    )
    received = lax.all_to_all(packed.reshape(-1, 2, LANES), ("tm", "tile"), 0, 0, tiled=True)
    received = received.reshape(-1, LANES)
    rows = p.subs * p.pitch
    field = pltpu.VMEM((rows + p.pitch, 2 * p.vars, LANES), f32)
    back = pl.pallas_call(
        functools.partial(chain_kernel, p),
        out_shape=jax.ShapeDtypeStruct((p.count * p.lat * 3, LANES), f32),
        in_specs=[vmem],
        out_specs=vmem,
        scratch_shapes=[field] * 8
        + [
            pltpu.VMEM((ITERS * rows + p.pitch, 2 * p.vars, LANES), f32),
            pltpu.VMEM((p.pitch, 2 * p.vars, LANES), f32),
            pltpu.VMEM((p.vars * p.count * p.lat, LANES), f32),
            pltpu.VMEM((9, p.count, p.tiles * p.slots), f32),
        ],
        compiler_params=params,
        name="chains",
    )(received)
    back = back.reshape(-1, 4, LANES)
    returned = lax.all_to_all(back, ("tm", "tile"), 0, 0, tiled=True)
    returned = returned.reshape(-1, LANES)
    increment = pl.pallas_call(
        functools.partial(finish_kernel, p),
        out_shape=jax.ShapeDtypeStruct(var.shape, f32),
        in_specs=[vmem] * 2,
        out_specs=vmem,
        compiler_params=params,
        name="finish",
    )(returned, var)
    return increment[None]


def solution(mesh):
    def run(*args):
        plan = Plan(mesh.shape, args[3].shape, args[4].shape)
        work = functools.partial(transposed, plan) if plan.fits() else per_device
        return jax.shard_map(
            work,
            mesh=mesh,
            in_specs=(
                P("tm", None, "tile", None),
                P("tm", None, "tile", None),
                P("tm", None, "tile", None),
                P("tm", None, None, "tile", None),
                P("tm", "tile", None),
                P("tm", "tile", None),
                P("tm", "tile", None),
                P("tm", "tile", None),
            ),
            out_specs=P("tm", None, None, "tile", None),
            check_vma=False,
        )(*args)

    return run
```

```python
import functools

import jax
import jax.numpy as jnp
from jax import lax
from jax.experimental import pallas as pl
from jax.experimental.pallas import tpu as pltpu
from jax.sharding import PartitionSpec as P

STEPS = 2
ITERS = 2
CHAINS = 3
LANES = 128
BLOCK = 96
VMEM_LIMIT = 48 * 1024 * 1024


def padded(block, sides, width):
    for axis, dim in sides:
        count = lax.axis_size(axis)
        forward = [(i, i + 1) for i in range(count - 1)]
        backward = [(target, source) for source, target in forward]
        low = lax.ppermute(
            lax.slice_in_dim(block, block.shape[dim] - width, None, axis=dim), axis, forward
        )
        high = lax.ppermute(lax.slice_in_dim(block, 0, width, axis=dim), axis, backward)
        block = jnp.concatenate([low, block, high], axis=dim)
    return block


def shifted(value, axis, steps):
    count = lax.axis_size(axis)
    first, last = (max(0, -steps), min(count, count - steps))
    return lax.ppermute(value, axis, [(source, source + steps) for source in range(first, last)])


def apply_step(field, coef, adjoint):
    east_c = coef[0]
    north_c = coef[1]
    diff_c = coef[2]
    if adjoint:
        to_east = (diff_c - 0.5 * east_c) * field
        to_west = (diff_c + 0.5 * east_c) * field
        to_north = (diff_c - 0.5 * north_c) * field
        to_south = (diff_c + 0.5 * north_c) * field
        middle = (1.0 - 4.0 * diff_c[:, 1:-1]) * field[:, :, 1:-1]
        return (
            middle
            + jnp.roll(to_east[:, :, 1:-1], 1, axis=-1)
            + jnp.roll(to_west[:, :, 1:-1], -1, axis=-1)
            + to_north[:, :, :-2]
            + to_south[:, :, 2:]
        )
    inner = field[:, :, 1:-1]
    diff_in = diff_c[:, 1:-1]
    east_in = east_c[:, 1:-1]
    north_in = north_c[:, 1:-1]
    return (
        (1.0 - 4.0 * diff_in) * inner
        + (diff_in - 0.5 * east_in) * jnp.roll(inner, -1, axis=-1)
        + (diff_in + 0.5 * east_in) * jnp.roll(inner, 1, axis=-1)
        + (diff_in - 0.5 * north_in) * field[:, :, 2:]
        + (diff_in + 0.5 * north_in) * field[:, :, :-2]
    )


def advance(field, coef, adjoint):
    for repeat in range(STEPS):
        extended = padded(field, (("tile", 2),), 1)
        field = apply_step(extended, coef, adjoint)
    return field


def per_device(
    advect_east, advect_north, diffusion, background_var, obs_cell, obs_value, obs_weight, obs_count
):
    windows_count = lax.axis_size("tm")
    tiles = lax.axis_size("tile")
    coefs = jnp.stack([advect_east[0], advect_north[0], diffusion[0]])
    coef_ext = padded(coefs, (("tile", 2),), 1)
    cells = obs_cell.reshape(tiles, -1)
    slot_count = cells.shape[1]
    live = jnp.arange(slot_count, dtype=jnp.int32)[None, :] < obs_count.reshape(tiles)[:, None]
    masked = obs_weight.reshape(tiles, -1) * live.astype(jnp.float32)
    received = lax.all_to_all(
        jnp.stack([obs_value.reshape(tiles, -1), masked]),
        "tile",
        split_axis=1,
        concat_axis=1,
        tiled=True,
    )
    received_cells = lax.all_to_all(cells, "tile", split_axis=0, concat_axis=0, tiled=True)
    departures = received[0].reshape(-1)
    obs_weights = received[1].reshape(-1)
    flat_cells = received_cells.reshape(-1)
    local_var = background_var[0]
    state_shape = local_var.shape
    cell_total = state_shape[0] * state_shape[1] * state_shape[2] * state_shape[3]
    increment = jnp.zeros(state_shape, jnp.float32)
    for iteration in range(ITERS):
        if iteration == 0:
            innov = obs_weights * (0.0 - departures)
        else:
            forward_carried = advance(increment, coef_ext, False)
            for forward_window in range(windows_count - 1):
                forward_incoming = shifted(forward_carried, "tm", 1)
                forward_carried = advance(forward_incoming + increment, coef_ext, False)
            innov = obs_weights * (
                jnp.take(forward_carried.reshape(cell_total), flat_cells, axis=0) - departures
            )
        gridded = jnp.zeros((cell_total,), jnp.float32).at[flat_cells].add(innov)
        source = gridded.reshape(state_shape)
        carried = advance(source, coef_ext, True)
        for window in range(windows_count - 1):
            incoming = shifted(carried, "tm", -1)
            carried = advance(incoming + source, coef_ext, True)
        increment = increment - 0.5 * (increment + local_var * carried)
    return increment[None]


class Plan:
    def __init__(self, mesh_shape, var_shape, slot_shape):
        self.subs, self.tiles = mesh_shape["tm"], mesh_shape["tile"]
        self.count = self.subs * self.tiles
        _, self.vars, self.lev, self.nlat, self.lon = var_shape
        self.lat = self.nlat // self.tiles
        self.slots = slot_shape[2] // self.tiles
        self.cols = self.count // self.lev
        self.width = self.lon // self.cols
        self.half = self.width // 2
        self.halo = CHAINS * STEPS * self.subs
        self.margin = (LANES - self.width) // 2
        self.extra = self.halo - self.margin
        self.span = self.width + 2 * self.halo
        self.coef_row = self.lat * self.vars
        self.obs_row = self.coef_row + 3 * self.lat
        self.rows = self.obs_row + 6
        self.pitch = self.nlat + STEPS

    def borrows(self, k):
        return (CHAINS - 1) * STEPS * self.subs + STEPS * (k + 1) > self.margin

    def fits(self):
        if self.count % self.lev or self.lon % self.cols or self.width % 2:
            return False
        for k in range(self.subs):
            spare = self.margin - STEPS * (2 * self.subs - k)
            if spare < 0 or (self.borrows(k) and spare < self.extra):
                return False
        return (
            self.half + 2 * self.halo <= LANES
            and 0 <= self.extra
            and self.vars == 4
            and self.lat % 2 == 0
            and self.tiles == 8
            and self.slots & (self.slots - 1) == 0
            and self.slots * self.tiles == 2 * LANES
            and self.width + 2 * self.margin == LANES
            and self.width * self.vars <= 3 * LANES
            and self.nlat % BLOCK == 0
            and BLOCK % self.lat == 0
            and self.count * self.rows % 8 == 0
            and self.rows % 2 == 0
        )


def pack_kernel(
    plan, count_ref, cell_ref, value_ref, weight_ref, east_ref, north_ref, diff_ref, var_ref, out_ref, wide
):
    p = plan
    pad = 2 * LANES
    right = wide.shape[-1] - pad - p.lon
    per_level = p.vars + 3

    def fill(z, carry):
        for v in range(per_level):
            field = var_ref[v, z] if v < p.vars else (east_ref, north_ref, diff_ref)[v - p.vars][z]
            at = z * per_level + v
            wide[at, :, pad : pad + p.lon] = field
            wide[at, :, :pad] = field[:, p.lon - pad :]
            wide[at, :, pad + p.lon :] = field[:, :right]
        return carry

    lax.fori_loop(0, p.lev, fill, 0)

    lane = lax.broadcasted_iota(jnp.int32, (1, p.tiles * p.slots), 1)
    filled = jnp.zeros_like(lane)
    for t in range(p.tiles):
        filled = jnp.where(lane >= t * p.slots, count_ref[0, t], filled)
    weight = jnp.where((lane & (p.slots - 1)) < filled, weight_ref[...], 0.0)
    obs = []
    for x in (weight, weight * value_ref[...], cell_ref[...].astype(jnp.float32)):
        obs += [x[:, :LANES], x[:, LANES:]]
    obs = jnp.concatenate(obs, axis=0)
    lanes = lax.broadcasted_iota(jnp.int32, (p.lat, LANES), 1)
    borrows = jnp.where(p.borrows(lax.axis_index("tm")), p.extra, 0)

    def blocks(z, carry):
        for j in range(p.cols):

            def take(a, start):
                return wide[z * per_level + a, :, pad + start : pad + start + LANES]

            base = (z * p.cols + j) * p.rows
            start = j * p.width
            for v in range(p.vars):
                piece = take(v, start - p.margin)
                if v < 3:
                    beyond = take(p.vars + v, start + p.width + p.margin)
                    before = take(p.vars + v, start - p.margin - LANES)
                    piece = jnp.where(lanes < borrows, beyond, piece)
                    piece = jnp.where(lanes >= LANES - borrows, before, piece)
                out_ref[pl.ds(base + v, p.lat, stride=p.vars), :] = piece
            for c in range(3):
                rows = pl.ds(base + p.coef_row + c * p.lat, p.lat)
                out_ref[rows, :] = take(p.vars + c, start - p.margin)
            out_ref[pl.ds(base + p.obs_row, 6), :] = obs
        return carry

    lax.fori_loop(0, p.lev, blocks, 0)


class Stores:
    def __init__(self):
        self.held = []

    def put(self, ref, at, value):
        self.held.append((ref, at, value))

    def flush(self):
        for ref, at, value in self.held:
            ref[at] = value
        self.held = []


def looped(count, unroll, body):
    def many(i, carry):
        stores = Stores()
        for u in range(unroll):
            body(i * unroll + u, stores)
        stores.flush()
        return carry

    lax.fori_loop(0, count // unroll, many, 0)


def swap_blocks(x, slots):
    size = x.shape[0]
    sub = lax.broadcasted_iota(jnp.int32, x.shape, 0)
    block = lax.broadcasted_iota(jnp.int32, x.shape, 1) >> (slots.bit_length() - 1)
    out = x
    for d in range(1, size):
        moved = pltpu.roll(pltpu.roll(x, size - d, 0), d * slots, 1)
        out = jnp.where(block == ((sub + d) & (size - 1)), moved, out)
    return out


def spread(a, b, count):
    return (
        jnp.concatenate([a[:count], b[:count]], axis=0),
        jnp.concatenate([a[count:], b[count:]], axis=0),
    )


def chain_kernel(
    plan,
    recv_ref,
    out_ref,
    mid_c,
    east_c,
    west_c,
    north_c,
    south_c,
    weight_g,
    innov,
    results,
    carried,
    by_var,
    obs_tab,
):
    p = plan
    f32 = jnp.float32
    me = lax.axis_index("tm") * p.tiles + lax.axis_index("tile")
    level = (me // p.cols).astype(f32)
    origin = ((me % p.cols) * p.width - p.halo).astype(f32)
    shape = (2 * p.vars, LANES)
    sub = lax.broadcasted_iota(jnp.int32, shape, 0)
    lane = lax.broadcasted_iota(jnp.int32, shape, 1)
    lower = sub < p.vars
    n = p.nlat
    pitch = p.pitch
    whole = p.subs * pitch
    zero = jnp.zeros(shape, f32)

    def row_of(kt):
        return kt * p.lat + kt // p.tiles * STEPS

    for k in range(p.subs):
        for l in range(n, pitch):
            for ref in (mid_c, east_c, west_c, north_c, south_c, innov, results):
                ref[k * pitch + l] = zero
            innov[whole + k * pitch + l] = zero

    def observe(k, stores):
        raw = []
        for i in range(6):
            raw.append(recv_ref[pl.ds(k * p.tiles * p.rows + p.obs_row + i, p.tiles, stride=p.rows), :])
        w, wy, cell = (jnp.concatenate(raw[2 * i : 2 * i + 2], axis=1) for i in range(3))
        w, wy, cell = (swap_blocks(x, p.slots) for x in (w, wy, cell))
        row = jnp.floor((cell + 0.5) * (1.0 / p.lon))
        lon = cell - row * p.lon
        group = jnp.floor((row + 0.5) * (1.0 / p.lat))
        lat = row - group * p.lat
        var = jnp.floor((group + 0.5) * (1.0 / p.lev))
        lev = group - var * p.lev
        at = lon - origin
        at = jnp.where(at < 0, at + p.lon, at)
        at = jnp.where(at >= p.lon, at - p.lon, at)
        place = at - p.extra
        place = jnp.where(place < 0, place + LANES, place)
        place = jnp.where(place >= LANES, place - LANES, place)
        here = lev == level
        in_a = here & (at < p.half + 2 * p.halo)
        in_b = here & (at >= p.half) & (at < p.span)
        rows = pl.ds(k * p.tiles, p.tiles)
        stores.put(obs_tab, (0, rows), lat * p.vars + var)
        stores.put(obs_tab, (1, rows), jnp.where(in_a, place, -1.0))
        stores.put(obs_tab, (2, rows), jnp.where(in_b, place, -1.0))
        for i, x in ((3, w), (6, -wy)):
            one = x.astype(jnp.bfloat16).astype(f32)
            two = (x - one).astype(jnp.bfloat16).astype(f32)
            stores.put(obs_tab, (i, rows), one)
            stores.put(obs_tab, (i + 1, rows), two)
            stores.put(obs_tab, (i + 2, rows), x - one - two)

    looped(p.subs, 1, observe)

    n_rows = p.lat * p.vars
    slots = p.tiles * p.slots
    row_id = lax.broadcasted_iota(jnp.int32, (n_rows, slots), 0).astype(f32)
    lane_id = lax.broadcasted_iota(jnp.int32, (LANES, slots), 0).astype(f32)

    def grid(kt, stores):
        def entry(i):
            return obs_tab[i, pl.ds(kt, 1), :]

        match = row_id == entry(0)
        left = jnp.concatenate(
            [jnp.where(match, entry(i), 0.0).astype(jnp.bfloat16) for i in range(3, 9)], axis=0
        )
        right = jnp.concatenate(
            [jnp.where(lane_id == entry(i), 1.0, 0.0).astype(jnp.bfloat16) for i in (1, 2)], axis=0
        )
        full = lax.dot_general(left, right, (((1,), (1,)), ((), ())), preferred_element_type=f32)
        for i, ref in ((0, weight_g), (3, innov)):
            parts = [full[(i + q) * n_rows : (i + q + 1) * n_rows] for q in range(3)]
            summed = parts[0] + (parts[1] + parts[2])
            for pair in range(p.lat // 2):
                rows = slice(2 * p.vars * pair, 2 * p.vars * (pair + 1))
                one, two = spread(summed[rows, :LANES], summed[rows, LANES:], p.vars)
                at = row_of(kt) + 2 * pair
                stores.put(ref, at, one)
                stores.put(ref, at + 1, two)

    looped(p.count, 2, grid)

    def widen(kt, stores):
        base = kt * p.rows
        count = jnp.where(p.borrows(kt // p.tiles), p.extra, 0)
        mask = (lower & (lane >= LANES - count)) | (~lower & (lane < count))
        for l in range(p.lat):
            got = []
            for c in range(3):
                main = recv_ref[pl.ds(base + p.coef_row + c * p.lat + l, 1), :]
                edge = recv_ref[pl.ds(base + l * p.vars + c, 1), :]
                got.append(
                    jnp.where(mask, jnp.broadcast_to(edge, shape), jnp.broadcast_to(main, shape))
                )
            east, north, diff = got
            east = 0.5 * east
            north = 0.5 * north
            at = row_of(kt) + l
            stores.put(mid_c, at, 1.0 - 4.0 * diff)
            stores.put(east_c, at, diff - east)
            stores.put(west_c, at, diff + east)
            stores.put(north_c, at, diff - north)
            stores.put(south_c, at, diff + north)

    looped(p.count, 1, widen)

    nothing = ITERS * whole

    def sweep(base, load, emit, stage, width):
        state, _ = stage(base, (zero,) * width, load(0, 0), True)

        def many(g, state):
            stores = Stores()
            for u in range(BLOCK):
                r = g * BLOCK + u
                x = load(r + 1, u + 1)
                state, y = stage(base + r + 1, state, x, False)
                emit(r, y, stores)
            stores.flush()
            return state

        lax.fori_loop(0, n // BLOCK, many, state)

    def adjoint_stage(at, state, x, fresh):
        here, below, north = state
        now = (
            mid_c[at] * x
            + pltpu.roll(east_c[at] * x, 1, 1)
            + pltpu.roll(west_c[at] * x, LANES - 1, 1)
        )
        done = None if fresh else here + below + south_c[at] * x
        return (now, north, north_c[at] * x), done

    def forward_stage(at, state, x, fresh):
        if fresh:
            return (zero, x), None
        below, last = state
        row = at - 1
        done = (
            mid_c[row] * last
            + east_c[row] * pltpu.roll(last, LANES - 1, 1)
            + west_c[row] * pltpu.roll(last, 1, 1)
            + north_c[row] * x
            + south_c[row] * below
        )
        return (last, x), done

    def clear(ref, start):
        def body(i, carry):
            for u in range(7):
                ref[start + i * 7 + u] = zero
            return carry

        lax.fori_loop(0, pitch // 7, body, 0)
        for l in range(pitch // 7 * 7, pitch):
            ref[start + l] = zero

    for ref in (innov, results):
        clear(ref, nothing)

    def adjoint(phase):
        clear(carried, 0)

        def one(i, carry):
            base = (p.subs - 1 - i // STEPS) * pitch
            into = phase * whole + base
            source = jnp.where(i % STEPS == 0, into, nothing)

            def load(l, u):
                return carried[l] + innov[source + l]

            def emit(r, y, stores):
                stores.put(carried, r, y)
                stores.put(results, into + r, y)

            sweep(base, load, emit, adjoint_stage, 3)
            return carry

        lax.fori_loop(0, p.subs * STEPS, one, 0)

    def forward():
        clear(carried, 0)

        def one(i, carry):
            k = i // STEPS
            base = k * pitch
            source = jnp.where(i % STEPS == 0, base, nothing)
            held = {}

            def load(l, u):
                even = u - u % 2
                if held.get("pair") != even or u == 1:
                    tile = jnp.minimum((l - u) // p.lat + even // p.lat, p.tiles - 1)
                    row = (k * p.tiles + tile) * p.rows + even % p.lat * p.vars
                    var = recv_ref[pl.ds(row, 2 * p.vars), :]
                    held.update(pair=even, var=spread(var, var, p.vars))
                return carried[l] - 0.5 * (held["var"][u % 2] * results[source + l])

            def emit(r, y, stores):
                stores.put(carried, r, y)
                stores.put(innov, whole + base + r, weight_g[base + r] * y + innov[base + r])

            sweep(base, load, emit, forward_stage, 2)
            return carry

        lax.fori_loop(0, p.subs * STEPS, one, 0)

    def iteration(phase, carry):
        adjoint(phase)

        @pl.when(phase < ITERS - 1)
        def _():
            forward()

        return carry

    lax.fori_loop(0, ITERS, iteration, 0)

    in_half = (lane < p.margin + p.half)[: p.vars]

    def fold(kt, stores):
        for l in range(p.lat):
            at = row_of(kt) + l
            y = 0.5 * results[at] + results[whole + at]
            y = jnp.where(in_half, y[: p.vars], y[p.vars :])
            stores.put(by_var, (pl.ds(kt * p.lat + l, p.vars, stride=p.count * p.lat),), y)

    looped(p.count, 4, fold)

    def join(kt, stores):
        own = slice(p.margin, p.margin + p.width)
        cols = [by_var[pl.ds(v * p.count * p.lat + kt * p.lat, p.lat), :][:, own] for v in range(p.vars)]
        spare = 3 * LANES - p.vars * p.width
        line = jnp.concatenate(cols + [jnp.zeros((p.lat, spare), f32)], axis=1)
        for i in range(3):
            at = (pl.ds(kt * p.lat * 3 + i, p.lat, stride=3),)
            stores.put(out_ref, at, line[:, i * LANES : (i + 1) * LANES])

    looped(p.count, 4, join)


def finish_kernel(plan, recv_ref, var_ref, out_ref):
    p = plan

    def level(z, carry):
        for j in range(p.cols):
            start = (z * p.cols + j) * p.lat * 3
            rows = [recv_ref[pl.ds(start + i, p.lat, stride=3), :] for i in range(3)]
            for v in range(p.vars):
                at, end = v * p.width, (v + 1) * p.width
                col = j * p.width
                while at < end:
                    i, low = divmod(at, LANES)
                    size = min(end - at, LANES - low)
                    cols = slice(col, col + size)
                    scale = -0.5 * var_ref[v, z, :, cols]
                    out_ref[v, z, :, cols] = scale * rows[i][:, low : low + size]
                    at, col = at + size, col + size
        return carry

    lax.fori_loop(0, p.lev, level, 0)


def transposed(
    plan, advect_east, advect_north, diffusion, background_var, obs_cell, obs_value, obs_weight, obs_count
):
    p = plan
    f32 = jnp.float32
    vmem = pl.BlockSpec(memory_space=pltpu.VMEM)
    params = pltpu.CompilerParams(vmem_limit_bytes=VMEM_LIMIT)
    var = background_var[0]
    packed = pl.pallas_call(
        functools.partial(pack_kernel, p),
        out_shape=jax.ShapeDtypeStruct((p.count * p.rows, LANES), f32),
        in_specs=[pl.BlockSpec(memory_space=pltpu.SMEM)] + [vmem] * 7,
        out_specs=vmem,
        scratch_shapes=[pltpu.VMEM(((p.vars + 3) * p.lev, p.lat, 15 * LANES), f32)],
        compiler_params=params,
        name="pack",
    )(
        obs_count.reshape(1, -1),
        obs_cell.reshape(1, -1),
        obs_value.reshape(1, -1),
        obs_weight.reshape(1, -1),
        advect_east[0],
        advect_north[0],
        diffusion[0],
        var,
    )
    received = lax.all_to_all(packed.reshape(-1, 2, LANES), ("tm", "tile"), 0, 0, tiled=True)
    received = received.reshape(-1, LANES)
    rows = p.subs * p.pitch
    field = pltpu.VMEM((rows, 2 * p.vars, LANES), f32)
    back = pl.pallas_call(
        functools.partial(chain_kernel, p),
        out_shape=jax.ShapeDtypeStruct((p.count * p.lat * 3, LANES), f32),
        in_specs=[vmem],
        out_specs=vmem,
        scratch_shapes=[field] * 6
        + [pltpu.VMEM((ITERS * rows + p.pitch, 2 * p.vars, LANES), f32)] * 2
        + [
            pltpu.VMEM((p.pitch, 2 * p.vars, LANES), f32),
            pltpu.VMEM((p.vars * p.count * p.lat, LANES), f32),
            pltpu.VMEM((9, p.count, p.tiles * p.slots), f32),
        ],
        compiler_params=params,
        name="chains",
    )(received)
    back = back.reshape(-1, 4, LANES)
    returned = lax.all_to_all(back, ("tm", "tile"), 0, 0, tiled=True)
    returned = returned.reshape(-1, LANES)
    increment = pl.pallas_call(
        functools.partial(finish_kernel, p),
        out_shape=jax.ShapeDtypeStruct(var.shape, f32),
        in_specs=[vmem] * 2,
        out_specs=vmem,
        compiler_params=params,
        name="finish",
    )(returned, var)
    return increment[None]


def solution(mesh):
    def run(*args):
        plan = Plan(mesh.shape, args[3].shape, args[4].shape)
        work = functools.partial(transposed, plan) if plan.fits() else per_device
        return jax.shard_map(
            work,
            mesh=mesh,
            in_specs=(
                P("tm", None, "tile", None),
                P("tm", None, "tile", None),
                P("tm", None, "tile", None),
                P("tm", None, None, "tile", None),
                P("tm", "tile", None),
                P("tm", "tile", None),
                P("tm", "tile", None),
                P("tm", "tile", None),
            ),
            out_specs=P("tm", None, None, "tile", None),
            check_vma=False,
        )(*args)

    return run
```

```python
import functools

import jax
import jax.numpy as jnp
from jax import lax
from jax.experimental import pallas as pl
from jax.experimental.pallas import tpu as pltpu
from jax.sharding import PartitionSpec as P

STEPS = 2
ITERS = 2
CHAINS = 3
LANES = 128
VMEM_LIMIT = 48 * 1024 * 1024


def padded(block, sides, width):
    for axis, dim in sides:
        count = lax.axis_size(axis)
        forward = [(i, i + 1) for i in range(count - 1)]
        backward = [(target, source) for source, target in forward]
        low = lax.ppermute(
            lax.slice_in_dim(block, block.shape[dim] - width, None, axis=dim), axis, forward
        )
        high = lax.ppermute(lax.slice_in_dim(block, 0, width, axis=dim), axis, backward)
        block = jnp.concatenate([low, block, high], axis=dim)
    return block


def shifted(value, axis, steps):
    count = lax.axis_size(axis)
    first, last = (max(0, -steps), min(count, count - steps))
    return lax.ppermute(value, axis, [(source, source + steps) for source in range(first, last)])


def apply_step(field, coef, adjoint):
    east_c = coef[0]
    north_c = coef[1]
    diff_c = coef[2]
    if adjoint:
        to_east = (diff_c - 0.5 * east_c) * field
        to_west = (diff_c + 0.5 * east_c) * field
        to_north = (diff_c - 0.5 * north_c) * field
        to_south = (diff_c + 0.5 * north_c) * field
        middle = (1.0 - 4.0 * diff_c[:, 1:-1]) * field[:, :, 1:-1]
        return (
            middle
            + jnp.roll(to_east[:, :, 1:-1], 1, axis=-1)
            + jnp.roll(to_west[:, :, 1:-1], -1, axis=-1)
            + to_north[:, :, :-2]
            + to_south[:, :, 2:]
        )
    inner = field[:, :, 1:-1]
    diff_in = diff_c[:, 1:-1]
    east_in = east_c[:, 1:-1]
    north_in = north_c[:, 1:-1]
    return (
        (1.0 - 4.0 * diff_in) * inner
        + (diff_in - 0.5 * east_in) * jnp.roll(inner, -1, axis=-1)
        + (diff_in + 0.5 * east_in) * jnp.roll(inner, 1, axis=-1)
        + (diff_in - 0.5 * north_in) * field[:, :, 2:]
        + (diff_in + 0.5 * north_in) * field[:, :, :-2]
    )


def advance(field, coef, adjoint):
    for repeat in range(STEPS):
        extended = padded(field, (("tile", 2),), 1)
        field = apply_step(extended, coef, adjoint)
    return field


def per_device(
    advect_east, advect_north, diffusion, background_var, obs_cell, obs_value, obs_weight, obs_count
):
    windows_count = lax.axis_size("tm")
    tiles = lax.axis_size("tile")
    coefs = jnp.stack([advect_east[0], advect_north[0], diffusion[0]])
    coef_ext = padded(coefs, (("tile", 2),), 1)
    cells = obs_cell.reshape(tiles, -1)
    slot_count = cells.shape[1]
    live = jnp.arange(slot_count, dtype=jnp.int32)[None, :] < obs_count.reshape(tiles)[:, None]
    masked = obs_weight.reshape(tiles, -1) * live.astype(jnp.float32)
    received = lax.all_to_all(
        jnp.stack([obs_value.reshape(tiles, -1), masked]),
        "tile",
        split_axis=1,
        concat_axis=1,
        tiled=True,
    )
    received_cells = lax.all_to_all(cells, "tile", split_axis=0, concat_axis=0, tiled=True)
    departures = received[0].reshape(-1)
    obs_weights = received[1].reshape(-1)
    flat_cells = received_cells.reshape(-1)
    local_var = background_var[0]
    state_shape = local_var.shape
    cell_total = state_shape[0] * state_shape[1] * state_shape[2] * state_shape[3]
    increment = jnp.zeros(state_shape, jnp.float32)
    for iteration in range(ITERS):
        if iteration == 0:
            innov = obs_weights * (0.0 - departures)
        else:
            forward_carried = advance(increment, coef_ext, False)
            for forward_window in range(windows_count - 1):
                forward_incoming = shifted(forward_carried, "tm", 1)
                forward_carried = advance(forward_incoming + increment, coef_ext, False)
            innov = obs_weights * (
                jnp.take(forward_carried.reshape(cell_total), flat_cells, axis=0) - departures
            )
        gridded = jnp.zeros((cell_total,), jnp.float32).at[flat_cells].add(innov)
        source = gridded.reshape(state_shape)
        carried = advance(source, coef_ext, True)
        for window in range(windows_count - 1):
            incoming = shifted(carried, "tm", -1)
            carried = advance(incoming + source, coef_ext, True)
        increment = increment - 0.5 * (increment + local_var * carried)
    return increment[None]


class Plan:
    def __init__(self, mesh_shape, var_shape, slot_shape):
        self.subs, self.tiles = mesh_shape["tm"], mesh_shape["tile"]
        self.count = self.subs * self.tiles
        _, self.vars, self.lev, self.nlat, self.lon = var_shape
        self.lat = self.nlat // self.tiles
        self.slots = slot_shape[2] // self.tiles
        self.cols = self.count // self.lev
        self.width = self.lon // self.cols
        self.half = self.width // 2
        self.halo = CHAINS * STEPS * self.subs
        self.margin = (LANES - self.width) // 2
        self.extra = self.halo - self.margin
        self.span = self.width + 2 * self.halo
        self.coef_row = self.lat * self.vars
        self.obs_row = self.coef_row + 3 * self.lat
        self.rows = self.obs_row + 6
        self.pitch = self.nlat + STEPS
        self.wide = -(-self.extra // STEPS)
        self.area = self.nlat * self.vars

    def borrows(self, k):
        return (CHAINS - 1) * STEPS * self.subs + STEPS * (k + 1) > self.margin

    def fits(self):
        if self.count % self.lev or self.lon % self.cols or self.width % 2:
            return False
        for k in range(self.subs):
            spare = self.margin - STEPS * (2 * self.subs - k)
            if spare < 0 or (self.borrows(k) and spare < self.extra):
                return False
        return (
            self.half + 2 * self.halo <= LANES
            and 0 <= self.extra
            and self.vars == 4
            and self.lat % 2 == 0
            and 0 < self.wide < self.subs
            and self.tiles == 8
            and self.slots & (self.slots - 1) == 0
            and self.slots * self.tiles == 2 * LANES
            and self.width + 2 * self.margin == LANES
            and self.width * self.vars <= 3 * LANES
            and self.count * self.rows % 8 == 0
            and self.rows % 2 == 0
        )


def pack_kernel(
    plan, count_ref, cell_ref, value_ref, weight_ref, east_ref, north_ref, diff_ref, var_ref, out_ref, wide
):
    p = plan
    pad = 2 * LANES
    right = wide.shape[-1] - pad - p.lon
    per_level = p.vars + 3

    def fill(z, carry):
        for v in range(per_level):
            field = var_ref[v, z] if v < p.vars else (east_ref, north_ref, diff_ref)[v - p.vars][z]
            at = z * per_level + v
            wide[at, :, pad : pad + p.lon] = field
            wide[at, :, :pad] = field[:, p.lon - pad :]
            wide[at, :, pad + p.lon :] = field[:, :right]
        return carry

    lax.fori_loop(0, p.lev, fill, 0)

    lane = lax.broadcasted_iota(jnp.int32, (1, p.tiles * p.slots), 1)
    filled = jnp.zeros_like(lane)
    for t in range(p.tiles):
        filled = jnp.where(lane >= t * p.slots, count_ref[0, t], filled)
    weight = jnp.where((lane & (p.slots - 1)) < filled, weight_ref[...], 0.0)
    obs = []
    for x in (weight, weight * value_ref[...], cell_ref[...].astype(jnp.float32)):
        obs += [x[:, :LANES], x[:, LANES:]]
    obs = jnp.concatenate(obs, axis=0)
    lanes = lax.broadcasted_iota(jnp.int32, (p.lat, LANES), 1)
    borrows = jnp.where(p.borrows(lax.axis_index("tm")), p.extra, 0)

    def blocks(z, carry):
        for j in range(p.cols):
            first = pad + j * p.width - p.margin
            tile, low = divmod(first, LANES)

            def moved(a, t):
                x = wide[z * per_level + a, :, t * LANES : (t + 1) * LANES]
                return pltpu.roll(x, LANES - low, 1)

            base = (z * p.cols + j) * p.rows
            for v in range(p.vars):
                piece = jnp.where(lanes < LANES - low, moved(v, tile), moved(v, tile + 1))
                if v < 3:
                    here, after = moved(p.vars + v, tile), moved(p.vars + v, tile + 1)
                    rows = pl.ds(base + p.coef_row + v * p.lat, p.lat)
                    out_ref[rows, :] = jnp.where(lanes < LANES - low, here, after)
                    if low < p.extra:
                        here = jnp.where(lanes < LANES - low, moved(p.vars + v, tile - 1), here)
                    if low + p.extra > LANES:
                        after = jnp.where(lanes < LANES - low, after, moved(p.vars + v, tile + 2))
                    piece = jnp.where(lanes < borrows, after, piece)
                    piece = jnp.where(lanes >= LANES - borrows, here, piece)
                out_ref[pl.ds(base + v, p.lat, stride=p.vars), :] = piece
            out_ref[pl.ds(base + p.obs_row, 6), :] = obs
        return carry

    lax.fori_loop(0, p.lev, blocks, 0)


class Stores:
    def __init__(self):
        self.held = []

    def put(self, ref, at, value):
        self.held.append((ref, at, value))

    def flush(self):
        for ref, at, value in self.held:
            ref[at] = value
        self.held = []


def looped(count, unroll, body):
    def many(i, carry):
        stores = Stores()
        for u in range(unroll):
            body(i * unroll + u, stores)
        stores.flush()
        return carry

    lax.fori_loop(0, count // unroll, many, 0)


def swap_blocks(x, slots):
    size = x.shape[0]
    sub = lax.broadcasted_iota(jnp.int32, x.shape, 0)
    block = lax.broadcasted_iota(jnp.int32, x.shape, 1) >> (slots.bit_length() - 1)
    out = x
    for d in range(1, size):
        moved = pltpu.roll(pltpu.roll(x, size - d, 0), d * slots, 1)
        out = jnp.where(block == ((sub + d) & (size - 1)), moved, out)
    return out


def spread(a, b, count):
    return (
        jnp.concatenate([a[:count], b[:count]], axis=0),
        jnp.concatenate([a[count:], b[count:]], axis=0),
    )


def chain_kernel(
    plan,
    recv_ref,
    out_ref,
    mid_w,
    east_w,
    west_w,
    north_w,
    south_w,
    source_w,
    result_w,
    carried_w,
    mid_c,
    east_c,
    west_c,
    north_c,
    south_c,
    weight_g,
    innov,
    results,
    carried,
    obs_tab,
):
    p = plan
    f32 = jnp.float32
    me = lax.axis_index("tm") * p.tiles + lax.axis_index("tile")
    level = (me // p.cols).astype(f32)
    origin = ((me % p.cols) * p.width - p.halo).astype(f32)
    two = 2 * p.vars
    shape = (two, LANES)
    sub = lax.broadcasted_iota(jnp.int32, shape, 0)
    lane = lax.broadcasted_iota(jnp.int32, shape, 1)
    lower = sub < p.vars
    in_half = lane < p.margin + p.half
    n = p.nlat
    pitch = p.pitch
    area = p.area
    whole = p.subs * area
    nothing = ITERS * whole
    lead = two
    low_wide = p.subs - p.wide
    zero = jnp.zeros(shape, f32)

    def rows8(start):
        return pl.ds(pl.multiple_of(start, two), two)

    def clear(ref, start, count):
        def body(i, carry):
            for u in range(8):
                ref[rows8(start + (i * 8 + u) * two), :] = zero
            return carry

        lax.fori_loop(0, count // (8 * two), body, 0)

    clear(innov, nothing, area)
    clear(results, nothing, area)
    for ref in (mid_c, east_c, west_c, north_c, south_c, carried):
        ref[:lead, :] = zero
        ref[ref.shape[0] - lead :, :] = zero
    for k in range(p.wide):
        for l in range(n, pitch):
            for ref in (mid_w, east_w, west_w, north_w, south_w, source_w):
                ref[k * pitch + l] = zero
    for l in range(n, pitch):
        carried_w[l * two : (l + 1) * two, :] = zero

    def observe(k, stores):
        raw = []
        for i in range(6):
            raw.append(recv_ref[pl.ds(k * p.tiles * p.rows + p.obs_row + i, p.tiles, stride=p.rows), :])
        w, wy, cell = (jnp.concatenate(raw[2 * i : 2 * i + 2], axis=1) for i in range(3))
        w, wy, cell = (swap_blocks(x, p.slots) for x in (w, wy, cell))
        row = jnp.floor((cell + 0.5) * (1.0 / p.lon))
        lon = cell - row * p.lon
        group = jnp.floor((row + 0.5) * (1.0 / p.lat))
        lat = row - group * p.lat
        var = jnp.floor((group + 0.5) * (1.0 / p.lev))
        lev = group - var * p.lev
        at = lon - origin
        at = jnp.where(at < 0, at + p.lon, at)
        at = jnp.where(at >= p.lon, at - p.lon, at)
        place = at - p.extra
        place = jnp.where(place < 0, place + LANES, place)
        place = jnp.where(place >= LANES, place - LANES, place)
        here = lev == level
        in_a = here & (at < p.half + 2 * p.halo)
        in_b = here & (at >= p.half) & (at < p.span)
        rows = pl.ds(k * p.tiles, p.tiles)
        stores.put(obs_tab, (0, rows), lat * p.vars + var)
        stores.put(obs_tab, (1, rows), jnp.where(in_a, place, -1.0))
        stores.put(obs_tab, (2, rows), jnp.where(in_b, place, -1.0))
        for i, x in ((3, w), (6, -wy)):
            one = x.astype(jnp.bfloat16).astype(f32)
            two = (x - one).astype(jnp.bfloat16).astype(f32)
            stores.put(obs_tab, (i, rows), one)
            stores.put(obs_tab, (i + 1, rows), two)
            stores.put(obs_tab, (i + 2, rows), x - one - two)

    looped(p.subs, 1, observe)

    n_rows = p.lat * p.vars
    slots = p.tiles * p.slots
    row_id = lax.broadcasted_iota(jnp.int32, (n_rows, slots), 0).astype(f32)
    lane_id = lax.broadcasted_iota(jnp.int32, (LANES, slots), 0).astype(f32)
    first_half = lax.broadcasted_iota(jnp.int32, (n_rows, LANES), 1) < p.margin + p.half

    def row_of(kt):
        return kt * p.lat + kt // p.tiles * STEPS

    def grid(kt, stores):
        def entry(i):
            return obs_tab[i, pl.ds(kt, 1), :]

        match = row_id == entry(0)
        left = jnp.concatenate(
            [jnp.where(match, entry(i), 0.0).astype(jnp.bfloat16) for i in range(3, 9)], axis=0
        )
        right = jnp.concatenate(
            [jnp.where(lane_id == entry(i), 1.0, 0.0).astype(jnp.bfloat16) for i in (1, 2)], axis=0
        )
        full = lax.dot_general(left, right, (((1,), (1,)), ((), ())), preferred_element_type=f32)
        for i, ref in ((0, weight_g), (3, innov)):
            parts = [full[(i + q) * n_rows : (i + q + 1) * n_rows] for q in range(3)]
            summed = parts[0] + (parts[1] + parts[2])
            left, right = summed[:, :LANES], summed[:, LANES:]
            joined = jnp.where(first_half, left, right)
            stores.put(ref, (pl.ds(pl.multiple_of(kt * n_rows, two), n_rows),), joined)
            if i:
                tile = jnp.maximum(kt - low_wide * p.tiles, kt % p.tiles)
                for pair in range(p.lat // 2):
                    rows = slice(two * pair, two * (pair + 1))
                    one, other = spread(left[rows], right[rows], p.vars)
                    at = row_of(tile) + 2 * pair
                    stores.put(source_w, at, one)
                    stores.put(source_w, at + 1, other)

    looped(p.count, 2, grid)

    def derive(got):
        east, north, diff = got
        east = 0.5 * east
        north = 0.5 * north
        return 1.0 - 4.0 * diff, diff - east, diff + east, diff - north, diff + north

    def one_row(at):
        return jnp.broadcast_to(recv_ref[pl.ds(at, 1), :], shape)

    edge_mask = (lower & (lane >= LANES - p.extra)) | (~lower & (lane < p.extra))

    def widen(i, stores):
        kt = i + low_wide * p.tiles
        base = kt * p.rows
        for l in range(p.lat):
            got = []
            for c in range(3):
                main = one_row(base + p.coef_row + c * p.lat + l)
                got.append(jnp.where(edge_mask, one_row(base + l * p.vars + c), main))
            for ref, value in zip((mid_w, east_w, west_w, north_w, south_w), derive(got)):
                stores.put(ref, row_of(i) + l, value)

    looped(p.wide * p.tiles, 1, widen)

    def double(kt, stores):
        base = kt * p.rows + p.coef_row
        for l in range(0, p.lat, 2):
            got = []
            for c in range(3):
                at = base + c * p.lat + l
                got.append(jnp.where(lower, one_row(at), one_row(at + 1)))
            at = rows8(lead + kt * n_rows + l * p.vars)
            for ref, value in zip((mid_c, east_c, west_c, north_c, south_c), derive(got)):
                stores.put(ref, (at,), value)

    looped(p.count, 2, double)

    def wide_step(i, carry):
        k = p.wide - 1 - i // STEPS
        base = k * pitch
        starts = (i % STEPS == 0).astype(f32)
        stores = Stores()

        def terms(l):
            x = carried_w[l * two : (l + 1) * two, :] + starts * source_w[base + l]
            at = base + l
            here = (
                mid_w[at] * x
                + pltpu.roll(east_w[at] * x, 1, 1)
                + pltpu.roll(west_w[at] * x, LANES - 1, 1)
            )
            return here, north_w[at] * x, south_w[at] * x

        below = zero
        here, north, _ = terms(0)
        for l in range(n):
            now, next_north, south = terms(l + 1)
            y = here + below + south
            here, below, north = now, north, next_north
            stores.put(carried_w, (slice(l * two, (l + 1) * two),), y)
            stores.put(result_w, (rows8((k * n + l) * two),), y)
        stores.flush()
        return carry

    def narrow(ref, at):
        mixed = ref[pl.ds(at + p.vars, two), :]
        left = jnp.where(lower, ref[pl.ds(at, two), :], mixed)
        right = jnp.where(lower, mixed, ref[pl.ds(at + two, two), :])
        return jnp.where(in_half, left, right)

    def narrow_results(i, stores):
        stores.put(results, (rows8(low_wide * area + i * two),), narrow(result_w, i * 2 * two))

    def narrow_carried(i, stores):
        value = narrow(carried_w, i * 2 * two) + innov[rows8((low_wide - 1) * area + i * two), :]
        stores.put(carried, (rows8(lead + i * two),), value)

    def begin_adjoint(i, stores):
        stores.put(carried, (rows8(lead + i * two),), innov[rows8(whole + (p.subs - 1) * area + i * two), :])

    def scaled(k, tile, q, at):
        var = recv_ref[pl.ds((k * p.tiles + tile) * p.rows + q * two, two), :]
        return 0.5 * (var * results[at, :])

    def begin_forward(tile, stores):
        for q in range(p.lat // 2):
            at = tile * n_rows + q * two
            stores.put(carried, (rows8(lead + at),), -scaled(0, tile, q, rows8(at)))

    def near(ref, base, at, shift):
        return ref[pl.ds(base + at + lead + shift * p.vars, two), :]

    def adjoint_step(i, phase):
        k = p.subs - 1 - i // STEPS
        base = k * area
        into = phase * whole + base
        ends = (i % STEPS == STEPS - 1) & (k > 0)
        source = jnp.where(ends, into - area, nothing)
        stores = Stores()
        for at in range(0, area, two):
            x = near(carried, 0, at, 0)
            y = (
                near(mid_c, base, at, 0) * x
                + pltpu.roll(near(east_c, base, at, 0) * x, 1, 1)
                + pltpu.roll(near(west_c, base, at, 0) * x, LANES - 1, 1)
                + near(north_c, base, at, -1) * near(carried, 0, at, -1)
                + near(south_c, base, at, 1) * near(carried, 0, at, 1)
            )
            stores.put(results, (rows8(into + at),), y)
            stores.put(carried, (slice(lead + at, lead + at + two),), y + innov[rows8(source + at), :])
        stores.flush()
        return phase

    def forward_step(i, carry):
        k = i // STEPS
        base = k * area
        ends = (i % STEPS == STEPS - 1) & (k < p.subs - 1)
        source = jnp.where(ends, base + area, nothing)
        later = jnp.minimum(k + 1, p.subs - 1)
        stores = Stores()
        for at in range(0, area, two):
            x = near(carried, 0, at, 0)
            y = (
                near(mid_c, base, at, 0) * x
                + near(east_c, base, at, 0) * pltpu.roll(x, LANES - 1, 1)
                + near(west_c, base, at, 0) * pltpu.roll(x, 1, 1)
                + near(north_c, base, at, 0) * near(carried, 0, at, 1)
                + near(south_c, base, at, 0) * near(carried, 0, at, -1)
            )
            here = rows8(base + at)
            stores.put(innov, (rows8(whole + base + at),), weight_g[here, :] * y + innov[here, :])
            force = scaled(later, at // n_rows, at % n_rows // two, rows8(source + at))
            stores.put(carried, (slice(lead + at, lead + at + two),), y - force)
        stores.flush()
        return carry

    def clear_wide(i, stores):
        stores.put(carried_w, (rows8(i * two),), zero)

    def iteration(phase, carry):
        @pl.when(phase == 0)
        def _():
            looped(n, 8, clear_wide)
            lax.fori_loop(0, p.wide * STEPS, wide_step, 0)
            looped(p.wide * n // 2, 12, narrow_results)
            looped(n // 2, 12, narrow_carried)

        @pl.when(phase > 0)
        def _():
            looped(n // 2, 12, begin_adjoint)

        lax.fori_loop(jnp.where(phase == 0, p.wide * STEPS, 0), p.subs * STEPS, adjoint_step, phase)

        @pl.when(phase < ITERS - 1)
        def _():
            looped(p.tiles, 2, begin_forward)
            lax.fori_loop(0, p.subs * STEPS, forward_step, 0)

        return carry

    lax.fori_loop(0, ITERS, iteration, 0)

    own = slice(p.margin, p.margin + p.width)

    def join(kt, stores):
        cols = []
        for v in range(p.vars):
            at = kt * n_rows + v
            early = results[pl.ds(at, p.lat, stride=p.vars), :]
            late = results[pl.ds(whole + at, p.lat, stride=p.vars), :]
            cols.append((0.5 * early + late)[:, own])
        spare = 3 * LANES - p.vars * p.width
        line = jnp.concatenate(cols + [jnp.zeros((p.lat, spare), f32)], axis=1)
        for i in range(3):
            at = (pl.ds(kt * p.lat * 3 + i, p.lat, stride=3),)
            stores.put(out_ref, at, line[:, i * LANES : (i + 1) * LANES])

    looped(p.count, 4, join)


def finish_kernel(plan, recv_ref, var_ref, out_ref):
    p = plan

    def level(z, carry):
        for j in range(p.cols):
            start = (z * p.cols + j) * p.lat * 3
            rows = [recv_ref[pl.ds(start + i, p.lat, stride=3), :] for i in range(3)]
            for v in range(p.vars):
                at, end = v * p.width, (v + 1) * p.width
                col = j * p.width
                while at < end:
                    i, low = divmod(at, LANES)
                    size = min(end - at, LANES - low)
                    cols = slice(col, col + size)
                    scale = -0.5 * var_ref[v, z, :, cols]
                    out_ref[v, z, :, cols] = scale * rows[i][:, low : low + size]
                    at, col = at + size, col + size
        return carry

    lax.fori_loop(0, p.lev, level, 0)


def transposed(
    plan, advect_east, advect_north, diffusion, background_var, obs_cell, obs_value, obs_weight, obs_count
):
    p = plan
    f32 = jnp.float32
    vmem = pl.BlockSpec(memory_space=pltpu.VMEM)
    params = pltpu.CompilerParams(vmem_limit_bytes=VMEM_LIMIT)
    var = background_var[0]
    packed = pl.pallas_call(
        functools.partial(pack_kernel, p),
        out_shape=jax.ShapeDtypeStruct((p.count * p.rows, LANES), f32),
        in_specs=[pl.BlockSpec(memory_space=pltpu.SMEM)] + [vmem] * 7,
        out_specs=vmem,
        scratch_shapes=[pltpu.VMEM(((p.vars + 3) * p.lev, p.lat, 15 * LANES), f32)],
        compiler_params=params,
        name="pack",
    )(
        obs_count.reshape(1, -1),
        obs_cell.reshape(1, -1),
        obs_value.reshape(1, -1),
        obs_weight.reshape(1, -1),
        advect_east[0],
        advect_north[0],
        diffusion[0],
        var,
    )
    received = lax.all_to_all(packed.reshape(-1, 2, LANES), ("tm", "tile"), 0, 0, tiled=True)
    received = received.reshape(-1, LANES)
    wide = pltpu.VMEM((p.wide * p.pitch, 2 * p.vars, LANES), f32)
    narrow = pltpu.VMEM((p.subs * p.area + 4 * p.vars, LANES), f32)
    both = pltpu.VMEM(((ITERS * p.subs + 1) * p.area, LANES), f32)
    back = pl.pallas_call(
        functools.partial(chain_kernel, p),
        out_shape=jax.ShapeDtypeStruct((p.count * p.lat * 3, LANES), f32),
        in_specs=[vmem],
        out_specs=vmem,
        scratch_shapes=[wide] * 6
        + [
            pltpu.VMEM((p.wide * p.nlat * 2 * p.vars, LANES), f32),
            pltpu.VMEM((p.pitch * 2 * p.vars, LANES), f32),
        ]
        + [narrow] * 5
        + [
            pltpu.VMEM((p.subs * p.area, LANES), f32),
            both,
            both,
            pltpu.VMEM((p.area + 4 * p.vars, LANES), f32),
            pltpu.VMEM((9, p.count, p.tiles * p.slots), f32),
        ],
        compiler_params=params,
        name="chains",
    )(received)
    back = back.reshape(-1, 4, LANES)
    returned = lax.all_to_all(back, ("tm", "tile"), 0, 0, tiled=True)
    returned = returned.reshape(-1, LANES)
    increment = pl.pallas_call(
        functools.partial(finish_kernel, p),
        out_shape=jax.ShapeDtypeStruct(var.shape, f32),
        in_specs=[vmem] * 2,
        out_specs=vmem,
        compiler_params=params,
        name="finish",
    )(returned, var)
    return increment[None]


def solution(mesh):
    def run(*args):
        plan = Plan(mesh.shape, args[3].shape, args[4].shape)
        work = functools.partial(transposed, plan) if plan.fits() else per_device
        return jax.shard_map(
            work,
            mesh=mesh,
            in_specs=(
                P("tm", None, "tile", None),
                P("tm", None, "tile", None),
                P("tm", None, "tile", None),
                P("tm", None, None, "tile", None),
                P("tm", "tile", None),
                P("tm", "tile", None),
                P("tm", "tile", None),
                P("tm", "tile", None),
            ),
            out_specs=P("tm", None, None, "tile", None),
            check_vma=False,
        )(*args)

    return run
```

```python
import functools

import jax
import jax.numpy as jnp
from jax import lax
from jax.experimental import pallas as pl
from jax.experimental.pallas import tpu as pltpu
from jax.sharding import PartitionSpec as P

STEPS = 2
ITERS = 2
CHAINS = 3
LANES = 128
VMEM_LIMIT = 48 * 1024 * 1024


def padded(block, sides, width):
    for axis, dim in sides:
        count = lax.axis_size(axis)
        forward = [(i, i + 1) for i in range(count - 1)]
        backward = [(target, source) for source, target in forward]
        low = lax.ppermute(
            lax.slice_in_dim(block, block.shape[dim] - width, None, axis=dim), axis, forward
        )
        high = lax.ppermute(lax.slice_in_dim(block, 0, width, axis=dim), axis, backward)
        block = jnp.concatenate([low, block, high], axis=dim)
    return block


def shifted(value, axis, steps):
    count = lax.axis_size(axis)
    first, last = (max(0, -steps), min(count, count - steps))
    return lax.ppermute(value, axis, [(source, source + steps) for source in range(first, last)])


def apply_step(field, coef, adjoint):
    east_c = coef[0]
    north_c = coef[1]
    diff_c = coef[2]
    if adjoint:
        to_east = (diff_c - 0.5 * east_c) * field
        to_west = (diff_c + 0.5 * east_c) * field
        to_north = (diff_c - 0.5 * north_c) * field
        to_south = (diff_c + 0.5 * north_c) * field
        middle = (1.0 - 4.0 * diff_c[:, 1:-1]) * field[:, :, 1:-1]
        return (
            middle
            + jnp.roll(to_east[:, :, 1:-1], 1, axis=-1)
            + jnp.roll(to_west[:, :, 1:-1], -1, axis=-1)
            + to_north[:, :, :-2]
            + to_south[:, :, 2:]
        )
    inner = field[:, :, 1:-1]
    diff_in = diff_c[:, 1:-1]
    east_in = east_c[:, 1:-1]
    north_in = north_c[:, 1:-1]
    return (
        (1.0 - 4.0 * diff_in) * inner
        + (diff_in - 0.5 * east_in) * jnp.roll(inner, -1, axis=-1)
        + (diff_in + 0.5 * east_in) * jnp.roll(inner, 1, axis=-1)
        + (diff_in - 0.5 * north_in) * field[:, :, 2:]
        + (diff_in + 0.5 * north_in) * field[:, :, :-2]
    )


def advance(field, coef, adjoint):
    for repeat in range(STEPS):
        extended = padded(field, (("tile", 2),), 1)
        field = apply_step(extended, coef, adjoint)
    return field


def per_device(
    advect_east, advect_north, diffusion, background_var, obs_cell, obs_value, obs_weight, obs_count
):
    windows_count = lax.axis_size("tm")
    tiles = lax.axis_size("tile")
    coefs = jnp.stack([advect_east[0], advect_north[0], diffusion[0]])
    coef_ext = padded(coefs, (("tile", 2),), 1)
    cells = obs_cell.reshape(tiles, -1)
    slot_count = cells.shape[1]
    live = jnp.arange(slot_count, dtype=jnp.int32)[None, :] < obs_count.reshape(tiles)[:, None]
    masked = obs_weight.reshape(tiles, -1) * live.astype(jnp.float32)
    received = lax.all_to_all(
        jnp.stack([obs_value.reshape(tiles, -1), masked]),
        "tile",
        split_axis=1,
        concat_axis=1,
        tiled=True,
    )
    received_cells = lax.all_to_all(cells, "tile", split_axis=0, concat_axis=0, tiled=True)
    departures = received[0].reshape(-1)
    obs_weights = received[1].reshape(-1)
    flat_cells = received_cells.reshape(-1)
    local_var = background_var[0]
    state_shape = local_var.shape
    cell_total = state_shape[0] * state_shape[1] * state_shape[2] * state_shape[3]
    increment = jnp.zeros(state_shape, jnp.float32)
    for iteration in range(ITERS):
        if iteration == 0:
            innov = obs_weights * (0.0 - departures)
        else:
            forward_carried = advance(increment, coef_ext, False)
            for forward_window in range(windows_count - 1):
                forward_incoming = shifted(forward_carried, "tm", 1)
                forward_carried = advance(forward_incoming + increment, coef_ext, False)
            innov = obs_weights * (
                jnp.take(forward_carried.reshape(cell_total), flat_cells, axis=0) - departures
            )
        gridded = jnp.zeros((cell_total,), jnp.float32).at[flat_cells].add(innov)
        source = gridded.reshape(state_shape)
        carried = advance(source, coef_ext, True)
        for window in range(windows_count - 1):
            incoming = shifted(carried, "tm", -1)
            carried = advance(incoming + source, coef_ext, True)
        increment = increment - 0.5 * (increment + local_var * carried)
    return increment[None]


class Plan:
    def __init__(self, mesh_shape, var_shape, slot_shape):
        self.subs, self.tiles = mesh_shape["tm"], mesh_shape["tile"]
        self.count = self.subs * self.tiles
        _, self.vars, self.lev, self.nlat, self.lon = var_shape
        self.lat = self.nlat // self.tiles
        self.slots = slot_shape[2] // self.tiles
        self.cols = self.count // self.lev
        self.width = self.lon // self.cols
        self.half = self.width // 2
        self.halo = CHAINS * STEPS * self.subs
        self.margin = (LANES - self.width) // 2
        self.extra = self.halo - self.margin
        self.span = self.width + 2 * self.halo
        self.coef_row = self.lat * self.vars
        self.obs_row = self.coef_row + 3 * self.lat
        self.rows = self.obs_row + 6
        self.pitch = self.nlat + STEPS
        self.wide = -(-self.extra // STEPS)
        self.area = self.nlat * self.vars

    def borrows(self, k):
        return (CHAINS - 1) * STEPS * self.subs + STEPS * (k + 1) > self.margin

    def fits(self):
        if self.count % self.lev or self.lon % self.cols or self.width % 2:
            return False
        for k in range(self.subs):
            spare = self.margin - STEPS * (2 * self.subs - k)
            if spare < 0 or (self.borrows(k) and spare < self.extra):
                return False
        return (
            self.half + 2 * self.halo <= LANES
            and 0 <= self.extra
            and self.vars == 4
            and self.lat % 2 == 0
            and 0 < self.wide < self.subs
            and self.tiles == 8
            and self.slots & (self.slots - 1) == 0
            and self.slots * self.tiles == 2 * LANES
            and self.width + 2 * self.margin == LANES
            and self.width * self.vars <= 3 * LANES
            and self.count * self.rows % 8 == 0
            and self.rows % 2 == 0
        )


def pack_kernel(
    plan, count_ref, cell_ref, value_ref, weight_ref, east_ref, north_ref, diff_ref, var_ref, out_ref, wide
):
    p = plan
    pad = 2 * LANES
    right = wide.shape[-1] - pad - p.lon
    per_level = p.vars + 3

    def fill(z, carry):
        for v in range(per_level):
            field = var_ref[v, z] if v < p.vars else (east_ref, north_ref, diff_ref)[v - p.vars][z]
            at = z * per_level + v
            wide[at, :, pad : pad + p.lon] = field
            wide[at, :, :pad] = field[:, p.lon - pad :]
            wide[at, :, pad + p.lon :] = field[:, :right]
        return carry

    lax.fori_loop(0, p.lev, fill, 0)

    lane = lax.broadcasted_iota(jnp.int32, (1, p.tiles * p.slots), 1)
    filled = jnp.zeros_like(lane)
    for t in range(p.tiles):
        filled = jnp.where(lane >= t * p.slots, count_ref[0, t], filled)
    weight = jnp.where((lane & (p.slots - 1)) < filled, weight_ref[...], 0.0)
    obs = []
    for x in (weight, weight * value_ref[...], cell_ref[...].astype(jnp.float32)):
        obs += [x[:, :LANES], x[:, LANES:]]
    obs = jnp.concatenate(obs, axis=0)
    lanes = lax.broadcasted_iota(jnp.int32, (p.lat, LANES), 1)
    borrows = jnp.where(p.borrows(lax.axis_index("tm")), p.extra, 0)

    def blocks(z, carry):
        for j in range(p.cols):
            first = pad + j * p.width - p.margin
            tile, low = divmod(first, LANES)

            def moved(a, t):
                x = wide[z * per_level + a, :, t * LANES : (t + 1) * LANES]
                return pltpu.roll(x, LANES - low, 1)

            base = (z * p.cols + j) * p.rows
            for v in range(p.vars):
                piece = jnp.where(lanes < LANES - low, moved(v, tile), moved(v, tile + 1))
                if v < 3:
                    here, after = moved(p.vars + v, tile), moved(p.vars + v, tile + 1)
                    rows = pl.ds(base + p.coef_row + v * p.lat, p.lat)
                    out_ref[rows, :] = jnp.where(lanes < LANES - low, here, after)
                    if low < p.extra:
                        here = jnp.where(lanes < LANES - low, moved(p.vars + v, tile - 1), here)
                    if low + p.extra > LANES:
                        after = jnp.where(lanes < LANES - low, after, moved(p.vars + v, tile + 2))
                    piece = jnp.where(lanes < borrows, after, piece)
                    piece = jnp.where(lanes >= LANES - borrows, here, piece)
                out_ref[pl.ds(base + v, p.lat, stride=p.vars), :] = piece
            out_ref[pl.ds(base + p.obs_row, 6), :] = obs
        return carry

    lax.fori_loop(0, p.lev, blocks, 0)


class Stores:
    def __init__(self):
        self.held = []

    def put(self, ref, at, value):
        self.held.append((ref, at, value))

    def flush(self):
        for ref, at, value in self.held:
            ref[at] = value
        self.held = []


def looped(count, unroll, body):
    def many(i, carry):
        stores = Stores()
        for u in range(unroll):
            body(i * unroll + u, stores)
        stores.flush()
        return carry

    lax.fori_loop(0, count // unroll, many, 0)


def swap_blocks(x, slots):
    size = x.shape[0]
    sub = lax.broadcasted_iota(jnp.int32, x.shape, 0)
    block = lax.broadcasted_iota(jnp.int32, x.shape, 1) >> (slots.bit_length() - 1)
    out = x
    for d in range(1, size):
        moved = pltpu.roll(pltpu.roll(x, size - d, 0), d * slots, 1)
        out = jnp.where(block == ((sub + d) & (size - 1)), moved, out)
    return out


def spread(a, b, count):
    return (
        jnp.concatenate([a[:count], b[:count]], axis=0),
        jnp.concatenate([a[count:], b[count:]], axis=0),
    )


def chain_kernel(
    plan,
    recv_ref,
    out_ref,
    mid_w,
    east_w,
    west_w,
    north_w,
    south_w,
    source_w,
    result_w,
    carried_w,
    mid_c,
    east_c,
    west_c,
    north_c,
    south_c,
    weight_g,
    innov,
    results,
    carried,
    obs_tab,
):
    p = plan
    f32 = jnp.float32
    me = lax.axis_index("tm") * p.tiles + lax.axis_index("tile")
    level = (me // p.cols).astype(f32)
    origin = ((me % p.cols) * p.width - p.halo).astype(f32)
    two = 2 * p.vars
    shape = (two, LANES)
    sub = lax.broadcasted_iota(jnp.int32, shape, 0)
    lane = lax.broadcasted_iota(jnp.int32, shape, 1)
    lower = sub < p.vars
    in_half = lane < p.margin + p.half
    n = p.nlat
    pitch = p.pitch
    area = p.area
    whole = p.subs * area
    nothing = ITERS * whole
    lead = two
    low_wide = p.subs - p.wide
    zero = jnp.zeros(shape, f32)

    def rows8(start):
        return pl.ds(pl.multiple_of(start, two), two)

    def clear(ref, start, count):
        def body(i, carry):
            for u in range(8):
                ref[rows8(start + (i * 8 + u) * two), :] = zero
            return carry

        lax.fori_loop(0, count // (8 * two), body, 0)

    clear(innov, nothing, area)
    clear(results, nothing, area)
    for ref in (mid_c, east_c, west_c, north_c, south_c, carried):
        ref[:lead, :] = zero
        ref[ref.shape[0] - lead :, :] = zero
    for k in range(p.wide):
        for l in range(n, pitch):
            for ref in (mid_w, east_w, west_w, north_w, south_w, source_w):
                ref[k * pitch + l] = zero
    for l in range(n, pitch):
        carried_w[l * two : (l + 1) * two, :] = zero

    def observe(k, stores):
        raw = []
        for i in range(6):
            raw.append(recv_ref[pl.ds(k * p.tiles * p.rows + p.obs_row + i, p.tiles, stride=p.rows), :])
        w, wy, cell = (jnp.concatenate(raw[2 * i : 2 * i + 2], axis=1) for i in range(3))
        w, wy, cell = (swap_blocks(x, p.slots) for x in (w, wy, cell))
        row = jnp.floor((cell + 0.5) * (1.0 / p.lon))
        lon = cell - row * p.lon
        group = jnp.floor((row + 0.5) * (1.0 / p.lat))
        lat = row - group * p.lat
        var = jnp.floor((group + 0.5) * (1.0 / p.lev))
        lev = group - var * p.lev
        at = lon - origin
        at = jnp.where(at < 0, at + p.lon, at)
        at = jnp.where(at >= p.lon, at - p.lon, at)
        place = at - p.extra
        place = jnp.where(place < 0, place + LANES, place)
        place = jnp.where(place >= LANES, place - LANES, place)
        here = lev == level
        in_a = here & (at < p.half + 2 * p.halo)
        in_b = here & (at >= p.half) & (at < p.span)
        rows = pl.ds(k * p.tiles, p.tiles)
        stores.put(obs_tab, (0, rows), lat * p.vars + var)
        stores.put(obs_tab, (1, rows), jnp.where(in_a, place, -1.0))
        stores.put(obs_tab, (2, rows), jnp.where(in_b, place, -1.0))
        for i, x in ((3, w), (6, -wy)):
            one = x.astype(jnp.bfloat16).astype(f32)
            two = (x - one).astype(jnp.bfloat16).astype(f32)
            stores.put(obs_tab, (i, rows), one)
            stores.put(obs_tab, (i + 1, rows), two)
            stores.put(obs_tab, (i + 2, rows), x - one - two)

    looped(p.subs, 1, observe)

    n_rows = p.lat * p.vars
    slots = p.tiles * p.slots
    row_id = lax.broadcasted_iota(jnp.int32, (n_rows, slots), 0).astype(f32)
    lane_id = lax.broadcasted_iota(jnp.int32, (LANES, slots), 0).astype(f32)
    first_half = lax.broadcasted_iota(jnp.int32, (n_rows, LANES), 1) < p.margin + p.half

    def wide_tile(kt):
        return jnp.maximum(kt - low_wide * p.tiles, kt % p.tiles)

    def row_of(kt):
        return kt * p.lat + kt // p.tiles * STEPS

    def grid(kt, stores):
        def entry(i):
            return obs_tab[i, pl.ds(kt, 1), :]

        match = row_id == entry(0)
        left = jnp.concatenate(
            [jnp.where(match, entry(i), 0.0).astype(jnp.bfloat16) for i in range(3, 9)], axis=0
        )
        right = jnp.concatenate(
            [jnp.where(lane_id == entry(i), 1.0, 0.0).astype(jnp.bfloat16) for i in (1, 2)], axis=0
        )
        full = lax.dot_general(left, right, (((1,), (1,)), ((), ())), preferred_element_type=f32)
        for i, ref in ((0, weight_g), (3, innov)):
            parts = [full[(i + q) * n_rows : (i + q + 1) * n_rows] for q in range(3)]
            summed = parts[0] + (parts[1] + parts[2])
            left, right = summed[:, :LANES], summed[:, LANES:]
            joined = jnp.where(first_half, left, right)
            stores.put(ref, (pl.ds(pl.multiple_of(kt * n_rows, two), n_rows),), joined)
            if i:
                tile = wide_tile(kt)
                for pair in range(p.lat // 2):
                    rows = slice(two * pair, two * (pair + 1))
                    one, other = spread(left[rows], right[rows], p.vars)
                    at = row_of(tile) + 2 * pair
                    stores.put(source_w, at, one)
                    stores.put(source_w, at + 1, other)

    def derive(got):
        east, north, diff = got
        east = 0.5 * east
        north = 0.5 * north
        return 1.0 - 4.0 * diff, diff - east, diff + east, diff - north, diff + north

    def one_row(at):
        return jnp.broadcast_to(recv_ref[pl.ds(at, 1), :], shape)

    edge_mask = (lower & (lane >= LANES - p.extra)) | (~lower & (lane < p.extra))

    def widen(kt, stores):
        base = kt * p.rows
        for l in range(p.lat):
            got = []
            for c in range(3):
                main = one_row(base + p.coef_row + c * p.lat + l)
                got.append(jnp.where(edge_mask, one_row(base + l * p.vars + c), main))
            for ref, value in zip((mid_w, east_w, west_w, north_w, south_w), derive(got)):
                stores.put(ref, row_of(wide_tile(kt)) + l, value)

    def double(kt, stores):
        base = kt * p.rows + p.coef_row
        for l in range(0, p.lat, 2):
            got = []
            for c in range(3):
                at = base + c * p.lat + l
                got.append(jnp.where(lower, one_row(at), one_row(at + 1)))
            at = rows8(lead + kt * n_rows + l * p.vars)
            for ref, value in zip((mid_c, east_c, west_c, north_c, south_c), derive(got)):
                stores.put(ref, (at,), value)

    def prepare(kt, stores):
        grid(kt, stores)
        double(kt, stores)
        widen(kt, stores)

    looped(p.count, 2, prepare)

    def wide_step(i, carry):
        k = p.wide - 1 - i // STEPS
        base = k * pitch
        starts = (i % STEPS == 0).astype(f32)
        stores = Stores()

        def terms(l):
            x = carried_w[l * two : (l + 1) * two, :] + starts * source_w[base + l]
            at = base + l
            here = (
                mid_w[at] * x
                + pltpu.roll(east_w[at] * x, 1, 1)
                + pltpu.roll(west_w[at] * x, LANES - 1, 1)
            )
            return here, north_w[at] * x, south_w[at] * x

        below = zero
        here, north, _ = terms(0)
        for l in range(n):
            now, next_north, south = terms(l + 1)
            y = here + below + south
            here, below, north = now, north, next_north
            stores.put(carried_w, (slice(l * two, (l + 1) * two),), y)
            stores.put(result_w, (rows8((k * n + l) * two),), y)
        stores.flush()
        return carry

    def narrow(ref, at):
        mixed = ref[pl.ds(at + p.vars, two), :]
        left = jnp.where(lower, ref[pl.ds(at, two), :], mixed)
        right = jnp.where(lower, mixed, ref[pl.ds(at + two, two), :])
        return jnp.where(in_half, left, right)

    def narrow_results(i, stores):
        stores.put(results, (rows8(low_wide * area + i * two),), narrow(result_w, i * 2 * two))

    def narrow_carried(i, stores):
        value = narrow(carried_w, i * 2 * two) + innov[rows8((low_wide - 1) * area + i * two), :]
        stores.put(carried, (rows8(lead + i * two),), value)

    def begin_adjoint(i, stores):
        stores.put(carried, (rows8(lead + i * two),), innov[rows8(whole + (p.subs - 1) * area + i * two), :])

    def scaled(k, tile, q, at):
        var = recv_ref[pl.ds((k * p.tiles + tile) * p.rows + q * two, two), :]
        return 0.5 * (var * results[at, :])

    def begin_forward(tile, stores):
        for q in range(p.lat // 2):
            at = tile * n_rows + q * two
            stores.put(carried, (rows8(lead + at),), -scaled(0, tile, q, rows8(at)))

    def near(ref, base, at, shift):
        return ref[pl.ds(base + at + lead + shift * p.vars, two), :]

    def adjoint_step(i, phase):
        k = p.subs - 1 - i // STEPS
        base = k * area
        into = phase * whole + base
        ends = (i % STEPS == STEPS - 1) & (k > 0)
        source = jnp.where(ends, into - area, nothing)
        stores = Stores()
        for at in range(0, area, two):
            x = near(carried, 0, at, 0)
            y = (
                near(mid_c, base, at, 0) * x
                + pltpu.roll(near(east_c, base, at, 0) * x, 1, 1)
                + pltpu.roll(near(west_c, base, at, 0) * x, LANES - 1, 1)
                + near(north_c, base, at, -1) * near(carried, 0, at, -1)
                + near(south_c, base, at, 1) * near(carried, 0, at, 1)
            )
            stores.put(results, (rows8(into + at),), y)
            stores.put(carried, (slice(lead + at, lead + at + two),), y + innov[rows8(source + at), :])
        stores.flush()
        return phase

    def forward_step(i, carry):
        k = i // STEPS
        base = k * area
        ends = (i % STEPS == STEPS - 1) & (k < p.subs - 1)
        source = jnp.where(ends, base + area, nothing)
        later = jnp.minimum(k + 1, p.subs - 1)
        stores = Stores()
        for at in range(0, area, two):
            x = near(carried, 0, at, 0)
            y = (
                near(mid_c, base, at, 0) * x
                + near(east_c, base, at, 0) * pltpu.roll(x, LANES - 1, 1)
                + near(west_c, base, at, 0) * pltpu.roll(x, 1, 1)
                + near(north_c, base, at, 0) * near(carried, 0, at, 1)
                + near(south_c, base, at, 0) * near(carried, 0, at, -1)
            )
            here = rows8(base + at)
            stores.put(innov, (rows8(whole + base + at),), weight_g[here, :] * y + innov[here, :])
            force = scaled(later, at // n_rows, at % n_rows // two, rows8(source + at))
            stores.put(carried, (slice(lead + at, lead + at + two),), y - force)
        stores.flush()
        return carry

    def clear_wide(i, stores):
        stores.put(carried_w, (rows8(i * two),), zero)

    def iteration(phase, carry):
        @pl.when(phase == 0)
        def _():
            looped(n, 8, clear_wide)
            lax.fori_loop(0, p.wide * STEPS, wide_step, 0)
            looped(p.wide * n // 2, 12, narrow_results)
            looped(n // 2, 12, narrow_carried)

        @pl.when(phase > 0)
        def _():
            looped(n // 2, 12, begin_adjoint)

        lax.fori_loop(jnp.where(phase == 0, p.wide * STEPS, 0), p.subs * STEPS, adjoint_step, phase)

        @pl.when(phase < ITERS - 1)
        def _():
            looped(p.tiles, 2, begin_forward)
            lax.fori_loop(0, p.subs * STEPS, forward_step, 0)

        return carry

    lax.fori_loop(0, ITERS, iteration, 0)

    own = slice(p.margin, p.margin + p.width)

    def join(kt, stores):
        cols = []
        for v in range(p.vars):
            at = kt * n_rows + v
            early = results[pl.ds(at, p.lat, stride=p.vars), :]
            late = results[pl.ds(whole + at, p.lat, stride=p.vars), :]
            cols.append((0.5 * early + late)[:, own])
        spare = 3 * LANES - p.vars * p.width
        line = jnp.concatenate(cols + [jnp.zeros((p.lat, spare), f32)], axis=1)
        for i in range(3):
            at = (pl.ds(kt * p.lat * 3 + i, p.lat, stride=3),)
            stores.put(out_ref, at, line[:, i * LANES : (i + 1) * LANES])

    looped(p.count, 4, join)


def finish_kernel(plan, recv_ref, var_ref, out_ref):
    p = plan

    def level(z, carry):
        for j in range(p.cols):
            start = (z * p.cols + j) * p.lat * 3
            rows = [recv_ref[pl.ds(start + i, p.lat, stride=3), :] for i in range(3)]
            for v in range(p.vars):
                at, end = v * p.width, (v + 1) * p.width
                col = j * p.width
                while at < end:
                    i, low = divmod(at, LANES)
                    size = min(end - at, LANES - low)
                    cols = slice(col, col + size)
                    scale = -0.5 * var_ref[v, z, :, cols]
                    out_ref[v, z, :, cols] = scale * rows[i][:, low : low + size]
                    at, col = at + size, col + size
        return carry

    lax.fori_loop(0, p.lev, level, 0)


def transposed(
    plan, advect_east, advect_north, diffusion, background_var, obs_cell, obs_value, obs_weight, obs_count
):
    p = plan
    f32 = jnp.float32
    vmem = pl.BlockSpec(memory_space=pltpu.VMEM)
    params = pltpu.CompilerParams(vmem_limit_bytes=VMEM_LIMIT)
    var = background_var[0]
    packed = pl.pallas_call(
        functools.partial(pack_kernel, p),
        out_shape=jax.ShapeDtypeStruct((p.count * p.rows, LANES), f32),
        in_specs=[pl.BlockSpec(memory_space=pltpu.SMEM)] + [vmem] * 7,
        out_specs=vmem,
        scratch_shapes=[pltpu.VMEM(((p.vars + 3) * p.lev, p.lat, 15 * LANES), f32)],
        compiler_params=params,
        name="pack",
    )(
        obs_count.reshape(1, -1),
        obs_cell.reshape(1, -1),
        obs_value.reshape(1, -1),
        obs_weight.reshape(1, -1),
        advect_east[0],
        advect_north[0],
        diffusion[0],
        var,
    )
    received = lax.all_to_all(packed.reshape(-1, 2, LANES), ("tm", "tile"), 0, 0, tiled=True)
    received = received.reshape(-1, LANES)
    wide = pltpu.VMEM((p.wide * p.pitch, 2 * p.vars, LANES), f32)
    narrow = pltpu.VMEM((p.subs * p.area + 4 * p.vars, LANES), f32)
    both = pltpu.VMEM(((ITERS * p.subs + 1) * p.area, LANES), f32)
    back = pl.pallas_call(
        functools.partial(chain_kernel, p),
        out_shape=jax.ShapeDtypeStruct((p.count * p.lat * 3, LANES), f32),
        in_specs=[vmem],
        out_specs=vmem,
        scratch_shapes=[wide] * 6
        + [
            pltpu.VMEM((p.wide * p.nlat * 2 * p.vars, LANES), f32),
            pltpu.VMEM((p.pitch * 2 * p.vars, LANES), f32),
        ]
        + [narrow] * 5
        + [
            pltpu.VMEM((p.subs * p.area, LANES), f32),
            both,
            both,
            pltpu.VMEM((p.area + 4 * p.vars, LANES), f32),
            pltpu.VMEM((9, p.count, p.tiles * p.slots), f32),
        ],
        compiler_params=params,
        name="chains",
    )(received)
    back = back.reshape(-1, 4, LANES)
    returned = lax.all_to_all(back, ("tm", "tile"), 0, 0, tiled=True)
    returned = returned.reshape(-1, LANES)
    increment = pl.pallas_call(
        functools.partial(finish_kernel, p),
        out_shape=jax.ShapeDtypeStruct(var.shape, f32),
        in_specs=[vmem] * 2,
        out_specs=vmem,
        compiler_params=params,
        name="finish",
    )(returned, var)
    return increment[None]


def solution(mesh):
    def run(*args):
        plan = Plan(mesh.shape, args[3].shape, args[4].shape)
        work = functools.partial(transposed, plan) if plan.fits() else per_device
        return jax.shard_map(
            work,
            mesh=mesh,
            in_specs=(
                P("tm", None, "tile", None),
                P("tm", None, "tile", None),
                P("tm", None, "tile", None),
                P("tm", None, None, "tile", None),
                P("tm", "tile", None),
                P("tm", "tile", None),
                P("tm", "tile", None),
                P("tm", "tile", None),
            ),
            out_specs=P("tm", None, None, "tile", None),
            check_vma=False,
        )(*args)

    return run
```

```python
import functools

import jax
import jax.numpy as jnp
from jax import lax
from jax.experimental import pallas as pl
from jax.experimental.pallas import tpu as pltpu
from jax.sharding import PartitionSpec as P

STEPS = 2
ITERS = 2
CHAINS = 3
LANES = 128
VMEM_LIMIT = 48 * 1024 * 1024


def padded(block, sides, width):
    for axis, dim in sides:
        count = lax.axis_size(axis)
        forward = [(i, i + 1) for i in range(count - 1)]
        backward = [(target, source) for source, target in forward]
        low = lax.ppermute(
            lax.slice_in_dim(block, block.shape[dim] - width, None, axis=dim), axis, forward
        )
        high = lax.ppermute(lax.slice_in_dim(block, 0, width, axis=dim), axis, backward)
        block = jnp.concatenate([low, block, high], axis=dim)
    return block


def shifted(value, axis, steps):
    count = lax.axis_size(axis)
    first, last = (max(0, -steps), min(count, count - steps))
    return lax.ppermute(value, axis, [(source, source + steps) for source in range(first, last)])


def apply_step(field, coef, adjoint):
    east_c = coef[0]
    north_c = coef[1]
    diff_c = coef[2]
    if adjoint:
        to_east = (diff_c - 0.5 * east_c) * field
        to_west = (diff_c + 0.5 * east_c) * field
        to_north = (diff_c - 0.5 * north_c) * field
        to_south = (diff_c + 0.5 * north_c) * field
        middle = (1.0 - 4.0 * diff_c[:, 1:-1]) * field[:, :, 1:-1]
        return (
            middle
            + jnp.roll(to_east[:, :, 1:-1], 1, axis=-1)
            + jnp.roll(to_west[:, :, 1:-1], -1, axis=-1)
            + to_north[:, :, :-2]
            + to_south[:, :, 2:]
        )
    inner = field[:, :, 1:-1]
    diff_in = diff_c[:, 1:-1]
    east_in = east_c[:, 1:-1]
    north_in = north_c[:, 1:-1]
    return (
        (1.0 - 4.0 * diff_in) * inner
        + (diff_in - 0.5 * east_in) * jnp.roll(inner, -1, axis=-1)
        + (diff_in + 0.5 * east_in) * jnp.roll(inner, 1, axis=-1)
        + (diff_in - 0.5 * north_in) * field[:, :, 2:]
        + (diff_in + 0.5 * north_in) * field[:, :, :-2]
    )


def advance(field, coef, adjoint):
    for repeat in range(STEPS):
        extended = padded(field, (("tile", 2),), 1)
        field = apply_step(extended, coef, adjoint)
    return field


def per_device(
    advect_east, advect_north, diffusion, background_var, obs_cell, obs_value, obs_weight, obs_count
):
    windows_count = lax.axis_size("tm")
    tiles = lax.axis_size("tile")
    coefs = jnp.stack([advect_east[0], advect_north[0], diffusion[0]])
    coef_ext = padded(coefs, (("tile", 2),), 1)
    cells = obs_cell.reshape(tiles, -1)
    slot_count = cells.shape[1]
    live = jnp.arange(slot_count, dtype=jnp.int32)[None, :] < obs_count.reshape(tiles)[:, None]
    masked = obs_weight.reshape(tiles, -1) * live.astype(jnp.float32)
    received = lax.all_to_all(
        jnp.stack([obs_value.reshape(tiles, -1), masked]),
        "tile",
        split_axis=1,
        concat_axis=1,
        tiled=True,
    )
    received_cells = lax.all_to_all(cells, "tile", split_axis=0, concat_axis=0, tiled=True)
    departures = received[0].reshape(-1)
    obs_weights = received[1].reshape(-1)
    flat_cells = received_cells.reshape(-1)
    local_var = background_var[0]
    state_shape = local_var.shape
    cell_total = state_shape[0] * state_shape[1] * state_shape[2] * state_shape[3]
    increment = jnp.zeros(state_shape, jnp.float32)
    for iteration in range(ITERS):
        if iteration == 0:
            innov = obs_weights * (0.0 - departures)
        else:
            forward_carried = advance(increment, coef_ext, False)
            for forward_window in range(windows_count - 1):
                forward_incoming = shifted(forward_carried, "tm", 1)
                forward_carried = advance(forward_incoming + increment, coef_ext, False)
            innov = obs_weights * (
                jnp.take(forward_carried.reshape(cell_total), flat_cells, axis=0) - departures
            )
        gridded = jnp.zeros((cell_total,), jnp.float32).at[flat_cells].add(innov)
        source = gridded.reshape(state_shape)
        carried = advance(source, coef_ext, True)
        for window in range(windows_count - 1):
            incoming = shifted(carried, "tm", -1)
            carried = advance(incoming + source, coef_ext, True)
        increment = increment - 0.5 * (increment + local_var * carried)
    return increment[None]


class Plan:
    def __init__(self, mesh_shape, var_shape, slot_shape):
        self.subs, self.tiles = mesh_shape["tm"], mesh_shape["tile"]
        self.count = self.subs * self.tiles
        _, self.vars, self.lev, self.nlat, self.lon = var_shape
        self.lat = self.nlat // self.tiles
        self.slots = slot_shape[2] // self.tiles
        self.cols = self.count // self.lev
        self.width = self.lon // self.cols
        self.half = self.width // 2
        self.halo = CHAINS * STEPS * self.subs
        self.margin = (LANES - self.width) // 2
        self.extra = self.halo - self.margin
        self.span = self.width + 2 * self.halo
        self.coef_row = self.lat * self.vars
        self.obs_row = self.coef_row + 3 * self.lat
        self.rows = self.obs_row + 6
        self.pitch = self.nlat + STEPS
        self.wide = -(-self.extra // STEPS)
        self.area = self.nlat * self.vars

    def borrows(self, k):
        return (CHAINS - 1) * STEPS * self.subs + STEPS * (k + 1) > self.margin

    def fits(self):
        if self.count % self.lev or self.lon % self.cols or self.width % 2:
            return False
        for k in range(self.subs):
            spare = self.margin - STEPS * (2 * self.subs - k)
            if spare < 0 or (self.borrows(k) and spare < self.extra):
                return False
        return (
            self.half + 2 * self.halo <= LANES
            and 0 <= self.extra <= 16
            and self.vars == 4
            and self.lat % 2 == 0
            and 0 < self.wide < self.subs
            and self.tiles == 8
            and self.slots & (self.slots - 1) == 0
            and self.slots * self.tiles == 2 * LANES
            and self.width + 2 * self.margin == LANES
            and self.width * self.vars <= 3 * LANES
            and self.count * self.rows % 8 == 0
            and self.rows % 2 == 0
        )


def pack_kernel(
    plan, count_ref, cell_ref, value_ref, weight_ref, east_ref, north_ref, diff_ref, var_ref, out_ref, wide
):
    p = plan
    pad = 2 * LANES
    right = wide.shape[-1] - pad - p.lon
    per_level = p.vars + 3

    def fill(z, carry):
        for v in range(per_level):
            field = var_ref[v, z] if v < p.vars else (east_ref, north_ref, diff_ref)[v - p.vars][z]
            at = z * per_level + v
            wide[at, :, pad : pad + p.lon] = field
            wide[at, :, :pad] = field[:, p.lon - pad :]
            wide[at, :, pad + p.lon :] = field[:, :right]
        return carry

    lax.fori_loop(0, p.lev, fill, 0)

    lane = lax.broadcasted_iota(jnp.int32, (1, p.tiles * p.slots), 1)
    filled = jnp.zeros_like(lane)
    for t in range(p.tiles):
        filled = jnp.where(lane >= t * p.slots, count_ref[0, t], filled)
    weight = jnp.where((lane & (p.slots - 1)) < filled, weight_ref[...], 0.0)
    obs = []
    for x in (weight, weight * value_ref[...], cell_ref[...].astype(jnp.float32)):
        obs += [x[:, :LANES], x[:, LANES:]]
    obs = jnp.concatenate(obs, axis=0)
    lanes = lax.broadcasted_iota(jnp.int32, (p.lat, LANES), 1)
    borrows = jnp.where(p.borrows(lax.axis_index("tm")), p.extra, 0)

    def blocks(z, carry):
        for j in range(p.cols):
            first = pad + j * p.width - p.margin
            tile, low = divmod(first, LANES)

            def moved(a, t):
                x = wide[z * per_level + a, :, t * LANES : (t + 1) * LANES]
                return pltpu.roll(x, LANES - low, 1)

            base = (z * p.cols + j) * p.rows
            for v in range(p.vars):
                piece = jnp.where(lanes < LANES - low, moved(v, tile), moved(v, tile + 1))
                if v < 3:
                    here, after = moved(p.vars + v, tile), moved(p.vars + v, tile + 1)
                    rows = pl.ds(base + p.coef_row + v * p.lat, p.lat)
                    out_ref[rows, :] = jnp.where(lanes < LANES - low, here, after)
                    if low < p.extra:
                        here = jnp.where(lanes < LANES - low, moved(p.vars + v, tile - 1), here)
                    if low + p.extra > LANES:
                        after = jnp.where(lanes < LANES - low, after, moved(p.vars + v, tile + 2))
                    piece = jnp.where(lanes < borrows, after, piece)
                    piece = jnp.where(lanes >= LANES - borrows, here, piece)
                out_ref[pl.ds(base + v, p.lat, stride=p.vars), :] = piece
            out_ref[pl.ds(base + p.obs_row, 6), :] = obs
        return carry

    lax.fori_loop(0, p.lev, blocks, 0)


class Stores:
    def __init__(self):
        self.held = []

    def put(self, ref, at, value):
        self.held.append((ref, at, value))

    def flush(self):
        for ref, at, value in self.held:
            ref[at] = value
        self.held = []


def looped(count, unroll, body):
    def many(i, carry):
        stores = Stores()
        for u in range(unroll):
            body(i * unroll + u, stores)
        stores.flush()
        return carry

    lax.fori_loop(0, count // unroll, many, 0)


def swap_blocks(x, slots):
    size = x.shape[0]
    sub = lax.broadcasted_iota(jnp.int32, x.shape, 0)
    block = lax.broadcasted_iota(jnp.int32, x.shape, 1) >> (slots.bit_length() - 1)
    out = x
    for d in range(1, size):
        moved = pltpu.roll(pltpu.roll(x, size - d, 0), d * slots, 1)
        out = jnp.where(block == ((sub + d) & (size - 1)), moved, out)
    return out


def spread(a, b, count):
    return (
        jnp.concatenate([a[:count], b[:count]], axis=0),
        jnp.concatenate([a[count:], b[count:]], axis=0),
    )


def chain_kernel(
    plan,
    recv_ref,
    out_ref,
    mid_w,
    east_w,
    west_w,
    north_w,
    south_w,
    source_w,
    result_w,
    carried_w,
    mid_c,
    east_c,
    west_c,
    north_c,
    south_c,
    weight_g,
    innov,
    results,
    carried,
    obs_tab,
):
    p = plan
    f32 = jnp.float32
    me = lax.axis_index("tm") * p.tiles + lax.axis_index("tile")
    level = (me // p.cols).astype(f32)
    origin = ((me % p.cols) * p.width - p.halo).astype(f32)
    two = 2 * p.vars
    shape = (two, LANES)
    sub = lax.broadcasted_iota(jnp.int32, shape, 0)
    lane = lax.broadcasted_iota(jnp.int32, shape, 1)
    lower = sub < p.vars
    in_half = lane < p.margin + p.half
    n = p.nlat
    pitch = p.pitch
    area = p.area
    whole = p.subs * area
    nothing = ITERS * whole
    lead = two
    low_wide = p.subs - p.wide
    zero = jnp.zeros(shape, f32)

    def rows8(start):
        return pl.ds(pl.multiple_of(start, two), two)

    def clear(ref, start, count):
        def body(i, carry):
            for u in range(8):
                ref[rows8(start + (i * 8 + u) * two), :] = zero
            return carry

        lax.fori_loop(0, count // (8 * two), body, 0)

    clear(innov, nothing, area)
    clear(results, nothing, area)
    for ref in (mid_c, east_c, west_c, north_c, south_c, carried):
        ref[:lead, :] = zero
        ref[ref.shape[0] - lead :, :] = zero
    for k in range(p.wide):
        for l in range(n, pitch):
            for ref in (mid_w, east_w, west_w, north_w, south_w, source_w):
                ref[k * pitch + l] = zero
    for l in range(n, pitch):
        carried_w[l * two : (l + 1) * two, :] = zero

    def observe(k, stores):
        raw = []
        for i in range(6):
            raw.append(recv_ref[pl.ds(k * p.tiles * p.rows + p.obs_row + i, p.tiles, stride=p.rows), :])
        w, wy, cell = (jnp.concatenate(raw[2 * i : 2 * i + 2], axis=1) for i in range(3))
        w, wy, cell = (swap_blocks(x, p.slots) for x in (w, wy, cell))
        row = jnp.floor((cell + 0.5) * (1.0 / p.lon))
        lon = cell - row * p.lon
        group = jnp.floor((row + 0.5) * (1.0 / p.lat))
        lat = row - group * p.lat
        var = jnp.floor((group + 0.5) * (1.0 / p.lev))
        lev = group - var * p.lev
        at = lon - origin
        at = jnp.where(at < 0, at + p.lon, at)
        at = jnp.where(at >= p.lon, at - p.lon, at)
        place = at - p.extra
        here = (lev == level) & (at < p.span)
        main = here & (place >= 0) & (place < LANES)
        outside = here & ~main
        around = jnp.where(place < 0, place + LANES, place - LANES)
        rows = pl.ds(k * p.tiles, p.tiles)
        stores.put(obs_tab, (0, rows), lat * p.vars + var)
        stores.put(obs_tab, (1, rows), jnp.where(main, place, -1.0))
        stores.put(obs_tab, (2, rows), jnp.where(outside, around, -1.0))
        for i, x in ((3, w), (6, -wy)):
            one = x.astype(jnp.bfloat16).astype(f32)
            two = (x - one).astype(jnp.bfloat16).astype(f32)
            stores.put(obs_tab, (i, rows), one)
            stores.put(obs_tab, (i + 1, rows), two)
            stores.put(obs_tab, (i + 2, rows), x - one - two)

    looped(p.subs, 1, observe)

    n_rows = p.lat * p.vars
    slots = p.tiles * p.slots
    row_id = lax.broadcasted_iota(jnp.int32, (n_rows, slots), 0).astype(f32)
    lane_id = lax.broadcasted_iota(jnp.int32, (LANES, slots), 0).astype(f32)
    row_lane = lax.broadcasted_iota(jnp.int32, (n_rows, LANES), 1)

    def wide_tile(kt):
        return jnp.maximum(kt - low_wide * p.tiles, kt % p.tiles)

    def row_of(kt):
        return kt * p.lat + kt // p.tiles * STEPS

    def grid(kt, stores):
        def entry(i):
            return obs_tab[i, pl.ds(kt, 1), :]

        def factor(rows, i):
            return jnp.where(lane_id[rows] == entry(i), 1.0, 0.0).astype(jnp.bfloat16)

        def product(first, right):
            left = [jnp.where(match, entry(first + q), 0.0).astype(jnp.bfloat16) for q in range(3)]
            left = jnp.concatenate(left, axis=0)
            full = lax.dot_general(left, right, (((1,), (1,)), ((), ())), preferred_element_type=f32)
            parts = [full[q * n_rows : (q + 1) * n_rows] for q in range(3)]
            return parts[0] + (parts[1] + parts[2])

        match = row_id == entry(0)
        main = factor(slice(0, LANES), 1)
        ends = [factor(slice(0, 16), 2), jnp.zeros((LANES - 32, slots), jnp.bfloat16), factor(slice(LANES - 16, LANES), 2)]
        at = (pl.ds(pl.multiple_of(kt * n_rows, two), n_rows),)
        stores.put(weight_g, at, product(3, main))
        summed = product(6, jnp.concatenate([main] + ends, axis=0))
        inside, outside = summed[:, :LANES], summed[:, LANES:]
        stores.put(innov, at, inside)
        left = jnp.where(row_lane >= LANES - p.extra, outside, inside)
        right = jnp.where(row_lane < p.extra, outside, inside)
        tile = wide_tile(kt)
        for pair in range(p.lat // 2):
            rows = slice(two * pair, two * (pair + 1))
            one, other = spread(left[rows], right[rows], p.vars)
            stores.put(source_w, row_of(tile) + 2 * pair, one)
            stores.put(source_w, row_of(tile) + 2 * pair + 1, other)

    def derive(got):
        east, north, diff = got
        east = 0.5 * east
        north = 0.5 * north
        return 1.0 - 4.0 * diff, diff - east, diff + east, diff - north, diff + north

    def one_row(at):
        return jnp.broadcast_to(recv_ref[pl.ds(at, 1), :], shape)

    edge_mask = (lower & (lane >= LANES - p.extra)) | (~lower & (lane < p.extra))

    def widen(kt, stores):
        base = kt * p.rows
        for l in range(p.lat):
            got = []
            for c in range(3):
                main = one_row(base + p.coef_row + c * p.lat + l)
                got.append(jnp.where(edge_mask, one_row(base + l * p.vars + c), main))
            for ref, value in zip((mid_w, east_w, west_w, north_w, south_w), derive(got)):
                stores.put(ref, row_of(wide_tile(kt)) + l, value)

    def double(kt, stores):
        base = kt * p.rows + p.coef_row
        for l in range(0, p.lat, 2):
            got = []
            for c in range(3):
                at = base + c * p.lat + l
                got.append(jnp.where(lower, one_row(at), one_row(at + 1)))
            at = rows8(lead + kt * n_rows + l * p.vars)
            for ref, value in zip((mid_c, east_c, west_c, north_c, south_c), derive(got)):
                stores.put(ref, (at,), value)

    def prepare(kt, stores):
        grid(kt, stores)
        double(kt, stores)
        widen(kt, stores)

    looped(p.count, 2, prepare)

    def wide_step(i, carry):
        k = p.wide - 1 - i // STEPS
        base = k * pitch
        starts = (i % STEPS == 0).astype(f32)
        stores = Stores()

        def terms(l):
            x = carried_w[l * two : (l + 1) * two, :] + starts * source_w[base + l]
            at = base + l
            here = (
                mid_w[at] * x
                + pltpu.roll(east_w[at] * x, 1, 1)
                + pltpu.roll(west_w[at] * x, LANES - 1, 1)
            )
            return here, north_w[at] * x, south_w[at] * x

        below = zero
        here, north, _ = terms(0)
        for l in range(n):
            now, next_north, south = terms(l + 1)
            y = here + below + south
            here, below, north = now, north, next_north
            stores.put(carried_w, (slice(l * two, (l + 1) * two),), y)
            stores.put(result_w, (rows8((k * n + l) * two),), y)
        stores.flush()
        return carry

    def narrow(ref, at):
        mixed = ref[pl.ds(at + p.vars, two), :]
        left = jnp.where(lower, ref[pl.ds(at, two), :], mixed)
        right = jnp.where(lower, mixed, ref[pl.ds(at + two, two), :])
        return jnp.where(in_half, left, right)

    def narrow_results(i, stores):
        stores.put(results, (rows8(low_wide * area + i * two),), narrow(result_w, i * 2 * two))

    def narrow_carried(i, stores):
        value = narrow(carried_w, i * 2 * two) + innov[rows8((low_wide - 1) * area + i * two), :]
        stores.put(carried, (rows8(lead + i * two),), value)

    def begin_adjoint(i, stores):
        stores.put(carried, (rows8(lead + i * two),), innov[rows8(whole + (p.subs - 1) * area + i * two), :])

    def scaled(k, tile, q, at):
        var = recv_ref[pl.ds((k * p.tiles + tile) * p.rows + q * two, two), :]
        return 0.5 * (var * results[at, :])

    def begin_forward(tile, stores):
        for q in range(p.lat // 2):
            at = tile * n_rows + q * two
            stores.put(carried, (rows8(lead + at),), -scaled(0, tile, q, rows8(at)))

    def near(ref, base, at, shift):
        return ref[pl.ds(base + at + lead + shift * p.vars, two), :]

    def adjoint_step(i, phase):
        k = p.subs - 1 - i // STEPS
        base = k * area
        into = phase * whole + base
        ends = (i % STEPS == STEPS - 1) & (k > 0)
        source = jnp.where(ends, into - area, nothing)
        stores = Stores()
        for at in range(0, area, two):
            x = near(carried, 0, at, 0)
            y = (
                near(mid_c, base, at, 0) * x
                + pltpu.roll(near(east_c, base, at, 0) * x, 1, 1)
                + pltpu.roll(near(west_c, base, at, 0) * x, LANES - 1, 1)
                + near(north_c, base, at, -1) * near(carried, 0, at, -1)
                + near(south_c, base, at, 1) * near(carried, 0, at, 1)
            )
            stores.put(results, (rows8(into + at),), y)
            stores.put(carried, (slice(lead + at, lead + at + two),), y + innov[rows8(source + at), :])
        stores.flush()
        return phase

    def forward_step(i, carry):
        k = i // STEPS
        base = k * area
        ends = (i % STEPS == STEPS - 1) & (k < p.subs - 1)
        source = jnp.where(ends, base + area, nothing)
        later = jnp.minimum(k + 1, p.subs - 1)
        stores = Stores()
        for at in range(0, area, two):
            x = near(carried, 0, at, 0)
            y = (
                near(mid_c, base, at, 0) * x
                + near(east_c, base, at, 0) * pltpu.roll(x, LANES - 1, 1)
                + near(west_c, base, at, 0) * pltpu.roll(x, 1, 1)
                + near(north_c, base, at, 0) * near(carried, 0, at, 1)
                + near(south_c, base, at, 0) * near(carried, 0, at, -1)
            )
            here = rows8(base + at)
            stores.put(innov, (rows8(whole + base + at),), weight_g[here, :] * y + innov[here, :])
            force = scaled(later, at // n_rows, at % n_rows // two, rows8(source + at))
            stores.put(carried, (slice(lead + at, lead + at + two),), y - force)
        stores.flush()
        return carry

    def clear_wide(i, stores):
        stores.put(carried_w, (rows8(i * two),), zero)

    def iteration(phase, carry):
        @pl.when(phase == 0)
        def _():
            looped(n, 8, clear_wide)
            lax.fori_loop(0, p.wide * STEPS, wide_step, 0)
            looped(p.wide * n // 2, 12, narrow_results)
            looped(n // 2, 12, narrow_carried)

        @pl.when(phase > 0)
        def _():
            looped(n // 2, 12, begin_adjoint)

        lax.fori_loop(jnp.where(phase == 0, p.wide * STEPS, 0), p.subs * STEPS, adjoint_step, phase)

        @pl.when(phase < ITERS - 1)
        def _():
            looped(p.tiles, 2, begin_forward)
            lax.fori_loop(0, p.subs * STEPS, forward_step, 0)

        return carry

    lax.fori_loop(0, ITERS, iteration, 0)

    own = slice(p.margin, p.margin + p.width)

    def join(kt, stores):
        cols = []
        for v in range(p.vars):
            at = kt * n_rows + v
            early = results[pl.ds(at, p.lat, stride=p.vars), :]
            late = results[pl.ds(whole + at, p.lat, stride=p.vars), :]
            cols.append((0.5 * early + late)[:, own])
        spare = 3 * LANES - p.vars * p.width
        line = jnp.concatenate(cols + [jnp.zeros((p.lat, spare), f32)], axis=1)
        for i in range(3):
            at = (pl.ds(kt * p.lat * 3 + i, p.lat, stride=3),)
            stores.put(out_ref, at, line[:, i * LANES : (i + 1) * LANES])

    looped(p.count, 8, join)


def finish_kernel(plan, recv_ref, var_ref, out_ref):
    p = plan

    def level(z, carry):
        for j in range(p.cols):
            start = (z * p.cols + j) * p.lat * 3
            rows = [recv_ref[pl.ds(start + i, p.lat, stride=3), :] for i in range(3)]
            for v in range(p.vars):
                at, end = v * p.width, (v + 1) * p.width
                col = j * p.width
                while at < end:
                    i, low = divmod(at, LANES)
                    size = min(end - at, LANES - low)
                    cols = slice(col, col + size)
                    scale = -0.5 * var_ref[v, z, :, cols]
                    out_ref[v, z, :, cols] = scale * rows[i][:, low : low + size]
                    at, col = at + size, col + size
        return carry

    lax.fori_loop(0, p.lev, level, 0)


def transposed(
    plan, advect_east, advect_north, diffusion, background_var, obs_cell, obs_value, obs_weight, obs_count
):
    p = plan
    f32 = jnp.float32
    vmem = pl.BlockSpec(memory_space=pltpu.VMEM)
    params = pltpu.CompilerParams(vmem_limit_bytes=VMEM_LIMIT)
    var = background_var[0]
    packed = pl.pallas_call(
        functools.partial(pack_kernel, p),
        out_shape=jax.ShapeDtypeStruct((p.count * p.rows, LANES), f32),
        in_specs=[pl.BlockSpec(memory_space=pltpu.SMEM)] + [vmem] * 7,
        out_specs=vmem,
        scratch_shapes=[pltpu.VMEM(((p.vars + 3) * p.lev, p.lat, 15 * LANES), f32)],
        compiler_params=params,
        name="pack",
    )(
        obs_count.reshape(1, -1),
        obs_cell.reshape(1, -1),
        obs_value.reshape(1, -1),
        obs_weight.reshape(1, -1),
        advect_east[0],
        advect_north[0],
        diffusion[0],
        var,
    )
    received = lax.all_to_all(packed.reshape(-1, 2, LANES), ("tm", "tile"), 0, 0, tiled=True)
    received = received.reshape(-1, LANES)
    wide = pltpu.VMEM((p.wide * p.pitch, 2 * p.vars, LANES), f32)
    narrow = pltpu.VMEM((p.subs * p.area + 4 * p.vars, LANES), f32)
    both = pltpu.VMEM(((ITERS * p.subs + 1) * p.area, LANES), f32)
    back = pl.pallas_call(
        functools.partial(chain_kernel, p),
        out_shape=jax.ShapeDtypeStruct((p.count * p.lat * 3, LANES), f32),
        in_specs=[vmem],
        out_specs=vmem,
        scratch_shapes=[wide] * 6
        + [
            pltpu.VMEM((p.wide * p.nlat * 2 * p.vars, LANES), f32),
            pltpu.VMEM((p.pitch * 2 * p.vars, LANES), f32),
        ]
        + [narrow] * 5
        + [
            pltpu.VMEM((p.subs * p.area, LANES), f32),
            both,
            both,
            pltpu.VMEM((p.area + 4 * p.vars, LANES), f32),
            pltpu.VMEM((9, p.count, p.tiles * p.slots), f32),
        ],
        compiler_params=params,
        name="chains",
    )(received)
    back = back.reshape(-1, 4, LANES)
    returned = lax.all_to_all(back, ("tm", "tile"), 0, 0, tiled=True)
    returned = returned.reshape(-1, LANES)
    increment = pl.pallas_call(
        functools.partial(finish_kernel, p),
        out_shape=jax.ShapeDtypeStruct(var.shape, f32),
        in_specs=[vmem] * 2,
        out_specs=vmem,
        compiler_params=params,
        name="finish",
    )(returned, var)
    return increment[None]


def solution(mesh):
    def run(*args):
        plan = Plan(mesh.shape, args[3].shape, args[4].shape)
        work = functools.partial(transposed, plan) if plan.fits() else per_device
        return jax.shard_map(
            work,
            mesh=mesh,
            in_specs=(
                P("tm", None, "tile", None),
                P("tm", None, "tile", None),
                P("tm", None, "tile", None),
                P("tm", None, None, "tile", None),
                P("tm", "tile", None),
                P("tm", "tile", None),
                P("tm", "tile", None),
                P("tm", "tile", None),
            ),
            out_specs=P("tm", None, None, "tile", None),
            check_vma=False,
        )(*args)

    return run
```

```python
import functools

import jax
import jax.numpy as jnp
from jax import lax
from jax.experimental import pallas as pl
from jax.experimental.pallas import tpu as pltpu
from jax.sharding import PartitionSpec as P

STEPS = 2
ITERS = 2
CHAINS = 3
LANES = 128
BLOCK = 48
VMEM_LIMIT = 48 * 1024 * 1024


def padded(block, sides, width):
    for axis, dim in sides:
        count = lax.axis_size(axis)
        forward = [(i, i + 1) for i in range(count - 1)]
        backward = [(target, source) for source, target in forward]
        low = lax.ppermute(
            lax.slice_in_dim(block, block.shape[dim] - width, None, axis=dim), axis, forward
        )
        high = lax.ppermute(lax.slice_in_dim(block, 0, width, axis=dim), axis, backward)
        block = jnp.concatenate([low, block, high], axis=dim)
    return block


def shifted(value, axis, steps):
    count = lax.axis_size(axis)
    first, last = (max(0, -steps), min(count, count - steps))
    return lax.ppermute(value, axis, [(source, source + steps) for source in range(first, last)])


def apply_step(field, coef, adjoint):
    east_c = coef[0]
    north_c = coef[1]
    diff_c = coef[2]
    if adjoint:
        to_east = (diff_c - 0.5 * east_c) * field
        to_west = (diff_c + 0.5 * east_c) * field
        to_north = (diff_c - 0.5 * north_c) * field
        to_south = (diff_c + 0.5 * north_c) * field
        middle = (1.0 - 4.0 * diff_c[:, 1:-1]) * field[:, :, 1:-1]
        return (
            middle
            + jnp.roll(to_east[:, :, 1:-1], 1, axis=-1)
            + jnp.roll(to_west[:, :, 1:-1], -1, axis=-1)
            + to_north[:, :, :-2]
            + to_south[:, :, 2:]
        )
    inner = field[:, :, 1:-1]
    diff_in = diff_c[:, 1:-1]
    east_in = east_c[:, 1:-1]
    north_in = north_c[:, 1:-1]
    return (
        (1.0 - 4.0 * diff_in) * inner
        + (diff_in - 0.5 * east_in) * jnp.roll(inner, -1, axis=-1)
        + (diff_in + 0.5 * east_in) * jnp.roll(inner, 1, axis=-1)
        + (diff_in - 0.5 * north_in) * field[:, :, 2:]
        + (diff_in + 0.5 * north_in) * field[:, :, :-2]
    )


def advance(field, coef, adjoint):
    for repeat in range(STEPS):
        extended = padded(field, (("tile", 2),), 1)
        field = apply_step(extended, coef, adjoint)
    return field


def per_device(
    advect_east, advect_north, diffusion, background_var, obs_cell, obs_value, obs_weight, obs_count
):
    windows_count = lax.axis_size("tm")
    tiles = lax.axis_size("tile")
    coefs = jnp.stack([advect_east[0], advect_north[0], diffusion[0]])
    coef_ext = padded(coefs, (("tile", 2),), 1)
    cells = obs_cell.reshape(tiles, -1)
    slot_count = cells.shape[1]
    live = jnp.arange(slot_count, dtype=jnp.int32)[None, :] < obs_count.reshape(tiles)[:, None]
    masked = obs_weight.reshape(tiles, -1) * live.astype(jnp.float32)
    received = lax.all_to_all(
        jnp.stack([obs_value.reshape(tiles, -1), masked]),
        "tile",
        split_axis=1,
        concat_axis=1,
        tiled=True,
    )
    received_cells = lax.all_to_all(cells, "tile", split_axis=0, concat_axis=0, tiled=True)
    departures = received[0].reshape(-1)
    obs_weights = received[1].reshape(-1)
    flat_cells = received_cells.reshape(-1)
    local_var = background_var[0]
    state_shape = local_var.shape
    cell_total = state_shape[0] * state_shape[1] * state_shape[2] * state_shape[3]
    increment = jnp.zeros(state_shape, jnp.float32)
    for iteration in range(ITERS):
        if iteration == 0:
            innov = obs_weights * (0.0 - departures)
        else:
            forward_carried = advance(increment, coef_ext, False)
            for forward_window in range(windows_count - 1):
                forward_incoming = shifted(forward_carried, "tm", 1)
                forward_carried = advance(forward_incoming + increment, coef_ext, False)
            innov = obs_weights * (
                jnp.take(forward_carried.reshape(cell_total), flat_cells, axis=0) - departures
            )
        gridded = jnp.zeros((cell_total,), jnp.float32).at[flat_cells].add(innov)
        source = gridded.reshape(state_shape)
        carried = advance(source, coef_ext, True)
        for window in range(windows_count - 1):
            incoming = shifted(carried, "tm", -1)
            carried = advance(incoming + source, coef_ext, True)
        increment = increment - 0.5 * (increment + local_var * carried)
    return increment[None]


class Plan:
    def __init__(self, mesh_shape, var_shape, slot_shape):
        self.subs, self.tiles = mesh_shape["tm"], mesh_shape["tile"]
        self.count = self.subs * self.tiles
        _, self.vars, self.lev, self.nlat, self.lon = var_shape
        self.lat = self.nlat // self.tiles
        self.slots = slot_shape[2] // self.tiles
        self.cols = self.count // self.lev
        self.width = self.lon // self.cols
        self.half = self.width // 2
        self.halo = CHAINS * STEPS * self.subs
        self.margin = (LANES - self.width) // 2
        self.extra = self.halo - self.margin
        self.span = self.width + 2 * self.halo
        self.coef_row = self.lat * self.vars
        self.obs_row = self.coef_row + 3 * self.lat
        self.rows = self.obs_row + 6
        self.pitch = self.nlat + STEPS
        self.wide = -(-self.extra // STEPS)
        self.area = self.nlat * self.vars

    def borrows(self, k):
        return (CHAINS - 1) * STEPS * self.subs + STEPS * (k + 1) > self.margin

    def fits(self):
        if self.count % self.lev or self.lon % self.cols or self.width % 2:
            return False
        for k in range(self.subs):
            spare = self.margin - STEPS * (2 * self.subs - k)
            if spare < 0 or (self.borrows(k) and spare < self.extra):
                return False
        return (
            self.half + 2 * self.halo <= LANES
            and 0 <= self.extra <= 16
            and self.vars == 4
            and self.lat % 2 == 0
            and 0 < self.wide < self.subs
            and self.tiles == 8
            and self.nlat % BLOCK == 0
            and self.slots & (self.slots - 1) == 0
            and self.slots * self.tiles == 2 * LANES
            and self.width + 2 * self.margin == LANES
            and self.width * self.vars <= 3 * LANES
            and self.count * self.rows % 8 == 0
            and self.rows % 2 == 0
        )


def pack_kernel(
    plan, count_ref, cell_ref, value_ref, weight_ref, east_ref, north_ref, diff_ref, var_ref, out_ref, wide
):
    p = plan
    pad = 2 * LANES
    right = wide.shape[-1] - pad - p.lon
    per_level = p.vars + 3

    def fill(z, carry):
        for v in range(per_level):
            field = var_ref[v, z] if v < p.vars else (east_ref, north_ref, diff_ref)[v - p.vars][z]
            at = z * per_level + v
            wide[at, :, pad : pad + p.lon] = field
            wide[at, :, :pad] = field[:, p.lon - pad :]
            wide[at, :, pad + p.lon :] = field[:, :right]
        return carry

    lax.fori_loop(0, p.lev, fill, 0)

    lane = lax.broadcasted_iota(jnp.int32, (1, p.tiles * p.slots), 1)
    filled = jnp.zeros_like(lane)
    for t in range(p.tiles):
        filled = jnp.where(lane >= t * p.slots, count_ref[0, t], filled)
    weight = jnp.where((lane & (p.slots - 1)) < filled, weight_ref[...], 0.0)
    obs = []
    for x in (weight, weight * value_ref[...], cell_ref[...].astype(jnp.float32)):
        obs += [x[:, :LANES], x[:, LANES:]]
    obs = jnp.concatenate(obs, axis=0)
    lanes = lax.broadcasted_iota(jnp.int32, (p.lat, LANES), 1)
    borrows = jnp.where(p.borrows(lax.axis_index("tm")), p.extra, 0)

    def blocks(z, carry):
        for j in range(p.cols):
            first = pad + j * p.width - p.margin
            tile, low = divmod(first, LANES)

            def moved(a, t):
                x = wide[z * per_level + a, :, t * LANES : (t + 1) * LANES]
                return pltpu.roll(x, LANES - low, 1)

            base = (z * p.cols + j) * p.rows
            for v in range(p.vars):
                piece = jnp.where(lanes < LANES - low, moved(v, tile), moved(v, tile + 1))
                if v < 3:
                    here, after = moved(p.vars + v, tile), moved(p.vars + v, tile + 1)
                    rows = pl.ds(base + p.coef_row + v * p.lat, p.lat)
                    out_ref[rows, :] = jnp.where(lanes < LANES - low, here, after)
                    if low < p.extra:
                        here = jnp.where(lanes < LANES - low, moved(p.vars + v, tile - 1), here)
                    if low + p.extra > LANES:
                        after = jnp.where(lanes < LANES - low, after, moved(p.vars + v, tile + 2))
                    piece = jnp.where(lanes < borrows, after, piece)
                    piece = jnp.where(lanes >= LANES - borrows, here, piece)
                out_ref[pl.ds(base + v, p.lat, stride=p.vars), :] = piece
            out_ref[pl.ds(base + p.obs_row, 6), :] = obs
        return carry

    lax.fori_loop(0, p.lev, blocks, 0)


class Stores:
    def __init__(self):
        self.held = []

    def put(self, ref, at, value):
        self.held.append((ref, at, value))

    def flush(self):
        for ref, at, value in self.held:
            ref[at] = value
        self.held = []


def looped(count, unroll, body):
    def many(i, carry):
        stores = Stores()
        for u in range(unroll):
            body(i * unroll + u, stores)
        stores.flush()
        return carry

    lax.fori_loop(0, count // unroll, many, 0)


def swap_blocks(x, slots):
    size = x.shape[0]
    sub = lax.broadcasted_iota(jnp.int32, x.shape, 0)
    block = lax.broadcasted_iota(jnp.int32, x.shape, 1) >> (slots.bit_length() - 1)
    out = x
    for d in range(1, size):
        moved = pltpu.roll(pltpu.roll(x, size - d, 0), d * slots, 1)
        out = jnp.where(block == ((sub + d) & (size - 1)), moved, out)
    return out


def spread(a, b, count):
    return (
        jnp.concatenate([a[:count], b[:count]], axis=0),
        jnp.concatenate([a[count:], b[count:]], axis=0),
    )


def chain_kernel(
    plan,
    recv_ref,
    out_ref,
    mid_w,
    east_w,
    west_w,
    north_w,
    south_w,
    source_w,
    result_w,
    carried_w,
    mid_c,
    east_c,
    west_c,
    north_c,
    south_c,
    weight_g,
    innov,
    results,
    carried,
    obs_tab,
):
    p = plan
    f32 = jnp.float32
    me = lax.axis_index("tm") * p.tiles + lax.axis_index("tile")
    level = (me // p.cols).astype(f32)
    origin = ((me % p.cols) * p.width - p.halo).astype(f32)
    two = 2 * p.vars
    shape = (two, LANES)
    sub = lax.broadcasted_iota(jnp.int32, shape, 0)
    lane = lax.broadcasted_iota(jnp.int32, shape, 1)
    lower = sub < p.vars
    in_half = lane < p.margin + p.half
    n = p.nlat
    pitch = p.pitch
    area = p.area
    whole = p.subs * area
    nothing = ITERS * whole
    lead = two
    low_wide = p.subs - p.wide
    zero = jnp.zeros(shape, f32)

    def rows8(start):
        return pl.ds(pl.multiple_of(start, two), two)

    def clear(ref, start, count):
        def body(i, carry):
            for u in range(8):
                ref[rows8(start + (i * 8 + u) * two), :] = zero
            return carry

        lax.fori_loop(0, count // (8 * two), body, 0)

    clear(innov, nothing, area)
    clear(results, nothing, area)
    for ref in (mid_c, east_c, west_c, north_c, south_c, carried):
        ref[:lead, :] = zero
        ref[ref.shape[0] - lead :, :] = zero
    for k in range(p.wide):
        for l in range(n, pitch):
            for ref in (mid_w, east_w, west_w, north_w, south_w, source_w):
                ref[k * pitch + l] = zero
    for l in range(n, pitch):
        carried_w[l * two : (l + 1) * two, :] = zero

    def observe(k, stores):
        raw = []
        for i in range(6):
            raw.append(recv_ref[pl.ds(k * p.tiles * p.rows + p.obs_row + i, p.tiles, stride=p.rows), :])
        w, wy, cell = (jnp.concatenate(raw[2 * i : 2 * i + 2], axis=1) for i in range(3))
        w, wy, cell = (swap_blocks(x, p.slots) for x in (w, wy, cell))
        row = jnp.floor((cell + 0.5) * (1.0 / p.lon))
        lon = cell - row * p.lon
        group = jnp.floor((row + 0.5) * (1.0 / p.lat))
        lat = row - group * p.lat
        var = jnp.floor((group + 0.5) * (1.0 / p.lev))
        lev = group - var * p.lev
        at = lon - origin
        at = jnp.where(at < 0, at + p.lon, at)
        at = jnp.where(at >= p.lon, at - p.lon, at)
        place = at - p.extra
        here = (lev == level) & (at < p.span)
        main = here & (place >= 0) & (place < LANES)
        outside = here & ~main
        around = jnp.where(place < 0, place + LANES, place - LANES)
        rows = pl.ds(k * p.tiles, p.tiles)
        stores.put(obs_tab, (0, rows), lat * p.vars + var)
        stores.put(obs_tab, (1, rows), jnp.where(main, place, -1.0))
        stores.put(obs_tab, (2, rows), jnp.where(outside, around, -1.0))
        for i, x in ((3, w), (6, -wy)):
            one = x.astype(jnp.bfloat16).astype(f32)
            two = (x - one).astype(jnp.bfloat16).astype(f32)
            stores.put(obs_tab, (i, rows), one)
            stores.put(obs_tab, (i + 1, rows), two)
            stores.put(obs_tab, (i + 2, rows), x - one - two)

    looped(p.subs, 1, observe)

    n_rows = p.lat * p.vars
    slots = p.tiles * p.slots
    row_id = lax.broadcasted_iota(jnp.int32, (n_rows, slots), 0).astype(f32)
    lane_id = lax.broadcasted_iota(jnp.int32, (LANES, slots), 0).astype(f32)
    row_lane = lax.broadcasted_iota(jnp.int32, (n_rows, LANES), 1)

    def wide_tile(kt):
        return jnp.maximum(kt - low_wide * p.tiles, kt % p.tiles)

    def row_of(kt):
        return kt * p.lat + kt // p.tiles * STEPS

    def grid(kt, stores):
        def entry(i):
            return obs_tab[i, pl.ds(kt, 1), :]

        def factor(rows, i):
            return jnp.where(lane_id[rows] == entry(i), 1.0, 0.0).astype(jnp.bfloat16)

        def product(first, right):
            left = [jnp.where(match, entry(first + q), 0.0).astype(jnp.bfloat16) for q in range(3)]
            left = jnp.concatenate(left, axis=0)
            full = lax.dot_general(left, right, (((1,), (1,)), ((), ())), preferred_element_type=f32)
            parts = [full[q * n_rows : (q + 1) * n_rows] for q in range(3)]
            return parts[0] + (parts[1] + parts[2])

        match = row_id == entry(0)
        main = factor(slice(0, LANES), 1)
        ends = [factor(slice(0, 16), 2), jnp.zeros((LANES - 32, slots), jnp.bfloat16), factor(slice(LANES - 16, LANES), 2)]
        at = (pl.ds(pl.multiple_of(kt * n_rows, two), n_rows),)
        stores.put(weight_g, at, product(3, main))
        summed = product(6, jnp.concatenate([main] + ends, axis=0))
        inside, outside = summed[:, :LANES], summed[:, LANES:]
        stores.put(innov, at, inside)
        left = jnp.where(row_lane >= LANES - p.extra, outside, inside)
        right = jnp.where(row_lane < p.extra, outside, inside)
        tile = wide_tile(kt)
        for pair in range(p.lat // 2):
            rows = slice(two * pair, two * (pair + 1))
            one, other = spread(left[rows], right[rows], p.vars)
            stores.put(source_w, row_of(tile) + 2 * pair, one)
            stores.put(source_w, row_of(tile) + 2 * pair + 1, other)

    def derive(got):
        east, north, diff = got
        east = 0.5 * east
        north = 0.5 * north
        return 1.0 - 4.0 * diff, diff - east, diff + east, diff - north, diff + north

    def one_row(at):
        return jnp.broadcast_to(recv_ref[pl.ds(at, 1), :], shape)

    edge_mask = (lower & (lane >= LANES - p.extra)) | (~lower & (lane < p.extra))

    def widen(kt, stores):
        base = kt * p.rows
        for l in range(p.lat):
            got = []
            for c in range(3):
                main = one_row(base + p.coef_row + c * p.lat + l)
                got.append(jnp.where(edge_mask, one_row(base + l * p.vars + c), main))
            for ref, value in zip((mid_w, east_w, west_w, north_w, south_w), derive(got)):
                stores.put(ref, row_of(wide_tile(kt)) + l, value)

    def double(kt, stores):
        base = kt * p.rows + p.coef_row
        for l in range(0, p.lat, 2):
            got = []
            for c in range(3):
                at = base + c * p.lat + l
                got.append(jnp.where(lower, one_row(at), one_row(at + 1)))
            at = rows8(lead + kt * n_rows + l * p.vars)
            for ref, value in zip((mid_c, east_c, west_c, north_c, south_c), derive(got)):
                stores.put(ref, (at,), value)

    def prepare(kt, stores):
        grid(kt, stores)
        double(kt, stores)
        widen(kt, stores)

    looped(p.count, 2, prepare)

    def wide_step(i, carry):
        k = p.wide - 1 - i // STEPS
        base = k * pitch
        starts = (i % STEPS == 0).astype(f32)

        def terms(l):
            x = carried_w[rows8(l * two), :] + starts * source_w[base + l]
            at = base + l
            here = (
                mid_w[at] * x
                + pltpu.roll(east_w[at] * x, 1, 1)
                + pltpu.roll(west_w[at] * x, LANES - 1, 1)
            )
            return here, north_w[at] * x, south_w[at] * x

        def block(g, state):
            here, below, north = state
            stores = Stores()
            for u in range(BLOCK):
                l = g * BLOCK + u
                now, next_north, south = terms(l + 1)
                y = here + below + south
                here, below, north = now, north, next_north
                stores.put(carried_w, (rows8(l * two),), y)
                stores.put(result_w, (rows8((k * n + l) * two),), y)
            stores.flush()
            return here, below, north

        here, north, _ = terms(0)
        lax.fori_loop(0, n // BLOCK, block, (here, zero, north))
        return carry

    def narrow(ref, at):
        mixed = ref[pl.ds(at + p.vars, two), :]
        left = jnp.where(lower, ref[pl.ds(at, two), :], mixed)
        right = jnp.where(lower, mixed, ref[pl.ds(at + two, two), :])
        return jnp.where(in_half, left, right)

    def narrow_results(i, stores):
        stores.put(results, (rows8(low_wide * area + i * two),), narrow(result_w, i * 2 * two))

    def narrow_carried(i, stores):
        value = narrow(carried_w, i * 2 * two) + innov[rows8((low_wide - 1) * area + i * two), :]
        stores.put(carried, (rows8(lead + i * two),), value)

    def begin_adjoint(i, stores):
        stores.put(carried, (rows8(lead + i * two),), innov[rows8(whole + (p.subs - 1) * area + i * two), :])

    def scaled(k, tile, q, at):
        var = recv_ref[pl.ds((k * p.tiles + tile) * p.rows + q * two, two), :]
        return 0.5 * (var * results[at, :])

    def begin_forward(tile, stores):
        for q in range(p.lat // 2):
            at = tile * n_rows + q * two
            stores.put(carried, (rows8(lead + at),), -scaled(0, tile, q, rows8(at)))

    def near(ref, base, at, shift):
        return ref[pl.ds(base + at + lead + shift * p.vars, two), :]

    def adjoint_step(i, phase):
        k = p.subs - 1 - i // STEPS
        base = k * area
        into = phase * whole + base
        ends = (i % STEPS == STEPS - 1) & (k > 0)
        source = jnp.where(ends, into - area, nothing)
        stores = Stores()
        for at in range(0, area, two):
            x = near(carried, 0, at, 0)
            y = (
                near(mid_c, base, at, 0) * x
                + pltpu.roll(near(east_c, base, at, 0) * x, 1, 1)
                + pltpu.roll(near(west_c, base, at, 0) * x, LANES - 1, 1)
                + near(north_c, base, at, -1) * near(carried, 0, at, -1)
                + near(south_c, base, at, 1) * near(carried, 0, at, 1)
            )
            stores.put(results, (rows8(into + at),), y)
            stores.put(carried, (slice(lead + at, lead + at + two),), y + innov[rows8(source + at), :])
        stores.flush()
        return phase

    def forward_step(i, carry):
        k = i // STEPS
        base = k * area
        ends = (i % STEPS == STEPS - 1) & (k < p.subs - 1)
        source = jnp.where(ends, base + area, nothing)
        later = jnp.minimum(k + 1, p.subs - 1)
        stores = Stores()
        for at in range(0, area, two):
            x = near(carried, 0, at, 0)
            y = (
                near(mid_c, base, at, 0) * x
                + near(east_c, base, at, 0) * pltpu.roll(x, LANES - 1, 1)
                + near(west_c, base, at, 0) * pltpu.roll(x, 1, 1)
                + near(north_c, base, at, 0) * near(carried, 0, at, 1)
                + near(south_c, base, at, 0) * near(carried, 0, at, -1)
            )
            here = rows8(base + at)
            stores.put(innov, (rows8(whole + base + at),), weight_g[here, :] * y + innov[here, :])
            force = scaled(later, at // n_rows, at % n_rows // two, rows8(source + at))
            stores.put(carried, (slice(lead + at, lead + at + two),), y - force)
        stores.flush()
        return carry

    def clear_wide(i, stores):
        stores.put(carried_w, (rows8(i * two),), zero)

    def iteration(phase, carry):
        @pl.when(phase == 0)
        def _():
            looped(n, 8, clear_wide)
            lax.fori_loop(0, p.wide * STEPS, wide_step, 0)
            looped(p.wide * n // 2, 12, narrow_results)
            looped(n // 2, 12, narrow_carried)

        @pl.when(phase > 0)
        def _():
            looped(n // 2, 12, begin_adjoint)

        lax.fori_loop(jnp.where(phase == 0, p.wide * STEPS, 0), p.subs * STEPS, adjoint_step, phase)

        @pl.when(phase < ITERS - 1)
        def _():
            looped(p.tiles, 2, begin_forward)
            lax.fori_loop(0, p.subs * STEPS, forward_step, 0)

        return carry

    lax.fori_loop(0, ITERS, iteration, 0)

    own = slice(p.margin, p.margin + p.width)

    def join(kt, stores):
        cols = []
        for v in range(p.vars):
            at = kt * n_rows + v
            early = results[pl.ds(at, p.lat, stride=p.vars), :]
            late = results[pl.ds(whole + at, p.lat, stride=p.vars), :]
            cols.append((0.5 * early + late)[:, own])
        spare = 3 * LANES - p.vars * p.width
        line = jnp.concatenate(cols + [jnp.zeros((p.lat, spare), f32)], axis=1)
        for i in range(3):
            at = (pl.ds(kt * p.lat * 3 + i, p.lat, stride=3),)
            stores.put(out_ref, at, line[:, i * LANES : (i + 1) * LANES])

    looped(p.count, 4, join)


def finish_kernel(plan, recv_ref, var_ref, out_ref):
    p = plan

    def level(z, carry):
        for j in range(p.cols):
            start = (z * p.cols + j) * p.lat * 3
            rows = [recv_ref[pl.ds(start + i, p.lat, stride=3), :] for i in range(3)]
            for v in range(p.vars):
                at, end = v * p.width, (v + 1) * p.width
                col = j * p.width
                while at < end:
                    i, low = divmod(at, LANES)
                    size = min(end - at, LANES - low)
                    cols = slice(col, col + size)
                    scale = -0.5 * var_ref[v, z, :, cols]
                    out_ref[v, z, :, cols] = scale * rows[i][:, low : low + size]
                    at, col = at + size, col + size
        return carry

    lax.fori_loop(0, p.lev, level, 0)


def transposed(
    plan, advect_east, advect_north, diffusion, background_var, obs_cell, obs_value, obs_weight, obs_count
):
    p = plan
    f32 = jnp.float32
    vmem = pl.BlockSpec(memory_space=pltpu.VMEM)
    params = pltpu.CompilerParams(vmem_limit_bytes=VMEM_LIMIT)
    var = background_var[0]
    packed = pl.pallas_call(
        functools.partial(pack_kernel, p),
        out_shape=jax.ShapeDtypeStruct((p.count * p.rows, LANES), f32),
        in_specs=[pl.BlockSpec(memory_space=pltpu.SMEM)] + [vmem] * 7,
        out_specs=vmem,
        scratch_shapes=[pltpu.VMEM(((p.vars + 3) * p.lev, p.lat, 15 * LANES), f32)],
        compiler_params=params,
        name="pack",
    )(
        obs_count.reshape(1, -1),
        obs_cell.reshape(1, -1),
        obs_value.reshape(1, -1),
        obs_weight.reshape(1, -1),
        advect_east[0],
        advect_north[0],
        diffusion[0],
        var,
    )
    received = lax.all_to_all(packed.reshape(-1, 2, LANES), ("tm", "tile"), 0, 0, tiled=True)
    received = received.reshape(-1, LANES)
    wide = pltpu.VMEM((p.wide * p.pitch, 2 * p.vars, LANES), f32)
    narrow = pltpu.VMEM((p.subs * p.area + 4 * p.vars, LANES), f32)
    both = pltpu.VMEM(((ITERS * p.subs + 1) * p.area, LANES), f32)
    back = pl.pallas_call(
        functools.partial(chain_kernel, p),
        out_shape=jax.ShapeDtypeStruct((p.count * p.lat * 3, LANES), f32),
        in_specs=[vmem],
        out_specs=vmem,
        scratch_shapes=[wide] * 6
        + [
            pltpu.VMEM((p.wide * p.nlat * 2 * p.vars, LANES), f32),
            pltpu.VMEM((p.pitch * 2 * p.vars, LANES), f32),
        ]
        + [narrow] * 5
        + [
            pltpu.VMEM((p.subs * p.area, LANES), f32),
            both,
            both,
            pltpu.VMEM((p.area + 4 * p.vars, LANES), f32),
            pltpu.VMEM((9, p.count, p.tiles * p.slots), f32),
        ],
        compiler_params=params,
        name="chains",
    )(received)
    back = back.reshape(-1, 4, LANES)
    returned = lax.all_to_all(back, ("tm", "tile"), 0, 0, tiled=True)
    returned = returned.reshape(-1, LANES)
    increment = pl.pallas_call(
        functools.partial(finish_kernel, p),
        out_shape=jax.ShapeDtypeStruct(var.shape, f32),
        in_specs=[vmem] * 2,
        out_specs=vmem,
        compiler_params=params,
        name="finish",
    )(returned, var)
    return increment[None]


def solution(mesh):
    def run(*args):
        plan = Plan(mesh.shape, args[3].shape, args[4].shape)
        work = functools.partial(transposed, plan) if plan.fits() else per_device
        return jax.shard_map(
            work,
            mesh=mesh,
            in_specs=(
                P("tm", None, "tile", None),
                P("tm", None, "tile", None),
                P("tm", None, "tile", None),
                P("tm", None, None, "tile", None),
                P("tm", "tile", None),
                P("tm", "tile", None),
                P("tm", "tile", None),
                P("tm", "tile", None),
            ),
            out_specs=P("tm", None, None, "tile", None),
            check_vma=False,
        )(*args)

    return run
```

```python
import functools

import jax
import jax.numpy as jnp
from jax import lax
from jax.experimental import pallas as pl
from jax.experimental.pallas import tpu as pltpu
from jax.sharding import PartitionSpec as P

STEPS = 2
ITERS = 2
CHAINS = 3
LANES = 128
VMEM_LIMIT = 48 * 1024 * 1024


def padded(block, sides, width):
    for axis, dim in sides:
        count = lax.axis_size(axis)
        forward = [(i, i + 1) for i in range(count - 1)]
        backward = [(target, source) for source, target in forward]
        low = lax.ppermute(
            lax.slice_in_dim(block, block.shape[dim] - width, None, axis=dim), axis, forward
        )
        high = lax.ppermute(lax.slice_in_dim(block, 0, width, axis=dim), axis, backward)
        block = jnp.concatenate([low, block, high], axis=dim)
    return block


def shifted(value, axis, steps):
    count = lax.axis_size(axis)
    first, last = (max(0, -steps), min(count, count - steps))
    return lax.ppermute(value, axis, [(source, source + steps) for source in range(first, last)])


def apply_step(field, coef, adjoint):
    east_c = coef[0]
    north_c = coef[1]
    diff_c = coef[2]
    if adjoint:
        to_east = (diff_c - 0.5 * east_c) * field
        to_west = (diff_c + 0.5 * east_c) * field
        to_north = (diff_c - 0.5 * north_c) * field
        to_south = (diff_c + 0.5 * north_c) * field
        middle = (1.0 - 4.0 * diff_c[:, 1:-1]) * field[:, :, 1:-1]
        return (
            middle
            + jnp.roll(to_east[:, :, 1:-1], 1, axis=-1)
            + jnp.roll(to_west[:, :, 1:-1], -1, axis=-1)
            + to_north[:, :, :-2]
            + to_south[:, :, 2:]
        )
    inner = field[:, :, 1:-1]
    diff_in = diff_c[:, 1:-1]
    east_in = east_c[:, 1:-1]
    north_in = north_c[:, 1:-1]
    return (
        (1.0 - 4.0 * diff_in) * inner
        + (diff_in - 0.5 * east_in) * jnp.roll(inner, -1, axis=-1)
        + (diff_in + 0.5 * east_in) * jnp.roll(inner, 1, axis=-1)
        + (diff_in - 0.5 * north_in) * field[:, :, 2:]
        + (diff_in + 0.5 * north_in) * field[:, :, :-2]
    )


def advance(field, coef, adjoint):
    for repeat in range(STEPS):
        extended = padded(field, (("tile", 2),), 1)
        field = apply_step(extended, coef, adjoint)
    return field


def per_device(
    advect_east, advect_north, diffusion, background_var, obs_cell, obs_value, obs_weight, obs_count
):
    windows_count = lax.axis_size("tm")
    tiles = lax.axis_size("tile")
    coefs = jnp.stack([advect_east[0], advect_north[0], diffusion[0]])
    coef_ext = padded(coefs, (("tile", 2),), 1)
    cells = obs_cell.reshape(tiles, -1)
    slot_count = cells.shape[1]
    live = jnp.arange(slot_count, dtype=jnp.int32)[None, :] < obs_count.reshape(tiles)[:, None]
    masked = obs_weight.reshape(tiles, -1) * live.astype(jnp.float32)
    received = lax.all_to_all(
        jnp.stack([obs_value.reshape(tiles, -1), masked]),
        "tile",
        split_axis=1,
        concat_axis=1,
        tiled=True,
    )
    received_cells = lax.all_to_all(cells, "tile", split_axis=0, concat_axis=0, tiled=True)
    departures = received[0].reshape(-1)
    obs_weights = received[1].reshape(-1)
    flat_cells = received_cells.reshape(-1)
    local_var = background_var[0]
    state_shape = local_var.shape
    cell_total = state_shape[0] * state_shape[1] * state_shape[2] * state_shape[3]
    increment = jnp.zeros(state_shape, jnp.float32)
    for iteration in range(ITERS):
        if iteration == 0:
            innov = obs_weights * (0.0 - departures)
        else:
            forward_carried = advance(increment, coef_ext, False)
            for forward_window in range(windows_count - 1):
                forward_incoming = shifted(forward_carried, "tm", 1)
                forward_carried = advance(forward_incoming + increment, coef_ext, False)
            innov = obs_weights * (
                jnp.take(forward_carried.reshape(cell_total), flat_cells, axis=0) - departures
            )
        gridded = jnp.zeros((cell_total,), jnp.float32).at[flat_cells].add(innov)
        source = gridded.reshape(state_shape)
        carried = advance(source, coef_ext, True)
        for window in range(windows_count - 1):
            incoming = shifted(carried, "tm", -1)
            carried = advance(incoming + source, coef_ext, True)
        increment = increment - 0.5 * (increment + local_var * carried)
    return increment[None]


class Plan:
    def __init__(self, mesh_shape, var_shape, slot_shape):
        self.subs, self.tiles = mesh_shape["tm"], mesh_shape["tile"]
        self.count = self.subs * self.tiles
        _, self.vars, self.lev, self.nlat, self.lon = var_shape
        self.lat = self.nlat // self.tiles
        self.slots = slot_shape[2] // self.tiles
        self.cols = self.count // self.lev
        self.width = self.lon // self.cols
        self.half = self.width // 2
        self.halo = CHAINS * STEPS * self.subs
        self.margin = (LANES - self.width) // 2
        self.extra = self.halo - self.margin
        self.span = self.width + 2 * self.halo
        self.coef_row = self.lat * self.vars
        self.obs_row = self.coef_row + 3 * self.lat
        self.rows = self.obs_row + 6
        self.pitch = self.nlat + STEPS
        self.wide = -(-self.extra // STEPS)
        self.area = self.nlat * self.vars

    def borrows(self, k):
        return (CHAINS - 1) * STEPS * self.subs + STEPS * (k + 1) > self.margin

    def fits(self):
        if self.count % self.lev or self.lon % self.cols or self.width % 2:
            return False
        for k in range(self.subs):
            spare = self.margin - STEPS * (2 * self.subs - k)
            if spare < 0 or (self.borrows(k) and spare < self.extra):
                return False
        return (
            self.half + 2 * self.halo <= LANES
            and 0 <= self.extra <= 16
            and self.vars == 4
            and self.lat % 2 == 0
            and 0 < self.wide < self.subs
            and self.tiles == 8
            and self.slots & (self.slots - 1) == 0
            and self.slots * self.tiles == 2 * LANES
            and self.width + 2 * self.margin == LANES
            and self.width * self.vars <= 3 * LANES
            and self.count * self.rows % 8 == 0
            and self.rows % 2 == 0
        )


def pack_kernel(
    plan, count_ref, cell_ref, value_ref, weight_ref, east_ref, north_ref, diff_ref, var_ref, out_ref, wide
):
    p = plan
    pad = 2 * LANES
    right = wide.shape[-1] - pad - p.lon
    per_level = p.vars + 3

    def fill(z, carry):
        for v in range(per_level):
            field = var_ref[v, z] if v < p.vars else (east_ref, north_ref, diff_ref)[v - p.vars][z]
            at = z * per_level + v
            wide[at, :, pad : pad + p.lon] = field
            wide[at, :, :pad] = field[:, p.lon - pad :]
            wide[at, :, pad + p.lon :] = field[:, :right]
        return carry

    lax.fori_loop(0, p.lev, fill, 0)

    lane = lax.broadcasted_iota(jnp.int32, (1, p.tiles * p.slots), 1)
    filled = jnp.zeros_like(lane)
    for t in range(p.tiles):
        filled = jnp.where(lane >= t * p.slots, count_ref[0, t], filled)
    weight = jnp.where((lane & (p.slots - 1)) < filled, weight_ref[...], 0.0)
    obs = []
    for x in (weight, weight * value_ref[...], cell_ref[...].astype(jnp.float32)):
        obs += [x[:, :LANES], x[:, LANES:]]
    obs = jnp.concatenate(obs, axis=0)
    lanes = lax.broadcasted_iota(jnp.int32, (p.lat, LANES), 1)
    borrows = jnp.where(p.borrows(lax.axis_index("tm")), p.extra, 0)

    def blocks(z, carry):
        for j in range(p.cols):
            first = pad + j * p.width - p.margin
            tile, low = divmod(first, LANES)

            def moved(a, t):
                x = wide[z * per_level + a, :, t * LANES : (t + 1) * LANES]
                return pltpu.roll(x, LANES - low, 1)

            base = (z * p.cols + j) * p.rows
            for v in range(p.vars):
                piece = jnp.where(lanes < LANES - low, moved(v, tile), moved(v, tile + 1))
                if v < 3:
                    here, after = moved(p.vars + v, tile), moved(p.vars + v, tile + 1)
                    rows = pl.ds(base + p.coef_row + v * p.lat, p.lat)
                    out_ref[rows, :] = jnp.where(lanes < LANES - low, here, after)
                    if low < p.extra:
                        here = jnp.where(lanes < LANES - low, moved(p.vars + v, tile - 1), here)
                    if low + p.extra > LANES:
                        after = jnp.where(lanes < LANES - low, after, moved(p.vars + v, tile + 2))
                    piece = jnp.where(lanes < borrows, after, piece)
                    piece = jnp.where(lanes >= LANES - borrows, here, piece)
                out_ref[pl.ds(base + v, p.lat, stride=p.vars), :] = piece
            out_ref[pl.ds(base + p.obs_row, 6), :] = obs
        return carry

    lax.fori_loop(0, p.lev, blocks, 0)


class Stores:
    def __init__(self):
        self.held = []

    def put(self, ref, at, value):
        self.held.append((ref, at, value))

    def flush(self):
        for ref, at, value in self.held:
            ref[at] = value
        self.held = []


def looped(count, unroll, body):
    def many(i, carry):
        stores = Stores()
        for u in range(unroll):
            body(i * unroll + u, stores)
        stores.flush()
        return carry

    lax.fori_loop(0, count // unroll, many, 0)


def swap_blocks(x, slots):
    size = x.shape[0]
    sub = lax.broadcasted_iota(jnp.int32, x.shape, 0)
    block = lax.broadcasted_iota(jnp.int32, x.shape, 1) >> (slots.bit_length() - 1)
    out = x
    for d in range(1, size):
        moved = pltpu.roll(pltpu.roll(x, size - d, 0), d * slots, 1)
        out = jnp.where(block == ((sub + d) & (size - 1)), moved, out)
    return out


def spread(a, b, count):
    return (
        jnp.concatenate([a[:count], b[:count]], axis=0),
        jnp.concatenate([a[count:], b[count:]], axis=0),
    )


def chain_kernel(
    plan,
    recv_ref,
    out_ref,
    mid_w,
    east_w,
    west_w,
    north_w,
    south_w,
    source_w,
    result_w,
    carried_w,
    mid_c,
    east_c,
    west_c,
    north_c,
    south_c,
    weight_g,
    innov,
    results,
    carried,
    obs_tab,
):
    p = plan
    f32 = jnp.float32
    me = lax.axis_index("tm") * p.tiles + lax.axis_index("tile")
    level = (me // p.cols).astype(f32)
    origin = ((me % p.cols) * p.width - p.halo).astype(f32)
    two = 2 * p.vars
    shape = (two, LANES)
    sub = lax.broadcasted_iota(jnp.int32, shape, 0)
    lane = lax.broadcasted_iota(jnp.int32, shape, 1)
    lower = sub < p.vars
    in_half = lane < p.margin + p.half
    n = p.nlat
    pitch = p.pitch
    area = p.area
    whole = p.subs * area
    nothing = ITERS * whole
    lead = two
    low_wide = p.subs - p.wide
    zero = jnp.zeros(shape, f32)

    def rows8(start):
        return pl.ds(pl.multiple_of(start, two), two)

    def clear(ref, start, count):
        def body(i, carry):
            for u in range(8):
                ref[rows8(start + (i * 8 + u) * two), :] = zero
            return carry

        lax.fori_loop(0, count // (8 * two), body, 0)

    clear(innov, nothing, area)
    clear(results, nothing, area)
    for ref in (mid_c, east_c, west_c, north_c, south_c, carried):
        ref[:lead, :] = zero
        ref[ref.shape[0] - lead :, :] = zero
    for k in range(p.wide):
        for l in range(n, pitch):
            for ref in (mid_w, east_w, west_w, north_w, south_w, source_w):
                ref[k * pitch + l] = zero
    for l in range(n, pitch):
        carried_w[l * two : (l + 1) * two, :] = zero

    def observe(k, stores):
        raw = []
        for i in range(6):
            raw.append(recv_ref[pl.ds(k * p.tiles * p.rows + p.obs_row + i, p.tiles, stride=p.rows), :])
        w, wy, cell = (jnp.concatenate(raw[2 * i : 2 * i + 2], axis=1) for i in range(3))
        w, wy, cell = (swap_blocks(x, p.slots) for x in (w, wy, cell))
        row = jnp.floor((cell + 0.5) * (1.0 / p.lon))
        lon = cell - row * p.lon
        group = jnp.floor((row + 0.5) * (1.0 / p.lat))
        lat = row - group * p.lat
        var = jnp.floor((group + 0.5) * (1.0 / p.lev))
        lev = group - var * p.lev
        at = lon - origin
        at = jnp.where(at < 0, at + p.lon, at)
        at = jnp.where(at >= p.lon, at - p.lon, at)
        place = at - p.extra
        here = (lev == level) & (at < p.span)
        main = here & (place >= 0) & (place < LANES)
        outside = here & ~main
        around = jnp.where(place < 0, place + LANES, place - LANES)
        rows = pl.ds(k * p.tiles, p.tiles)
        stores.put(obs_tab, (0, rows), lat * p.vars + var)
        stores.put(obs_tab, (1, rows), jnp.where(main, place, -1.0))
        stores.put(obs_tab, (2, rows), jnp.where(outside, around, -1.0))
        for i, x in ((3, w), (6, -wy)):
            one = x.astype(jnp.bfloat16).astype(f32)
            two = (x - one).astype(jnp.bfloat16).astype(f32)
            stores.put(obs_tab, (i, rows), one)
            stores.put(obs_tab, (i + 1, rows), two)
            stores.put(obs_tab, (i + 2, rows), x - one - two)

    looped(p.subs, 1, observe)

    n_rows = p.lat * p.vars
    slots = p.tiles * p.slots
    row_id = lax.broadcasted_iota(jnp.int32, (n_rows, slots), 0).astype(f32)
    lane_id = lax.broadcasted_iota(jnp.int32, (LANES, slots), 0).astype(f32)
    row_lane = lax.broadcasted_iota(jnp.int32, (n_rows, LANES), 1)

    def wide_tile(kt):
        return jnp.maximum(kt - low_wide * p.tiles, kt % p.tiles)

    def row_of(kt):
        return kt * p.lat + kt // p.tiles * STEPS

    def grid(kt, stores):
        def entry(i):
            return obs_tab[i, pl.ds(kt, 1), :]

        def factor(rows, i):
            return jnp.where(lane_id[rows] == entry(i), 1.0, 0.0).astype(jnp.bfloat16)

        def product(first, right):
            left = [jnp.where(match, entry(first + q), 0.0).astype(jnp.bfloat16) for q in range(3)]
            left = jnp.concatenate(left, axis=0)
            full = lax.dot_general(left, right, (((1,), (1,)), ((), ())), preferred_element_type=f32)
            parts = [full[q * n_rows : (q + 1) * n_rows] for q in range(3)]
            return parts[0] + (parts[1] + parts[2])

        match = row_id == entry(0)
        main = factor(slice(0, LANES), 1)
        ends = [factor(slice(0, 16), 2), jnp.zeros((LANES - 32, slots), jnp.bfloat16), factor(slice(LANES - 16, LANES), 2)]
        at = (pl.ds(pl.multiple_of(kt * n_rows, two), n_rows),)
        stores.put(weight_g, at, product(3, main))
        summed = product(6, jnp.concatenate([main] + ends, axis=0))
        inside, outside = summed[:, :LANES], summed[:, LANES:]
        stores.put(innov, at, inside)
        left = jnp.where(row_lane >= LANES - p.extra, outside, inside)
        right = jnp.where(row_lane < p.extra, outside, inside)
        tile = wide_tile(kt)
        for pair in range(p.lat // 2):
            rows = slice(two * pair, two * (pair + 1))
            one, other = spread(left[rows], right[rows], p.vars)
            stores.put(source_w, row_of(tile) + 2 * pair, one)
            stores.put(source_w, row_of(tile) + 2 * pair + 1, other)

    def derive(got):
        east, north, diff = got
        east = 0.5 * east
        north = 0.5 * north
        return 1.0 - 4.0 * diff, diff - east, diff + east, diff - north, diff + north

    def one_row(at):
        return jnp.broadcast_to(recv_ref[pl.ds(at, 1), :], shape)

    edge_mask = (lower & (lane >= LANES - p.extra)) | (~lower & (lane < p.extra))

    def widen(kt, stores):
        base = kt * p.rows
        for l in range(p.lat):
            got = []
            for c in range(3):
                main = one_row(base + p.coef_row + c * p.lat + l)
                got.append(jnp.where(edge_mask, one_row(base + l * p.vars + c), main))
            for ref, value in zip((mid_w, east_w, west_w, north_w, south_w), derive(got)):
                stores.put(ref, row_of(wide_tile(kt)) + l, value)

    def double(kt, stores):
        base = kt * p.rows + p.coef_row
        for l in range(0, p.lat, 2):
            got = []
            for c in range(3):
                at = base + c * p.lat + l
                got.append(jnp.where(lower, one_row(at), one_row(at + 1)))
            at = rows8(lead + kt * n_rows + l * p.vars)
            for ref, value in zip((mid_c, east_c, west_c, north_c, south_c), derive(got)):
                stores.put(ref, (at,), value)

    def prepare(kt, stores):
        grid(kt, stores)
        double(kt, stores)
        widen(kt, stores)

    looped(p.count, 4, prepare)

    def wide_step(i, carry):
        k = p.wide - 1 - i // STEPS
        base = k * pitch
        starts = (i % STEPS == 0).astype(f32)
        stores = Stores()

        def terms(l):
            x = carried_w[l * two : (l + 1) * two, :] + starts * source_w[base + l]
            at = base + l
            here = (
                mid_w[at] * x
                + pltpu.roll(east_w[at] * x, 1, 1)
                + pltpu.roll(west_w[at] * x, LANES - 1, 1)
            )
            return here, north_w[at] * x, south_w[at] * x

        below = zero
        here, north, _ = terms(0)
        for l in range(n):
            now, next_north, south = terms(l + 1)
            y = here + below + south
            here, below, north = now, north, next_north
            stores.put(carried_w, (slice(l * two, (l + 1) * two),), y)
            stores.put(result_w, (rows8((k * n + l) * two),), y)
        stores.flush()
        return carry

    def narrow(ref, at):
        mixed = ref[pl.ds(at + p.vars, two), :]
        left = jnp.where(lower, ref[pl.ds(at, two), :], mixed)
        right = jnp.where(lower, mixed, ref[pl.ds(at + two, two), :])
        return jnp.where(in_half, left, right)

    def narrow_results(i, stores):
        stores.put(results, (rows8(low_wide * area + i * two),), narrow(result_w, i * 2 * two))

    def narrow_carried(i, stores):
        value = narrow(carried_w, i * 2 * two) + innov[rows8((low_wide - 1) * area + i * two), :]
        stores.put(carried, (rows8(lead + i * two),), value)

    def begin_adjoint(i, stores):
        stores.put(carried, (rows8(lead + i * two),), innov[rows8(whole + (p.subs - 1) * area + i * two), :])

    def scaled(k, tile, q, at):
        var = recv_ref[pl.ds((k * p.tiles + tile) * p.rows + q * two, two), :]
        return 0.5 * (var * results[at, :])

    def begin_forward(tile, stores):
        for q in range(p.lat // 2):
            at = tile * n_rows + q * two
            stores.put(carried, (rows8(lead + at),), -scaled(0, tile, q, rows8(at)))

    def near(ref, base, at, shift):
        return ref[pl.ds(base + at + lead + shift * p.vars, two), :]

    def adjoint_step(i, phase):
        k = p.subs - 1 - i // STEPS
        base = k * area
        into = phase * whole + base
        ends = (i % STEPS == STEPS - 1) & (k > 0)
        source = jnp.where(ends, into - area, nothing)
        stores = Stores()
        for at in range(0, area, two):
            x = near(carried, 0, at, 0)
            y = (
                near(mid_c, base, at, 0) * x
                + pltpu.roll(near(east_c, base, at, 0) * x, 1, 1)
                + pltpu.roll(near(west_c, base, at, 0) * x, LANES - 1, 1)
                + near(north_c, base, at, -1) * near(carried, 0, at, -1)
                + near(south_c, base, at, 1) * near(carried, 0, at, 1)
            )
            stores.put(results, (rows8(into + at),), y)
            stores.put(carried, (slice(lead + at, lead + at + two),), y + innov[rows8(source + at), :])
        stores.flush()
        return phase

    def forward_step(i, carry):
        k = i // STEPS
        base = k * area
        ends = (i % STEPS == STEPS - 1) & (k < p.subs - 1)
        source = jnp.where(ends, base + area, nothing)
        later = jnp.minimum(k + 1, p.subs - 1)
        stores = Stores()
        for at in range(0, area, two):
            x = near(carried, 0, at, 0)
            y = (
                near(mid_c, base, at, 0) * x
                + near(east_c, base, at, 0) * pltpu.roll(x, LANES - 1, 1)
                + near(west_c, base, at, 0) * pltpu.roll(x, 1, 1)
                + near(north_c, base, at, 0) * near(carried, 0, at, 1)
                + near(south_c, base, at, 0) * near(carried, 0, at, -1)
            )
            here = rows8(base + at)
            stores.put(innov, (rows8(whole + base + at),), weight_g[here, :] * y + innov[here, :])
            force = scaled(later, at // n_rows, at % n_rows // two, rows8(source + at))
            stores.put(carried, (slice(lead + at, lead + at + two),), y - force)
        stores.flush()
        return carry

    def clear_wide(i, stores):
        stores.put(carried_w, (rows8(i * two),), zero)

    def iteration(phase, carry):
        @pl.when(phase == 0)
        def _():
            looped(n, 8, clear_wide)
            lax.fori_loop(0, p.wide * STEPS, wide_step, 0)
            looped(p.wide * n // 2, 12, narrow_results)
            looped(n // 2, 12, narrow_carried)

        @pl.when(phase > 0)
        def _():
            looped(n // 2, 12, begin_adjoint)

        lax.fori_loop(jnp.where(phase == 0, p.wide * STEPS, 0), p.subs * STEPS, adjoint_step, phase)

        @pl.when(phase < ITERS - 1)
        def _():
            looped(p.tiles, 2, begin_forward)
            lax.fori_loop(0, p.subs * STEPS, forward_step, 0)

        return carry

    lax.fori_loop(0, ITERS, iteration, 0)

    own = slice(p.margin, p.margin + p.width)

    def join(kt, stores):
        cols = []
        for v in range(p.vars):
            at = kt * n_rows + v
            early = results[pl.ds(at, p.lat, stride=p.vars), :]
            late = results[pl.ds(whole + at, p.lat, stride=p.vars), :]
            cols.append((0.5 * early + late)[:, own])
        spare = 3 * LANES - p.vars * p.width
        line = jnp.concatenate(cols + [jnp.zeros((p.lat, spare), f32)], axis=1)
        for i in range(3):
            at = (pl.ds(kt * p.lat * 3 + i, p.lat, stride=3),)
            stores.put(out_ref, at, line[:, i * LANES : (i + 1) * LANES])

    looped(p.count, 4, join)


def finish_kernel(plan, recv_ref, var_ref, out_ref):
    p = plan

    def level(z, carry):
        for j in range(p.cols):
            start = (z * p.cols + j) * p.lat * 3
            rows = [recv_ref[pl.ds(start + i, p.lat, stride=3), :] for i in range(3)]
            for v in range(p.vars):
                at, end = v * p.width, (v + 1) * p.width
                col = j * p.width
                while at < end:
                    i, low = divmod(at, LANES)
                    size = min(end - at, LANES - low)
                    cols = slice(col, col + size)
                    scale = -0.5 * var_ref[v, z, :, cols]
                    out_ref[v, z, :, cols] = scale * rows[i][:, low : low + size]
                    at, col = at + size, col + size
        return carry

    lax.fori_loop(0, p.lev, level, 0)


def transposed(
    plan, advect_east, advect_north, diffusion, background_var, obs_cell, obs_value, obs_weight, obs_count
):
    p = plan
    f32 = jnp.float32
    vmem = pl.BlockSpec(memory_space=pltpu.VMEM)
    params = pltpu.CompilerParams(vmem_limit_bytes=VMEM_LIMIT)
    var = background_var[0]
    packed = pl.pallas_call(
        functools.partial(pack_kernel, p),
        out_shape=jax.ShapeDtypeStruct((p.count * p.rows, LANES), f32),
        in_specs=[pl.BlockSpec(memory_space=pltpu.SMEM)] + [vmem] * 7,
        out_specs=vmem,
        scratch_shapes=[pltpu.VMEM(((p.vars + 3) * p.lev, p.lat, 15 * LANES), f32)],
        compiler_params=params,
        name="pack",
    )(
        obs_count.reshape(1, -1),
        obs_cell.reshape(1, -1),
        obs_value.reshape(1, -1),
        obs_weight.reshape(1, -1),
        advect_east[0],
        advect_north[0],
        diffusion[0],
        var,
    )
    received = lax.all_to_all(packed.reshape(-1, 2, LANES), ("tm", "tile"), 0, 0, tiled=True)
    received = received.reshape(-1, LANES)
    wide = pltpu.VMEM((p.wide * p.pitch, 2 * p.vars, LANES), f32)
    narrow = pltpu.VMEM((p.subs * p.area + 4 * p.vars, LANES), f32)
    both = pltpu.VMEM(((ITERS * p.subs + 1) * p.area, LANES), f32)
    back = pl.pallas_call(
        functools.partial(chain_kernel, p),
        out_shape=jax.ShapeDtypeStruct((p.count * p.lat * 3, LANES), f32),
        in_specs=[vmem],
        out_specs=vmem,
        scratch_shapes=[wide] * 6
        + [
            pltpu.VMEM((p.wide * p.nlat * 2 * p.vars, LANES), f32),
            pltpu.VMEM((p.pitch * 2 * p.vars, LANES), f32),
        ]
        + [narrow] * 5
        + [
            pltpu.VMEM((p.subs * p.area, LANES), f32),
            both,
            both,
            pltpu.VMEM((p.area + 4 * p.vars, LANES), f32),
            pltpu.VMEM((9, p.count, p.tiles * p.slots), f32),
        ],
        compiler_params=params,
        name="chains",
    )(received)
    back = back.reshape(-1, 4, LANES)
    returned = lax.all_to_all(back, ("tm", "tile"), 0, 0, tiled=True)
    returned = returned.reshape(-1, LANES)
    increment = pl.pallas_call(
        functools.partial(finish_kernel, p),
        out_shape=jax.ShapeDtypeStruct(var.shape, f32),
        in_specs=[vmem] * 2,
        out_specs=vmem,
        compiler_params=params,
        name="finish",
    )(returned, var)
    return increment[None]


def solution(mesh):
    def run(*args):
        plan = Plan(mesh.shape, args[3].shape, args[4].shape)
        work = functools.partial(transposed, plan) if plan.fits() else per_device
        return jax.shard_map(
            work,
            mesh=mesh,
            in_specs=(
                P("tm", None, "tile", None),
                P("tm", None, "tile", None),
                P("tm", None, "tile", None),
                P("tm", None, None, "tile", None),
                P("tm", "tile", None),
                P("tm", "tile", None),
                P("tm", "tile", None),
                P("tm", "tile", None),
            ),
            out_specs=P("tm", None, None, "tile", None),
            check_vma=False,
        )(*args)

    return run
```

```python
import functools

import jax
import jax.numpy as jnp
from jax import lax
from jax.experimental import pallas as pl
from jax.experimental.pallas import tpu as pltpu
from jax.sharding import PartitionSpec as P

STEPS = 2
ITERS = 2
CHAINS = 3
LANES = 128
LAG = 12
VMEM_LIMIT = 48 * 1024 * 1024


def padded(block, sides, width):
    for axis, dim in sides:
        count = lax.axis_size(axis)
        forward = [(i, i + 1) for i in range(count - 1)]
        backward = [(target, source) for source, target in forward]
        low = lax.ppermute(
            lax.slice_in_dim(block, block.shape[dim] - width, None, axis=dim), axis, forward
        )
        high = lax.ppermute(lax.slice_in_dim(block, 0, width, axis=dim), axis, backward)
        block = jnp.concatenate([low, block, high], axis=dim)
    return block


def shifted(value, axis, steps):
    count = lax.axis_size(axis)
    first, last = (max(0, -steps), min(count, count - steps))
    return lax.ppermute(value, axis, [(source, source + steps) for source in range(first, last)])


def apply_step(field, coef, adjoint):
    east_c = coef[0]
    north_c = coef[1]
    diff_c = coef[2]
    if adjoint:
        to_east = (diff_c - 0.5 * east_c) * field
        to_west = (diff_c + 0.5 * east_c) * field
        to_north = (diff_c - 0.5 * north_c) * field
        to_south = (diff_c + 0.5 * north_c) * field
        middle = (1.0 - 4.0 * diff_c[:, 1:-1]) * field[:, :, 1:-1]
        return (
            middle
            + jnp.roll(to_east[:, :, 1:-1], 1, axis=-1)
            + jnp.roll(to_west[:, :, 1:-1], -1, axis=-1)
            + to_north[:, :, :-2]
            + to_south[:, :, 2:]
        )
    inner = field[:, :, 1:-1]
    diff_in = diff_c[:, 1:-1]
    east_in = east_c[:, 1:-1]
    north_in = north_c[:, 1:-1]
    return (
        (1.0 - 4.0 * diff_in) * inner
        + (diff_in - 0.5 * east_in) * jnp.roll(inner, -1, axis=-1)
        + (diff_in + 0.5 * east_in) * jnp.roll(inner, 1, axis=-1)
        + (diff_in - 0.5 * north_in) * field[:, :, 2:]
        + (diff_in + 0.5 * north_in) * field[:, :, :-2]
    )


def advance(field, coef, adjoint):
    for repeat in range(STEPS):
        extended = padded(field, (("tile", 2),), 1)
        field = apply_step(extended, coef, adjoint)
    return field


def per_device(
    advect_east, advect_north, diffusion, background_var, obs_cell, obs_value, obs_weight, obs_count
):
    windows_count = lax.axis_size("tm")
    tiles = lax.axis_size("tile")
    coefs = jnp.stack([advect_east[0], advect_north[0], diffusion[0]])
    coef_ext = padded(coefs, (("tile", 2),), 1)
    cells = obs_cell.reshape(tiles, -1)
    slot_count = cells.shape[1]
    live = jnp.arange(slot_count, dtype=jnp.int32)[None, :] < obs_count.reshape(tiles)[:, None]
    masked = obs_weight.reshape(tiles, -1) * live.astype(jnp.float32)
    received = lax.all_to_all(
        jnp.stack([obs_value.reshape(tiles, -1), masked]),
        "tile",
        split_axis=1,
        concat_axis=1,
        tiled=True,
    )
    received_cells = lax.all_to_all(cells, "tile", split_axis=0, concat_axis=0, tiled=True)
    departures = received[0].reshape(-1)
    obs_weights = received[1].reshape(-1)
    flat_cells = received_cells.reshape(-1)
    local_var = background_var[0]
    state_shape = local_var.shape
    cell_total = state_shape[0] * state_shape[1] * state_shape[2] * state_shape[3]
    increment = jnp.zeros(state_shape, jnp.float32)
    for iteration in range(ITERS):
        if iteration == 0:
            innov = obs_weights * (0.0 - departures)
        else:
            forward_carried = advance(increment, coef_ext, False)
            for forward_window in range(windows_count - 1):
                forward_incoming = shifted(forward_carried, "tm", 1)
                forward_carried = advance(forward_incoming + increment, coef_ext, False)
            innov = obs_weights * (
                jnp.take(forward_carried.reshape(cell_total), flat_cells, axis=0) - departures
            )
        gridded = jnp.zeros((cell_total,), jnp.float32).at[flat_cells].add(innov)
        source = gridded.reshape(state_shape)
        carried = advance(source, coef_ext, True)
        for window in range(windows_count - 1):
            incoming = shifted(carried, "tm", -1)
            carried = advance(incoming + source, coef_ext, True)
        increment = increment - 0.5 * (increment + local_var * carried)
    return increment[None]


class Plan:
    def __init__(self, mesh_shape, var_shape, slot_shape):
        self.subs, self.tiles = mesh_shape["tm"], mesh_shape["tile"]
        self.count = self.subs * self.tiles
        _, self.vars, self.lev, self.nlat, self.lon = var_shape
        self.lat = self.nlat // self.tiles
        self.slots = slot_shape[2] // self.tiles
        self.cols = self.count // self.lev
        self.width = self.lon // self.cols
        self.half = self.width // 2
        self.halo = CHAINS * STEPS * self.subs
        self.margin = (LANES - self.width) // 2
        self.extra = self.halo - self.margin
        self.span = self.width + 2 * self.halo
        self.coef_row = self.lat * self.vars
        self.obs_row = self.coef_row + 3 * self.lat
        self.rows = self.obs_row + 6
        self.pitch = self.nlat + STEPS
        self.wide = -(-self.extra // STEPS)
        self.area = self.nlat * self.vars

    def borrows(self, k):
        return (CHAINS - 1) * STEPS * self.subs + STEPS * (k + 1) > self.margin

    def fits(self):
        if self.count % self.lev or self.lon % self.cols or self.width % 2:
            return False
        for k in range(self.subs):
            spare = self.margin - STEPS * (2 * self.subs - k)
            if spare < 0 or (self.borrows(k) and spare < self.extra):
                return False
        return (
            self.half + 2 * self.halo <= LANES
            and 0 <= self.extra <= 16
            and self.vars == 4
            and self.lat % 2 == 0
            and 0 < self.wide < self.subs
            and self.tiles == 8
            and self.slots & (self.slots - 1) == 0
            and self.slots * self.tiles == 2 * LANES
            and self.width + 2 * self.margin == LANES
            and self.width * self.vars <= 3 * LANES
            and self.count * self.rows % 8 == 0
            and self.rows % 2 == 0
        )


def pack_kernel(
    plan, count_ref, cell_ref, value_ref, weight_ref, east_ref, north_ref, diff_ref, var_ref, out_ref, wide
):
    p = plan
    pad = 2 * LANES
    right = wide.shape[-1] - pad - p.lon
    per_level = p.vars + 3

    def fill(z, carry):
        for v in range(per_level):
            field = var_ref[v, z] if v < p.vars else (east_ref, north_ref, diff_ref)[v - p.vars][z]
            at = z * per_level + v
            wide[at, :, pad : pad + p.lon] = field
            wide[at, :, :pad] = field[:, p.lon - pad :]
            wide[at, :, pad + p.lon :] = field[:, :right]
        return carry

    lax.fori_loop(0, p.lev, fill, 0)

    lane = lax.broadcasted_iota(jnp.int32, (1, p.tiles * p.slots), 1)
    filled = jnp.zeros_like(lane)
    for t in range(p.tiles):
        filled = jnp.where(lane >= t * p.slots, count_ref[0, t], filled)
    weight = jnp.where((lane & (p.slots - 1)) < filled, weight_ref[...], 0.0)
    obs = []
    for x in (weight, weight * value_ref[...], cell_ref[...].astype(jnp.float32)):
        obs += [x[:, :LANES], x[:, LANES:]]
    obs = jnp.concatenate(obs, axis=0)
    lanes = lax.broadcasted_iota(jnp.int32, (p.lat, LANES), 1)
    borrows = jnp.where(p.borrows(lax.axis_index("tm")), p.extra, 0)

    def blocks(z, carry):
        for j in range(p.cols):
            first = pad + j * p.width - p.margin
            tile, low = divmod(first, LANES)

            def moved(a, t):
                x = wide[z * per_level + a, :, t * LANES : (t + 1) * LANES]
                return pltpu.roll(x, LANES - low, 1)

            base = (z * p.cols + j) * p.rows
            for v in range(p.vars):
                piece = jnp.where(lanes < LANES - low, moved(v, tile), moved(v, tile + 1))
                if v < 3:
                    here, after = moved(p.vars + v, tile), moved(p.vars + v, tile + 1)
                    rows = pl.ds(base + p.coef_row + v * p.lat, p.lat)
                    out_ref[rows, :] = jnp.where(lanes < LANES - low, here, after)
                    if low < p.extra:
                        here = jnp.where(lanes < LANES - low, moved(p.vars + v, tile - 1), here)
                    if low + p.extra > LANES:
                        after = jnp.where(lanes < LANES - low, after, moved(p.vars + v, tile + 2))
                    piece = jnp.where(lanes < borrows, after, piece)
                    piece = jnp.where(lanes >= LANES - borrows, here, piece)
                out_ref[pl.ds(base + v, p.lat, stride=p.vars), :] = piece
            out_ref[pl.ds(base + p.obs_row, 6), :] = obs
        return carry

    lax.fori_loop(0, p.lev, blocks, 0)


class Stores:
    def __init__(self):
        self.held = []

    def put(self, ref, at, value):
        self.held.append((ref, at, value))

    def flush(self):
        for ref, at, value in self.held:
            ref[at] = value
        self.held = []


def looped(count, unroll, body):
    def many(i, carry):
        stores = Stores()
        for u in range(unroll):
            body(i * unroll + u, stores)
        stores.flush()
        return carry

    lax.fori_loop(0, count // unroll, many, 0)


def swap_blocks(x, slots):
    size = x.shape[0]
    sub = lax.broadcasted_iota(jnp.int32, x.shape, 0)
    block = lax.broadcasted_iota(jnp.int32, x.shape, 1) >> (slots.bit_length() - 1)
    out = x
    for d in range(1, size):
        moved = pltpu.roll(pltpu.roll(x, size - d, 0), d * slots, 1)
        out = jnp.where(block == ((sub + d) & (size - 1)), moved, out)
    return out


def spread(a, b, count):
    return (
        jnp.concatenate([a[:count], b[:count]], axis=0),
        jnp.concatenate([a[count:], b[count:]], axis=0),
    )


def chain_kernel(
    plan,
    recv_ref,
    out_ref,
    mid_w,
    east_w,
    west_w,
    north_w,
    south_w,
    source_w,
    result_w,
    carried_w,
    mid_c,
    east_c,
    west_c,
    north_c,
    south_c,
    weight_g,
    innov,
    results,
    carried,
    passed,
    obs_tab,
):
    p = plan
    f32 = jnp.float32
    me = lax.axis_index("tm") * p.tiles + lax.axis_index("tile")
    level = (me // p.cols).astype(f32)
    origin = ((me % p.cols) * p.width - p.halo).astype(f32)
    two = 2 * p.vars
    shape = (two, LANES)
    sub = lax.broadcasted_iota(jnp.int32, shape, 0)
    lane = lax.broadcasted_iota(jnp.int32, shape, 1)
    lower = sub < p.vars
    in_half = lane < p.margin + p.half
    n = p.nlat
    pitch = p.pitch
    area = p.area
    whole = p.subs * area
    nothing = ITERS * whole
    lead = two
    low_wide = p.subs - p.wide
    zero = jnp.zeros(shape, f32)

    def rows8(start):
        return pl.ds(pl.multiple_of(start, two), two)

    def clear(ref, start, count):
        def body(i, carry):
            for u in range(8):
                ref[rows8(start + (i * 8 + u) * two), :] = zero
            return carry

        lax.fori_loop(0, count // (8 * two), body, 0)

    clear(innov, nothing, area)
    clear(results, nothing, area)
    for ref in (mid_c, east_c, west_c, north_c, south_c, carried, passed):
        ref[:lead, :] = zero
        ref[ref.shape[0] - lead :, :] = zero
    for k in range(p.wide):
        for l in range(n, pitch):
            for ref in (mid_w, east_w, west_w, north_w, south_w, source_w):
                ref[k * pitch + l] = zero
    for l in range(n, pitch):
        carried_w[l * two : (l + 1) * two, :] = zero

    def observe(k, stores):
        raw = []
        for i in range(6):
            raw.append(recv_ref[pl.ds(k * p.tiles * p.rows + p.obs_row + i, p.tiles, stride=p.rows), :])
        w, wy, cell = (jnp.concatenate(raw[2 * i : 2 * i + 2], axis=1) for i in range(3))
        w, wy, cell = (swap_blocks(x, p.slots) for x in (w, wy, cell))
        row = jnp.floor((cell + 0.5) * (1.0 / p.lon))
        lon = cell - row * p.lon
        group = jnp.floor((row + 0.5) * (1.0 / p.lat))
        lat = row - group * p.lat
        var = jnp.floor((group + 0.5) * (1.0 / p.lev))
        lev = group - var * p.lev
        at = lon - origin
        at = jnp.where(at < 0, at + p.lon, at)
        at = jnp.where(at >= p.lon, at - p.lon, at)
        place = at - p.extra
        here = (lev == level) & (at < p.span)
        main = here & (place >= 0) & (place < LANES)
        outside = here & ~main
        around = jnp.where(place < 0, place + LANES, place - LANES)
        rows = pl.ds(k * p.tiles, p.tiles)
        stores.put(obs_tab, (0, rows), lat * p.vars + var)
        stores.put(obs_tab, (1, rows), jnp.where(main, place, -1.0))
        stores.put(obs_tab, (2, rows), jnp.where(outside, around, -1.0))
        for i, x in ((3, w), (6, -wy)):
            one = x.astype(jnp.bfloat16).astype(f32)
            two = (x - one).astype(jnp.bfloat16).astype(f32)
            stores.put(obs_tab, (i, rows), one)
            stores.put(obs_tab, (i + 1, rows), two)
            stores.put(obs_tab, (i + 2, rows), x - one - two)

    looped(p.subs, 1, observe)

    n_rows = p.lat * p.vars
    slots = p.tiles * p.slots
    row_id = lax.broadcasted_iota(jnp.int32, (n_rows, slots), 0).astype(f32)
    lane_id = lax.broadcasted_iota(jnp.int32, (LANES, slots), 0).astype(f32)
    row_lane = lax.broadcasted_iota(jnp.int32, (n_rows, LANES), 1)

    def wide_tile(kt):
        return jnp.maximum(kt - low_wide * p.tiles, kt % p.tiles)

    def row_of(kt):
        return kt * p.lat + kt // p.tiles * STEPS

    def grid(kt, stores):
        def entry(i):
            return obs_tab[i, pl.ds(kt, 1), :]

        def factor(rows, i):
            return jnp.where(lane_id[rows] == entry(i), 1.0, 0.0).astype(jnp.bfloat16)

        def product(first, right):
            left = [jnp.where(match, entry(first + q), 0.0).astype(jnp.bfloat16) for q in range(3)]
            left = jnp.concatenate(left, axis=0)
            full = lax.dot_general(left, right, (((1,), (1,)), ((), ())), preferred_element_type=f32)
            parts = [full[q * n_rows : (q + 1) * n_rows] for q in range(3)]
            return parts[0] + (parts[1] + parts[2])

        match = row_id == entry(0)
        main = factor(slice(0, LANES), 1)
        ends = [factor(slice(0, 16), 2), jnp.zeros((LANES - 32, slots), jnp.bfloat16), factor(slice(LANES - 16, LANES), 2)]
        at = (pl.ds(pl.multiple_of(kt * n_rows, two), n_rows),)
        stores.put(weight_g, at, product(3, main))
        summed = product(6, jnp.concatenate([main] + ends, axis=0))
        inside, outside = summed[:, :LANES], summed[:, LANES:]
        stores.put(innov, at, inside)
        left = jnp.where(row_lane >= LANES - p.extra, outside, inside)
        right = jnp.where(row_lane < p.extra, outside, inside)
        tile = wide_tile(kt)
        for pair in range(p.lat // 2):
            rows = slice(two * pair, two * (pair + 1))
            one, other = spread(left[rows], right[rows], p.vars)
            stores.put(source_w, row_of(tile) + 2 * pair, one)
            stores.put(source_w, row_of(tile) + 2 * pair + 1, other)

    def derive(got):
        east, north, diff = got
        east = 0.5 * east
        north = 0.5 * north
        return 1.0 - 4.0 * diff, diff - east, diff + east, diff - north, diff + north

    def one_row(at):
        return jnp.broadcast_to(recv_ref[pl.ds(at, 1), :], shape)

    edge_mask = (lower & (lane >= LANES - p.extra)) | (~lower & (lane < p.extra))

    def widen(kt, stores):
        base = kt * p.rows
        for l in range(p.lat):
            got = []
            for c in range(3):
                main = one_row(base + p.coef_row + c * p.lat + l)
                got.append(jnp.where(edge_mask, one_row(base + l * p.vars + c), main))
            for ref, value in zip((mid_w, east_w, west_w, north_w, south_w), derive(got)):
                stores.put(ref, row_of(wide_tile(kt)) + l, value)

    def double(kt, stores):
        base = kt * p.rows + p.coef_row
        for l in range(0, p.lat, 2):
            got = []
            for c in range(3):
                at = base + c * p.lat + l
                got.append(jnp.where(lower, one_row(at), one_row(at + 1)))
            at = rows8(lead + kt * n_rows + l * p.vars)
            for ref, value in zip((mid_c, east_c, west_c, north_c, south_c), derive(got)):
                stores.put(ref, (at,), value)

    def prepare(kt, stores):
        grid(kt, stores)
        double(kt, stores)
        widen(kt, stores)

    looped(p.count, 4, prepare)

    def wide_step(i, carry):
        k = p.wide - 1 - i // STEPS
        base = k * pitch
        starts = (i % STEPS == 0).astype(f32)
        stores = Stores()

        def terms(l):
            x = carried_w[l * two : (l + 1) * two, :] + starts * source_w[base + l]
            at = base + l
            here = (
                mid_w[at] * x
                + pltpu.roll(east_w[at] * x, 1, 1)
                + pltpu.roll(west_w[at] * x, LANES - 1, 1)
            )
            return here, north_w[at] * x, south_w[at] * x

        below = zero
        here, north, _ = terms(0)
        for l in range(n):
            now, next_north, south = terms(l + 1)
            y = here + below + south
            here, below, north = now, north, next_north
            stores.put(carried_w, (slice(l * two, (l + 1) * two),), y)
            stores.put(result_w, (rows8((k * n + l) * two),), y)
        stores.flush()
        return carry

    def narrow(ref, at):
        mixed = ref[pl.ds(at + p.vars, two), :]
        left = jnp.where(lower, ref[pl.ds(at, two), :], mixed)
        right = jnp.where(lower, mixed, ref[pl.ds(at + two, two), :])
        return jnp.where(in_half, left, right)

    def narrow_results(i, stores):
        stores.put(results, (rows8(low_wide * area + i * two),), narrow(result_w, i * 2 * two))

    def narrow_carried(i, stores):
        value = narrow(carried_w, i * 2 * two) + innov[rows8((low_wide - 1) * area + i * two), :]
        stores.put(carried, (rows8(lead + i * two),), value)

    def begin_adjoint(i, stores):
        stores.put(carried, (rows8(lead + i * two),), innov[rows8(whole + (p.subs - 1) * area + i * two), :])

    def scaled(k, tile, q, at):
        var = recv_ref[pl.ds((k * p.tiles + tile) * p.rows + q * two, two), :]
        return 0.5 * (var * results[at, :])

    def begin_forward(tile, stores):
        for q in range(p.lat // 2):
            at = tile * n_rows + q * two
            stores.put(carried, (rows8(lead + at),), -scaled(0, tile, q, rows8(at)))

    def near(ref, base, at, shift):
        return ref[pl.ds(base + at + lead + shift * p.vars, two), :]

    def adjoint_at(base, ref, at):
        x = near(ref, 0, at, 0)
        return (
            near(mid_c, base, at, 0) * x
            + pltpu.roll(near(east_c, base, at, 0) * x, 1, 1)
            + pltpu.roll(near(west_c, base, at, 0) * x, LANES - 1, 1)
            + near(north_c, base, at, -1) * near(ref, 0, at, -1)
            + near(south_c, base, at, 1) * near(ref, 0, at, 1)
        )

    def forward_at(base, ref, at):
        x = near(ref, 0, at, 0)
        return (
            near(mid_c, base, at, 0) * x
            + near(east_c, base, at, 0) * pltpu.roll(x, LANES - 1, 1)
            + near(west_c, base, at, 0) * pltpu.roll(x, 1, 1)
            + near(north_c, base, at, 0) * near(ref, 0, at, 1)
            + near(south_c, base, at, 0) * near(ref, 0, at, -1)
        )

    def window(one, base, last):
        for at in range(0, area + LAG * two, two):
            if at < area:
                passed[lead + at : lead + at + two, :] = one(base, carried, at)
            at -= LAG * two
            if at >= 0:
                carried[lead + at : lead + at + two, :] = last(at, one(base, passed, at))

    def adjoint_window(i, phase):
        k = p.subs - 1 - i
        into = phase * whole + k * area
        source = jnp.where(k > 0, into - area, nothing)
        stores = Stores()

        def last(at, y):
            stores.put(results, (rows8(into + at),), y)
            return y + innov[rows8(source + at), :]

        window(adjoint_at, k * area, last)
        stores.flush()
        return phase

    def forward_window(k, carry):
        base = k * area
        source = jnp.where(k < p.subs - 1, base + area, nothing)
        later = jnp.minimum(k + 1, p.subs - 1)
        stores = Stores()

        def last(at, y):
            here = rows8(base + at)
            stores.put(innov, (rows8(whole + base + at),), weight_g[here, :] * y + innov[here, :])
            return y - scaled(later, at // n_rows, at % n_rows // two, rows8(source + at))

        window(forward_at, base, last)
        stores.flush()
        return carry

    def clear_wide(i, stores):
        stores.put(carried_w, (rows8(i * two),), zero)

    def iteration(phase, carry):
        @pl.when(phase == 0)
        def _():
            looped(n, 8, clear_wide)
            lax.fori_loop(0, p.wide * STEPS, wide_step, 0)
            looped(p.wide * n // 2, 12, narrow_results)
            looped(n // 2, 12, narrow_carried)

        @pl.when(phase > 0)
        def _():
            looped(n // 2, 12, begin_adjoint)

        lax.fori_loop(jnp.where(phase == 0, p.wide, 0), p.subs, adjoint_window, phase)

        @pl.when(phase < ITERS - 1)
        def _():
            looped(p.tiles, 2, begin_forward)
            lax.fori_loop(0, p.subs, forward_window, 0)

        return carry

    lax.fori_loop(0, ITERS, iteration, 0)

    own = slice(p.margin, p.margin + p.width)

    def join(kt, stores):
        cols = []
        for v in range(p.vars):
            at = kt * n_rows + v
            early = results[pl.ds(at, p.lat, stride=p.vars), :]
            late = results[pl.ds(whole + at, p.lat, stride=p.vars), :]
            cols.append((0.5 * early + late)[:, own])
        spare = 3 * LANES - p.vars * p.width
        line = jnp.concatenate(cols + [jnp.zeros((p.lat, spare), f32)], axis=1)
        for i in range(3):
            at = (pl.ds(kt * p.lat * 3 + i, p.lat, stride=3),)
            stores.put(out_ref, at, line[:, i * LANES : (i + 1) * LANES])

    looped(p.count, 4, join)


def finish_kernel(plan, recv_ref, var_ref, out_ref):
    p = plan

    def level(z, carry):
        for j in range(p.cols):
            start = (z * p.cols + j) * p.lat * 3
            rows = [recv_ref[pl.ds(start + i, p.lat, stride=3), :] for i in range(3)]
            for v in range(p.vars):
                at, end = v * p.width, (v + 1) * p.width
                col = j * p.width
                while at < end:
                    i, low = divmod(at, LANES)
                    size = min(end - at, LANES - low)
                    cols = slice(col, col + size)
                    scale = -0.5 * var_ref[v, z, :, cols]
                    out_ref[v, z, :, cols] = scale * rows[i][:, low : low + size]
                    at, col = at + size, col + size
        return carry

    lax.fori_loop(0, p.lev, level, 0)


def transposed(
    plan, advect_east, advect_north, diffusion, background_var, obs_cell, obs_value, obs_weight, obs_count
):
    p = plan
    f32 = jnp.float32
    vmem = pl.BlockSpec(memory_space=pltpu.VMEM)
    params = pltpu.CompilerParams(vmem_limit_bytes=VMEM_LIMIT)
    var = background_var[0]
    packed = pl.pallas_call(
        functools.partial(pack_kernel, p),
        out_shape=jax.ShapeDtypeStruct((p.count * p.rows, LANES), f32),
        in_specs=[pl.BlockSpec(memory_space=pltpu.SMEM)] + [vmem] * 7,
        out_specs=vmem,
        scratch_shapes=[pltpu.VMEM(((p.vars + 3) * p.lev, p.lat, 15 * LANES), f32)],
        compiler_params=params,
        name="pack",
    )(
        obs_count.reshape(1, -1),
        obs_cell.reshape(1, -1),
        obs_value.reshape(1, -1),
        obs_weight.reshape(1, -1),
        advect_east[0],
        advect_north[0],
        diffusion[0],
        var,
    )
    received = lax.all_to_all(packed.reshape(-1, 2, LANES), ("tm", "tile"), 0, 0, tiled=True)
    received = received.reshape(-1, LANES)
    wide = pltpu.VMEM((p.wide * p.pitch, 2 * p.vars, LANES), f32)
    narrow = pltpu.VMEM((p.subs * p.area + 4 * p.vars, LANES), f32)
    both = pltpu.VMEM(((ITERS * p.subs + 1) * p.area, LANES), f32)
    back = pl.pallas_call(
        functools.partial(chain_kernel, p),
        out_shape=jax.ShapeDtypeStruct((p.count * p.lat * 3, LANES), f32),
        in_specs=[vmem],
        out_specs=vmem,
        scratch_shapes=[wide] * 6
        + [
            pltpu.VMEM((p.wide * p.nlat * 2 * p.vars, LANES), f32),
            pltpu.VMEM((p.pitch * 2 * p.vars, LANES), f32),
        ]
        + [narrow] * 5
        + [
            pltpu.VMEM((p.subs * p.area, LANES), f32),
            both,
            both,
            pltpu.VMEM((p.area + 4 * p.vars, LANES), f32),
            pltpu.VMEM((p.area + 4 * p.vars, LANES), f32),
            pltpu.VMEM((9, p.count, p.tiles * p.slots), f32),
        ],
        compiler_params=params,
        name="chains",
    )(received)
    back = back.reshape(-1, 4, LANES)
    returned = lax.all_to_all(back, ("tm", "tile"), 0, 0, tiled=True)
    returned = returned.reshape(-1, LANES)
    increment = pl.pallas_call(
        functools.partial(finish_kernel, p),
        out_shape=jax.ShapeDtypeStruct(var.shape, f32),
        in_specs=[vmem] * 2,
        out_specs=vmem,
        compiler_params=params,
        name="finish",
    )(returned, var)
    return increment[None]


def solution(mesh):
    def run(*args):
        plan = Plan(mesh.shape, args[3].shape, args[4].shape)
        work = functools.partial(transposed, plan) if plan.fits() else per_device
        return jax.shard_map(
            work,
            mesh=mesh,
            in_specs=(
                P("tm", None, "tile", None),
                P("tm", None, "tile", None),
                P("tm", None, "tile", None),
                P("tm", None, None, "tile", None),
                P("tm", "tile", None),
                P("tm", "tile", None),
                P("tm", "tile", None),
                P("tm", "tile", None),
            ),
            out_specs=P("tm", None, None, "tile", None),
            check_vma=False,
        )(*args)

    return run
```

```python
import functools

import jax
import jax.numpy as jnp
from jax import lax
from jax.experimental import pallas as pl
from jax.experimental.pallas import tpu as pltpu
from jax.sharding import PartitionSpec as P

STEPS = 2
ITERS = 2
CHAINS = 3
LANES = 128
LAG = 12
PACK_LIMIT = 55 * 1024 * 1024
VMEM_LIMIT = 48 * 1024 * 1024


def padded(block, sides, width):
    for axis, dim in sides:
        count = lax.axis_size(axis)
        forward = [(i, i + 1) for i in range(count - 1)]
        backward = [(target, source) for source, target in forward]
        low = lax.ppermute(
            lax.slice_in_dim(block, block.shape[dim] - width, None, axis=dim), axis, forward
        )
        high = lax.ppermute(lax.slice_in_dim(block, 0, width, axis=dim), axis, backward)
        block = jnp.concatenate([low, block, high], axis=dim)
    return block


def shifted(value, axis, steps):
    count = lax.axis_size(axis)
    first, last = (max(0, -steps), min(count, count - steps))
    return lax.ppermute(value, axis, [(source, source + steps) for source in range(first, last)])


def apply_step(field, coef, adjoint):
    east_c = coef[0]
    north_c = coef[1]
    diff_c = coef[2]
    if adjoint:
        to_east = (diff_c - 0.5 * east_c) * field
        to_west = (diff_c + 0.5 * east_c) * field
        to_north = (diff_c - 0.5 * north_c) * field
        to_south = (diff_c + 0.5 * north_c) * field
        middle = (1.0 - 4.0 * diff_c[:, 1:-1]) * field[:, :, 1:-1]
        return (
            middle
            + jnp.roll(to_east[:, :, 1:-1], 1, axis=-1)
            + jnp.roll(to_west[:, :, 1:-1], -1, axis=-1)
            + to_north[:, :, :-2]
            + to_south[:, :, 2:]
        )
    inner = field[:, :, 1:-1]
    diff_in = diff_c[:, 1:-1]
    east_in = east_c[:, 1:-1]
    north_in = north_c[:, 1:-1]
    return (
        (1.0 - 4.0 * diff_in) * inner
        + (diff_in - 0.5 * east_in) * jnp.roll(inner, -1, axis=-1)
        + (diff_in + 0.5 * east_in) * jnp.roll(inner, 1, axis=-1)
        + (diff_in - 0.5 * north_in) * field[:, :, 2:]
        + (diff_in + 0.5 * north_in) * field[:, :, :-2]
    )


def advance(field, coef, adjoint):
    for repeat in range(STEPS):
        extended = padded(field, (("tile", 2),), 1)
        field = apply_step(extended, coef, adjoint)
    return field


def per_device(
    advect_east, advect_north, diffusion, background_var, obs_cell, obs_value, obs_weight, obs_count
):
    windows_count = lax.axis_size("tm")
    tiles = lax.axis_size("tile")
    coefs = jnp.stack([advect_east[0], advect_north[0], diffusion[0]])
    coef_ext = padded(coefs, (("tile", 2),), 1)
    cells = obs_cell.reshape(tiles, -1)
    slot_count = cells.shape[1]
    live = jnp.arange(slot_count, dtype=jnp.int32)[None, :] < obs_count.reshape(tiles)[:, None]
    masked = obs_weight.reshape(tiles, -1) * live.astype(jnp.float32)
    received = lax.all_to_all(
        jnp.stack([obs_value.reshape(tiles, -1), masked]),
        "tile",
        split_axis=1,
        concat_axis=1,
        tiled=True,
    )
    received_cells = lax.all_to_all(cells, "tile", split_axis=0, concat_axis=0, tiled=True)
    departures = received[0].reshape(-1)
    obs_weights = received[1].reshape(-1)
    flat_cells = received_cells.reshape(-1)
    local_var = background_var[0]
    state_shape = local_var.shape
    cell_total = state_shape[0] * state_shape[1] * state_shape[2] * state_shape[3]
    increment = jnp.zeros(state_shape, jnp.float32)
    for iteration in range(ITERS):
        if iteration == 0:
            innov = obs_weights * (0.0 - departures)
        else:
            forward_carried = advance(increment, coef_ext, False)
            for forward_window in range(windows_count - 1):
                forward_incoming = shifted(forward_carried, "tm", 1)
                forward_carried = advance(forward_incoming + increment, coef_ext, False)
            innov = obs_weights * (
                jnp.take(forward_carried.reshape(cell_total), flat_cells, axis=0) - departures
            )
        gridded = jnp.zeros((cell_total,), jnp.float32).at[flat_cells].add(innov)
        source = gridded.reshape(state_shape)
        carried = advance(source, coef_ext, True)
        for window in range(windows_count - 1):
            incoming = shifted(carried, "tm", -1)
            carried = advance(incoming + source, coef_ext, True)
        increment = increment - 0.5 * (increment + local_var * carried)
    return increment[None]


class Plan:
    def __init__(self, mesh_shape, var_shape, slot_shape):
        self.subs, self.tiles = mesh_shape["tm"], mesh_shape["tile"]
        self.count = self.subs * self.tiles
        _, self.vars, self.lev, self.nlat, self.lon = var_shape
        self.lat = self.nlat // self.tiles
        self.slots = slot_shape[2] // self.tiles
        self.cols = self.count // self.lev
        self.width = self.lon // self.cols
        self.half = self.width // 2
        self.halo = CHAINS * STEPS * self.subs
        self.margin = (LANES - self.width) // 2
        self.extra = self.halo - self.margin
        self.span = self.width + 2 * self.halo
        self.coef_row = self.lat * self.vars
        self.obs_row = self.coef_row + 3 * self.lat
        self.rows = self.obs_row + 6
        self.pitch = self.nlat + STEPS
        self.wide = -(-self.extra // STEPS)
        self.area = self.nlat * self.vars

    def borrows(self, k):
        return (CHAINS - 1) * STEPS * self.subs + STEPS * (k + 1) > self.margin

    def fits(self):
        if self.count % self.lev or self.lon % self.cols or self.width % 2:
            return False
        for k in range(self.subs):
            spare = self.margin - STEPS * (2 * self.subs - k)
            if spare < 0 or (self.borrows(k) and spare < self.extra):
                return False
        return (
            self.half + 2 * self.halo <= LANES
            and 0 <= self.extra <= 16
            and self.vars == 4
            and self.lat % 2 == 0
            and 0 < self.wide < self.subs
            and self.tiles == 8
            and self.slots & (self.slots - 1) == 0
            and self.slots * self.tiles == 2 * LANES
            and self.width + 2 * self.margin == LANES
            and self.width * self.vars <= 3 * LANES
            and self.count * self.rows % 8 == 0
            and self.rows % 2 == 0
        )


def fetch(sources, targets, sems):
    copies = [pltpu.make_async_copy(x, y, sems.at[i]) for i, (x, y) in enumerate(zip(sources, targets))]
    for copy in copies:
        copy.start()
    return copies


def pack_kernel(plan, *refs):
    p = plan
    sources, (out_hbm, wide, out_ref), targets, sems, out_sems = refs[:8], refs[8:11], refs[11:19], refs[19], refs[20]
    copies = fetch(sources, targets, sems)
    count_ref, cell_ref, value_ref, weight_ref, east_ref, north_ref, diff_ref, var_ref = targets
    for copy in copies:
        copy.wait()
    pad = 2 * LANES
    right = wide.shape[-1] - pad - p.lon
    per_level = p.vars + 3

    def fill(v, field):
        for low in range(0, p.lon, LANES):
            size = min(LANES, p.lon - low)
            both = jnp.swapaxes(field[:, :, low : low + size], 0, 1)
            for z in range(p.lev):
                wide[z * per_level + v, :, pad + low : pad + low + size] = both[z]

    def fill_var(v, carry):
        fill(v, var_ref.at[v])
        return carry

    lax.fori_loop(0, p.vars, fill_var, 0)
    for c, ref in enumerate((east_ref, north_ref, diff_ref)):
        fill(p.vars + c, ref)

    def wrap(at, carry):
        wide[at, :, :pad] = wide[at, :, p.lon : p.lon + pad]
        wide[at, :, pad + p.lon :] = wide[at, :, pad : pad + right]
        return carry

    lax.fori_loop(0, p.lev * per_level, wrap, 0)

    lane = lax.broadcasted_iota(jnp.int32, (1, p.tiles * p.slots), 1)
    filled = jnp.zeros_like(lane)
    for t in range(p.tiles):
        filled = jnp.where(lane >= t * p.slots, jnp.broadcast_to(count_ref[:, t : t + 1], lane.shape), filled)
    weight = jnp.where((lane & (p.slots - 1)) < filled, weight_ref[...], 0.0)
    obs = []
    for x in (weight, weight * value_ref[...], cell_ref[...].astype(jnp.float32)):
        obs += [x[:, :LANES], x[:, LANES:]]
    obs = jnp.concatenate(obs, axis=0)
    lanes = lax.broadcasted_iota(jnp.int32, (p.lat, LANES), 1)
    borrows = jnp.where(p.borrows(lax.axis_index("tm")), p.extra, 0)

    def blocks(z, carry):
        for j in range(p.cols):
            first = pad + j * p.width - p.margin
            tile, low = divmod(first, LANES)

            def moved(a, t):
                x = wide[z * per_level + a, :, t * LANES : (t + 1) * LANES]
                return pltpu.roll(x, LANES - low, 1)

            base = (z * p.cols + j) * p.rows
            for v in range(p.vars):
                piece = jnp.where(lanes < LANES - low, moved(v, tile), moved(v, tile + 1))
                if v < 3:
                    here, after = moved(p.vars + v, tile), moved(p.vars + v, tile + 1)
                    rows = pl.ds(base + p.coef_row + v * p.lat, p.lat)
                    out_ref[rows, :] = jnp.where(lanes < LANES - low, here, after)
                    if low < p.extra:
                        here = jnp.where(lanes < LANES - low, moved(p.vars + v, tile - 1), here)
                    if low + p.extra > LANES:
                        after = jnp.where(lanes < LANES - low, after, moved(p.vars + v, tile + 2))
                    piece = jnp.where(lanes < borrows, after, piece)
                    piece = jnp.where(lanes >= LANES - borrows, here, piece)
                out_ref[pl.ds(base + v, p.lat, stride=p.vars), :] = piece
            out_ref[pl.ds(base + p.obs_row, 6), :] = obs
        leave(z).start()
        return carry

    def leave(z):
        count = p.cols * p.rows
        rows = pl.ds(pl.multiple_of(z * count, 8), count)
        return pltpu.make_async_copy(out_ref.at[rows, :], out_hbm.at[rows, :], out_sems.at[z])

    lax.fori_loop(0, p.lev, blocks, 0)
    for z in range(p.lev):
        leave(z).wait()


class Stores:
    def __init__(self):
        self.held = []

    def put(self, ref, at, value):
        self.held.append((ref, at, value))

    def flush(self):
        for ref, at, value in self.held:
            ref[at] = value
        self.held = []


def looped(count, unroll, body):
    def many(i, carry):
        stores = Stores()
        for u in range(unroll):
            body(i * unroll + u, stores)
        stores.flush()
        return carry

    lax.fori_loop(0, count // unroll, many, 0)


def swap_blocks(x, slots):
    size = x.shape[0]
    sub = lax.broadcasted_iota(jnp.int32, x.shape, 0)
    block = lax.broadcasted_iota(jnp.int32, x.shape, 1) >> (slots.bit_length() - 1)
    out = x
    for d in range(1, size):
        moved = pltpu.roll(pltpu.roll(x, size - d, 0), d * slots, 1)
        out = jnp.where(block == ((sub + d) & (size - 1)), moved, out)
    return out


def spread(a, b, count):
    return (
        jnp.concatenate([a[:count], b[:count]], axis=0),
        jnp.concatenate([a[count:], b[count:]], axis=0),
    )


def chain_kernel(
    plan,
    recv_ref,
    out_ref,
    mid_w,
    east_w,
    west_w,
    north_w,
    south_w,
    source_w,
    result_w,
    carried_w,
    mid_c,
    east_c,
    west_c,
    north_c,
    south_c,
    weight_g,
    innov,
    results,
    carried,
    passed,
    obs_tab,
):
    p = plan
    f32 = jnp.float32
    me = lax.axis_index("tm") * p.tiles + lax.axis_index("tile")
    level = (me // p.cols).astype(f32)
    origin = ((me % p.cols) * p.width - p.halo).astype(f32)
    two = 2 * p.vars
    shape = (two, LANES)
    sub = lax.broadcasted_iota(jnp.int32, shape, 0)
    lane = lax.broadcasted_iota(jnp.int32, shape, 1)
    lower = sub < p.vars
    in_half = lane < p.margin + p.half
    n = p.nlat
    pitch = p.pitch
    area = p.area
    whole = p.subs * area
    nothing = ITERS * whole
    lead = two
    low_wide = p.subs - p.wide
    zero = jnp.zeros(shape, f32)

    def rows8(start):
        return pl.ds(pl.multiple_of(start, two), two)

    def clear(ref, start, count):
        def body(i, carry):
            for u in range(8):
                ref[rows8(start + (i * 8 + u) * two), :] = zero
            return carry

        lax.fori_loop(0, count // (8 * two), body, 0)

    clear(innov, nothing, area)
    clear(results, nothing, area)
    for ref in (mid_c, east_c, west_c, north_c, south_c, carried, passed):
        ref[:lead, :] = zero
        ref[ref.shape[0] - lead :, :] = zero
    for k in range(p.wide):
        for l in range(n, pitch):
            for ref in (mid_w, east_w, west_w, north_w, south_w, source_w):
                ref[k * pitch + l] = zero
    for l in range(n, pitch):
        carried_w[l * two : (l + 1) * two, :] = zero

    def observe(k, stores):
        raw = []
        for i in range(6):
            raw.append(recv_ref[pl.ds(k * p.tiles * p.rows + p.obs_row + i, p.tiles, stride=p.rows), :])
        w, wy, cell = (jnp.concatenate(raw[2 * i : 2 * i + 2], axis=1) for i in range(3))
        w, wy, cell = (swap_blocks(x, p.slots) for x in (w, wy, cell))
        row = jnp.floor((cell + 0.5) * (1.0 / p.lon))
        lon = cell - row * p.lon
        group = jnp.floor((row + 0.5) * (1.0 / p.lat))
        lat = row - group * p.lat
        var = jnp.floor((group + 0.5) * (1.0 / p.lev))
        lev = group - var * p.lev
        at = lon - origin
        at = jnp.where(at < 0, at + p.lon, at)
        at = jnp.where(at >= p.lon, at - p.lon, at)
        place = at - p.extra
        here = (lev == level) & (at < p.span)
        main = here & (place >= 0) & (place < LANES)
        outside = here & ~main
        around = jnp.where(place < 0, place + LANES, place - LANES)
        rows = pl.ds(k * p.tiles, p.tiles)
        stores.put(obs_tab, (0, rows), lat * p.vars + var)
        stores.put(obs_tab, (1, rows), jnp.where(main, place, -1.0))
        stores.put(obs_tab, (2, rows), jnp.where(outside, around, -1.0))
        for i, x in ((3, w), (6, -wy)):
            one = x.astype(jnp.bfloat16).astype(f32)
            two = (x - one).astype(jnp.bfloat16).astype(f32)
            stores.put(obs_tab, (i, rows), one)
            stores.put(obs_tab, (i + 1, rows), two)
            stores.put(obs_tab, (i + 2, rows), x - one - two)

    looped(p.subs, 1, observe)

    n_rows = p.lat * p.vars
    slots = p.tiles * p.slots
    row_id = lax.broadcasted_iota(jnp.int32, (n_rows, slots), 0).astype(f32)
    lane_id = lax.broadcasted_iota(jnp.int32, (LANES, slots), 0).astype(f32)
    row_lane = lax.broadcasted_iota(jnp.int32, (n_rows, LANES), 1)

    def wide_tile(kt):
        return jnp.maximum(kt - low_wide * p.tiles, kt % p.tiles)

    def row_of(kt):
        return kt * p.lat + kt // p.tiles * STEPS

    def grid(kt, stores):
        def entry(i):
            return obs_tab[i, pl.ds(kt, 1), :]

        def factor(rows, i):
            return jnp.where(lane_id[rows] == entry(i), 1.0, 0.0).astype(jnp.bfloat16)

        def product(first, right):
            left = [jnp.where(match, entry(first + q), 0.0).astype(jnp.bfloat16) for q in range(3)]
            left = jnp.concatenate(left, axis=0)
            full = lax.dot_general(left, right, (((1,), (1,)), ((), ())), preferred_element_type=f32)
            parts = [full[q * n_rows : (q + 1) * n_rows] for q in range(3)]
            return parts[0] + (parts[1] + parts[2])

        match = row_id == entry(0)
        main = factor(slice(0, LANES), 1)
        ends = [factor(slice(0, 16), 2), jnp.zeros((LANES - 32, slots), jnp.bfloat16), factor(slice(LANES - 16, LANES), 2)]
        at = (pl.ds(pl.multiple_of(kt * n_rows, two), n_rows),)
        stores.put(weight_g, at, product(3, main))
        summed = product(6, jnp.concatenate([main] + ends, axis=0))
        inside, outside = summed[:, :LANES], summed[:, LANES:]
        stores.put(innov, at, inside)
        left = jnp.where(row_lane >= LANES - p.extra, outside, inside)
        right = jnp.where(row_lane < p.extra, outside, inside)
        tile = wide_tile(kt)
        for pair in range(p.lat // 2):
            rows = slice(two * pair, two * (pair + 1))
            one, other = spread(left[rows], right[rows], p.vars)
            stores.put(source_w, row_of(tile) + 2 * pair, one)
            stores.put(source_w, row_of(tile) + 2 * pair + 1, other)

    def derive(got):
        east, north, diff = got
        east = 0.5 * east
        north = 0.5 * north
        return 1.0 - 4.0 * diff, diff - east, diff + east, diff - north, diff + north

    def one_row(at):
        return jnp.broadcast_to(recv_ref[pl.ds(at, 1), :], shape)

    edge_mask = (lower & (lane >= LANES - p.extra)) | (~lower & (lane < p.extra))

    def widen(kt, stores):
        base = kt * p.rows
        for l in range(p.lat):
            got = []
            for c in range(3):
                main = one_row(base + p.coef_row + c * p.lat + l)
                got.append(jnp.where(edge_mask, one_row(base + l * p.vars + c), main))
            for ref, value in zip((mid_w, east_w, west_w, north_w, south_w), derive(got)):
                stores.put(ref, row_of(wide_tile(kt)) + l, value)

    def double(kt, stores):
        base = kt * p.rows + p.coef_row
        for l in range(0, p.lat, 2):
            got = []
            for c in range(3):
                at = base + c * p.lat + l
                got.append(jnp.where(lower, one_row(at), one_row(at + 1)))
            at = rows8(lead + kt * n_rows + l * p.vars)
            for ref, value in zip((mid_c, east_c, west_c, north_c, south_c), derive(got)):
                stores.put(ref, (at,), value)

    def prepare(kt, stores):
        grid(kt, stores)
        double(kt, stores)
        widen(kt, stores)

    looped(p.count, 4, prepare)

    def wide_step(i, carry):
        k = p.wide - 1 - i // STEPS
        base = k * pitch
        starts = (i % STEPS == 0).astype(f32)
        stores = Stores()

        def terms(l):
            x = carried_w[l * two : (l + 1) * two, :] + starts * source_w[base + l]
            at = base + l
            here = (
                mid_w[at] * x
                + pltpu.roll(east_w[at] * x, 1, 1)
                + pltpu.roll(west_w[at] * x, LANES - 1, 1)
            )
            return here, north_w[at] * x, south_w[at] * x

        below = zero
        here, north, _ = terms(0)
        for l in range(n):
            now, next_north, south = terms(l + 1)
            y = here + below + south
            here, below, north = now, north, next_north
            stores.put(carried_w, (slice(l * two, (l + 1) * two),), y)
            stores.put(result_w, (rows8((k * n + l) * two),), y)
        stores.flush()
        return carry

    def narrow(ref, at):
        mixed = ref[pl.ds(at + p.vars, two), :]
        left = jnp.where(lower, ref[pl.ds(at, two), :], mixed)
        right = jnp.where(lower, mixed, ref[pl.ds(at + two, two), :])
        return jnp.where(in_half, left, right)

    def narrow_results(i, stores):
        stores.put(results, (rows8(low_wide * area + i * two),), narrow(result_w, i * 2 * two))

    def narrow_carried(i, stores):
        value = narrow(carried_w, i * 2 * two) + innov[rows8((low_wide - 1) * area + i * two), :]
        stores.put(carried, (rows8(lead + i * two),), value)

    def begin_adjoint(i, stores):
        stores.put(carried, (rows8(lead + i * two),), innov[rows8(whole + (p.subs - 1) * area + i * two), :])

    def scaled(k, tile, q, at):
        var = recv_ref[pl.ds((k * p.tiles + tile) * p.rows + q * two, two), :]
        return 0.5 * (var * results[at, :])

    def begin_forward(tile, stores):
        for q in range(p.lat // 2):
            at = tile * n_rows + q * two
            stores.put(carried, (rows8(lead + at),), -scaled(0, tile, q, rows8(at)))

    def near(ref, base, at, shift):
        return ref[pl.ds(base + at + lead + shift * p.vars, two), :]

    def adjoint_at(base, ref, at):
        x = near(ref, 0, at, 0)
        return (
            near(mid_c, base, at, 0) * x
            + pltpu.roll(near(east_c, base, at, 0) * x, 1, 1)
            + pltpu.roll(near(west_c, base, at, 0) * x, LANES - 1, 1)
            + near(north_c, base, at, -1) * near(ref, 0, at, -1)
            + near(south_c, base, at, 1) * near(ref, 0, at, 1)
        )

    def forward_at(base, ref, at):
        x = near(ref, 0, at, 0)
        return (
            near(mid_c, base, at, 0) * x
            + near(east_c, base, at, 0) * pltpu.roll(x, LANES - 1, 1)
            + near(west_c, base, at, 0) * pltpu.roll(x, 1, 1)
            + near(north_c, base, at, 0) * near(ref, 0, at, 1)
            + near(south_c, base, at, 0) * near(ref, 0, at, -1)
        )

    def window(one, base, last):
        for at in range(0, area + LAG * two, two):
            if at < area:
                passed[lead + at : lead + at + two, :] = one(base, carried, at)
            at -= LAG * two
            if at >= 0:
                carried[lead + at : lead + at + two, :] = last(at, one(base, passed, at))

    def adjoint_window(i, phase):
        k = p.subs - 1 - i
        into = phase * whole + k * area
        source = jnp.where(k > 0, into - area, nothing)
        stores = Stores()

        def last(at, y):
            stores.put(results, (rows8(into + at),), y)
            return y + innov[rows8(source + at), :]

        window(adjoint_at, k * area, last)
        stores.flush()
        return phase

    def forward_window(k, carry):
        base = k * area
        source = jnp.where(k < p.subs - 1, base + area, nothing)
        later = jnp.minimum(k + 1, p.subs - 1)
        stores = Stores()

        def last(at, y):
            here = rows8(base + at)
            stores.put(innov, (rows8(whole + base + at),), weight_g[here, :] * y + innov[here, :])
            return y - scaled(later, at // n_rows, at % n_rows // two, rows8(source + at))

        window(forward_at, base, last)
        stores.flush()
        return carry

    def clear_wide(i, stores):
        stores.put(carried_w, (rows8(i * two),), zero)

    def iteration(phase, carry):
        @pl.when(phase == 0)
        def _():
            looped(n, 8, clear_wide)
            lax.fori_loop(0, p.wide * STEPS, wide_step, 0)
            looped(p.wide * n // 2, 12, narrow_results)
            looped(n // 2, 12, narrow_carried)

        @pl.when(phase > 0)
        def _():
            looped(n // 2, 12, begin_adjoint)

        lax.fori_loop(jnp.where(phase == 0, p.wide, 0), p.subs, adjoint_window, phase)

        @pl.when(phase < ITERS - 1)
        def _():
            looped(p.tiles, 2, begin_forward)
            lax.fori_loop(0, p.subs, forward_window, 0)

        return carry

    lax.fori_loop(0, ITERS, iteration, 0)

    own = slice(p.margin, p.margin + p.width)

    def join(kt, stores):
        cols = []
        for v in range(p.vars):
            at = kt * n_rows + v
            early = results[pl.ds(at, p.lat, stride=p.vars), :]
            late = results[pl.ds(whole + at, p.lat, stride=p.vars), :]
            cols.append((0.5 * early + late)[:, own])
        spare = 3 * LANES - p.vars * p.width
        line = jnp.concatenate(cols + [jnp.zeros((p.lat, spare), f32)], axis=1)
        for i in range(3):
            at = (pl.ds(kt * p.lat * 3 + i, p.lat, stride=3),)
            stores.put(out_ref, at, line[:, i * LANES : (i + 1) * LANES])

    looped(p.count, 4, join)


def finish_kernel(plan, recv_ref, var_hbm, out_ref, wide, var_ref, sems):
    p = plan
    (copy,) = fetch([var_hbm], [var_ref], sems)

    def level(z, carry):
        for j in range(p.cols):
            start = (z * p.cols + j) * p.lat * 3
            rows = [recv_ref[pl.ds(start + i, p.lat, stride=3), :] for i in range(3)]
            for v in range(p.vars):
                at, end = v * p.width, (v + 1) * p.width
                col = j * p.width
                while at < end:
                    i, low = divmod(at, LANES)
                    size = min(end - at, LANES - low)
                    wide[v, z, :, col : col + size] = rows[i][:, low : low + size]
                    at, col = at + size, col + size
        return carry

    lax.fori_loop(0, p.lev, level, 0)

    copy.wait()

    def scale(v, carry):
        for low in range(0, p.lon, LANES):
            cols = slice(low, min(low + LANES, p.lon))
            got = jnp.swapaxes(wide[v, :, :, cols], 0, 1)
            out_ref[v, :, :, cols] = -0.5 * (var_ref[v, :, :, cols] * got)
        return carry

    lax.fori_loop(0, p.vars, scale, 0)


def transposed(
    plan, advect_east, advect_north, diffusion, background_var, obs_cell, obs_value, obs_weight, obs_count
):
    p = plan
    f32 = jnp.float32
    vmem = pl.BlockSpec(memory_space=pltpu.VMEM)
    params = pltpu.CompilerParams(vmem_limit_bytes=VMEM_LIMIT)

    def swap(x):
        return jnp.swapaxes(x, -3, -2)

    var = swap(background_var[0])
    anywhere = pl.BlockSpec(memory_space=pltpu.HBM)
    inputs = (
        obs_count.reshape(1, -1),
        obs_cell.reshape(1, -1),
        obs_value.reshape(1, -1),
        obs_weight.reshape(1, -1),
        swap(advect_east[0]),
        swap(advect_north[0]),
        swap(diffusion[0]),
        var,
    )
    packed = pl.pallas_call(
        functools.partial(pack_kernel, p),
        out_shape=jax.ShapeDtypeStruct((p.count * p.rows, LANES), f32),
        in_specs=[anywhere] * len(inputs),
        out_specs=anywhere,
        scratch_shapes=[
            pltpu.VMEM(((p.vars + 3) * p.lev, p.lat, 15 * LANES), f32),
            pltpu.VMEM((p.count * p.rows, LANES), f32),
        ]
        + [pltpu.VMEM(x.shape, x.dtype) for x in inputs]
        + [pltpu.SemaphoreType.DMA((len(inputs),)), pltpu.SemaphoreType.DMA((p.lev,))],
        compiler_params=pltpu.CompilerParams(vmem_limit_bytes=PACK_LIMIT),
        name="pack",
    )(*inputs)
    received = lax.all_to_all(packed.reshape(-1, 2, LANES), ("tm", "tile"), 0, 0, tiled=True)
    received = received.reshape(-1, LANES)
    wide = pltpu.VMEM((p.wide * p.pitch, 2 * p.vars, LANES), f32)
    narrow = pltpu.VMEM((p.subs * p.area + 4 * p.vars, LANES), f32)
    both = pltpu.VMEM(((ITERS * p.subs + 1) * p.area, LANES), f32)
    back = pl.pallas_call(
        functools.partial(chain_kernel, p),
        out_shape=jax.ShapeDtypeStruct((p.count * p.lat * 3, LANES), f32),
        in_specs=[vmem],
        out_specs=vmem,
        scratch_shapes=[wide] * 6
        + [
            pltpu.VMEM((p.wide * p.nlat * 2 * p.vars, LANES), f32),
            pltpu.VMEM((p.pitch * 2 * p.vars, LANES), f32),
        ]
        + [narrow] * 5
        + [
            pltpu.VMEM((p.subs * p.area, LANES), f32),
            both,
            both,
            pltpu.VMEM((p.area + 4 * p.vars, LANES), f32),
            pltpu.VMEM((p.area + 4 * p.vars, LANES), f32),
            pltpu.VMEM((9, p.count, p.tiles * p.slots), f32),
        ],
        compiler_params=params,
        name="chains",
    )(received)
    back = back.reshape(-1, 4, LANES)
    returned = lax.all_to_all(back, ("tm", "tile"), 0, 0, tiled=True)
    returned = returned.reshape(-1, LANES)
    increment = pl.pallas_call(
        functools.partial(finish_kernel, p),
        out_shape=jax.ShapeDtypeStruct(var.shape, f32),
        in_specs=[vmem, anywhere],
        out_specs=vmem,
        scratch_shapes=[
            pltpu.VMEM((p.vars, p.lev, p.lat, p.lon), f32),
            pltpu.VMEM(var.shape, f32),
            pltpu.SemaphoreType.DMA((1,)),
        ],
        compiler_params=params,
        name="finish",
    )(returned, var)
    return swap(increment)[None]


def solution(mesh):
    def run(*args):
        plan = Plan(mesh.shape, args[3].shape, args[4].shape)
        work = functools.partial(transposed, plan) if plan.fits() else per_device
        return jax.shard_map(
            work,
            mesh=mesh,
            in_specs=(
                P("tm", None, "tile", None),
                P("tm", None, "tile", None),
                P("tm", None, "tile", None),
                P("tm", None, None, "tile", None),
                P("tm", "tile", None),
                P("tm", "tile", None),
                P("tm", "tile", None),
                P("tm", "tile", None),
            ),
            out_specs=P("tm", None, None, "tile", None),
            check_vma=False,
        )(*args)

    return run
```

```python
import functools

import jax
import jax.numpy as jnp
from jax import lax
from jax.experimental import pallas as pl
from jax.experimental.pallas import tpu as pltpu
from jax.sharding import PartitionSpec as P

STEPS = 2
ITERS = 2
CHAINS = 3
LANES = 128
LAG = 12
VMEM_LIMIT = 48 * 1024 * 1024


def padded(block, sides, width):
    for axis, dim in sides:
        count = lax.axis_size(axis)
        forward = [(i, i + 1) for i in range(count - 1)]
        backward = [(target, source) for source, target in forward]
        low = lax.ppermute(
            lax.slice_in_dim(block, block.shape[dim] - width, None, axis=dim), axis, forward
        )
        high = lax.ppermute(lax.slice_in_dim(block, 0, width, axis=dim), axis, backward)
        block = jnp.concatenate([low, block, high], axis=dim)
    return block


def shifted(value, axis, steps):
    count = lax.axis_size(axis)
    first, last = (max(0, -steps), min(count, count - steps))
    return lax.ppermute(value, axis, [(source, source + steps) for source in range(first, last)])


def apply_step(field, coef, adjoint):
    east_c = coef[0]
    north_c = coef[1]
    diff_c = coef[2]
    if adjoint:
        to_east = (diff_c - 0.5 * east_c) * field
        to_west = (diff_c + 0.5 * east_c) * field
        to_north = (diff_c - 0.5 * north_c) * field
        to_south = (diff_c + 0.5 * north_c) * field
        middle = (1.0 - 4.0 * diff_c[:, 1:-1]) * field[:, :, 1:-1]
        return (
            middle
            + jnp.roll(to_east[:, :, 1:-1], 1, axis=-1)
            + jnp.roll(to_west[:, :, 1:-1], -1, axis=-1)
            + to_north[:, :, :-2]
            + to_south[:, :, 2:]
        )
    inner = field[:, :, 1:-1]
    diff_in = diff_c[:, 1:-1]
    east_in = east_c[:, 1:-1]
    north_in = north_c[:, 1:-1]
    return (
        (1.0 - 4.0 * diff_in) * inner
        + (diff_in - 0.5 * east_in) * jnp.roll(inner, -1, axis=-1)
        + (diff_in + 0.5 * east_in) * jnp.roll(inner, 1, axis=-1)
        + (diff_in - 0.5 * north_in) * field[:, :, 2:]
        + (diff_in + 0.5 * north_in) * field[:, :, :-2]
    )


def advance(field, coef, adjoint):
    for repeat in range(STEPS):
        extended = padded(field, (("tile", 2),), 1)
        field = apply_step(extended, coef, adjoint)
    return field


def per_device(
    advect_east, advect_north, diffusion, background_var, obs_cell, obs_value, obs_weight, obs_count
):
    windows_count = lax.axis_size("tm")
    tiles = lax.axis_size("tile")
    coefs = jnp.stack([advect_east[0], advect_north[0], diffusion[0]])
    coef_ext = padded(coefs, (("tile", 2),), 1)
    cells = obs_cell.reshape(tiles, -1)
    slot_count = cells.shape[1]
    live = jnp.arange(slot_count, dtype=jnp.int32)[None, :] < obs_count.reshape(tiles)[:, None]
    masked = obs_weight.reshape(tiles, -1) * live.astype(jnp.float32)
    received = lax.all_to_all(
        jnp.stack([obs_value.reshape(tiles, -1), masked]),
        "tile",
        split_axis=1,
        concat_axis=1,
        tiled=True,
    )
    received_cells = lax.all_to_all(cells, "tile", split_axis=0, concat_axis=0, tiled=True)
    departures = received[0].reshape(-1)
    obs_weights = received[1].reshape(-1)
    flat_cells = received_cells.reshape(-1)
    local_var = background_var[0]
    state_shape = local_var.shape
    cell_total = state_shape[0] * state_shape[1] * state_shape[2] * state_shape[3]
    increment = jnp.zeros(state_shape, jnp.float32)
    for iteration in range(ITERS):
        if iteration == 0:
            innov = obs_weights * (0.0 - departures)
        else:
            forward_carried = advance(increment, coef_ext, False)
            for forward_window in range(windows_count - 1):
                forward_incoming = shifted(forward_carried, "tm", 1)
                forward_carried = advance(forward_incoming + increment, coef_ext, False)
            innov = obs_weights * (
                jnp.take(forward_carried.reshape(cell_total), flat_cells, axis=0) - departures
            )
        gridded = jnp.zeros((cell_total,), jnp.float32).at[flat_cells].add(innov)
        source = gridded.reshape(state_shape)
        carried = advance(source, coef_ext, True)
        for window in range(windows_count - 1):
            incoming = shifted(carried, "tm", -1)
            carried = advance(incoming + source, coef_ext, True)
        increment = increment - 0.5 * (increment + local_var * carried)
    return increment[None]


class Plan:
    def __init__(self, mesh_shape, var_shape, slot_shape):
        self.subs, self.tiles = mesh_shape["tm"], mesh_shape["tile"]
        self.count = self.subs * self.tiles
        _, self.vars, self.lev, self.nlat, self.lon = var_shape
        self.lat = self.nlat // self.tiles
        self.slots = slot_shape[2] // self.tiles
        self.cols = self.count // self.lev
        self.width = self.lon // self.cols
        self.half = self.width // 2
        self.halo = CHAINS * STEPS * self.subs
        self.margin = (LANES - self.width) // 2
        self.extra = self.halo - self.margin
        self.span = self.width + 2 * self.halo
        self.coef_row = self.lat * self.vars
        self.obs_row = self.coef_row + 3 * self.lat
        self.rows = self.obs_row + 6
        self.pitch = self.nlat + STEPS
        self.wide = -(-self.extra // STEPS)
        self.area = self.nlat * self.vars

    def borrows(self, k):
        return (CHAINS - 1) * STEPS * self.subs + STEPS * (k + 1) > self.margin

    def fits(self):
        if self.count % self.lev or self.lon % self.cols or self.width % 2:
            return False
        for k in range(self.subs):
            spare = self.margin - STEPS * (2 * self.subs - k)
            if spare < 0 or (self.borrows(k) and spare < self.extra):
                return False
        return (
            self.half + 2 * self.halo <= LANES
            and 0 <= self.extra <= 16
            and self.vars == 4
            and self.lat % 2 == 0
            and 0 < self.wide < self.subs
            and self.tiles == 8
            and self.slots & (self.slots - 1) == 0
            and self.slots * self.tiles == 2 * LANES
            and self.width + 2 * self.margin == LANES
            and self.width % 3 == 0
            and 4 * self.width <= 3 * LANES
            and self.lat % 4 == 0
            and self.count * self.rows % 8 == 0
            and self.rows % 2 == 0
        )


def pack_kernel(
    plan, count_ref, cell_ref, value_ref, weight_ref, east_ref, north_ref, diff_ref, var_ref, out_ref, wide
):
    p = plan
    pad = 2 * LANES
    right = wide.shape[-1] - pad - p.lon
    per_level = p.vars + 3

    def fill(z, carry):
        for v in range(per_level):
            field = var_ref[v, z] if v < p.vars else (east_ref, north_ref, diff_ref)[v - p.vars][z]
            at = z * per_level + v
            wide[at, :, pad : pad + p.lon] = field
            wide[at, :, :pad] = field[:, p.lon - pad :]
            wide[at, :, pad + p.lon :] = field[:, :right]
        return carry

    lax.fori_loop(0, p.lev, fill, 0)

    lane = lax.broadcasted_iota(jnp.int32, (1, p.tiles * p.slots), 1)
    filled = jnp.zeros_like(lane)
    for t in range(p.tiles):
        filled = jnp.where(lane >= t * p.slots, count_ref[0, t], filled)
    weight = jnp.where((lane & (p.slots - 1)) < filled, weight_ref[...], 0.0)
    obs = []
    for x in (weight, weight * value_ref[...], cell_ref[...].astype(jnp.float32)):
        obs += [x[:, :LANES], x[:, LANES:]]
    obs = jnp.concatenate(obs, axis=0)
    lanes = lax.broadcasted_iota(jnp.int32, (p.lat, LANES), 1)
    borrows = jnp.where(p.borrows(lax.axis_index("tm")), p.extra, 0)

    def blocks(z, carry):
        for j in range(p.cols):
            first = pad + j * p.width - p.margin
            tile, low = divmod(first, LANES)

            def moved(a, t):
                x = wide[z * per_level + a, :, t * LANES : (t + 1) * LANES]
                return pltpu.roll(x, LANES - low, 1)

            base = (z * p.cols + j) * p.rows
            for v in range(p.vars):
                piece = jnp.where(lanes < LANES - low, moved(v, tile), moved(v, tile + 1))
                if v < 3:
                    here, after = moved(p.vars + v, tile), moved(p.vars + v, tile + 1)
                    rows = pl.ds(base + p.coef_row + v * p.lat, p.lat)
                    out_ref[rows, :] = jnp.where(lanes < LANES - low, here, after)
                    if low < p.extra:
                        here = jnp.where(lanes < LANES - low, moved(p.vars + v, tile - 1), here)
                    if low + p.extra > LANES:
                        after = jnp.where(lanes < LANES - low, after, moved(p.vars + v, tile + 2))
                    piece = jnp.where(lanes < borrows, after, piece)
                    piece = jnp.where(lanes >= LANES - borrows, here, piece)
                out_ref[pl.ds(base + v, p.lat, stride=p.vars), :] = piece
            out_ref[pl.ds(base + p.obs_row, 6), :] = obs
        return carry

    lax.fori_loop(0, p.lev, blocks, 0)


class Stores:
    def __init__(self):
        self.held = []

    def put(self, ref, at, value):
        self.held.append((ref, at, value))

    def flush(self):
        for ref, at, value in self.held:
            ref[at] = value
        self.held = []


def looped(count, unroll, body):
    def many(i, carry):
        stores = Stores()
        for u in range(unroll):
            body(i * unroll + u, stores)
        stores.flush()
        return carry

    lax.fori_loop(0, count // unroll, many, 0)


def swap_blocks(x, slots):
    size = x.shape[0]
    sub = lax.broadcasted_iota(jnp.int32, x.shape, 0)
    block = lax.broadcasted_iota(jnp.int32, x.shape, 1) >> (slots.bit_length() - 1)
    out = x
    for d in range(1, size):
        moved = pltpu.roll(pltpu.roll(x, size - d, 0), d * slots, 1)
        out = jnp.where(block == ((sub + d) & (size - 1)), moved, out)
    return out


def spread(a, b, count):
    return (
        jnp.concatenate([a[:count], b[:count]], axis=0),
        jnp.concatenate([a[count:], b[count:]], axis=0),
    )


def chain_kernel(
    plan,
    recv_ref,
    out_ref,
    mid_w,
    east_w,
    west_w,
    north_w,
    south_w,
    source_w,
    result_w,
    carried_w,
    mid_c,
    east_c,
    west_c,
    north_c,
    south_c,
    weight_g,
    innov,
    results,
    carried,
    passed,
    obs_tab,
):
    p = plan
    f32 = jnp.float32
    me = lax.axis_index("tm") * p.tiles + lax.axis_index("tile")
    level = (me // p.cols).astype(f32)
    origin = ((me % p.cols) * p.width - p.halo).astype(f32)
    two = 2 * p.vars
    shape = (two, LANES)
    sub = lax.broadcasted_iota(jnp.int32, shape, 0)
    lane = lax.broadcasted_iota(jnp.int32, shape, 1)
    lower = sub < p.vars
    in_half = lane < p.margin + p.half
    n = p.nlat
    pitch = p.pitch
    area = p.area
    whole = p.subs * area
    nothing = ITERS * whole
    lead = two
    low_wide = p.subs - p.wide
    zero = jnp.zeros(shape, f32)

    def rows8(start):
        return pl.ds(pl.multiple_of(start, two), two)

    def clear(ref, start, count):
        def body(i, carry):
            for u in range(8):
                ref[rows8(start + (i * 8 + u) * two), :] = zero
            return carry

        lax.fori_loop(0, count // (8 * two), body, 0)

    clear(innov, nothing, area)
    clear(results, nothing, area)
    for ref in (mid_c, east_c, west_c, north_c, south_c, carried, passed):
        ref[:lead, :] = zero
        ref[ref.shape[0] - lead :, :] = zero
    for k in range(p.wide):
        for l in range(n, pitch):
            for ref in (mid_w, east_w, west_w, north_w, south_w, source_w):
                ref[k * pitch + l] = zero
    for l in range(n, pitch):
        carried_w[l * two : (l + 1) * two, :] = zero

    def observe(k, stores):
        raw = []
        for i in range(6):
            raw.append(recv_ref[pl.ds(k * p.tiles * p.rows + p.obs_row + i, p.tiles, stride=p.rows), :])
        w, wy, cell = (jnp.concatenate(raw[2 * i : 2 * i + 2], axis=1) for i in range(3))
        w, wy, cell = (swap_blocks(x, p.slots) for x in (w, wy, cell))
        row = jnp.floor((cell + 0.5) * (1.0 / p.lon))
        lon = cell - row * p.lon
        group = jnp.floor((row + 0.5) * (1.0 / p.lat))
        lat = row - group * p.lat
        var = jnp.floor((group + 0.5) * (1.0 / p.lev))
        lev = group - var * p.lev
        at = lon - origin
        at = jnp.where(at < 0, at + p.lon, at)
        at = jnp.where(at >= p.lon, at - p.lon, at)
        place = at - p.extra
        here = (lev == level) & (at < p.span)
        main = here & (place >= 0) & (place < LANES)
        outside = here & ~main
        around = jnp.where(place < 0, place + LANES, place - LANES)
        rows = pl.ds(k * p.tiles, p.tiles)
        stores.put(obs_tab, (0, rows), lat * p.vars + var)
        stores.put(obs_tab, (1, rows), jnp.where(main, place, -1.0))
        stores.put(obs_tab, (2, rows), jnp.where(outside, around, -1.0))
        for i, x in ((3, w), (6, -wy)):
            one = x.astype(jnp.bfloat16).astype(f32)
            two = (x - one).astype(jnp.bfloat16).astype(f32)
            stores.put(obs_tab, (i, rows), one)
            stores.put(obs_tab, (i + 1, rows), two)
            stores.put(obs_tab, (i + 2, rows), x - one - two)

    looped(p.subs, 1, observe)

    n_rows = p.lat * p.vars
    slots = p.tiles * p.slots
    row_id = lax.broadcasted_iota(jnp.int32, (n_rows, slots), 0).astype(f32)
    lane_id = lax.broadcasted_iota(jnp.int32, (LANES, slots), 0).astype(f32)
    row_lane = lax.broadcasted_iota(jnp.int32, (n_rows, LANES), 1)

    def wide_tile(kt):
        return jnp.maximum(kt - low_wide * p.tiles, kt % p.tiles)

    def row_of(kt):
        return kt * p.lat + kt // p.tiles * STEPS

    def grid(kt, stores):
        def entry(i):
            return obs_tab[i, pl.ds(kt, 1), :]

        def factor(rows, i):
            return jnp.where(lane_id[rows] == entry(i), 1.0, 0.0).astype(jnp.bfloat16)

        def product(first, right):
            left = [jnp.where(match, entry(first + q), 0.0).astype(jnp.bfloat16) for q in range(3)]
            left = jnp.concatenate(left, axis=0)
            full = lax.dot_general(left, right, (((1,), (1,)), ((), ())), preferred_element_type=f32)
            parts = [full[q * n_rows : (q + 1) * n_rows] for q in range(3)]
            return parts[0] + (parts[1] + parts[2])

        match = row_id == entry(0)
        main = factor(slice(0, LANES), 1)
        ends = [factor(slice(0, 16), 2), jnp.zeros((LANES - 32, slots), jnp.bfloat16), factor(slice(LANES - 16, LANES), 2)]
        at = (pl.ds(pl.multiple_of(kt * n_rows, two), n_rows),)
        stores.put(weight_g, at, product(3, main))
        summed = product(6, jnp.concatenate([main] + ends, axis=0))
        inside, outside = summed[:, :LANES], summed[:, LANES:]
        stores.put(innov, at, inside)
        left = jnp.where(row_lane >= LANES - p.extra, outside, inside)
        right = jnp.where(row_lane < p.extra, outside, inside)
        tile = wide_tile(kt)
        for pair in range(p.lat // 2):
            rows = slice(two * pair, two * (pair + 1))
            one, other = spread(left[rows], right[rows], p.vars)
            stores.put(source_w, row_of(tile) + 2 * pair, one)
            stores.put(source_w, row_of(tile) + 2 * pair + 1, other)

    def derive(got):
        east, north, diff = got
        east = 0.5 * east
        north = 0.5 * north
        return 1.0 - 4.0 * diff, diff - east, diff + east, diff - north, diff + north

    def one_row(at):
        return jnp.broadcast_to(recv_ref[pl.ds(at, 1), :], shape)

    edge_mask = (lower & (lane >= LANES - p.extra)) | (~lower & (lane < p.extra))

    def widen(kt, stores):
        base = kt * p.rows
        for l in range(p.lat):
            got = []
            for c in range(3):
                main = one_row(base + p.coef_row + c * p.lat + l)
                got.append(jnp.where(edge_mask, one_row(base + l * p.vars + c), main))
            for ref, value in zip((mid_w, east_w, west_w, north_w, south_w), derive(got)):
                stores.put(ref, row_of(wide_tile(kt)) + l, value)

    def double(kt, stores):
        base = kt * p.rows + p.coef_row
        for l in range(0, p.lat, 2):
            got = []
            for c in range(3):
                at = base + c * p.lat + l
                got.append(jnp.where(lower, one_row(at), one_row(at + 1)))
            at = rows8(lead + kt * n_rows + l * p.vars)
            for ref, value in zip((mid_c, east_c, west_c, north_c, south_c), derive(got)):
                stores.put(ref, (at,), value)

    def prepare(kt, stores):
        grid(kt, stores)
        double(kt, stores)
        widen(kt, stores)

    looped(p.count, 4, prepare)

    def wide_step(i, carry):
        k = p.wide - 1 - i // STEPS
        base = k * pitch
        starts = (i % STEPS == 0).astype(f32)
        stores = Stores()

        def terms(l):
            x = carried_w[l * two : (l + 1) * two, :] + starts * source_w[base + l]
            at = base + l
            here = (
                mid_w[at] * x
                + pltpu.roll(east_w[at] * x, 1, 1)
                + pltpu.roll(west_w[at] * x, LANES - 1, 1)
            )
            return here, north_w[at] * x, south_w[at] * x

        below = zero
        here, north, _ = terms(0)
        for l in range(n):
            now, next_north, south = terms(l + 1)
            y = here + below + south
            here, below, north = now, north, next_north
            stores.put(carried_w, (slice(l * two, (l + 1) * two),), y)
            stores.put(result_w, (rows8((k * n + l) * two),), y)
        stores.flush()
        return carry

    def narrow(ref, at):
        mixed = ref[pl.ds(at + p.vars, two), :]
        left = jnp.where(lower, ref[pl.ds(at, two), :], mixed)
        right = jnp.where(lower, mixed, ref[pl.ds(at + two, two), :])
        return jnp.where(in_half, left, right)

    def narrow_results(i, stores):
        stores.put(results, (rows8(low_wide * area + i * two),), narrow(result_w, i * 2 * two))

    def narrow_carried(i, stores):
        value = narrow(carried_w, i * 2 * two) + innov[rows8((low_wide - 1) * area + i * two), :]
        stores.put(carried, (rows8(lead + i * two),), value)

    def begin_adjoint(i, stores):
        stores.put(carried, (rows8(lead + i * two),), innov[rows8(whole + (p.subs - 1) * area + i * two), :])

    def scaled(k, tile, q, at):
        var = recv_ref[pl.ds((k * p.tiles + tile) * p.rows + q * two, two), :]
        return 0.5 * (var * results[at, :])

    def begin_forward(tile, stores):
        for q in range(p.lat // 2):
            at = tile * n_rows + q * two
            stores.put(carried, (rows8(lead + at),), -scaled(0, tile, q, rows8(at)))

    def near(ref, base, at, shift):
        return ref[pl.ds(base + at + lead + shift * p.vars, two), :]

    def adjoint_at(base, ref, at):
        x = near(ref, 0, at, 0)
        return (
            near(mid_c, base, at, 0) * x
            + pltpu.roll(near(east_c, base, at, 0) * x, 1, 1)
            + pltpu.roll(near(west_c, base, at, 0) * x, LANES - 1, 1)
            + near(north_c, base, at, -1) * near(ref, 0, at, -1)
            + near(south_c, base, at, 1) * near(ref, 0, at, 1)
        )

    def forward_at(base, ref, at):
        x = near(ref, 0, at, 0)
        return (
            near(mid_c, base, at, 0) * x
            + near(east_c, base, at, 0) * pltpu.roll(x, LANES - 1, 1)
            + near(west_c, base, at, 0) * pltpu.roll(x, 1, 1)
            + near(north_c, base, at, 0) * near(ref, 0, at, 1)
            + near(south_c, base, at, 0) * near(ref, 0, at, -1)
        )

    def window(one, base, last):
        for at in range(0, area + LAG * two, two):
            if at < area:
                passed[lead + at : lead + at + two, :] = one(base, carried, at)
            at -= LAG * two
            if at >= 0:
                carried[lead + at : lead + at + two, :] = last(at, one(base, passed, at))

    def adjoint_window(i, phase):
        k = p.subs - 1 - i
        into = phase * whole + k * area
        source = jnp.where(k > 0, into - area, nothing)
        stores = Stores()

        def last(at, y):
            stores.put(results, (rows8(into + at),), y)
            return y + innov[rows8(source + at), :]

        window(adjoint_at, k * area, last)
        stores.flush()
        return phase

    def forward_window(k, carry):
        base = k * area
        source = jnp.where(k < p.subs - 1, base + area, nothing)
        later = jnp.minimum(k + 1, p.subs - 1)
        stores = Stores()

        def last(at, y):
            here = rows8(base + at)
            stores.put(innov, (rows8(whole + base + at),), weight_g[here, :] * y + innov[here, :])
            return y - scaled(later, at // n_rows, at % n_rows // two, rows8(source + at))

        window(forward_at, base, last)
        stores.flush()
        return carry

    def clear_wide(i, stores):
        stores.put(carried_w, (rows8(i * two),), zero)

    def iteration(phase, carry):
        @pl.when(phase == 0)
        def _():
            looped(n, 8, clear_wide)
            lax.fori_loop(0, p.wide * STEPS, wide_step, 0)
            looped(p.wide * n // 2, 12, narrow_results)
            looped(n // 2, 12, narrow_carried)

        @pl.when(phase > 0)
        def _():
            looped(n // 2, 12, begin_adjoint)

        lax.fori_loop(jnp.where(phase == 0, p.wide, 0), p.subs, adjoint_window, phase)

        @pl.when(phase < ITERS - 1)
        def _():
            looped(p.tiles, 2, begin_forward)
            lax.fori_loop(0, p.subs, forward_window, 0)

        return carry

    lax.fori_loop(0, ITERS, iteration, 0)

    block = n_rows // 4
    third = p.width // 3
    block_lane = lax.broadcasted_iota(jnp.int32, (block, LANES), 1)
    own = (block_lane >= p.margin) & (block_lane < p.margin + p.width)

    def join(kt, stores):
        rows = []
        for q in range(4):
            at = kt * n_rows + q * block
            rows.append(0.5 * results[pl.ds(at, block), :] + results[pl.ds(whole + at, block), :])
        for q in range(3):
            guest = pltpu.roll(rows[3], p.width - third * q, 1)
            at = (pl.ds(kt * 3 * block + q * block, block),)
            stores.put(out_ref, at, jnp.where(own, rows[q], guest))

    looped(p.count, 4, join)


def finish_kernel(plan, recv_ref, var_ref, out_ref, tiles):
    p = plan
    n_rows = p.lat * p.vars
    block = n_rows // 4
    third = p.width // 3
    lane = lax.broadcasted_iota(jnp.int32, (block, LANES), 1)

    def level(z, carry):
        for j in range(p.cols):
            start = (z * p.cols + j) * 3 * block
            for q in range(3):
                host = recv_ref[pl.ds(start + q * block, block), :]
                tiles[j * n_rows + q * block : j * n_rows + (q + 1) * block, :] = host
                guest = pltpu.roll(host, LANES - p.width + third * q, 1)
                last = guest if q == 0 else jnp.where(lane >= p.margin + third * q, guest, last)
            tiles[j * n_rows + 3 * block : (j + 1) * n_rows, :] = last
        for j in range(p.cols):
            cols = slice(j * p.width, (j + 1) * p.width)
            for v in range(p.vars):
                piece = tiles[pl.ds(j * n_rows + v, p.lat, stride=p.vars), :][:, p.margin : p.margin + p.width]
                out_ref[v, z, :, cols] = -0.5 * (var_ref[v, z, :, cols] * piece)
        return carry

    lax.fori_loop(0, p.lev, level, 0)


def transposed(
    plan, advect_east, advect_north, diffusion, background_var, obs_cell, obs_value, obs_weight, obs_count
):
    p = plan
    f32 = jnp.float32
    vmem = pl.BlockSpec(memory_space=pltpu.VMEM)
    params = pltpu.CompilerParams(vmem_limit_bytes=VMEM_LIMIT)
    var = background_var[0]
    packed = pl.pallas_call(
        functools.partial(pack_kernel, p),
        out_shape=jax.ShapeDtypeStruct((p.count * p.rows, LANES), f32),
        in_specs=[pl.BlockSpec(memory_space=pltpu.SMEM)] + [vmem] * 7,
        out_specs=vmem,
        scratch_shapes=[pltpu.VMEM(((p.vars + 3) * p.lev, p.lat, 15 * LANES), f32)],
        compiler_params=params,
        name="pack",
    )(
        obs_count.reshape(1, -1),
        obs_cell.reshape(1, -1),
        obs_value.reshape(1, -1),
        obs_weight.reshape(1, -1),
        advect_east[0],
        advect_north[0],
        diffusion[0],
        var,
    )
    received = lax.all_to_all(packed.reshape(-1, 2, LANES), ("tm", "tile"), 0, 0, tiled=True)
    received = received.reshape(-1, LANES)
    wide = pltpu.VMEM((p.wide * p.pitch, 2 * p.vars, LANES), f32)
    narrow = pltpu.VMEM((p.subs * p.area + 4 * p.vars, LANES), f32)
    both = pltpu.VMEM(((ITERS * p.subs + 1) * p.area, LANES), f32)
    back = pl.pallas_call(
        functools.partial(chain_kernel, p),
        out_shape=jax.ShapeDtypeStruct((p.count * p.lat * 3, LANES), f32),
        in_specs=[vmem],
        out_specs=vmem,
        scratch_shapes=[wide] * 6
        + [
            pltpu.VMEM((p.wide * p.nlat * 2 * p.vars, LANES), f32),
            pltpu.VMEM((p.pitch * 2 * p.vars, LANES), f32),
        ]
        + [narrow] * 5
        + [
            pltpu.VMEM((p.subs * p.area, LANES), f32),
            both,
            both,
            pltpu.VMEM((p.area + 4 * p.vars, LANES), f32),
            pltpu.VMEM((p.area + 4 * p.vars, LANES), f32),
            pltpu.VMEM((9, p.count, p.tiles * p.slots), f32),
        ],
        compiler_params=params,
        name="chains",
    )(received)
    back = back.reshape(-1, 4, LANES)
    returned = lax.all_to_all(back, ("tm", "tile"), 0, 0, tiled=True)
    returned = returned.reshape(-1, LANES)
    increment = pl.pallas_call(
        functools.partial(finish_kernel, p),
        out_shape=jax.ShapeDtypeStruct(var.shape, f32),
        in_specs=[vmem] * 2,
        out_specs=vmem,
        scratch_shapes=[pltpu.VMEM((p.cols * p.lat * p.vars, LANES), f32)],
        compiler_params=params,
        name="finish",
    )(returned, var)
    return increment[None]


def solution(mesh):
    def run(*args):
        plan = Plan(mesh.shape, args[3].shape, args[4].shape)
        work = functools.partial(transposed, plan) if plan.fits() else per_device
        return jax.shard_map(
            work,
            mesh=mesh,
            in_specs=(
                P("tm", None, "tile", None),
                P("tm", None, "tile", None),
                P("tm", None, "tile", None),
                P("tm", None, None, "tile", None),
                P("tm", "tile", None),
                P("tm", "tile", None),
                P("tm", "tile", None),
                P("tm", "tile", None),
            ),
            out_specs=P("tm", None, None, "tile", None),
            check_vma=False,
        )(*args)

    return run
```

```python
import functools

import jax
import jax.numpy as jnp
from jax import lax
from jax.experimental import pallas as pl
from jax.experimental.pallas import tpu as pltpu
from jax.sharding import PartitionSpec as P

STEPS = 2
ITERS = 2
CHAINS = 3
LANES = 128
VMEM_LIMIT = 48 * 1024 * 1024


def padded(block, sides, width):
    for axis, dim in sides:
        count = lax.axis_size(axis)
        forward = [(i, i + 1) for i in range(count - 1)]
        backward = [(target, source) for source, target in forward]
        low = lax.ppermute(
            lax.slice_in_dim(block, block.shape[dim] - width, None, axis=dim), axis, forward
        )
        high = lax.ppermute(lax.slice_in_dim(block, 0, width, axis=dim), axis, backward)
        block = jnp.concatenate([low, block, high], axis=dim)
    return block


def shifted(value, axis, steps):
    count = lax.axis_size(axis)
    first, last = (max(0, -steps), min(count, count - steps))
    return lax.ppermute(value, axis, [(source, source + steps) for source in range(first, last)])


def apply_step(field, coef, adjoint):
    east_c = coef[0]
    north_c = coef[1]
    diff_c = coef[2]
    if adjoint:
        to_east = (diff_c - 0.5 * east_c) * field
        to_west = (diff_c + 0.5 * east_c) * field
        to_north = (diff_c - 0.5 * north_c) * field
        to_south = (diff_c + 0.5 * north_c) * field
        middle = (1.0 - 4.0 * diff_c[:, 1:-1]) * field[:, :, 1:-1]
        return (
            middle
            + jnp.roll(to_east[:, :, 1:-1], 1, axis=-1)
            + jnp.roll(to_west[:, :, 1:-1], -1, axis=-1)
            + to_north[:, :, :-2]
            + to_south[:, :, 2:]
        )
    inner = field[:, :, 1:-1]
    diff_in = diff_c[:, 1:-1]
    east_in = east_c[:, 1:-1]
    north_in = north_c[:, 1:-1]
    return (
        (1.0 - 4.0 * diff_in) * inner
        + (diff_in - 0.5 * east_in) * jnp.roll(inner, -1, axis=-1)
        + (diff_in + 0.5 * east_in) * jnp.roll(inner, 1, axis=-1)
        + (diff_in - 0.5 * north_in) * field[:, :, 2:]
        + (diff_in + 0.5 * north_in) * field[:, :, :-2]
    )


def advance(field, coef, adjoint):
    for repeat in range(STEPS):
        extended = padded(field, (("tile", 2),), 1)
        field = apply_step(extended, coef, adjoint)
    return field


def per_device(
    advect_east, advect_north, diffusion, background_var, obs_cell, obs_value, obs_weight, obs_count
):
    windows_count = lax.axis_size("tm")
    tiles = lax.axis_size("tile")
    coefs = jnp.stack([advect_east[0], advect_north[0], diffusion[0]])
    coef_ext = padded(coefs, (("tile", 2),), 1)
    cells = obs_cell.reshape(tiles, -1)
    slot_count = cells.shape[1]
    live = jnp.arange(slot_count, dtype=jnp.int32)[None, :] < obs_count.reshape(tiles)[:, None]
    masked = obs_weight.reshape(tiles, -1) * live.astype(jnp.float32)
    received = lax.all_to_all(
        jnp.stack([obs_value.reshape(tiles, -1), masked]),
        "tile",
        split_axis=1,
        concat_axis=1,
        tiled=True,
    )
    received_cells = lax.all_to_all(cells, "tile", split_axis=0, concat_axis=0, tiled=True)
    departures = received[0].reshape(-1)
    obs_weights = received[1].reshape(-1)
    flat_cells = received_cells.reshape(-1)
    local_var = background_var[0]
    state_shape = local_var.shape
    cell_total = state_shape[0] * state_shape[1] * state_shape[2] * state_shape[3]
    increment = jnp.zeros(state_shape, jnp.float32)
    for iteration in range(ITERS):
        if iteration == 0:
            innov = obs_weights * (0.0 - departures)
        else:
            forward_carried = advance(increment, coef_ext, False)
            for forward_window in range(windows_count - 1):
                forward_incoming = shifted(forward_carried, "tm", 1)
                forward_carried = advance(forward_incoming + increment, coef_ext, False)
            innov = obs_weights * (
                jnp.take(forward_carried.reshape(cell_total), flat_cells, axis=0) - departures
            )
        gridded = jnp.zeros((cell_total,), jnp.float32).at[flat_cells].add(innov)
        source = gridded.reshape(state_shape)
        carried = advance(source, coef_ext, True)
        for window in range(windows_count - 1):
            incoming = shifted(carried, "tm", -1)
            carried = advance(incoming + source, coef_ext, True)
        increment = increment - 0.5 * (increment + local_var * carried)
    return increment[None]


class Plan:
    def __init__(self, mesh_shape, var_shape, slot_shape):
        self.subs, self.tiles = mesh_shape["tm"], mesh_shape["tile"]
        self.count = self.subs * self.tiles
        _, self.vars, self.lev, self.nlat, self.lon = var_shape
        self.lat = self.nlat // self.tiles
        self.slots = slot_shape[2] // self.tiles
        self.cols = self.count // self.lev
        self.width = self.lon // self.cols
        self.half = self.width // 2
        self.halo = CHAINS * STEPS * self.subs
        self.margin = (LANES - self.width) // 2
        self.extra = self.halo - self.margin
        self.span = self.width + 2 * self.halo
        self.coef_row = self.lat * self.vars
        self.obs_row = self.coef_row + 3 * self.lat
        self.rows = self.obs_row + 6
        self.pitch = self.nlat + STEPS
        self.wide = -(-self.extra // STEPS)
        self.area = self.nlat * self.vars

    def borrows(self, k):
        return (CHAINS - 1) * STEPS * self.subs + STEPS * (k + 1) > self.margin

    def fits(self):
        if self.count % self.lev or self.lon % self.cols or self.width % 2:
            return False
        for k in range(self.subs):
            spare = self.margin - STEPS * (2 * self.subs - k)
            if spare < 0 or (self.borrows(k) and spare < self.extra):
                return False
        return (
            self.half + 2 * self.halo <= LANES
            and 0 <= self.extra <= 16
            and self.vars == 4
            and self.lat % 2 == 0
            and 0 < self.wide < self.subs
            and self.tiles == 8
            and self.slots & (self.slots - 1) == 0
            and self.slots * self.tiles == 2 * LANES
            and self.width + 2 * self.margin == LANES
            and self.width * self.vars <= 3 * LANES
            and self.count * self.rows % 8 == 0
            and self.rows % 2 == 0
        )


def pack_kernel(
    plan, count_ref, cell_ref, value_ref, weight_ref, east_ref, north_ref, diff_ref, var_ref, out_ref, wide
):
    p = plan
    pad = 2 * LANES
    right = wide.shape[-1] - pad - p.lon
    per_level = p.vars + 3

    def fill(z, carry):
        for v in range(per_level):
            field = var_ref[v, z] if v < p.vars else (east_ref, north_ref, diff_ref)[v - p.vars][z]
            at = z * per_level + v
            wide[at, :, pad : pad + p.lon] = field
            wide[at, :, :pad] = field[:, p.lon - pad :]
            wide[at, :, pad + p.lon :] = field[:, :right]
        return carry

    lax.fori_loop(0, p.lev, fill, 0)

    lane = lax.broadcasted_iota(jnp.int32, (1, p.tiles * p.slots), 1)
    filled = jnp.zeros_like(lane)
    for t in range(p.tiles):
        filled = jnp.where(lane >= t * p.slots, count_ref[0, t], filled)
    weight = jnp.where((lane & (p.slots - 1)) < filled, weight_ref[...], 0.0)
    obs = []
    for x in (weight, weight * value_ref[...], cell_ref[...].astype(jnp.float32)):
        obs += [x[:, :LANES], x[:, LANES:]]
    obs = jnp.concatenate(obs, axis=0)
    lanes = lax.broadcasted_iota(jnp.int32, (p.lat, LANES), 1)
    borrows = jnp.where(p.borrows(lax.axis_index("tm")), p.extra, 0)

    def blocks(z, carry):
        for j in range(p.cols):
            first = pad + j * p.width - p.margin
            tile, low = divmod(first, LANES)

            def moved(a, t):
                x = wide[z * per_level + a, :, t * LANES : (t + 1) * LANES]
                return pltpu.roll(x, LANES - low, 1)

            base = (z * p.cols + j) * p.rows
            for v in range(p.vars):
                piece = jnp.where(lanes < LANES - low, moved(v, tile), moved(v, tile + 1))
                if v < 3:
                    here, after = moved(p.vars + v, tile), moved(p.vars + v, tile + 1)
                    rows = pl.ds(base + p.coef_row + v * p.lat, p.lat)
                    out_ref[rows, :] = jnp.where(lanes < LANES - low, here, after)
                    if low < p.extra:
                        here = jnp.where(lanes < LANES - low, moved(p.vars + v, tile - 1), here)
                    if low + p.extra > LANES:
                        after = jnp.where(lanes < LANES - low, after, moved(p.vars + v, tile + 2))
                    piece = jnp.where(lanes < borrows, after, piece)
                    piece = jnp.where(lanes >= LANES - borrows, here, piece)
                out_ref[pl.ds(base + v, p.lat, stride=p.vars), :] = piece
            out_ref[pl.ds(base + p.obs_row, 6), :] = obs
        return carry

    lax.fori_loop(0, p.lev, blocks, 0)


class Stores:
    def __init__(self):
        self.held = []

    def put(self, ref, at, value):
        self.held.append((ref, at, value))

    def flush(self):
        for ref, at, value in self.held:
            ref[at] = value
        self.held = []


def looped(count, unroll, body):
    def many(i, carry):
        stores = Stores()
        for u in range(unroll):
            body(i * unroll + u, stores)
        stores.flush()
        return carry

    lax.fori_loop(0, count // unroll, many, 0)


def swap_blocks(x, slots):
    size = x.shape[0]
    sub = lax.broadcasted_iota(jnp.int32, x.shape, 0)
    block = lax.broadcasted_iota(jnp.int32, x.shape, 1) >> (slots.bit_length() - 1)
    out = x
    for d in range(1, size):
        moved = pltpu.roll(pltpu.roll(x, size - d, 0), d * slots, 1)
        out = jnp.where(block == ((sub + d) & (size - 1)), moved, out)
    return out


def spread(a, b, count):
    return (
        jnp.concatenate([a[:count], b[:count]], axis=0),
        jnp.concatenate([a[count:], b[count:]], axis=0),
    )


def chain_kernel(
    plan,
    recv_ref,
    out_ref,
    mid_w,
    east_w,
    west_w,
    north_w,
    south_w,
    source_w,
    result_w,
    carried_w,
    mid_c,
    east_c,
    west_c,
    north_c,
    south_c,
    weight_g,
    innov,
    results,
    carried,
    obs_tab,
):
    p = plan
    f32 = jnp.float32
    me = lax.axis_index("tm") * p.tiles + lax.axis_index("tile")
    level = (me // p.cols).astype(f32)
    origin = ((me % p.cols) * p.width - p.halo).astype(f32)
    two = 2 * p.vars
    shape = (two, LANES)
    sub = lax.broadcasted_iota(jnp.int32, shape, 0)
    lane = lax.broadcasted_iota(jnp.int32, shape, 1)
    lower = sub < p.vars
    in_half = lane < p.margin + p.half
    n = p.nlat
    pitch = p.pitch
    area = p.area
    whole = p.subs * area
    nothing = ITERS * whole
    lead = two
    low_wide = p.subs - p.wide
    zero = jnp.zeros(shape, f32)

    def rows8(start):
        return pl.ds(pl.multiple_of(start, two), two)

    def clear(ref, start, count):
        def body(i, carry):
            for u in range(8):
                ref[rows8(start + (i * 8 + u) * two), :] = zero
            return carry

        lax.fori_loop(0, count // (8 * two), body, 0)

    clear(innov, nothing, area)
    clear(results, nothing, area)
    for ref in (mid_c, east_c, west_c, north_c, south_c, carried):
        ref[:lead, :] = zero
        ref[ref.shape[0] - lead :, :] = zero
    for k in range(p.wide):
        for l in range(n, pitch):
            for ref in (mid_w, east_w, west_w, north_w, south_w, source_w):
                ref[k * pitch + l] = zero
    for l in range(n, pitch):
        carried_w[l * two : (l + 1) * two, :] = zero

    def observe(k, stores):
        raw = []
        for i in range(6):
            raw.append(recv_ref[pl.ds(k * p.tiles * p.rows + p.obs_row + i, p.tiles, stride=p.rows), :])
        w, wy, cell = (jnp.concatenate(raw[2 * i : 2 * i + 2], axis=1) for i in range(3))
        w, wy, cell = (swap_blocks(x, p.slots) for x in (w, wy, cell))
        row = jnp.floor((cell + 0.5) * (1.0 / p.lon))
        lon = cell - row * p.lon
        group = jnp.floor((row + 0.5) * (1.0 / p.lat))
        lat = row - group * p.lat
        var = jnp.floor((group + 0.5) * (1.0 / p.lev))
        lev = group - var * p.lev
        at = lon - origin
        at = jnp.where(at < 0, at + p.lon, at)
        at = jnp.where(at >= p.lon, at - p.lon, at)
        place = at - p.extra
        here = (lev == level) & (at < p.span)
        main = here & (place >= 0) & (place < LANES)
        outside = here & ~main
        around = jnp.where(place < 0, place + LANES, place - LANES)
        rows = pl.ds(k * p.tiles, p.tiles)
        stores.put(obs_tab, (0, rows), lat * p.vars + var)
        stores.put(obs_tab, (1, rows), jnp.where(main, place, -1.0))
        stores.put(obs_tab, (2, rows), jnp.where(outside, around, -1.0))
        for i, x in ((3, w), (6, -wy)):
            one = x.astype(jnp.bfloat16).astype(f32)
            two = (x - one).astype(jnp.bfloat16).astype(f32)
            stores.put(obs_tab, (i, rows), one)
            stores.put(obs_tab, (i + 1, rows), two)
            stores.put(obs_tab, (i + 2, rows), x - one - two)

    looped(p.subs, 2, observe)

    n_rows = p.lat * p.vars
    slots = p.tiles * p.slots
    row_id = lax.broadcasted_iota(jnp.int32, (n_rows, slots), 0).astype(f32)
    lane_id = lax.broadcasted_iota(jnp.int32, (LANES, slots), 0).astype(f32)
    row_lane = lax.broadcasted_iota(jnp.int32, (n_rows, LANES), 1)

    def wide_tile(kt):
        return jnp.maximum(kt - low_wide * p.tiles, kt % p.tiles)

    def row_of(kt):
        return kt * p.lat + kt // p.tiles * STEPS

    def grid(kt, stores):
        def entry(i):
            return obs_tab[i, pl.ds(kt, 1), :]

        def factor(rows, i):
            return jnp.where(lane_id[rows] == entry(i), 1.0, 0.0).astype(jnp.bfloat16)

        def product(first, right):
            left = [jnp.where(match, entry(first + q), 0.0).astype(jnp.bfloat16) for q in range(3)]
            left = jnp.concatenate(left, axis=0)
            full = lax.dot_general(left, right, (((1,), (1,)), ((), ())), preferred_element_type=f32)
            parts = [full[q * n_rows : (q + 1) * n_rows] for q in range(3)]
            return parts[0] + (parts[1] + parts[2])

        match = row_id == entry(0)
        main = factor(slice(0, LANES), 1)
        ends = [factor(slice(0, 16), 2), jnp.zeros((LANES - 32, slots), jnp.bfloat16), factor(slice(LANES - 16, LANES), 2)]
        at = (pl.ds(pl.multiple_of(kt * n_rows, two), n_rows),)
        stores.put(weight_g, at, product(3, main))
        summed = product(6, jnp.concatenate([main] + ends, axis=0))
        inside, outside = summed[:, :LANES], summed[:, LANES:]
        stores.put(innov, at, inside)
        left = jnp.where(row_lane >= LANES - p.extra, outside, inside)
        right = jnp.where(row_lane < p.extra, outside, inside)
        tile = wide_tile(kt)
        for pair in range(p.lat // 2):
            rows = slice(two * pair, two * (pair + 1))
            one, other = spread(left[rows], right[rows], p.vars)
            stores.put(source_w, row_of(tile) + 2 * pair, one)
            stores.put(source_w, row_of(tile) + 2 * pair + 1, other)

    def derive(got):
        east, north, diff = got
        east = 0.5 * east
        north = 0.5 * north
        return 1.0 - 4.0 * diff, diff - east, diff + east, diff - north, diff + north

    def one_row(at):
        return jnp.broadcast_to(recv_ref[pl.ds(at, 1), :], shape)

    edge_mask = (lower & (lane >= LANES - p.extra)) | (~lower & (lane < p.extra))

    def widen(kt, stores):
        base = kt * p.rows
        for l in range(p.lat):
            got = []
            for c in range(3):
                main = one_row(base + p.coef_row + c * p.lat + l)
                got.append(jnp.where(edge_mask, one_row(base + l * p.vars + c), main))
            for ref, value in zip((mid_w, east_w, west_w, north_w, south_w), derive(got)):
                stores.put(ref, row_of(wide_tile(kt)) + l, value)

    def double(kt, stores):
        base = kt * p.rows + p.coef_row
        for l in range(0, p.lat, 2):
            got = []
            for c in range(3):
                at = base + c * p.lat + l
                got.append(jnp.where(lower, one_row(at), one_row(at + 1)))
            at = rows8(lead + kt * n_rows + l * p.vars)
            for ref, value in zip((mid_c, east_c, west_c, north_c, south_c), derive(got)):
                stores.put(ref, (at,), value)

    def prepare(kt, stores):
        grid(kt, stores)
        double(kt, stores)
        widen(kt, stores)

    looped(p.count, 8, prepare)

    def wide_step(i, carry):
        k = p.wide - 1 - i // STEPS
        base = k * pitch
        starts = (i % STEPS == 0).astype(f32)
        stores = Stores()

        def terms(l):
            x = carried_w[l * two : (l + 1) * two, :] + starts * source_w[base + l]
            at = base + l
            here = (
                mid_w[at] * x
                + pltpu.roll(east_w[at] * x, 1, 1)
                + pltpu.roll(west_w[at] * x, LANES - 1, 1)
            )
            return here, north_w[at] * x, south_w[at] * x

        below = zero
        here, north, _ = terms(0)
        for l in range(n):
            now, next_north, south = terms(l + 1)
            y = here + below + south
            here, below, north = now, north, next_north
            stores.put(carried_w, (slice(l * two, (l + 1) * two),), y)
            stores.put(result_w, (rows8((k * n + l) * two),), y)
        stores.flush()
        return carry

    def narrow(ref, at):
        mixed = ref[pl.ds(at + p.vars, two), :]
        left = jnp.where(lower, ref[pl.ds(at, two), :], mixed)
        right = jnp.where(lower, mixed, ref[pl.ds(at + two, two), :])
        return jnp.where(in_half, left, right)

    def narrow_results(i, stores):
        stores.put(results, (rows8(low_wide * area + i * two),), narrow(result_w, i * 2 * two))

    def narrow_carried(i, stores):
        value = narrow(carried_w, i * 2 * two) + innov[rows8((low_wide - 1) * area + i * two), :]
        stores.put(carried, (rows8(lead + i * two),), value)

    def begin_adjoint(i, stores):
        stores.put(carried, (rows8(lead + i * two),), innov[rows8(whole + (p.subs - 1) * area + i * two), :])

    def scaled(k, tile, q, at):
        var = recv_ref[pl.ds((k * p.tiles + tile) * p.rows + q * two, two), :]
        return 0.5 * (var * results[at, :])

    def begin_forward(tile, stores):
        for q in range(p.lat // 2):
            at = tile * n_rows + q * two
            stores.put(carried, (rows8(lead + at),), -scaled(0, tile, q, rows8(at)))

    def near(ref, base, at, shift):
        return ref[pl.ds(base + at + lead + shift * p.vars, two), :]

    def adjoint_step(i, phase):
        k = p.subs - 1 - i // STEPS
        base = k * area
        into = phase * whole + base
        ends = (i % STEPS == STEPS - 1) & (k > 0)
        source = jnp.where(ends, into - area, nothing)
        stores = Stores()
        for at in range(0, area, two):
            x = near(carried, 0, at, 0)
            y = (
                near(mid_c, base, at, 0) * x
                + pltpu.roll(near(east_c, base, at, 0) * x, 1, 1)
                + pltpu.roll(near(west_c, base, at, 0) * x, LANES - 1, 1)
                + near(north_c, base, at, -1) * near(carried, 0, at, -1)
                + near(south_c, base, at, 1) * near(carried, 0, at, 1)
            )
            stores.put(results, (rows8(into + at),), y)
            stores.put(carried, (slice(lead + at, lead + at + two),), y + innov[rows8(source + at), :])
        stores.flush()
        return phase

    def forward_step(i, carry):
        k = i // STEPS
        base = k * area
        ends = (i % STEPS == STEPS - 1) & (k < p.subs - 1)
        source = jnp.where(ends, base + area, nothing)
        later = jnp.minimum(k + 1, p.subs - 1)
        stores = Stores()
        for at in range(0, area, two):
            x = near(carried, 0, at, 0)
            y = (
                near(mid_c, base, at, 0) * x
                + near(east_c, base, at, 0) * pltpu.roll(x, LANES - 1, 1)
                + near(west_c, base, at, 0) * pltpu.roll(x, 1, 1)
                + near(north_c, base, at, 0) * near(carried, 0, at, 1)
                + near(south_c, base, at, 0) * near(carried, 0, at, -1)
            )
            here = rows8(base + at)
            stores.put(innov, (rows8(whole + base + at),), weight_g[here, :] * y + innov[here, :])
            force = scaled(later, at // n_rows, at % n_rows // two, rows8(source + at))
            stores.put(carried, (slice(lead + at, lead + at + two),), y - force)
        stores.flush()
        return carry

    def clear_wide(i, stores):
        stores.put(carried_w, (rows8(i * two),), zero)

    def iteration(phase, carry):
        @pl.when(phase == 0)
        def _():
            looped(n, 8, clear_wide)
            lax.fori_loop(0, p.wide * STEPS, wide_step, 0)
            looped(p.wide * n // 2, 12, narrow_results)
            looped(n // 2, 12, narrow_carried)

        @pl.when(phase > 0)
        def _():
            looped(n // 2, 12, begin_adjoint)

        lax.fori_loop(jnp.where(phase == 0, p.wide * STEPS, 0), p.subs * STEPS, adjoint_step, phase)

        @pl.when(phase < ITERS - 1)
        def _():
            looped(p.tiles, 2, begin_forward)
            lax.fori_loop(0, p.subs * STEPS, forward_step, 0)

        return carry

    lax.fori_loop(0, ITERS, iteration, 0)

    own = slice(p.margin, p.margin + p.width)

    def join(kt, stores):
        cols = []
        for v in range(p.vars):
            at = kt * n_rows + v
            early = results[pl.ds(at, p.lat, stride=p.vars), :]
            late = results[pl.ds(whole + at, p.lat, stride=p.vars), :]
            cols.append((0.5 * early + late)[:, own])
        spare = 3 * LANES - p.vars * p.width
        line = jnp.concatenate(cols + [jnp.zeros((p.lat, spare), f32)], axis=1)
        for i in range(3):
            at = (pl.ds(kt * p.lat * 3 + i, p.lat, stride=3),)
            stores.put(out_ref, at, line[:, i * LANES : (i + 1) * LANES])

    looped(p.count, 4, join)


def finish_kernel(plan, recv_ref, var_ref, out_ref):
    p = plan

    def level(z, carry):
        for j in range(p.cols):
            start = (z * p.cols + j) * p.lat * 3
            rows = [recv_ref[pl.ds(start + i, p.lat, stride=3), :] for i in range(3)]
            for v in range(p.vars):
                at, end = v * p.width, (v + 1) * p.width
                col = j * p.width
                while at < end:
                    i, low = divmod(at, LANES)
                    size = min(end - at, LANES - low)
                    cols = slice(col, col + size)
                    scale = -0.5 * var_ref[v, z, :, cols]
                    out_ref[v, z, :, cols] = scale * rows[i][:, low : low + size]
                    at, col = at + size, col + size
        return carry

    lax.fori_loop(0, p.lev, level, 0)


def transposed(
    plan, advect_east, advect_north, diffusion, background_var, obs_cell, obs_value, obs_weight, obs_count
):
    p = plan
    f32 = jnp.float32
    vmem = pl.BlockSpec(memory_space=pltpu.VMEM)
    params = pltpu.CompilerParams(vmem_limit_bytes=VMEM_LIMIT)
    var = background_var[0]
    packed = pl.pallas_call(
        functools.partial(pack_kernel, p),
        out_shape=jax.ShapeDtypeStruct((p.count * p.rows, LANES), f32),
        in_specs=[pl.BlockSpec(memory_space=pltpu.SMEM)] + [vmem] * 7,
        out_specs=vmem,
        scratch_shapes=[pltpu.VMEM(((p.vars + 3) * p.lev, p.lat, 15 * LANES), f32)],
        compiler_params=params,
        name="pack",
    )(
        obs_count.reshape(1, -1),
        obs_cell.reshape(1, -1),
        obs_value.reshape(1, -1),
        obs_weight.reshape(1, -1),
        advect_east[0],
        advect_north[0],
        diffusion[0],
        var,
    )
    received = lax.all_to_all(packed.reshape(-1, 2, LANES), ("tm", "tile"), 0, 0, tiled=True)
    received = received.reshape(-1, LANES)
    wide = pltpu.VMEM((p.wide * p.pitch, 2 * p.vars, LANES), f32)
    narrow = pltpu.VMEM((p.subs * p.area + 4 * p.vars, LANES), f32)
    both = pltpu.VMEM(((ITERS * p.subs + 1) * p.area, LANES), f32)
    back = pl.pallas_call(
        functools.partial(chain_kernel, p),
        out_shape=jax.ShapeDtypeStruct((p.count * p.lat * 3, LANES), f32),
        in_specs=[vmem],
        out_specs=vmem,
        scratch_shapes=[wide] * 6
        + [
            pltpu.VMEM((p.wide * p.nlat * 2 * p.vars, LANES), f32),
            pltpu.VMEM((p.pitch * 2 * p.vars, LANES), f32),
        ]
        + [narrow] * 5
        + [
            pltpu.VMEM((p.subs * p.area, LANES), f32),
            both,
            both,
            pltpu.VMEM((p.area + 4 * p.vars, LANES), f32),
            pltpu.VMEM((9, p.count, p.tiles * p.slots), f32),
        ],
        compiler_params=params,
        name="chains",
    )(received)
    back = back.reshape(-1, 4, LANES)
    returned = lax.all_to_all(back, ("tm", "tile"), 0, 0, tiled=True)
    returned = returned.reshape(-1, LANES)
    increment = pl.pallas_call(
        functools.partial(finish_kernel, p),
        out_shape=jax.ShapeDtypeStruct(var.shape, f32),
        in_specs=[vmem] * 2,
        out_specs=vmem,
        compiler_params=params,
        name="finish",
    )(returned, var)
    return increment[None]


def solution(mesh):
    def run(*args):
        plan = Plan(mesh.shape, args[3].shape, args[4].shape)
        work = functools.partial(transposed, plan) if plan.fits() else per_device
        return jax.shard_map(
            work,
            mesh=mesh,
            in_specs=(
                P("tm", None, "tile", None),
                P("tm", None, "tile", None),
                P("tm", None, "tile", None),
                P("tm", None, None, "tile", None),
                P("tm", "tile", None),
                P("tm", "tile", None),
                P("tm", "tile", None),
                P("tm", "tile", None),
            ),
            out_specs=P("tm", None, None, "tile", None),
            check_vma=False,
        )(*args)

    return run
```
